128 devices in a mesh: dp: 4 (over x), expert: 32 (over z, y, core).
Axes of the slice: x: 4, y: 4, z: 4, core: 2. Of those that a mesh axis runs over, the one named last changes fastest.
Arguments:
- tokens: bfloat16 [16384, 1536], P(('dp', 'expert')), may hold values from -6 to 6
- segments: int32 [128, 128], P(('dp', 'expert')), may hold values from 0 to 3, never falling along the last dimension, each value on 1 to 96 neighbouring positions
- route_ids: int32 [2, 16384, 4], P(None, ('dp', 'expert')), may hold values from 0 to 31, all different within a row; in each aligned block of 128 rows (0 to 127, 128 to 255, ..., all dimensions but the last counted through in order) at most 24 rows name the same one
- w_query: bfloat16 [2, 1536, 1536], P(None, ('dp', 'expert')), may hold values from -0.15625 to 0.15625
- key_projection: bfloat16 [2, 1536, 256], P(None, ('dp', 'expert')), may hold values from -0.15625 to 0.15625
- value_projection: bfloat16 [2, 1536, 256], P(None, ('dp', 'expert')), may hold values from -0.15625 to 0.15625
- w_out: bfloat16 [2, 1536, 1536], P(None, ('dp', 'expert')), may hold values from -0.4375 to 0.4375
- w_router: bfloat16 [2, 1536, 32], P(None, ('dp', 'expert')), may hold values from -0.078125 to 0.078125
- gain_attn: bfloat16 [2, 1536], P(None, ('dp', 'expert')), may hold values from 0.5 to 1.5
- gain_moe: bfloat16 [2, 1536], P(None, ('dp', 'expert')), may hold values from 0.5 to 1.5
- w_gate: bfloat16 [2, 32, 1536, 768], P(None, 'expert', 'dp'), may hold values from -0.15625 to 0.15625
- w_up: bfloat16 [2, 32, 1536, 768], P(None, 'expert', 'dp'), may hold values from -0.15625 to 0.15625
- w_down: bfloat16 [2, 32, 1536, 768], P(None, 'expert', 'dp'), may hold values from -0.875 to 0.875
- cotangent: bfloat16 [16384, 1536], P(('dp', 'expert')), may hold values from -6 to 6
Outputs:
- activations: float32 [16384, 1536], P(('dp', 'expert'))
- grad_tokens: float32 [16384, 1536], P(('dp', 'expert'))
- grad_w_query: float32 [2, 1536, 1536], P(None, ('dp', 'expert'))
- grad_w_key: float32 [2, 1536, 256], P(None, ('dp', 'expert'))
- grad_w_value: float32 [2, 1536, 256], P(None, ('dp', 'expert'))
- grad_w_out: float32 [2, 1536, 1536], P(None, ('dp', 'expert'))
- grad_w_router: float32 [2, 1536, 32], P(None, ('dp', 'expert'))
- grad_gain_attn: float32 [2, 1536], P(None, ('dp', 'expert'))
- grad_gain_moe: float32 [2, 1536], P(None, ('dp', 'expert'))
- grad_w_gate: float32 [2, 32, 1536, 768], P(None, 'expert', 'dp')
- grad_w_up: float32 [2, 32, 1536, 768], P(None, 'expert', 'dp')
- grad_w_down: float32 [2, 32, 1536, 768], P(None, 'expert', 'dp')
The draws below stay inside these ranges and needn't reach their ends.
Inputs may be any that keep to these rules, and one draw needn't show every extreme that they name: `route_ids`: each row names 4 different experts. Among the rows of one device in one layer no expert is named by more than 24 rows, a bound that some block reaches. `segments`: within each sequence segment numbers never fall; a segment covers at most three quarters of the sequence.
All inputs are finite; a program needn't handle non-finite values.
Results may differ from the reference program's by a relative error of at most 0.025.
Values may be sent and summed in bfloat16 or wider, within the bound.
A program may use at most 320 MiB of HBM per device.

```python
import math
import jax
import jax.numpy as jnp
import numpy as np
from jax import lax

MODEL_DIMENSION = 1536
QUERY_HEADS = 12
KEY_VALUE_HEADS = 2
HEAD_DIMENSION = 128
FF = 768
TOP = 4
LAYER_COUNT = 2
TOKENS_PER_CARD = 128
EXPERTS = 32
SEQS = 128
TOKENS = 16384
C = 24


def block_scale(key, dims, pieces, least, high):
    level = 1.0
    for dim, blocks in pieces:
        draws = jax.random.uniform(jax.random.fold_in(jax.random.fold_in(key, 6), dim), (blocks,), jnp.float32, least / len(pieces), high / len(pieces))
        level = level * jnp.repeat(jnp.exp(draws), dims[dim] // blocks).reshape((-1,) + (1,) * (len(dims) - 1 - dim))
    return level


def split_up(count, total, bound, slope):
    portions = [(1 << 20) // math.isqrt(rank ** slope) + 1 for rank in range(2, count + 1)]
    surplus, counts = total - bound - (count - 1), [1] * (count - 1)
    while surplus > 0:
        candidates = [i for i in range(count - 1) if counts[i] < bound]
        pool, budget = sum([portions[i] for i in candidates]), surplus
        for i in candidates:
            addition = min(bound - counts[i], max(1, budget * portions[i] // pool), surplus)
            counts[i] = counts[i] + addition
            surplus = surplus - addition
    return np.array([bound] + counts)


def ragged(key, amount, total, most, slope):
    if amount == 2:
        one = jax.random.randint(key, (), max(1, total - most), min(most, total - 1) + 1)
        return jnp.stack([one, total - one])
    tallies = jnp.asarray(split_up(amount, total, most, slope), jnp.int32)
    pairs = (amount - 1) // 2
    giver, sink = tallies[1:1 + 2 * pairs:2], tallies[2:2 + 2 * pairs:2]
    margin = jnp.minimum(giver - 1, most - sink)
    moved = jax.random.randint(jax.random.fold_in(key, 1), (pairs,), 0, 1 << 20) % (margin + 1)
    tallies = tallies.at[1:1 + 2 * pairs:2].set(giver - moved).at[2:2 + 2 * pairs:2].set(sink + moved)
    return tallies[jax.random.permutation(jax.random.fold_in(key, 2), amount)]


def assign_block(stream_key, own, number, rows, count, top, reach, skew):
    ranking = jax.random.permutation(stream_key, count)
    packed, usual = portions_of(count, rows * top, reach, skew, True), portions_of(count, rows * top, reach, skew, False)
    places = jnp.arange(count)

    def named(lengths, offset_by):
        used = int((lengths > 0).sum())
        fixed = max(1, used // 4)
        shifted = fixed + (places - fixed + offset_by * (used - fixed)) % max(1, count - fixed)
        return jnp.zeros((count,), jnp.int32).at[ranking[jnp.where(places < fixed, places, shifted)]].set(jnp.asarray(lengths, jnp.int32))

    lengths = jnp.where(number % 4 == 0, named(packed, number // 4), named(usual, number - number // 4 - 1))
    mixed = jax.random.permutation(jax.random.fold_in(own, 3), count)
    source_of, sink = mixed[0:count // 2 * 2:2], mixed[1:count // 2 * 2:2]
    margin = jnp.minimum(lengths[source_of] - 1, reach - lengths[sink]) // 2
    margin = jnp.where((source_of == ranking[0]) | (sink == ranking[0]) | (lengths[sink] == 0), 0, jnp.maximum(margin, 0))
    shifted = jax.random.randint(jax.random.fold_in(own, 4), (count // 2,), 0, 1 << 20) % (margin + 1)
    lengths = lengths.at[source_of].add(-shifted).at[sink].add(shifted)
    members = jnp.searchsorted(jnp.cumsum(lengths), jnp.arange(rows * top), side="right").astype(jnp.int32)
    grid = members.reshape(top, rows).T
    grid = grid[jax.random.permutation(jax.random.fold_in(own, 1), rows)]
    offset_by = jax.random.randint(jax.random.fold_in(own, 2), (rows, 1), 0, top)
    return jnp.take_along_axis(grid, (jnp.arange(top)[None, :] + offset_by) % top, axis=1)


def portions_of(count, total, most, lean, full):
    loads = [(1 << 20) // math.isqrt(grade ** lean) + 1 for grade in range(1, count + 1)]
    largest = most if full else min(most, max(-(-total // count), total * loads[0] // sum(loads)))
    least = 1 if total - largest >= count - 1 else 0
    counts, spare = [largest] + [least] * (count - 1), total - largest - least * (count - 1)
    while spare > 0:
        movable = [i for i in range(1, count) if counts[i] < largest] or [i for i in range(1, count) if counts[i] < most]
        pool, remaining = sum([loads[i] for i in movable]), spare
        for i in movable:
            addition = min(most - counts[i], max(1, remaining * loads[i] // pool), spare)
            counts[i] = counts[i] + addition
            spare = spare - addition
    return np.array(counts)


def centred(key, shape, width, bound, pieces=(), kind=jnp.bfloat16):
    drawn = width * jax.random.normal(key, shape, jnp.float32)
    if pieces:
        drawn = drawn * block_scale(key, shape, pieces, -0.22, 0.18)
    return jnp.clip(drawn, -bound, bound).astype(kind)


def setup_inputs(seed: int = 0) -> dict:
    arg_keys = jax.random.split(jax.random.key(seed), 15)
    tokens = centred(arg_keys[0], (TOKENS, MODEL_DIMENSION), 1.0, 6.0, ((0, 128),))
    segments = jax.vmap(lambda own: jnp.searchsorted(jnp.cumsum(ragged(own, max(2, TOKENS_PER_CARD // 32), TOKENS_PER_CARD, 3 * TOKENS_PER_CARD // 4, 1)), jnp.arange(TOKENS_PER_CARD), side="right"))(jax.random.split(arg_keys[1], SEQS)).reshape((SEQS, TOKENS_PER_CARD)).astype(jnp.int32)
    route_ids_keys = jax.random.split(jax.random.fold_in(arg_keys[2], 1), LAYER_COUNT * TOKENS // TOKENS_PER_CARD)
    route_ids_turns = jax.random.permutation(jax.random.fold_in(arg_keys[2], 3), LAYER_COUNT * TOKENS // TOKENS_PER_CARD)
    route_ids = jax.vmap(lambda own, number: assign_block(jax.random.fold_in(arg_keys[2], 2), own, number, TOKENS_PER_CARD, EXPERTS, TOP, C, 1))(route_ids_keys, route_ids_turns).reshape((LAYER_COUNT, TOKENS, TOP))
    w_query = centred(arg_keys[3], (LAYER_COUNT, MODEL_DIMENSION, QUERY_HEADS * HEAD_DIMENSION), MODEL_DIMENSION ** -0.5, 0.15625, ((1, 128),))
    key_projection = centred(arg_keys[4], (LAYER_COUNT, MODEL_DIMENSION, KEY_VALUE_HEADS * HEAD_DIMENSION), MODEL_DIMENSION ** -0.5, 0.15625, ((1, 128),))
    value_projection = centred(arg_keys[5], (LAYER_COUNT, MODEL_DIMENSION, KEY_VALUE_HEADS * HEAD_DIMENSION), MODEL_DIMENSION ** -0.5, 0.15625, ((1, 128),))
    w_out = centred(arg_keys[6], (LAYER_COUNT, MODEL_DIMENSION, QUERY_HEADS * HEAD_DIMENSION), (QUERY_HEADS * HEAD_DIMENSION // 8) ** -0.5, 0.4375, ((1, 128),))
    w_router = centred(arg_keys[7], (LAYER_COUNT, MODEL_DIMENSION, EXPERTS), (4 * MODEL_DIMENSION) ** -0.5, 0.078125, ((1, 128),))
    gain_attn = jnp.clip(1.0 + 0.1 * jax.random.normal(arg_keys[8], (LAYER_COUNT, MODEL_DIMENSION), jnp.float32), 0.5, 1.5).astype(jnp.bfloat16)
    gain_moe = jnp.clip(1.0 + 0.1 * jax.random.normal(arg_keys[9], (LAYER_COUNT, MODEL_DIMENSION), jnp.float32), 0.5, 1.5).astype(jnp.bfloat16)
    w_gate = centred(arg_keys[10], (LAYER_COUNT, EXPERTS, MODEL_DIMENSION, FF), MODEL_DIMENSION ** -0.5, 0.15625, ((1, 32), (2, 4)))
    w_up = centred(arg_keys[11], (LAYER_COUNT, EXPERTS, MODEL_DIMENSION, FF), MODEL_DIMENSION ** -0.5, 0.15625, ((1, 32), (2, 4)))
    w_down = centred(arg_keys[12], (LAYER_COUNT, EXPERTS, MODEL_DIMENSION, FF), (FF // 16) ** -0.5, 0.875, ((1, 32), (2, 4)))
    cotangent = centred(arg_keys[13], (TOKENS, MODEL_DIMENSION), 1.0, 6.0, ((0, 128),))
    return {"tokens": tokens, "segments": segments, "route_ids": route_ids, "w_query": w_query, "key_projection": key_projection, "value_projection": value_projection, "w_out": w_out, "w_router": w_router, "gain_attn": gain_attn, "gain_moe": gain_moe, "w_gate": w_gate, "w_up": w_up, "w_down": w_down, "cotangent": cotangent}


highest_precision = lax.Precision.HIGHEST
theta_base = 1000000.0
norm_eps = 1e-06

@jax.custom_vjp
def lower_precision(v):
    return lax.optimization_barrier(v.astype(jnp.bfloat16)).astype(jnp.float32)

@jax.custom_vjp
def lower_precision_backward(v):
    return v

def low_keep(v):
    return (lower_precision(v), None)

def low_pass(kept, grad):
    return (grad,)

def back_keep(v):
    return (v, None)

def back_low(kept, grad):
    return (lower_precision(grad),)
lower_precision.defvjp(low_keep, low_pass)
lower_precision_backward.defvjp(back_keep, back_low)

def rope_tables():
    half_size = HEAD_DIMENSION // 2
    frequency = jnp.exp(-(2.0 * jnp.arange(half_size, dtype=jnp.float32) / HEAD_DIMENSION) * math.log(theta_base))
    angles = jnp.arange(TOKENS_PER_CARD, dtype=jnp.float32)[:, None] * frequency[None, :]
    return (jnp.cos(angles), jnp.sin(angles))

def apply_rotary(heads, cosine_lookup, sine_lookup):
    half_size = heads.shape[-1] // 2
    first_half = heads[..., :half_size]
    second_half = heads[..., half_size:]
    cos_wide = cosine_lookup[:, None, :]
    sin_wide = sine_lookup[:, None, :]
    return jnp.concatenate([first_half * cos_wide - second_half * sin_wide, second_half * cos_wide + first_half * sin_wide], axis=-1)

def rms_scale(inputs, gain):
    return inputs * lax.rsqrt(lax.optimization_barrier(jnp.mean(inputs * inputs, axis=-1, keepdims=True)) + norm_eps) * gain

def slot_tables(route_rows):
    flat_ids = route_rows.reshape(SEQS, TOKENS_PER_CARD * TOP)
    onehot = (flat_ids[:, :, None] == jnp.arange(EXPERTS, dtype=jnp.int32)[None, None, :]).astype(jnp.int32)
    before = jnp.cumsum(onehot, axis=1) - onehot
    rank_in = lax.optimization_barrier(jnp.sum(before * onehot, axis=2))
    block_start = jnp.arange(SEQS, dtype=jnp.int32)[:, None] * C
    slot_index = (flat_ids * (SEQS * C) + block_start + rank_in).astype(jnp.int32)
    route_numbers = jnp.arange(TOKENS * TOP, dtype=jnp.int32) // TOP
    slot_owner = jnp.full((EXPERTS * SEQS * C,), TOKENS, jnp.int32).at[slot_index.reshape(-1)].set(route_numbers)
    return (slot_index.reshape(TOKENS, TOP), slot_owner)

def attend_group(normalized_input, segment_ids, query_w, key_matrix, value_matrix, cosine_lookup, sine_lookup):
    query_groups = normalized_input.shape[0]
    query_rows = lower_precision_backward(jnp.einsum('sku,ui->ski', normalized_input, query_w, precision=highest_precision)).reshape(query_groups, TOKENS_PER_CARD, QUERY_HEADS, HEAD_DIMENSION)
    query_rows = lower_precision(apply_rotary(query_rows, cosine_lookup, sine_lookup)).reshape(query_groups, TOKENS_PER_CARD, KEY_VALUE_HEADS, QUERY_HEADS // KEY_VALUE_HEADS, HEAD_DIMENSION)
    key_head_rows = lower_precision_backward(jnp.einsum('sku,ui->ski', normalized_input, key_matrix, precision=highest_precision)).reshape(query_groups, TOKENS_PER_CARD, KEY_VALUE_HEADS, HEAD_DIMENSION)
    key_head_rows = lower_precision(apply_rotary(key_head_rows, cosine_lookup, sine_lookup))
    value_head_rows = lower_precision(lower_precision_backward(jnp.einsum('sku,ui->ski', normalized_input, value_matrix, precision=highest_precision))).reshape(query_groups, TOKENS_PER_CARD, KEY_VALUE_HEADS, HEAD_DIMENSION)
    raw_scores = lower_precision_backward(jnp.einsum('gqhjd,gkhd->ghjqk', query_rows, key_head_rows, precision=highest_precision))
    positions = jnp.arange(TOKENS_PER_CARD)
    causal = positions[:, None] >= positions[None, :]
    allowed = causal[None, :, :] & (segment_ids[:, :, None] == segment_ids[:, None, :])
    logits = jnp.where(allowed[:, None, None, :, :], raw_scores * (1.0 / math.sqrt(HEAD_DIMENSION)), -1e+30)
    probs = lower_precision(jax.nn.softmax(logits, axis=-1))
    attn_mixed = jnp.einsum('ghjqk,gkhd->gqhjd', probs, value_head_rows, precision=highest_precision)
    return lower_precision(lower_precision_backward(attn_mixed)).reshape(query_groups, TOKENS_PER_CARD, QUERY_HEADS * HEAD_DIMENSION)

def run_expert(block_item):
    rows_in, gate_w, up_w, down_w = block_item
    gate_pre = lower_precision_backward(jnp.dot(rows_in, gate_w, precision=highest_precision))
    up_pre = lower_precision_backward(jnp.dot(rows_in, up_w, precision=highest_precision))
    inner_act = lower_precision(jax.nn.silu(gate_pre) * up_pre)
    return lower_precision(lower_precision_backward(jnp.einsum('rf,df->rd', inner_act, down_w, precision=highest_precision)))

def block_forward(hidden, segments, route_rows, query_w, key_matrix, value_matrix, out_w, router_w, gain_one, gain_two, gate_w, up_w, down_w, cosine_lookup, sine_lookup, slot_index, slot_owner):
    normalized_input = lower_precision(rms_scale(hidden, gain_one))
    router_logits = lower_precision_backward(jnp.dot(normalized_input, router_w, precision=highest_precision))
    chosen = jnp.take_along_axis(router_logits, route_rows, axis=1)
    gate_weights = jax.nn.softmax(chosen, axis=-1)
    group_size = math.gcd(SEQS, max(1, 4096 // TOKENS_PER_CARD))
    stacked = normalized_input.reshape(SEQS // group_size, group_size, TOKENS_PER_CARD, MODEL_DIMENSION)
    segment_stack = segments.reshape(SEQS // group_size, group_size, TOKENS_PER_CARD)

    def attend_item(block_item):
        return attend_group(block_item[0], block_item[1], query_w, key_matrix, value_matrix, cosine_lookup, sine_lookup)
    attn_mixed = lax.map(jax.checkpoint(attend_item), (stacked, segment_stack)).reshape(TOKENS, QUERY_HEADS * HEAD_DIMENSION)
    attn_branch = lower_precision_backward(jnp.einsum('te,de->td', attn_mixed, out_w, precision=highest_precision))
    middle = hidden + attn_branch
    normed_two = lower_precision(rms_scale(middle, gain_two))
    padded = jnp.concatenate([normed_two, jnp.zeros((1, MODEL_DIMENSION), jnp.float32)], axis=0)
    rows_all = lower_precision_backward(padded[slot_owner]).reshape(EXPERTS, SEQS * C, MODEL_DIMENSION)
    produced = lax.map(jax.checkpoint(run_expert), (rows_all, gate_w, up_w, down_w)).reshape(EXPERTS * SEQS * C, MODEL_DIMENSION)
    routed = produced[slot_index]
    return middle + lax.optimization_barrier(jnp.sum(gate_weights[:, :, None] * routed, axis=1))

def reference(tokens, segments, route_ids, w_query, key_projection, value_projection, w_out, w_router, gain_attn, gain_moe, w_gate, w_up, w_down, cotangent):
    cosine_lookup, sine_lookup = rope_tables()
    tables = [slot_tables(route_ids[level]) for level in range(LAYER_COUNT)]

    def forward(hidden, query_all, key_all, value_all, out_all, router_all, gain_one_all, gain_two_all, gate_all, up_all, down_all):
        for level in range(LAYER_COUNT):
            hidden = block_forward(hidden, segments, route_ids[level], query_all[level], key_all[level], value_all[level], out_all[level], router_all[level], gain_one_all[level], gain_two_all[level], gate_all[level], up_all[level], down_all[level], cosine_lookup, sine_lookup, tables[level][0], tables[level][1])
        return hidden
    floats = tuple((array_value.astype(jnp.float32) for array_value in (tokens, w_query, key_projection, value_projection, w_out, w_router, gain_attn, gain_moe, w_gate, w_up, w_down)))
    output_value, pullback = jax.vjp(forward, *floats)
    grads = pullback(cotangent.astype(jnp.float32))
    return (output_value, grads[0], grads[1], grads[2], grads[3], grads[4], grads[5], grads[6], grads[7], grads[8], grads[9], grads[10])
```

```python
import math

import jax
import jax.numpy as jnp
from jax import lax
from jax.experimental import pallas as pl
from jax.experimental.pallas import tpu as pltpu
from jax.sharding import PartitionSpec as P

MESH = pl.DeviceIdType.MESH
BF = jnp.bfloat16
F32 = jnp.float32
HEADS, KV, HD, TOP, LAYERS = 12, 2, 128, 4, 2
GROUP = HEADS // KV
T, D, FF, E, C = 128, 1536, 768, 32, 24
SLOTS = E * C
THETA, EPS = 1000000.0, 1e-06
ANY = pl.BlockSpec(memory_space=pl.ANY)
QK, QV, QO, QR, COLS = 1536, 1792, 2048, 3584, 3712


def dot(a, b, dims=((1,), (0,))):
    return lax.dot_general(a, b, (dims, ((), ())), preferred_element_type=F32)


def split_two(v):
    high = v.astype(BF)
    return high, (v - high.astype(F32)).astype(BF)


def rope_tables():
    half = HD // 2
    frequency = jnp.exp(-(2.0 * jnp.arange(half, dtype=F32) / HD) * math.log(THETA))
    angles = jnp.arange(T, dtype=F32)[:, None] * frequency[None, :]
    return jnp.cos(angles)[:, None, :], jnp.sin(angles)[:, None, :]


def rotate(heads, cosine, sine):
    first, second = heads[..., : HD // 2], heads[..., HD // 2 :]
    return jnp.concatenate(
        [first * cosine - second * sine, second * cosine + first * sine], axis=-1
    )


def gather_ring_kernel(src, dst, local_sem, send_sem, recv_sem):
    x, e = lax.axis_index("dp"), lax.axis_index("expert")
    right, left = lax.rem(x + 1, 4), lax.rem(x + 3, 4)
    barrier = pltpu.get_barrier_semaphore()
    for peer in (right, left):
        pl.semaphore_signal(barrier, inc=1, device_id=(peer, e), device_id_type=MESH)
    pl.semaphore_wait(barrier, 2)
    rows = src.shape[0] // 2
    halves = [pl.ds(0, rows), pl.ds(rows, rows)]

    def send(source, shard, half, number, peer):
        return pltpu.make_async_remote_copy(
            source.at[halves[half]] if source is src else source.at[shard, halves[half]],
            dst.at[shard, halves[half]],
            send_sem.at[number],
            recv_sem.at[number],
            device_id=(peer, e),
            device_id_type=MESH,
        )

    first = [send(src, x, 0, 0, right), send(src, x, 1, 1, left)]
    second = [send(src, x, 1, 2, right), send(src, x, 0, 3, left)]
    for copy in first + second:
        copy.start()
    own = pltpu.make_async_copy(src, dst.at[x], local_sem)
    own.start()
    first[0].wait_recv()
    on_right = send(dst, left, 0, 4, right)
    on_right.start()
    first[1].wait_recv()
    on_left = send(dst, right, 1, 5, left)
    on_left.start()
    for copy in second:
        copy.wait_recv()
    for copy in first + second:
        copy.wait_send()
    on_right.wait()
    on_left.wait()
    own.wait()


def gather_ring(shard):
    return pl.pallas_call(
        gather_ring_kernel,
        name="gather_expert_weights",
        out_shape=jax.ShapeDtypeStruct((4,) + shard.shape, shard.dtype),
        in_specs=[ANY],
        out_specs=ANY,
        scratch_shapes=[
            pltpu.SemaphoreType.DMA,
            pltpu.SemaphoreType.DMA((6,)),
            pltpu.SemaphoreType.DMA((6,)),
        ],
        compiler_params=pltpu.CompilerParams(collective_id=1, has_side_effects=True),
    )(shard)


def route_tables(route_rows):
    named = (route_rows[:, :, None] == jnp.arange(E, dtype=jnp.int32)).astype(F32).sum(1)
    earlier = (jnp.arange(T)[:, None] > jnp.arange(T)[None, :]).astype(BF)
    rank = dot(earlier, named.astype(BF))
    named_t, rank_t = named.T, rank.T
    places = (named_t[:, None, :] > 0) & (
        rank_t[:, None, :] == jnp.arange(C, dtype=F32)[None, :, None]
    )
    return named, places.astype(F32)


def attention_forward(hidden, allowed, weights, rope):
    gain = weights[:, QR + E].astype(F32)
    scale = lax.rsqrt(jnp.mean(hidden * hidden, axis=-1, keepdims=True) + EPS)
    normed = (hidden * scale * gain).astype(BF)
    routing = dot(normed, weights[:, QR : QR + E])
    projected = dot(normed, weights[:, :QO])
    q = rotate(projected[:, :QK].reshape(T, HEADS, HD), *rope).astype(BF)
    q = q.reshape(T, KV, GROUP, HD)
    k = rotate(projected[:, QK:QV].reshape(T, KV, HD), *rope).astype(BF)
    v = projected[:, QV:].astype(BF).reshape(T, KV, HD)
    raw = jnp.einsum("qhjd,khd->hjqk", q, k, preferred_element_type=F32)
    logits = jnp.where(allowed[None, None], raw * (1.0 / math.sqrt(HD)), -1e30)
    top = jnp.max(logits, axis=-1, keepdims=True)
    terms = jnp.exp(logits - top)
    probs = terms / jnp.sum(terms, axis=-1, keepdims=True)
    att = jnp.einsum("hjqk,khd->qhjd", probs.astype(BF), v, preferred_element_type=F32)
    att = att.astype(BF).reshape(T, HEADS * HD)
    middle = hidden + dot(att, weights[:, QO:QR], ((1,), (1,)))
    return middle, (normed, routing, q, k, v, probs, att)


def expert_forward(rows, gate_w, up_w, down_w):
    a = dot(rows, gate_w)
    b = dot(rows, up_w)
    inner = (jax.nn.silu(a) * b).astype(BF)
    produced = dot(inner, down_w, ((1,), (1,))).astype(BF)
    return produced, (a, b, inner)


def expert_backward(rows, grads, kept, gate_w, up_w, down_w):
    a, b, inner = kept
    du = dot(grads, down_w)
    grad_down = dot(grads, inner, ((0,), (0,)))
    sig = jax.nn.sigmoid(a)
    da = (du * b * sig * (1.0 + a * (1.0 - sig))).astype(BF)
    db = (du * a * sig).astype(BF)
    grad_gate = dot(rows, da, ((0,), (0,)))
    grad_up = dot(rows, db, ((0,), (0,)))
    dx = (dot(da, gate_w, ((1,), (1,))) + dot(db, up_w, ((1,), (1,)))).astype(BF)
    return dx, (grad_gate.astype(BF), grad_up.astype(BF), grad_down.astype(BF))


def exchange(rows):
    return lax.all_to_all(rows, "expert", split_axis=0, concat_axis=0, tiled=True)


def gate_softmax(routing, named):
    masked = jnp.where(named > 0, routing, -jnp.inf)
    terms = jnp.exp(masked - jnp.max(masked, axis=-1, keepdims=True))
    return terms / jnp.sum(terms, axis=-1, keepdims=True)


def norm_backward(inputs, gain, grad_normed, grad_residual):
    scale = lax.rsqrt(jnp.mean(inputs * inputs, axis=-1, keepdims=True) + EPS)
    unit = inputs * scale
    grad_gain = jnp.sum(grad_normed * unit, axis=0)
    grad_unit = grad_normed * gain
    back = grad_unit - unit * jnp.mean(grad_unit * unit, axis=-1, keepdims=True)
    return grad_residual + scale * back, grad_gain


def attention_backward(hidden, grad_middle, grad_routing, kept, allowed, weights, rope):
    normed, _, q, k, v, probs, att = kept
    grad_out_rows = grad_middle.astype(BF)
    grad_att = dot(grad_out_rows, weights[:, QO:QR]).astype(BF).reshape(T, KV, GROUP, HD)
    dp = jnp.einsum("qhjd,khd->hjqk", grad_att, v, preferred_element_type=F32)
    draw = probs * (dp - jnp.sum(probs * dp, axis=-1, keepdims=True))
    draw = (draw * (1.0 / math.sqrt(HD))).astype(BF)
    dq = jnp.einsum("hjqk,khd->qhjd", draw, k, preferred_element_type=F32)
    dk = jnp.einsum("hjqk,qhjd->khd", draw, q, preferred_element_type=F32)
    dv = jnp.einsum("hjqk,qhjd->khd", probs.astype(BF), grad_att, preferred_element_type=F32)
    cosine, sine = rope
    dq = rotate(dq.reshape(T, HEADS, HD), cosine, -sine).astype(BF).reshape(T, HEADS * HD)
    dk = rotate(dk, cosine, -sine).astype(BF).reshape(T, KV * HD)
    dv = dv.astype(BF).reshape(T, KV * HD)
    grad_cols = jnp.concatenate([dq, dk, dv], axis=1)
    grad_normed = dot(grad_cols, weights[:, :QO], ((1,), (1,)))
    grad_normed = grad_normed + dot(grad_routing, weights[:, QR : QR + E], ((1,), (1,)))
    grad_hidden, grad_gain = norm_backward(
        hidden, weights[:, QR + E].astype(F32), grad_normed, grad_middle
    )
    right = jnp.concatenate(
        [grad_cols, att, grad_routing, jnp.zeros((T, COLS - QR - E), BF)], axis=1
    )
    return grad_hidden, grad_gain, (normed, grad_out_rows, right)


def reduce_mixer(factors):
    normed, grad_out_rows, right = factors
    right_all = lax.all_gather(right, "dp", axis=0, tiled=True)
    left = jnp.stack([normed, grad_out_rows]).reshape(2, T, 4, D // 4).transpose(2, 0, 1, 3)
    left = lax.all_to_all(left, "dp", split_axis=0, concat_axis=0, tiled=True)
    left = left.transpose(1, 0, 2, 3).reshape(2, 4 * T, D // 4)
    source = jnp.arange(D // 4)
    target = (source // 12) * 16 + source % 12
    spread = (target[:, None] == jnp.arange(512)[None, :]).astype(BF)
    left_n = dot(left[0], spread).astype(BF)
    left_o = dot(left[1], spread).astype(BF)
    parts = jnp.concatenate(
        [
            dot(left_n, right_all[:, :QO], ((0,), (0,))).astype(BF),
            dot(left_o, right_all[:, QO:QR], ((0,), (0,))).astype(BF),
            dot(left_n, right_all[:, QR:], ((0,), (0,))).astype(BF),
        ],
        axis=1,
    ).reshape(32, 16, COLS)
    return exchange(parts).astype(F32).sum(0)[:12]


def reduce_expert(grads):
    return [
        lax.psum_scatter(g, "dp", scatter_dimension=0, tiled=True).astype(F32) for g in grads
    ]


def per_device(
    tokens, segments, route_ids, w_query, key_projection, value_projection, w_out, w_router,
    gain_attn, gain_moe, w_gate, w_up, w_down, cotangent,
):
    rope = rope_tables()
    position = jnp.arange(T)
    segment = segments[0]
    allowed = (position[:, None] >= position[None, :]) & (segment[:, None] == segment[None, :])

    packed = jnp.concatenate(
        [
            w_query, key_projection, value_projection, w_out, w_router,
            gain_attn[:, :, None], gain_moe[:, :, None],
            jnp.zeros((LAYERS, 12, COLS - QR - E - 2), BF),
        ],
        axis=2,
    )
    packed = jnp.pad(packed, ((0, 0), (0, 4), (0, 0)))
    mixers = []
    for level in range(LAYERS):
        full = lax.all_gather(packed[level], ("dp", "expert"), axis=0, tiled=True)
        mixers.append(full.reshape(128, 16, COLS)[:, :12].reshape(D, COLS))
    shards = jnp.stack([w_gate[:, 0], w_up[:, 0], w_down[:, 0]], axis=1).reshape(6 * 384, FF)
    experts = gather_ring(shards).reshape(4, LAYERS, 3, 384, FF).transpose(1, 2, 0, 3, 4)
    experts = experts.reshape(LAYERS, 3, D, FF)

    tables = [route_tables(route_ids[level]) for level in range(LAYERS)]
    hidden = tokens.astype(F32)
    grad = cotangent.astype(F32)
    state = []
    for level in range(LAYERS):
        weights, (named, places) = mixers[level], tables[level]
        spread = places.astype(BF).reshape(SLOTS, T)
        middle, kept = attention_forward(hidden, allowed, weights, rope)
        gates = gate_softmax(kept[1], named)
        slot_gates = jnp.sum(places * gates.T[:, None, :], axis=-1).reshape(SLOTS, 1)
        scale = lax.rsqrt(jnp.mean(middle * middle, axis=-1, keepdims=True) + EPS)
        normed = (middle * scale * weights[:, QR + E + 1].astype(F32)).astype(BF)
        send = dot(spread, normed).astype(BF).reshape(E, C, D)
        if level == LAYERS - 1:
            grad_slots = dot(spread, cotangent)
            grad_send = (slot_gates * grad_slots).astype(BF).reshape(E, C, D)
            got = exchange(jnp.concatenate([send, grad_send], axis=1))
            rows, grad_rows = got[:, :C].reshape(SLOTS, D), got[:, C:].reshape(SLOTS, D)
            produced, inside = expert_forward(rows, *experts[level])
            dx, expert_grads = expert_backward(rows, grad_rows, inside, *experts[level])
            back = exchange(
                jnp.concatenate([produced.reshape(E, C, D), dx.reshape(E, C, D)], axis=1)
            )
            routed, dx = back[:, :C].reshape(SLOTS, D), back[:, C:].reshape(SLOTS, D)
        else:
            rows = exchange(send).reshape(SLOTS, D)
            produced, inside = expert_forward(rows, *experts[level])
            routed = exchange(produced.reshape(E, C, D)).reshape(SLOTS, D)
        mix_high, mix_low = split_two(slot_gates * places.reshape(SLOTS, T))
        out = middle + dot(mix_high, routed, ((0,), (0,))) + dot(mix_low, routed, ((0,), (0,)))
        state.append((hidden, middle, kept, gates, slot_gates, spread, rows, inside, routed))
        hidden = out

    mixer_sums, expert_sums, gain_sums = [None] * LAYERS, [None] * LAYERS, [None] * LAYERS
    for level in reversed(range(LAYERS)):
        weights, (named, places) = mixers[level], tables[level]
        before, middle, kept, gates, slot_gates, spread, rows, inside, routed = state[level]
        if level < LAYERS - 1:
            high, low = split_two(grad)
            grad_slots = dot(spread, high) + dot(spread, low)
            grad_send = (slot_gates * grad_slots).astype(BF).reshape(E, C, D)
            grad_rows = exchange(grad_send).reshape(SLOTS, D)
            dx, expert_grads = expert_backward(rows, grad_rows, inside, *experts[level])
            dx = exchange(dx.reshape(E, C, D)).reshape(SLOTS, D)
        expert_sums[level] = reduce_expert(expert_grads)
        slot_dots = jnp.sum(routed.astype(F32) * grad_slots, axis=-1).reshape(E, C, 1)
        gate_grads = jnp.sum(places * slot_dots, axis=1).T
        grad_routing = gates * (gate_grads - jnp.sum(gates * gate_grads, axis=-1, keepdims=True))
        grad_normed = dot(spread, dx, ((0,), (0,)))
        gain = weights[:, QR + E + 1].astype(F32)
        grad_middle, gain_two = norm_backward(middle, gain, grad_normed, grad)
        grad, gain_one, factors = attention_backward(
            before, grad_middle, grad_routing.astype(BF), kept, allowed, weights, rope
        )
        mixer_sums[level] = reduce_mixer(factors)
        gain_sums[level] = (gain_one, gain_two)

    gains = jnp.stack([g for pair in gain_sums for g in pair])
    gains = gains.reshape(4, 128, 12).transpose(1, 0, 2)
    gains = lax.psum_scatter(gains, ("dp", "expert"), scatter_dimension=0, tiled=True)
    gains = gains.reshape(LAYERS, 2, 12)
    mixer = jnp.stack(mixer_sums)
    expert_out = [
        jnp.stack([expert_sums[level][m] for level in range(LAYERS)])[:, None] for m in range(3)
    ]
    return (
        hidden, grad, mixer[:, :, :QK], mixer[:, :, QK:QV], mixer[:, :, QV:QO], mixer[:, :, QO:QR],
        mixer[:, :, QR : QR + E], gains[:, 0], gains[:, 1], *expert_out,
    )


def solution(mesh):
    rows = P(("dp", "expert"), None)
    mixer = P(None, ("dp", "expert"), None)
    gain = P(None, ("dp", "expert"))
    expert = P(None, "expert", "dp", None)
    return jax.shard_map(
        per_device,
        mesh=mesh,
        in_specs=(
            rows, rows, mixer, mixer, mixer, mixer, mixer, mixer, gain, gain, expert, expert,
            expert, rows,
        ),
        out_specs=(
            rows, rows, mixer, mixer, mixer, mixer, mixer, gain, gain, expert, expert, expert,
        ),
        check_vma=False,
    )
```

```python
import math

import jax
import jax.numpy as jnp
from jax import lax
from jax.experimental import pallas as pl
from jax.experimental.pallas import tpu as pltpu
from jax.sharding import PartitionSpec as P

MESH = pl.DeviceIdType.MESH
BF = jnp.bfloat16
F32 = jnp.float32
HEADS, KV, HD, TOP, LAYERS = 12, 2, 128, 4, 2
GROUP = HEADS // KV
T, D, FF, E, C = 128, 1536, 768, 32, 24
SLOTS = E * C
THETA, EPS = 1000000.0, 1e-06
ANY = pl.BlockSpec(memory_space=pl.ANY)
QK, QV, QO, QR, COLS = 1536, 1792, 2048, 3584, 3712


def dot(a, b, dims=((1,), (0,))):
    return lax.dot_general(a, b, (dims, ((), ())), preferred_element_type=F32)


def split_two(v):
    high = v.astype(BF)
    return high, (v - high.astype(F32)).astype(BF)


def rope_tables():
    half = HD // 2
    frequency = jnp.exp(-(2.0 * jnp.arange(half, dtype=F32) / HD) * math.log(THETA))
    angles = jnp.arange(T, dtype=F32)[:, None] * frequency[None, :]
    return jnp.cos(angles)[:, None, :], jnp.sin(angles)[:, None, :]


def rotate(heads, cosine, sine):
    first, second = heads[..., : HD // 2], heads[..., HD // 2 :]
    return jnp.concatenate(
        [first * cosine - second * sine, second * cosine + first * sine], axis=-1
    )


def gather_ring_kernel(src, dst, local_sem, send_sem, recv_sem):
    x, e = lax.axis_index("dp"), lax.axis_index("expert")
    right, left = lax.rem(x + 1, 4), lax.rem(x + 3, 4)
    barrier = pltpu.get_barrier_semaphore()
    for peer in (right, left):
        pl.semaphore_signal(barrier, inc=1, device_id=(peer, e), device_id_type=MESH)
    pl.semaphore_wait(barrier, 2)
    rows = src.shape[1] // 2
    halves = [pl.ds(0, rows), pl.ds(rows, rows)]

    def send(source, shard, half, number, peer):
        return pltpu.make_async_remote_copy(
            source.at[:, halves[half]] if source is src else source.at[:, shard, halves[half]],
            dst.at[:, shard, halves[half]],
            send_sem.at[number],
            recv_sem.at[number],
            device_id=(peer, e),
            device_id_type=MESH,
        )

    first = [send(src, x, 0, 0, right), send(src, x, 1, 1, left)]
    second = [send(src, x, 1, 2, right), send(src, x, 0, 3, left)]
    for copy in first + second:
        copy.start()
    own = pltpu.make_async_copy(src, dst.at[:, x], local_sem)
    own.start()
    first[0].wait_recv()
    on_right = send(dst, left, 0, 4, right)
    on_right.start()
    first[1].wait_recv()
    on_left = send(dst, right, 1, 5, left)
    on_left.start()
    for copy in second:
        copy.wait_recv()
    for copy in first + second:
        copy.wait_send()
    on_right.wait()
    on_left.wait()
    own.wait()


def gather_ring(shard):
    return pl.pallas_call(
        gather_ring_kernel,
        name="gather_expert_weights",
        out_shape=jax.ShapeDtypeStruct((3, 4) + shard.shape[1:], shard.dtype),
        in_specs=[ANY],
        out_specs=ANY,
        scratch_shapes=[
            pltpu.SemaphoreType.DMA,
            pltpu.SemaphoreType.DMA((6,)),
            pltpu.SemaphoreType.DMA((6,)),
        ],
        compiler_params=pltpu.CompilerParams(collective_id=1, has_side_effects=True),
    )(shard)


def route_tables(route_rows):
    named = (route_rows[:, :, None] == jnp.arange(E, dtype=jnp.int32)).astype(F32).sum(1)
    earlier = (jnp.arange(T)[:, None] > jnp.arange(T)[None, :]).astype(BF)
    rank = dot(earlier, named.astype(BF))
    named_t, rank_t = named.T, rank.T
    places = (named_t[:, None, :] > 0) & (
        rank_t[:, None, :] == jnp.arange(C, dtype=F32)[None, :, None]
    )
    return named, places.astype(F32)


def attention_forward(hidden, allowed, weights, rope):
    gain = weights[:, QR + E].astype(F32)
    scale = lax.rsqrt(jnp.mean(hidden * hidden, axis=-1, keepdims=True) + EPS)
    normed = (hidden * scale * gain).astype(BF)
    routing = dot(normed, weights[:, QR : QR + E])
    projected = dot(normed, weights[:, :QO])
    q = rotate(projected[:, :QK].reshape(T, HEADS, HD), *rope).astype(BF)
    q = q.reshape(T, KV, GROUP, HD)
    k = rotate(projected[:, QK:QV].reshape(T, KV, HD), *rope).astype(BF)
    v = projected[:, QV:].astype(BF).reshape(T, KV, HD)
    raw = jnp.einsum("qhjd,khd->hjqk", q, k, preferred_element_type=F32)
    logits = jnp.where(allowed[None, None], raw * (1.0 / math.sqrt(HD)), -1e30)
    top = jnp.max(logits, axis=-1, keepdims=True)
    terms = jnp.exp(logits - top)
    probs = terms / jnp.sum(terms, axis=-1, keepdims=True)
    att = jnp.einsum("hjqk,khd->qhjd", probs.astype(BF), v, preferred_element_type=F32)
    att = att.astype(BF).reshape(T, HEADS * HD)
    middle = hidden + dot(att, weights[:, QO:QR], ((1,), (1,)))
    return middle, (normed, routing, q, k, v, probs, att)


def expert_forward(rows, gate_w, up_w, down_w):
    a = dot(rows, gate_w)
    b = dot(rows, up_w)
    inner = (jax.nn.silu(a) * b).astype(BF)
    produced = dot(inner, down_w, ((1,), (1,))).astype(BF)
    return produced, (a, b, inner)


def expert_backward(rows, grads, kept, gate_w, up_w, down_w):
    a, b, inner = kept
    du = dot(grads, down_w)
    grad_down = dot(grads, inner, ((0,), (0,)))
    sig = jax.nn.sigmoid(a)
    da = (du * b * sig * (1.0 + a * (1.0 - sig))).astype(BF)
    db = (du * a * sig).astype(BF)
    grad_gate = dot(rows, da, ((0,), (0,)))
    grad_up = dot(rows, db, ((0,), (0,)))
    dx = (dot(da, gate_w, ((1,), (1,))) + dot(db, up_w, ((1,), (1,)))).astype(BF)
    return dx, (grad_gate.astype(BF), grad_up.astype(BF), grad_down.astype(BF))


def exchange(rows):
    return lax.all_to_all(rows, "expert", split_axis=0, concat_axis=0, tiled=True)


def gate_softmax(routing, named):
    masked = jnp.where(named > 0, routing, -jnp.inf)
    terms = jnp.exp(masked - jnp.max(masked, axis=-1, keepdims=True))
    return terms / jnp.sum(terms, axis=-1, keepdims=True)


def norm_backward(inputs, gain, grad_normed, grad_residual):
    scale = lax.rsqrt(jnp.mean(inputs * inputs, axis=-1, keepdims=True) + EPS)
    unit = inputs * scale
    grad_gain = jnp.sum(grad_normed * unit, axis=0)
    grad_unit = grad_normed * gain
    back = grad_unit - unit * jnp.mean(grad_unit * unit, axis=-1, keepdims=True)
    return grad_residual + scale * back, grad_gain


def attention_backward(hidden, grad_middle, grad_routing, kept, allowed, weights, rope):
    normed, _, q, k, v, probs, att = kept
    grad_out_rows = grad_middle.astype(BF)
    grad_att = dot(grad_out_rows, weights[:, QO:QR]).astype(BF).reshape(T, KV, GROUP, HD)
    dp = jnp.einsum("qhjd,khd->hjqk", grad_att, v, preferred_element_type=F32)
    draw = probs * (dp - jnp.sum(probs * dp, axis=-1, keepdims=True))
    draw = (draw * (1.0 / math.sqrt(HD))).astype(BF)
    dq = jnp.einsum("hjqk,khd->qhjd", draw, k, preferred_element_type=F32)
    dk = jnp.einsum("hjqk,qhjd->khd", draw, q, preferred_element_type=F32)
    dv = jnp.einsum("hjqk,qhjd->khd", probs.astype(BF), grad_att, preferred_element_type=F32)
    cosine, sine = rope
    dq = rotate(dq.reshape(T, HEADS, HD), cosine, -sine).astype(BF).reshape(T, HEADS * HD)
    dk = rotate(dk, cosine, -sine).astype(BF).reshape(T, KV * HD)
    dv = dv.astype(BF).reshape(T, KV * HD)
    grad_cols = jnp.concatenate([dq, dk, dv], axis=1)
    grad_normed = dot(grad_cols, weights[:, :QO], ((1,), (1,)))
    grad_normed = grad_normed + dot(grad_routing, weights[:, QR : QR + E], ((1,), (1,)))
    grad_hidden, grad_gain = norm_backward(
        hidden, weights[:, QR + E].astype(F32), grad_normed, grad_middle
    )
    right = jnp.concatenate(
        [grad_cols, att, grad_routing, jnp.zeros((T, COLS - QR - E), BF)], axis=1
    )
    return grad_hidden, grad_gain, (normed, grad_out_rows, right)


def reduce_mixer(factors, gain_one, gain_two):
    normed, grad_out_rows, right = factors
    one, one_rest = split_two(gain_one[None])
    two, two_rest = split_two(gain_two[None])
    gain_rows = jnp.concatenate([one, two, one_rest, two_rest, jnp.zeros((12, D), BF)])
    right_all = lax.all_gather(right, "dp", axis=0, tiled=True)
    left = jnp.concatenate([normed, grad_out_rows, gain_rows])
    left = left.reshape(2 * T + 16, 4, D // 4).transpose(1, 0, 2)
    left = lax.all_to_all(left, "dp", split_axis=0, concat_axis=0, tiled=True)
    source = jnp.arange(D // 4)
    target = (source // 12) * 16 + source % 12
    spread = (target[:, None] == jnp.arange(512)[None, :]).astype(BF)
    left_n = dot(left[:, :T].reshape(4 * T, D // 4), spread).astype(BF)
    left_o = dot(left[:, T : 2 * T].reshape(4 * T, D // 4), spread).astype(BF)
    left_g = dot(left[:, 2 * T :].reshape(64, D // 4), spread).astype(BF)
    number, column = jnp.arange(64)[:, None] % 16, jnp.arange(COLS - QR)[None, :]
    gain_place = ((number < 4) & (column == E + number % 2)).astype(BF)
    parts = jnp.concatenate(
        [
            dot(left_n, right_all[:, :QO], ((0,), (0,))).astype(BF),
            dot(left_o, right_all[:, QO:QR], ((0,), (0,))).astype(BF),
            (
                dot(left_n, right_all[:, QR:], ((0,), (0,)))
                + dot(left_g, gain_place, ((0,), (0,)))
            ).astype(BF),
        ],
        axis=1,
    ).reshape(32, 16, COLS)
    return exchange(parts).astype(F32).sum(0)[:12]


def reduce_expert(grads):
    return [
        lax.psum_scatter(g, "dp", scatter_dimension=0, tiled=True).astype(F32) for g in grads
    ]


def per_device(
    tokens, segments, route_ids, w_query, key_projection, value_projection, w_out, w_router,
    gain_attn, gain_moe, w_gate, w_up, w_down, cotangent,
):
    rope = rope_tables()
    position = jnp.arange(T)
    segment = segments[0]
    allowed = (position[:, None] >= position[None, :]) & (segment[:, None] == segment[None, :])

    packed = jnp.concatenate(
        [
            w_query, key_projection, value_projection, w_out, w_router,
            gain_attn[:, :, None], gain_moe[:, :, None],
            jnp.zeros((LAYERS, 12, COLS - QR - E - 2), BF),
        ],
        axis=2,
    )
    packed = jnp.pad(packed, ((0, 0), (0, 4), (0, 0)))
    padded_row = jnp.arange(128)
    keep = (jnp.arange(96)[:, None] == (padded_row - padded_row // 16 * 4)[None, :]) & (
        padded_row % 16 < 12
    )
    keep = jnp.broadcast_to(keep.astype(BF), (16, 96, 128))

    def fetch_mixer(level):
        return lax.all_gather(packed[level], ("dp", "expert"), axis=0, tiled=True)

    def close_rows(full):
        full = full.reshape(16, 128, COLS)
        full = jnp.einsum("grp,gpc->grc", keep, full, preferred_element_type=F32)
        return full.astype(BF).reshape(D, COLS)

    shards = jnp.stack([w_gate[:, 0], w_up[:, 0], w_down[:, 0]], axis=1)
    first_mixer, first_experts = lax.optimization_barrier(
        (fetch_mixer(0), gather_ring(shards[0]))
    )
    second_mixer = fetch_mixer(1)
    second_experts = lax.all_gather(shards[1].reshape(3 * 384, FF), "dp", axis=0)
    mixers = [close_rows(first_mixer), close_rows(second_mixer)]
    second_experts = second_experts.reshape(4, 3, 384, FF)
    experts = [
        [first_experts[m].reshape(D, FF) for m in range(3)],
        [second_experts[:, m].reshape(D, FF) for m in range(3)],
    ]

    tables = [route_tables(route_ids[level]) for level in range(LAYERS)]
    hidden = tokens.astype(F32)
    grad = cotangent.astype(F32)
    state = []
    for level in range(LAYERS):
        weights, (named, places) = mixers[level], tables[level]
        spread = places.astype(BF).reshape(SLOTS, T)
        middle, kept = attention_forward(hidden, allowed, weights, rope)
        gates = gate_softmax(kept[1], named)
        slot_gates = jnp.sum(places * gates.T[:, None, :], axis=-1).reshape(SLOTS, 1)
        scale = lax.rsqrt(jnp.mean(middle * middle, axis=-1, keepdims=True) + EPS)
        normed = (middle * scale * weights[:, QR + E + 1].astype(F32)).astype(BF)
        send = dot(spread, normed).astype(BF).reshape(E, C, D)
        if level == LAYERS - 1:
            grad_slots = dot(spread, cotangent)
            grad_send = (slot_gates * grad_slots).astype(BF).reshape(E, C, D)
            grad_rows = exchange(grad_send).reshape(SLOTS, D)
            rows = exchange(send).reshape(SLOTS, D)
            produced, inside = expert_forward(rows, *experts[level])
            dx, expert_grads = expert_backward(rows, grad_rows, inside, *experts[level])
            dx = exchange(dx.reshape(E, C, D)).reshape(SLOTS, D)
            routed = exchange(produced.reshape(E, C, D)).reshape(SLOTS, D)
            dx, expert_grads = lax.optimization_barrier((dx, expert_grads))
        else:
            rows = exchange(send).reshape(SLOTS, D)
            produced, inside = expert_forward(rows, *experts[level])
            routed = exchange(produced.reshape(E, C, D)).reshape(SLOTS, D)
        mix_high, mix_low = split_two(slot_gates * places.reshape(SLOTS, T))
        out = middle + dot(mix_high, routed, ((0,), (0,))) + dot(mix_low, routed, ((0,), (0,)))
        state.append((hidden, middle, kept, gates, slot_gates, spread, rows, inside, routed))
        hidden = out

    mixer_sums, expert_sums = [None] * LAYERS, [None] * LAYERS
    for level in reversed(range(LAYERS)):
        weights, (named, places) = mixers[level], tables[level]
        before, middle, kept, gates, slot_gates, spread, rows, inside, routed = state[level]
        if level < LAYERS - 1:
            high, low = split_two(grad)
            grad_slots = dot(spread, high) + dot(spread, low)
            grad_send = (slot_gates * grad_slots).astype(BF).reshape(E, C, D)
            grad_rows = exchange(grad_send).reshape(SLOTS, D)
            dx, expert_grads = expert_backward(rows, grad_rows, inside, *experts[level])
            dx = exchange(dx.reshape(E, C, D)).reshape(SLOTS, D)
            dx, expert_grads = lax.optimization_barrier((dx, expert_grads))
        expert_sums[level] = reduce_expert(expert_grads)
        slot_dots = jnp.sum(routed.astype(F32) * grad_slots, axis=-1).reshape(E, C, 1)
        gate_grads = jnp.sum(places * slot_dots, axis=1).T
        grad_routing = gates * (gate_grads - jnp.sum(gates * gate_grads, axis=-1, keepdims=True))
        grad_normed = dot(spread, dx, ((0,), (0,)))
        gain = weights[:, QR + E + 1].astype(F32)
        grad_middle, gain_two = norm_backward(middle, gain, grad_normed, grad)
        grad, gain_one, factors = attention_backward(
            before, grad_middle, grad_routing.astype(BF), kept, allowed, weights, rope
        )
        mixer_sums[level] = reduce_mixer(factors, gain_one, gain_two)

    mixer = jnp.stack(mixer_sums)
    expert_out = [
        jnp.stack([expert_sums[level][m] for level in range(LAYERS)])[:, None] for m in range(3)
    ]
    return (
        hidden, grad, mixer[:, :, :QK], mixer[:, :, QK:QV], mixer[:, :, QV:QO], mixer[:, :, QO:QR],
        mixer[:, :, QR : QR + E], mixer[:, :, QR + E], mixer[:, :, QR + E + 1], *expert_out,
    )


def solution(mesh):
    rows = P(("dp", "expert"), None)
    mixer = P(None, ("dp", "expert"), None)
    gain = P(None, ("dp", "expert"))
    expert = P(None, "expert", "dp", None)
    return jax.shard_map(
        per_device,
        mesh=mesh,
        in_specs=(
            rows, rows, mixer, mixer, mixer, mixer, mixer, mixer, gain, gain, expert, expert,
            expert, rows,
        ),
        out_specs=(
            rows, rows, mixer, mixer, mixer, mixer, mixer, gain, gain, expert, expert, expert,
        ),
        check_vma=False,
    )
```

```python
import math

import jax
import jax.numpy as jnp
from jax import lax
from jax.experimental import pallas as pl
from jax.experimental.pallas import tpu as pltpu
from jax.sharding import Mesh, PartitionSpec as P

MESH = pl.DeviceIdType.MESH
BF = jnp.bfloat16
F32 = jnp.float32
HEADS, KV, HD, TOP, LAYERS = 12, 2, 128, 4, 2
T, D, FF, E, C = 128, 1536, 768, 32, 24
SLOTS = E * C
THETA, EPS = 1000000.0, 1e-06
SCALE = 1.0 / math.sqrt(HD)
ANY = pl.BlockSpec(memory_space=pl.ANY)
VM = pl.BlockSpec(memory_space=pltpu.VMEM)
WO, WR, COLS = 1024, 1792, 1920
CUTS = (pl.ds(0, 1024), pl.ds(1024, COLS - 1024))
PART = 640
VMEM = 56 << 20
WIDE = D + 128
AXES = ("dp", "z", "y", "core")
GROUP = AXES[1:]


def dot(a, b, dims=((1,), (0,))):
    return lax.dot_general(a, b, (dims, ((), ())), preferred_element_type=F32)


def split_two(v):
    high = v.astype(BF)
    return high, (v - high.astype(F32)).astype(BF)


def rope_tables():
    frequency = jnp.exp(-(2.0 * jnp.arange(HD // 2, dtype=F32) / HD) * math.log(THETA))
    angles = jnp.arange(T, dtype=F32)[:, None] * frequency[None, :]
    cosine, sine = jnp.cos(angles), jnp.sin(angles)
    return jnp.concatenate([cosine, cosine], 1), jnp.concatenate([-sine, sine], 1)


def swap(v):
    return lax.ppermute(v, "core", [(0, 1), (1, 0)])


def neighbours():
    here = [lax.axis_index(axis) for axis in AXES]

    def along(axis, places):
        peer = list(here)
        peer[axis] = lax.rem(here[axis] + places, 4)
        return tuple(peer)

    return here, along


def greet(peers):
    barrier = pltpu.get_barrier_semaphore()
    for peer in peers:
        pl.semaphore_signal(barrier, inc=1, device_id=peer, device_id_type=MESH)
    pl.semaphore_wait(barrier, len(peers))


def sender(send_sem, recv_sem):
    def send(src, dst, number, peer):
        copy = pltpu.make_async_remote_copy(
            src, dst, send_sem.at[number], recv_sem.at[number], device_id=peer, device_id_type=MESH
        )
        copy.start()
        return copy

    return send


def ring_steps(own, view, me, right, left, send, number):
    first = [
        send(own(0), view(me, 0), number, right), send(own(1), view(me, 1), number + 1, left)
    ]
    second = [
        send(own(1), view(me, 1), number + 2, right), send(own(0), view(me, 0), number + 3, left)
    ]

    relays = []

    def relay():
        before, after = lax.rem(me + 3, 4), lax.rem(me + 1, 4)
        first[0].wait_recv()
        relays.append(send(view(before, 0), view(before, 0), number + 4, right))
        first[1].wait_recv()
        relays.append(send(view(after, 1), view(after, 1), number + 5, left))

    def finish():
        for copy in second:
            copy.wait_recv()
        for copy in first + second:
            copy.wait_send()
        for copy in relays:
            copy.wait()

    return relay, finish


def gather_kernel(block, shard, out, experts, local_sem, send_sem, recv_sem):
    (x, z, y, _), along = neighbours()
    greet([along(axis, o) for o in (1, 2, 3) for axis in range(3)])
    send = sender(send_sem, recv_sem)
    copies = [send(block, out.at[x, z, y], o - 1, along(0, o)) for o in (1, 3, 2)]
    on_experts = ring_steps(
        lambda half: shard.at[:, pl.ds(half * 192, 192)],
        lambda number, half: experts.at[:, number, pl.ds(half * 192, 192)],
        x, along(0, 1), along(0, 3), send, 27,
    )
    own = pltpu.make_async_copy(block, out.at[x, z, y], local_sem.at[0])
    own.start()
    own_experts = pltpu.make_async_copy(shard, experts.at[:, x], local_sem.at[1])
    own_experts.start()
    own.wait()
    for copy in copies:
        copy.wait()

    def ring(view, axis, me, number):
        return ring_steps(
            lambda half: view(me, half), view, me, along(axis, 1), along(axis, 3), send, number
        )

    def pair(half):
        return pl.ds(half * 2, 2)

    first = ring(lambda n, half: out.at[pair(half), n, y, :, CUTS[0]], 1, z, 3)
    second = ring(lambda n, half: out.at[pair(half), z, n, :, CUTS[1]], 2, y, 9)
    first[0]()
    second[0]()
    first[1]()
    first = ring(lambda n, half: out.at[pair(half), :, n, :, CUTS[0]], 2, y, 15)
    second[1]()
    second = ring(lambda n, half: out.at[pair(half), n, :, :, CUTS[1]], 1, z, 21)
    on_experts[0]()
    first[0]()
    second[0]()
    first[1]()
    second[1]()
    on_experts[1]()
    own_experts.wait()


def gather(block, shard):
    mixer, experts = pl.pallas_call(
        gather_kernel,
        name="gather_weights",
        out_shape=(
            jax.ShapeDtypeStruct((4, 4, 4, 24, COLS), BF),
            jax.ShapeDtypeStruct((2, 4, D // 4, FF), BF),
        ),
        in_specs=[ANY, ANY],
        out_specs=(ANY, ANY),
        scratch_shapes=[
            pltpu.SemaphoreType.DMA((2,)),
            pltpu.SemaphoreType.DMA((33,)),
            pltpu.SemaphoreType.DMA((33,)),
        ],
        compiler_params=pltpu.CompilerParams(
            collective_id=1, has_side_effects=True, vmem_limit_bytes=VMEM
        ),
    )(block, shard)
    return mixer.reshape(D, COLS), experts.reshape(1, 2, D, FF)


OFFSETS = sorted(
    ((a, b, c) for a in range(4) for b in range(4) for c in range(2) if a or b or c),
    key=lambda o: -min(o[0], 4 - o[0]) - min(o[1], 4 - o[1]),
)


def dispatch_kernel(rows, shard, out, experts, local_sem, send_sem, recv_sem):
    (x, z, y, core), along = neighbours()
    peers = [
        (x, lax.rem(z + a, 4), lax.rem(y + b, 4), lax.rem(core + c, 2)) for a, b, c in OFFSETS
    ]
    greet(peers + [along(0, 1), along(0, 3)])
    send = sender(send_sem, recv_sem)
    me = (z * 4 + y) * 2 + core
    ring = ring_steps(
        lambda half: shard.at[:, pl.ds(half * 192, 192)],
        lambda number, half: experts.at[:, number, pl.ds(half * 192, 192)],
        x, along(0, 1), along(0, 3), send, len(peers),
    )
    copies = []
    for n, peer in enumerate(peers):
        index = (peer[1] * 4 + peer[2]) * 2 + peer[3]
        copies.append(send(rows.at[index], out.at[me], n, peer))
    local = [
        pltpu.make_async_copy(rows.at[me], out.at[me], local_sem.at[0]),
        pltpu.make_async_copy(shard, experts.at[:, x], local_sem.at[1]),
    ]
    for copy in local:
        copy.start()
    ring[0]()
    for copy in copies + local:
        copy.wait()
    ring[1]()


def dispatch(rows, shard):
    rows, experts = pl.pallas_call(
        dispatch_kernel,
        name="dispatch_rows",
        out_shape=(
            jax.ShapeDtypeStruct((E, C, D), BF),
            jax.ShapeDtypeStruct((1, 4, D // 4, FF), BF),
        ),
        in_specs=[ANY, ANY],
        out_specs=(ANY, ANY),
        scratch_shapes=[
            pltpu.SemaphoreType.DMA((2,)),
            pltpu.SemaphoreType.DMA((len(OFFSETS) + 6,)),
            pltpu.SemaphoreType.DMA((len(OFFSETS) + 6,)),
        ],
        compiler_params=pltpu.CompilerParams(
            collective_id=3, has_side_effects=True, vmem_limit_bytes=VMEM
        ),
    )(rows.reshape(E, C, D), shard)
    return rows.reshape(SLOTS, D), experts.reshape(1, 1, D, FF)


def reduce_mixer_kernel(*refs):
    sources, out, scratch = refs[:6], refs[6], refs[7:]
    (x, z, y, _), along = neighbours()
    local_sem, send_sem, recv_sem = scratch[-3:]
    greet([along(axis, o) for o in (1, 2, 3) for axis in range(3)])
    send = sender(send_sem, recv_sem)
    jobs = []
    ways = (((1, z), (2, y), (0, x)), ((2, y), (1, z), (0, x)), ((0, x), (1, z), (2, y)))
    for level in reversed(range(LAYERS)):
        for group, way in enumerate(ways):
            number = level * 3 + group
            held = scratch[number * 7 : number * 7 + 7]
            jobs.append((number, sources[number], out.at[number], way, held))

    def start_first(job):
        number, source, _, ((axis, me), _, _), (got, own, *_) = job
        copies = [
            send(source.at[lax.rem(me + o, 4)], got.at[o - 1], number * 9 + o - 1, along(axis, o))
            for o in (2, 1, 3)
        ]
        mine = pltpu.make_async_copy(source.at[me], own, local_sem.at[number])
        mine.start()
        return copies + [mine]

    def start_second(job, copies):
        number, _, _, (_, (axis, me), _), (got, own, total, ready, after, *_) = job
        for copy in copies:
            copy.wait()
        total[...] = (
            own[...].astype(F32) + got[0].astype(F32) + got[1].astype(F32) + got[2].astype(F32)
        )
        started = []
        for o in (2, 1, 3):
            ready[o - 1] = total[lax.rem(me + o, 4)].astype(BF)
            started.append(
                send(ready.at[o - 1], after.at[o - 1], number * 9 + 2 + o, along(axis, o))
            )
        return started

    def start_third(job, copies):
        number, _, _, (_, (_, me), (axis, there)), (_, _, total, _, after, small, last) = job
        for copy in copies:
            copy.wait()
        rows = total[me]
        for o in range(3):
            rows = rows + after[o].astype(F32)
        for i in range(4):
            small[i] = rows[i * 24 : (i + 1) * 24]
        return [
            send(small.at[lax.rem(there + o, 4)], last.at[o - 1], number * 9 + 5 + o, along(axis, o))
            for o in (2, 1, 3)
        ]

    def end(job, copies):
        _, _, out, (_, _, (_, there)), (*_, small, last) = job
        for copy in copies:
            copy.wait()
        out[...] = small[there] + last[0] + last[1] + last[2]

    running = [start_first(job) for job in jobs]
    running = [start_second(job, copies) for job, copies in zip(jobs, running)]
    running = [start_third(job, copies) for job, copies in zip(jobs, running)]
    for job, copies in zip(jobs, running):
        end(job, copies)


def reduce_mixer(products):
    scratch = []
    for _ in products:
        scratch += [
            pltpu.VMEM((3, 4, 96, PART), BF),
            pltpu.VMEM((4, 96, PART), BF),
            pltpu.VMEM((4, 96, PART), F32),
            pltpu.VMEM((3, 96, PART), BF),
            pltpu.VMEM((3, 96, PART), BF),
            pltpu.VMEM((4, 24, PART), F32),
            pltpu.VMEM((3, 24, PART), F32),
        ]
    return pl.pallas_call(
        reduce_mixer_kernel,
        name="reduce_mixer_gradients",
        out_shape=jax.ShapeDtypeStruct((6, 24, PART), F32),
        in_specs=[ANY] * 6,
        out_specs=VM,
        scratch_shapes=scratch
        + [
            pltpu.SemaphoreType.DMA((6,)),
            pltpu.SemaphoreType.DMA((54,)),
            pltpu.SemaphoreType.DMA((54,)),
        ],
        compiler_params=pltpu.CompilerParams(
            collective_id=2, has_side_effects=True, vmem_limit_bytes=VMEM
        ),
    )(*products)


def turn(rows, cosine, sine):
    return rows * cosine + pltpu.roll(rows, HD // 2, 1) * sine


def head_rows(ref, sequence, heads):
    return jnp.concatenate([ref[sequence, :, h * HD : (h + 1) * HD] for h in heads], axis=0)


def weigh(queries, keys, mask):
    raw = dot(queries, keys, ((1,), (1,))).reshape(6, T, T)
    logits = jnp.where(mask[None] > 0, raw * SCALE, -1e30)
    terms = jnp.exp(logits - jnp.max(logits, axis=-1, keepdims=True))
    return (terms / jnp.sum(terms, axis=-1, keepdims=True)).reshape(6 * T, T)


def fetch_weights(mixers, weights, sem):
    copies = []
    for n, place in enumerate((pl.ds(0, WO), pl.ds(WO, COLS - WO))):
        copies.append(
            pltpu.make_async_copy(mixers.at[:, place], weights.at[:, place], sem.at[n])
        )
        copies[n].start()
    return copies


def attend_kernel(
    own, other, mixers, cosine, sine, mask,
    heads_out, att_out, own_out, other_out, routing_out, both, weights, sem,
):
    copies = fetch_weights(mixers, weights, sem)
    both[:T] = own[...]
    both[T:] = other[...]
    turns = [jnp.concatenate([t[...], t[...]], axis=0) for t in (cosine, sine)]
    copies[0].wait()
    for tile in range(4):
        wide = dot(both[...], weights[:, tile * 256 : (tile + 1) * 256])
        for part in range(2):
            head = tile * 2 + part
            rows = wide[:, part * HD : (part + 1) * HD]
            if head < 7:
                rows = turn(rows, *turns)
            rows = rows.astype(BF)
            for s in range(2):
                heads_out[s, :, head * HD : (head + 1) * HD] = rows[s * T : (s + 1) * T]
    for s in range(2):
        probs = weigh(head_rows(heads_out, s, range(6)), heads_out[s, :, 768:896], mask[s])
        mixed = dot(probs.astype(BF), heads_out[s, :, 896:]).astype(BF)
        for h in range(6):
            att_out[s, :, h * HD : (h + 1) * HD] = mixed[h * T : (h + 1) * T]
    copies[1].wait()
    att = att_out[...].reshape(2 * T, 768)
    for tile in range(6):
        place = slice(tile * 256, (tile + 1) * 256)
        rows = dot(att, weights[place, WO:WR], ((1,), (1,)))
        own_out[:, place] = rows[:T]
        other_out[:, place] = rows[T:].astype(BF)
    routing_out[...] = dot(own[...], weights[:, WR:])


def attend(own, other, mixers, cosine, sine, mask):
    return pl.pallas_call(
        attend_kernel,
        name="attention_forward",
        out_shape=(
            jax.ShapeDtypeStruct((2, T, 1024), BF),
            jax.ShapeDtypeStruct((2, T, 768), BF),
            jax.ShapeDtypeStruct((T, D), F32),
            jax.ShapeDtypeStruct((T, D), BF),
            jax.ShapeDtypeStruct((T, 128), F32),
        ),
        in_specs=[VM, VM, ANY, VM, VM, VM],
        out_specs=[VM] * 5,
        scratch_shapes=[
            pltpu.VMEM((2 * T, D), BF), pltpu.VMEM((D, COLS), BF), pltpu.SemaphoreType.DMA((2,))
        ],
        compiler_params=pltpu.CompilerParams(vmem_limit_bytes=VMEM),
        cost_estimate=pl.CostEstimate(flops=1700000000, bytes_accessed=9000000, transcendentals=200000),
    )(own, other, mixers, cosine, sine, mask)


def attend_back_kernel(
    own, other, routing, mixers, heads, cosine, sine, mask,
    grad_heads, own_out, other_out, both, grad_att, weights, sem,
):
    copies = fetch_weights(mixers, weights, sem)
    both[:T] = own[...]
    both[T:] = other[...]
    copies[1].wait()
    for tile in range(3):
        place = slice(tile * 256, (tile + 1) * 256)
        wide = dot(both[...], weights[:, WO + tile * 256 : WO + (tile + 1) * 256]).astype(BF)
        for s in range(2):
            grad_att[s, :, place] = wide[s * T : (s + 1) * T]
    cos, sin = cosine[...], -sine[...]
    for s in range(2):
        queries, grads = head_rows(heads, s, range(6)), head_rows(grad_att, s, range(6))
        keys, values = heads[s, :, 768:896], heads[s, :, 896:]
        probs = weigh(queries, keys, mask[s])
        dp = dot(grads, values, ((1,), (1,)))
        draw = probs * (dp - jnp.sum(probs * dp, axis=-1, keepdims=True))
        draw = (draw * SCALE).astype(BF)
        dq = dot(draw, keys)
        for h in range(6):
            rows = turn(dq[h * T : (h + 1) * T], cos, sin)
            grad_heads[s, :, h * HD : (h + 1) * HD] = rows.astype(BF)
        dk = dot(draw, queries, ((0,), (0,)))
        grad_heads[s, :, 768:896] = turn(dk, cos, sin).astype(BF)
        grad_heads[s, :, 896:] = dot(probs.astype(BF), grads, ((0,), (0,))).astype(BF)
    copies[0].wait()
    wide = grad_heads[...].reshape(2 * T, 1024)
    for tile in range(6):
        place = slice(tile * 256, (tile + 1) * 256)
        rows = dot(wide, weights[place, :WO], ((1,), (1,)))
        own_out[:, place] = rows[:T] + dot(routing[...], weights[place, WR:], ((1,), (1,)))
        other_out[:, place] = rows[T:].astype(BF)


def attend_back(own, other, routing, mixers, heads, cosine, sine, mask):
    return pl.pallas_call(
        attend_back_kernel,
        name="attention_backward",
        out_shape=(
            jax.ShapeDtypeStruct((2, T, 1024), BF),
            jax.ShapeDtypeStruct((T, D), F32),
            jax.ShapeDtypeStruct((T, D), BF),
        ),
        in_specs=[VM, VM, VM, ANY, VM, VM, VM, VM],
        out_specs=[VM] * 3,
        scratch_shapes=[
            pltpu.VMEM((2 * T, D), BF),
            pltpu.VMEM((2, T, 768), BF),
            pltpu.VMEM((D, COLS), BF),
            pltpu.SemaphoreType.DMA((2,)),
        ],
        compiler_params=pltpu.CompilerParams(vmem_limit_bytes=VMEM),
        cost_estimate=pl.CostEstimate(flops=2200000000, bytes_accessed=9000000, transcendentals=200000),
    )(own, other, routing, mixers, heads, cosine, sine, mask)

ROWS = 256


def load_weights(pieces, weights, sem):
    @pl.when(pl.program_id(0) == 0)
    def _():
        copies, matrix = [], 0
        for piece in pieces:
            count, several = piece.shape[:2]
            for n in range(count):
                place = pl.ds(matrix, several), pl.ds(n * (D // count), D // count)
                copy = pltpu.make_async_copy(piece.at[n], weights.at[place], sem.at[len(copies)])
                copy.start()
                copies.append(copy)
            matrix += several
        for copy in copies:
            copy.wait()


def expert_kernel(rows, *refs):
    *pieces, y_out, a_out, b_out, weights, sem = refs
    load_weights(pieces, weights, sem)
    a = dot(rows[...], weights[0])
    b = dot(rows[...], weights[1])
    a_out[...] = a
    b_out[...] = b
    inner = (a * jax.nn.sigmoid(a) * b).astype(BF)
    y_out[...] = dot(inner, weights[2], ((1,), (1,))).astype(BF)


def expert_both_kernel(rows, target, *refs):
    *pieces, dx_out, da_out, db_out, inner_out, y_out, dy_out, weights, sem = refs
    load_weights(pieces, weights, sem)
    normed = rows[:, :D]
    gate = rows[:, D : D + 1].astype(F32) + rows[:, D + 1 : D + 2].astype(F32)
    dy = (gate * target[...].astype(F32)).astype(BF)
    dy_out[...] = dy
    a = dot(normed, weights[0])
    b = dot(normed, weights[1])
    inner = expert_inner_gradients(a, b, dy, weights, dx_out, da_out, db_out, inner_out)
    y = dot(inner, weights[2], ((1,), (1,))).astype(BF)
    y_out[...] = y
    share = jnp.sum(y.astype(F32) * dy.astype(F32), axis=-1, keepdims=True)
    high = share.astype(BF).astype(F32)
    column = lax.broadcasted_iota(jnp.int32, (ROWS, WIDE - D), 1)
    parts = jnp.where(column == 0, high, jnp.where(column == 1, share - high, 0.0))
    dx_out[:, D:] = parts.astype(BF)


def expert_back_kernel(a_in, b_in, grads, *refs):
    *pieces, dx_out, da_out, db_out, inner_out, weights, sem = refs
    load_weights(pieces, weights, sem)
    expert_inner_gradients(
        a_in[...], b_in[...], grads[...], weights, dx_out, da_out, db_out, inner_out
    )


def expert_inner_gradients(a, b, dy, weights, dx_out, da_out, db_out, inner_out):
    du = dot(dy, weights[2])
    sig = jax.nn.sigmoid(a)
    act = a * sig
    inner = (act * b).astype(BF)
    da = (du * b * sig * (1.0 + a * (1.0 - sig))).astype(BF)
    db = (du * act).astype(BF)
    da_out[...], db_out[...], inner_out[...] = da, db, inner
    dx = dot(da, weights[0], ((1,), (1,))) + dot(db, weights[1], ((1,), (1,)))
    dx_out[:, :D] = dx.astype(BF)
    return inner


def expert_grad_kernel(rows, grads, da, db, inner, gate_out, up_out, down_out):
    gate_out[...] = dot(rows[...], da[...], ((0,), (0,))).astype(BF)
    up_out[...] = dot(rows[...], db[...], ((0,), (0,))).astype(BF)
    down_out[...] = dot(grads[...], inner[...], ((0,), (0,))).astype(BF)


def tiled(width):
    return pl.BlockSpec((ROWS, width), lambda i: (i, 0))


def expert_call(kernel, name, ins, pieces, out_widths, flops):
    outs = [jax.ShapeDtypeStruct((SLOTS, w), t) for w, t in out_widths]
    return pl.pallas_call(
        kernel,
        name=name,
        out_shape=outs,
        grid=(SLOTS // ROWS,),
        in_specs=[tiled(v.shape[1]) for v in ins] + [ANY] * len(pieces),
        out_specs=[tiled(w) for w, _ in out_widths],
        scratch_shapes=[pltpu.VMEM((3, D, FF), BF), pltpu.SemaphoreType.DMA((4,))],
        compiler_params=pltpu.CompilerParams(vmem_limit_bytes=VMEM),
        cost_estimate=pl.CostEstimate(
            flops=flops, bytes_accessed=18000000, transcendentals=SLOTS * FF
        ),
    )(*ins, *pieces)


UNIT = 2 * SLOTS * D * FF


def expert_forward(rows, pieces):
    return expert_call(
        expert_kernel, "expert_forward", [rows], pieces, [(D, BF), (FF, F32), (FF, F32)], 3 * UNIT
    )


def expert_both(rows, target, pieces):
    return expert_call(
        expert_both_kernel, "expert_forward_backward", [rows, target], pieces,
        [(WIDE, BF), (FF, BF), (FF, BF), (FF, BF), (D, BF), (D, BF)], 6 * UNIT,
    )


def expert_back(a, b, grads, pieces):
    return expert_call(
        expert_back_kernel, "expert_backward", [a, b, grads], pieces,
        [(D, BF), (FF, BF), (FF, BF), (FF, BF)], 3 * UNIT,
    )


def expert_grads(rows, grads, da, db, inner):
    columns = pl.BlockSpec((SLOTS, D // 4), lambda i: (0, i))
    whole = pl.BlockSpec((SLOTS, FF), lambda i: (0, 0), pipeline_mode=pl.Buffered(1))
    return pl.pallas_call(
        expert_grad_kernel,
        name="expert_weight_gradients",
        out_shape=[jax.ShapeDtypeStruct((D, FF), BF)] * 3,
        grid=(4,),
        in_specs=[columns, columns] + [whole] * 3,
        out_specs=[pl.BlockSpec((D // 4, FF), lambda i: (i, 0))] * 3,
        compiler_params=pltpu.CompilerParams(vmem_limit_bytes=VMEM),
        cost_estimate=pl.CostEstimate(
            flops=3 * UNIT, bytes_accessed=18000000, transcendentals=0
        ),
    )(rows, grads, da, db, inner)


def route_tables(route_rows):
    named = (route_rows[:, :, None] == jnp.arange(E, dtype=jnp.int32)).astype(F32).sum(1)
    earlier = (jnp.arange(T)[:, None] > jnp.arange(T)[None, :]).astype(BF)
    rank = dot(earlier, named.astype(BF))
    named_t, rank_t = named.T, rank.T
    places = (named_t[:, None, :] > 0) & (
        rank_t[:, None, :] == jnp.arange(C, dtype=F32)[None, :, None]
    )
    return named, places.astype(F32)


def exchange(rows):
    width = rows.shape[1]
    rows = rows.reshape(E, C, width)
    rows = lax.all_to_all(rows, GROUP, split_axis=0, concat_axis=0, tiled=True)
    return rows.reshape(SLOTS, width)


def gate_softmax(routing, named):
    masked = jnp.where(named > 0, routing, -jnp.inf)
    terms = jnp.exp(masked - jnp.max(masked, axis=-1, keepdims=True))
    return terms / jnp.sum(terms, axis=-1, keepdims=True)


def add_routed(middle, routed, slot_gates, places):
    high, low = split_two(slot_gates * places.reshape(SLOTS, T))
    return middle + dot(high, routed, ((0,), (0,))) + dot(low, routed, ((0,), (0,)))


def norm(inputs, gain):
    scale = lax.rsqrt(jnp.mean(inputs * inputs, axis=-1, keepdims=True) + EPS)
    return (inputs * scale * gain).astype(BF)


def norm_backward(inputs, gain, grad_normed, grad_residual):
    scale = lax.rsqrt(jnp.mean(inputs * inputs, axis=-1, keepdims=True) + EPS)
    unit = inputs * scale
    grad_gain = jnp.sum(grad_normed * unit, axis=0)
    grad_unit = grad_normed * gain
    back = grad_unit - unit * jnp.mean(grad_unit * unit, axis=-1, keepdims=True)
    return grad_residual + scale * back, grad_gain


def row_orders():
    place = jnp.arange(D)
    outer, middle, dp, row = place // 384, place // 96 % 4, place // 24 % 4, place % 24
    first = ((dp * 4 + outer) * 4 + middle) * 24 + row
    second = ((dp * 4 + middle) * 4 + outer) * 24 + row
    return [(place[:, None] == source[None, :]).astype(BF) for source in (first, second)]


def reorder(rows, order):
    return dot(rows, order).astype(BF)


def products_kernel(
    normed, normed_first, grads, grads_second, heads, att, routing, gains, gain_place,
    first_out, second_out, third_out,
):
    def product(left, right):
        return dot(left, right, ((0,), (0,)))

    first_out[0] = product(normed_first[...], heads[:, :PART]).astype(BF).reshape(4, 96, PART)
    second_out[0] = product(grads_second[...], att[:, :PART]).astype(BF).reshape(4, 96, PART)
    rows = normed[...]
    third = [
        product(rows, heads[:, PART:]),
        product(grads[...], att[:, PART:]),
        product(rows, routing[...]) + product(gains[...], gain_place[...]),
    ]
    third = jnp.concatenate(third, axis=1).astype(BF)
    third_out[0] = third.reshape(4, 96, PART)


def mixer_products(normed, normed_first, grads, grads_second, heads, att, routing, gains):
    rows = []
    for gain in gains:
        rows += list(split_two(gain[None]))
    gains = jnp.concatenate(rows + [jnp.zeros((12, D), BF)])
    number, column = jnp.arange(16)[:, None], jnp.arange(COLS - WR)[None, :]
    gain_place = ((number < 4) & (column == E + number // 2)).astype(BF)
    routing = jnp.concatenate([routing, jnp.zeros((T, COLS - WR), BF)])

    def block(v):
        return pl.BlockSpec((v.shape[0], D // 4), lambda i: (0, i))

    def whole(v):
        return pl.BlockSpec(v.shape, lambda i: (0, 0))

    lefts = [normed, normed_first, grads, grads_second]
    rights = [heads.reshape(2 * T, WO), att.reshape(2 * T, WR - WO), routing]
    return pl.pallas_call(
        products_kernel,
        name="mixer_products",
        grid=(4,),
        out_shape=[jax.ShapeDtypeStruct((4, 4, 96, PART), BF)] * 3,
        in_specs=[block(v) for v in lefts]
        + [whole(v) for v in rights]
        + [block(gains), whole(gain_place)],
        out_specs=[pl.BlockSpec((1, 4, 96, PART), lambda i: (i, 0, 0, 0))] * 3,
        compiler_params=pltpu.CompilerParams(vmem_limit_bytes=VMEM),
        cost_estimate=pl.CostEstimate(
            flops=2 * 2 * T * D * COLS, bytes_accessed=11000000, transcendentals=0
        ),
    )(*lefts, *rights, gains, gain_place)


def outputs_kernel(core, mine, theirs, q_out, k_out, v_out, o_out, routing_out):
    first = core[0] == 0
    for level in range(LAYERS):

        def rows(ref, group):
            return jnp.where(first, ref[level * 3 + group, :12], ref[level * 3 + group, 12:])

        halves = []
        for ref in (mine, theirs):
            a, b, c = (rows(ref, group) for group in range(3))
            halves.append(
                (
                    jnp.concatenate([a, c[:, :HD]], axis=1),
                    c[:, HD : 2 * HD],
                    c[:, 2 * HD : 3 * HD],
                    jnp.concatenate([b, c[:, 3 * HD : 4 * HD]], axis=1),
                )
            )
            halves[-1] += (c[:, 4 * HD :],)
        for out, own, other in zip((q_out, k_out, v_out, o_out), *halves):
            width = own.shape[1]
            out[level, :, :width] = jnp.where(first, own, other)
            out[level, :, width:] = jnp.where(first, other, own)
        routing_out[level] = halves[0][4] + halves[1][4]


def mixer_outputs(sums, core):
    widths = (D, 2 * HD, 2 * HD, D, HD)
    *outs, routing = pl.pallas_call(
        outputs_kernel,
        name="mixer_outputs",
        out_shape=[jax.ShapeDtypeStruct((LAYERS, 12, width), F32) for width in widths],
        in_specs=[pl.BlockSpec(memory_space=pltpu.SMEM), VM, VM],
        out_specs=[VM] * 5,
    )(core.reshape(1), sums, swap(sums))
    return (*outs, routing[:, :, :E], routing[:, :, E], routing[:, :, E + 1])


def reduce_expert(grads):
    return [
        lax.psum_scatter(g, "dp", scatter_dimension=0, tiled=True).astype(F32) for g in grads
    ]


def per_device(
    tokens, segments, route_ids, w_query, key_projection, value_projection, w_out, w_router,
    gain_attn, gain_moe, w_gate, w_up, w_down, cotangent,
):
    core = lax.axis_index("core")
    orders = row_orders()
    cosine, sine = rope_tables()
    position = jnp.arange(T)

    shared = jnp.concatenate(
        [
            w_router, gain_attn[:, :, None], gain_moe[:, :, None],
            jnp.zeros((LAYERS, 12, COLS - WR - E - 2), BF),
        ],
        axis=2,
    )

    def half(number):
        def cut(v):
            width = v.shape[2] // 2
            return v[:, :, number * width : (number + 1) * width]

        return jnp.concatenate(
            [cut(v) for v in (w_query, key_projection, value_projection, w_out)] + [shared], axis=2
        )

    halves = (half(0), half(1))
    mine = jnp.where(core == 0, halves[0], halves[1])
    theirs = swap(jnp.where(core == 0, halves[1], halves[0]))
    blocks = jnp.where(
        core == 0,
        jnp.concatenate([mine, theirs], axis=1),
        jnp.concatenate([theirs, mine], axis=1),
    )
    shards = jnp.stack([w_gate[:, 0], w_up[:, 0], w_down[:, 0]], axis=1)
    tables = [route_tables(route_ids[level]) for level in range(LAYERS)]
    target = dot(tables[1][1].astype(BF).reshape(SLOTS, T), cotangent).astype(BF)
    first_mixer, first_experts = gather(blocks[0], shards[0, :2])
    second = lax.optimization_barrier((blocks[1], shards[1].reshape(3 * 384, FF), first_experts))
    second_mixer = lax.all_gather(second[0], AXES[:3], axis=0).reshape(D, COLS)
    second_experts = lax.all_gather(second[1], "dp", axis=0)
    mixers = [first_mixer, second_mixer]
    experts = [None, (second_experts.reshape(4, 3, 384, FF),)]

    segment = segments.astype(F32)
    segment = jnp.concatenate([segment, swap(segment)])
    mask = (position[:, None] >= position[None, :])[None] & (
        segment[:, :, None] == segment[:, None, :]
    )
    mask = mask.astype(F32)

    hidden = tokens.astype(F32)
    grad = cotangent.astype(F32)
    state = []
    for level in range(LAYERS):
        named, places = tables[level]
        gain_one = mixers[level][:, WR + E].astype(F32)
        gain_two = mixers[level][:, WR + E + 1].astype(F32)
        spread = places.astype(BF).reshape(SLOTS, T)
        normed = norm(hidden, gain_one)
        normed_other = swap(normed)
        heads, att, own, other, routing = attend(
            normed, normed_other, mixers[level], cosine, sine, mask
        )
        gates = gate_softmax(routing[:, :E], named)
        slot_gates = jnp.sum(places * gates.T[:, None, :], axis=-1).reshape(SLOTS, 1)
        middle = hidden + own + swap(other).astype(F32)
        send = dot(spread, norm(middle, gain_two)).astype(BF)
        if level == LAYERS - 1:
            gate_high, gate_low = split_two(slot_gates)
            send = jnp.concatenate(
                [send, gate_high, gate_low, jnp.zeros((SLOTS, WIDE - D - 2), BF)], axis=1
            )
            rows = exchange(send)
            dx, da, db, inner, produced, dy = expert_both(rows, target, experts[level])
            dx = exchange(dx)
            routed = exchange(produced)
            expert_parts = expert_grads(rows, dy, da, db, inner)
            dx, expert_parts = lax.optimization_barrier((dx, expert_parts))
            inside = None
        else:
            rows, last_expert = dispatch(send, shards[0, 2:])
            experts[0] = (first_experts, last_expert)
            produced, *inside = expert_forward(rows, experts[level])
            routed = exchange(produced)
            routed, target = lax.optimization_barrier((routed, target))
            target = exchange(target)
        state.append(
            (hidden, middle, normed, normed_other, heads, att, gates, slot_gates, spread, rows,
             inside, routed, gain_one, gain_two)
        )
        if level < LAYERS - 1:
            hidden = add_routed(middle, routed, slot_gates, places)
        else:
            last_routed = routed

    products, expert_sums = [None] * LAYERS, [None] * LAYERS
    for level in reversed(range(LAYERS)):
        named, places = tables[level]
        (before, middle, normed, normed_other, heads, att, gates, slot_gates, spread, rows,
         inside, routed, gain_one, gain_two) = state[level]
        if level < LAYERS - 1:
            high, low = split_two(grad)
            grad_slots = dot(spread, high) + dot(spread, low)
            grad_rows = exchange((slot_gates * grad_slots).astype(BF))
            dx, da, db, inner = expert_back(*inside, grad_rows, experts[level])
            dx = exchange(dx)
            expert_parts = expert_grads(rows, grad_rows, da, db, inner)
            dx, expert_parts, expert_sums[1], products[1] = lax.optimization_barrier(
                (dx, expert_parts, expert_sums[1], products[1])
            )
            shares = slot_gates * jnp.sum(routed.astype(F32) * grad_slots, axis=-1, keepdims=True)
        else:
            shares = dx[:, D : D + 1].astype(F32) + dx[:, D + 1 : D + 2].astype(F32)
            dx = dx[:, :D]
        expert_sums[level] = reduce_expert(expert_parts)
        shares = jnp.sum(places * shares.reshape(E, C, 1), axis=1).T
        grad_routing = shares - gates * jnp.sum(shares, axis=-1, keepdims=True)
        grad_routing = jnp.pad(grad_routing.astype(BF), ((0, 0), (0, 128 - E)))
        grad_normed = dot(spread, dx, ((0,), (0,)))
        grad_middle, grad_two = norm_backward(middle, gain_two, grad_normed, grad)
        grad_out = grad_middle.astype(BF)
        grad_out_other = swap(grad_out)
        grad_heads, own, other = attend_back(
            grad_out, grad_out_other, grad_routing, mixers[level], heads, cosine, sine, mask
        )
        grad_normed = own + swap(other).astype(F32)
        grad, grad_one = norm_backward(before, gain_one, grad_normed, grad_middle)
        if level == 0:
            late, grad_heads = lax.optimization_barrier((last_routed, grad_heads))
            hidden = add_routed(state[1][1], late, *state[1][7:8], tables[1][1])
        both_normed = jnp.concatenate([normed, normed_other])
        grads = jnp.concatenate([grad_out, grad_out_other])
        products[level] = mixer_products(
            both_normed, reorder(both_normed, orders[0]), grads, reorder(grads, orders[1]),
            grad_heads, att, grad_routing, (grad_one, grad_two),
        )

    sums = reduce_mixer(products[0] + products[1])
    mixer_out = mixer_outputs(sums, core)
    expert_out = [
        jnp.stack([expert_sums[level][m] for level in range(LAYERS)])[:, None] for m in range(3)
    ]
    return (hidden, grad, *mixer_out, *expert_out)


def solution(mesh):
    mesh = Mesh(mesh.devices.reshape(4, 4, 4, 2), AXES)
    rows = P(AXES, None)
    mixer = P(None, AXES, None)
    gain = P(None, AXES)
    expert = P(None, GROUP, "dp", None)
    return jax.shard_map(
        per_device,
        mesh=mesh,
        in_specs=(
            rows, rows, mixer, mixer, mixer, mixer, mixer, mixer, gain, gain, expert, expert,
            expert, rows,
        ),
        out_specs=(
            rows, rows, mixer, mixer, mixer, mixer, mixer, gain, gain, expert, expert, expert,
        ),
        check_vma=False,
    )
```

```python
import math

import jax
import jax.numpy as jnp
import numpy as np
from jax import lax
from jax.experimental import pallas as pl
from jax.experimental.pallas import tpu as pltpu
from jax.sharding import Mesh, PartitionSpec as P

MESH = pl.DeviceIdType.MESH
BF = jnp.bfloat16
F32 = jnp.float32
HEADS, KV, HD, TOP, LAYERS = 12, 2, 128, 4, 2
T, D, FF, E, C = 128, 1536, 768, 32, 24
SLOTS = E * C
THETA, EPS = 1000000.0, 1e-06
SCALE = 1.0 / math.sqrt(HD)
ANY = pl.BlockSpec(memory_space=pl.ANY)
VM = pl.BlockSpec(memory_space=pltpu.VMEM)
WO, WR, COLS = 1024, 1792, 1920
CUTS = (pl.ds(0, 1024), pl.ds(1024, COLS - 1024))
PART = 640
VMEM = 56 << 20
WIDE = D + 128
AXES = ("dp", "z", "y", "core")
GROUP = AXES[1:]


def dot(a, b, dims=((1,), (0,))):
    return lax.dot_general(a, b, (dims, ((), ())), preferred_element_type=F32)


def split_two(v):
    high = v.astype(BF)
    return high, (v - high.astype(F32)).astype(BF)


def rope_tables():
    frequency = np.exp(-(2.0 * np.arange(HD // 2) / HD) * math.log(THETA)).astype(np.float32)
    angles = np.arange(T, dtype=np.float32)[:, None] * frequency[None, :]
    cosine, sine = np.cos(angles), np.sin(angles)
    return (
        jnp.asarray(np.concatenate([cosine, cosine], 1), F32),
        jnp.asarray(np.concatenate([-sine, sine], 1), F32),
    )


def swap(v):
    return lax.ppermute(v, "core", [(0, 1), (1, 0)])


def neighbours():
    here = [lax.axis_index(axis) for axis in AXES]

    def along(axis, places):
        peer = list(here)
        peer[axis] = lax.rem(here[axis] + places, 4)
        return tuple(peer)

    return here, along


def greet(peers):
    barrier = pltpu.get_barrier_semaphore()
    for peer in peers:
        pl.semaphore_signal(barrier, inc=1, device_id=peer, device_id_type=MESH)
    pl.semaphore_wait(barrier, len(peers))


def sender(send_sem, recv_sem):
    def send(src, dst, number, peer):
        copy = pltpu.make_async_remote_copy(
            src, dst, send_sem.at[number], recv_sem.at[number], device_id=peer, device_id_type=MESH
        )
        copy.start()
        return copy

    return send


def ring_steps(own, view, me, right, left, send, number):
    first = [
        send(own(0), view(me, 0), number, right), send(own(1), view(me, 1), number + 1, left)
    ]
    second = [
        send(own(1), view(me, 1), number + 2, right), send(own(0), view(me, 0), number + 3, left)
    ]

    relays = []

    def relay():
        before, after = lax.rem(me + 3, 4), lax.rem(me + 1, 4)
        first[0].wait_recv()
        relays.append(send(view(before, 0), view(before, 0), number + 4, right))
        first[1].wait_recv()
        relays.append(send(view(after, 1), view(after, 1), number + 5, left))

    def finish():
        for copy in second:
            copy.wait_recv()
        for copy in first + second:
            copy.wait_send()
        for copy in relays:
            copy.wait()

    return relay, finish


def ring_of(shard, out, x, along, send, number):
    return ring_steps(
        lambda half: shard.at[pl.ds(half * 192, 192)],
        lambda place, half: out.at[place, pl.ds(half * 192, 192)],
        x, along(0, 1), along(0, 3), send, number,
    )


def gather_kernel(blocks, gate, up, out, experts, local_sem, send_sem, recv_sem):
    (x, z, y, _), along = neighbours()
    greet([along(axis, o) for o in (1, 2, 3) for axis in range(3)])
    send = sender(send_sem, recv_sem)
    block = blocks.at[0]
    copies = [send(block, out.at[x, z, y], o - 1, along(0, o)) for o in (1, 3, 2)]
    shards = [gate.at[0, 0], up.at[0, 0]]
    rings = [
        ring_of(shard, experts.at[n], x, along, send, 27 + 6 * n) for n, shard in enumerate(shards)
    ]
    own = pltpu.make_async_copy(block, out.at[x, z, y], local_sem.at[0])
    own.start()
    own_experts = [
        pltpu.make_async_copy(shard, experts.at[n, x], local_sem.at[1 + n])
        for n, shard in enumerate(shards)
    ]
    for copy in own_experts:
        copy.start()
    own.wait()
    for copy in copies:
        copy.wait()

    def ring(view, axis, me, number):
        return ring_steps(
            lambda half: view(me, half), view, me, along(axis, 1), along(axis, 3), send, number
        )

    def pair(half):
        return pl.ds(half * 2, 2)

    first = ring(lambda n, half: out.at[pair(half), n, y, :, CUTS[0]], 1, z, 3)
    second = ring(lambda n, half: out.at[pair(half), z, n, :, CUTS[1]], 2, y, 9)
    first[0]()
    second[0]()
    first[1]()
    first = ring(lambda n, half: out.at[pair(half), :, n, :, CUTS[0]], 2, y, 15)
    second[1]()
    second = ring(lambda n, half: out.at[pair(half), n, :, :, CUTS[1]], 1, z, 21)
    rings[0][0]()
    first[0]()
    second[0]()
    rings[1][0]()
    first[1]()
    second[1]()
    for ring in rings:
        ring[1]()
    for copy in own_experts:
        copy.wait()


def gather(blocks, gate, up):
    mixer, experts = pl.pallas_call(
        gather_kernel,
        name="gather_weights",
        out_shape=(
            jax.ShapeDtypeStruct((4, 4, 4, 24, COLS), BF),
            jax.ShapeDtypeStruct((2, 4, D // 4, FF), BF),
        ),
        in_specs=[ANY] * 3,
        out_specs=(ANY, ANY),
        scratch_shapes=[
            pltpu.SemaphoreType.DMA((3,)),
            pltpu.SemaphoreType.DMA((39,)),
            pltpu.SemaphoreType.DMA((39,)),
        ],
        compiler_params=pltpu.CompilerParams(
            collective_id=1, has_side_effects=True, vmem_limit_bytes=VMEM
        ),
    )(blocks, gate, up)
    return mixer.reshape(D, COLS), experts.reshape(1, 2, D, FF)


OFFSETS = sorted(
    ((a, b, c) for a in range(4) for b in range(4) for c in range(2) if a or b or c),
    key=lambda o: -min(o[0], 4 - o[0]) - min(o[1], 4 - o[1]),
)


def dispatch_kernel(level, rows, shards, out, experts, local_sem, send_sem, recv_sem):
    (x, z, y, core), along = neighbours()
    peers = [
        (x, lax.rem(z + a, 4), lax.rem(y + b, 4), lax.rem(core + c, 2)) for a, b, c in OFFSETS
    ]
    greet(peers + [along(0, 1), along(0, 3)])
    send = sender(send_sem, recv_sem)
    me = (z * 4 + y) * 2 + core
    shard = shards.at[level, 0]
    ring = ring_of(shard, experts.at[0], x, along, send, len(peers))
    copies = []
    for n, peer in enumerate(peers):
        index = (peer[1] * 4 + peer[2]) * 2 + peer[3]
        copies.append(send(rows.at[index], out.at[me], n, peer))
    local = [
        pltpu.make_async_copy(rows.at[me], out.at[me], local_sem.at[0]),
        pltpu.make_async_copy(shard, experts.at[0, x], local_sem.at[1]),
    ]
    for copy in local:
        copy.start()
    ring[0]()
    for copy in copies + local:
        copy.wait()
    ring[1]()


def dispatch(rows, shards, level):
    rows, experts = pl.pallas_call(
        lambda *refs: dispatch_kernel(level, *refs),
        name="dispatch_rows",
        out_shape=(
            jax.ShapeDtypeStruct((E, C, D), BF),
            jax.ShapeDtypeStruct((1, 4, D // 4, FF), BF),
        ),
        in_specs=[ANY, ANY],
        out_specs=(ANY, ANY),
        scratch_shapes=[
            pltpu.SemaphoreType.DMA((2,)),
            pltpu.SemaphoreType.DMA((len(OFFSETS) + 6,)),
            pltpu.SemaphoreType.DMA((len(OFFSETS) + 6,)),
        ],
        compiler_params=pltpu.CompilerParams(
            collective_id=3 + level, has_side_effects=True, vmem_limit_bytes=VMEM
        ),
    )(rows.reshape(E, C, D), shards)
    return rows.reshape(SLOTS, D), experts.reshape(1, 1, D, FF)


def reduce_mixer_kernel(*refs):
    sources, out, scratch = refs[:6], refs[6], refs[7:]
    (x, z, y, _), along = neighbours()
    local_sem, send_sem, recv_sem = scratch[-3:]
    greet([along(axis, o) for o in (1, 2, 3) for axis in range(3)])
    send = sender(send_sem, recv_sem)
    jobs = []
    ways = (((1, z), (2, y), (0, x)), ((2, y), (1, z), (0, x)), ((0, x), (1, z), (2, y)))
    for level in reversed(range(LAYERS)):
        for group, way in enumerate(ways):
            number = level * 3 + group
            held = scratch[number * 10 : number * 10 + 10]
            jobs.append((number, sources[number], out.at[number], way, held))

    def start_first(job):
        number, source, _, ((axis, me), _, _), (got, passed, relay, mine, own, *_) = job
        right, left = along(axis, 1), along(axis, 3)
        after, far, before = (lax.rem(me + o, 4) for o in (1, 2, 3))
        low, high = pl.ds(0, 2), pl.ds(2, 2)
        base = number * 12
        copies = [
            send(source.at[far, low], passed.at[0], base, right),
            send(source.at[far, high], passed.at[1], base + 1, left),
            send(source.at[after, high], got.at[0, high], base + 2, right),
            send(source.at[before, low], got.at[1, low], base + 3, left),
        ]
        local = []
        for n, (src, dst) in enumerate(
            (
                (source.at[after, low], mine.at[0]),
                (source.at[before, high], mine.at[1]),
                (source.at[me], own),
            )
        ):
            local.append(pltpu.make_async_copy(src, dst, local_sem.at[number * 3 + n]))
            local[n].start()

        def pass_on():
            for n, (part, peer) in enumerate(((low, right), (high, left))):
                copies[n].wait()
                local[n].wait()
                total = mine[n].astype(F32) + passed[n].astype(F32)
                relay[n] = total.astype(BF)
                copies.append(send(relay.at[n], got.at[n, part], base + 4 + n, peer))

        def finish():
            for copy in copies[2:]:
                copy.wait()
            local[2].wait()

        return pass_on, finish

    def start_second(job):
        number, _, _, (_, (axis, me), _), (got, _, _, _, own, total, ready, after, *_) = job
        total[...] = own[...].astype(F32) + got[0].astype(F32) + got[1].astype(F32)
        started = []
        for o in (2, 1, 3):
            ready[o - 1] = total[lax.rem(me + o, 4)].astype(BF)
            started.append(
                send(ready.at[o - 1], after.at[o - 1], number * 12 + 5 + o, along(axis, o))
            )
        return started

    def start_third(job, copies):
        number, _, _, (_, (_, me), (axis, there)), (*_, total, _, after, small, last) = job
        for copy in copies:
            copy.wait()
        rows = total[me]
        for o in range(3):
            rows = rows + after[o].astype(F32)
        for i in range(4):
            small[i] = rows[i * 24 : (i + 1) * 24]
        return [
            send(small.at[lax.rem(there + o, 4)], last.at[o - 1], number * 12 + 8 + o, along(axis, o))
            for o in (2, 1, 3)
        ]

    def end(job, copies):
        _, _, out, (_, _, (_, there)), (*_, small, last) = job
        for copy in copies:
            copy.wait()
        out[...] = small[there] + last[0] + last[1] + last[2]

    running = [start_first(job) for job in jobs]
    for pass_on, _ in running:
        pass_on()
    seconds = []
    for job, (_, finish) in zip(jobs, running):
        finish()
        seconds.append(start_second(job))
    running = seconds
    running = [start_third(job, copies) for job, copies in zip(jobs, running)]
    for job, copies in zip(jobs, running):
        end(job, copies)


def reduce_mixer(products):
    scratch = []
    for _ in products:
        scratch += [
            pltpu.VMEM((2, 4, 96, PART), BF),
            pltpu.VMEM((2, 2, 96, PART), BF),
            pltpu.VMEM((2, 2, 96, PART), BF),
            pltpu.VMEM((2, 2, 96, PART), BF),
            pltpu.VMEM((4, 96, PART), BF),
            pltpu.VMEM((4, 96, PART), F32),
            pltpu.VMEM((3, 96, PART), BF),
            pltpu.VMEM((3, 96, PART), BF),
            pltpu.VMEM((4, 24, PART), F32),
            pltpu.VMEM((3, 24, PART), F32),
        ]
    return pl.pallas_call(
        reduce_mixer_kernel,
        name="reduce_mixer_gradients",
        out_shape=jax.ShapeDtypeStruct((6, 24, PART), F32),
        in_specs=[ANY] * 6,
        out_specs=VM,
        scratch_shapes=scratch
        + [
            pltpu.SemaphoreType.DMA((18,)),
            pltpu.SemaphoreType.DMA((72,)),
            pltpu.SemaphoreType.DMA((72,)),
        ],
        compiler_params=pltpu.CompilerParams(
            collective_id=2, has_side_effects=True, vmem_limit_bytes=VMEM
        ),
    )(*products)


def columns(shape):
    return lax.broadcasted_iota(jnp.int32, shape, 1)


def rows_of(shape):
    return lax.broadcasted_iota(jnp.int32, shape, 0)


def plain(kernel, name, outs, flops=0, bytes_accessed=4000000, ins=None, scratch=()):
    def call(*args):
        return pl.pallas_call(
            kernel,
            name=name,
            out_shape=[jax.ShapeDtypeStruct(shape, kind) for shape, kind in outs],
            in_specs=ins or [VM] * len(args),
            out_specs=[VM] * len(outs),
            scratch_shapes=list(scratch),
            compiler_params=pltpu.CompilerParams(vmem_limit_bytes=VMEM),
            cost_estimate=pl.CostEstimate(
                flops=flops, bytes_accessed=bytes_accessed, transcendentals=0
            ),
        )(*args)

    return call


def tables_kernel(routes, *outs):
    wide = (T, 128)
    earlier = (rows_of(wide) < columns(wide)).astype(BF)
    same = (rows_of(wide) == columns(wide)).astype(BF)
    for level in range(LAYERS):
        named = jnp.zeros(wide, F32)
        for k in range(TOP):
            named = named + (routes[level, :, k : k + 1] == columns(wide)).astype(F32)
        outs[level][...] = named
        turned = dot(named.astype(BF), same, ((0,), (0,)))[:E]
        rank = dot(named.astype(BF), earlier, ((0,), (0,)))[:E]
        place = lax.broadcasted_iota(jnp.int32, (E, C, T), 1).astype(F32)
        hit = jnp.where(rank[:, None, :] == place, turned[:, None, :], 0.0)
        outs[LAYERS + level][...] = hit.reshape(SLOTS, T).astype(BF)


def route_tables(routes):
    return plain(
        tables_kernel, "route_tables",
        [((T, 128), F32)] * LAYERS + [((SLOTS, T), BF)] * LAYERS,
    )(routes)


def unit_rows(rows):
    scale = lax.rsqrt(jnp.mean(rows * rows, axis=-1, keepdims=True) + EPS)
    return rows * scale, scale


def gain_rows(router):
    pick = (columns((8, 128)) == E + rows_of((8, 128))) & (rows_of((8, 128)) < 2)
    return dot(pick.astype(BF), router, ((1,), (1,)))


def slot_columns():
    shape = (SLOTS, 128)
    start = columns(shape) * C
    return (rows_of(shape) >= start) & (rows_of(shape) < start + C)


def post_kernel(
    hidden, own, other, gains, routing, named, spread, middle_out, send_out, gates_out, slot_out
):
    middle = hidden[...].astype(F32) + own[...] + other[...].astype(F32)
    middle_out[...] = middle
    normed = (unit_rows(middle)[0] * gains[1:2]).astype(BF)
    send_out[:, :D] = dot(spread[...], normed).astype(BF)
    masked = jnp.where(named[...] > 0, routing[...], -1e30)
    terms = jnp.exp(masked - jnp.max(masked, axis=-1, keepdims=True))
    terms = jnp.where(named[...] > 0, terms, 0.0)
    gates = terms / jnp.sum(terms, axis=-1, keepdims=True)
    gates_out[...] = gates
    high, low = split_two(gates)
    all_gates = dot(spread[...], high) + dot(spread[...], low)
    slot = jnp.sum(jnp.where(slot_columns(), all_gates, 0.0), axis=-1, keepdims=True)
    slot_out[...] = slot
    if send_out.shape[1] > D:
        send_out[:, D:] = two_columns(slot)


def two_columns(value):
    high = value.astype(BF).astype(F32)
    column = columns((value.shape[0], WIDE - D))
    return jnp.where(column == 0, high, jnp.where(column == 1, value - high, 0.0)).astype(BF)


def post(width, *args):
    return plain(
        post_kernel, "dispatch_rows_of_tokens",
        [((T, D), F32), ((SLOTS, width), BF), ((T, 128), F32), ((SLOTS, 1), F32)], 2 * SLOTS * T * D,
    )(*args)


def combine_kernel(middle, routed, spread, slot, *refs):
    mix = spread[...].astype(F32) * slot[...]
    high, low = split_two(mix)
    rows = routed[...]
    hidden = middle[...] + dot(high, rows, ((0,), (0,))) + dot(low, rows, ((0,), (0,)))
    if len(refs) == 1:
        refs[0][...] = hidden
        return
    mixers, hidden_out, normed_out, gains_out, router, sem = refs
    copy = pltpu.make_async_copy(mixers.at[:, pl.ds(WR, COLS - WR)], router, sem)
    copy.start()
    hidden_out[...] = hidden
    copy.wait()
    gains = gain_rows(router[...])
    gains_out[...] = gains
    normed_out[...] = (unit_rows(hidden)[0] * gains[0:1]).astype(BF)


def combine(middle, routed, spread, slot):
    return plain(combine_kernel, "add_expert_outputs", [((T, D), F32)], 4 * SLOTS * T * D)(
        middle, routed, spread, slot
    )[0]


def combine_next(middle, routed, spread, slot, mixers):
    return plain(
        combine_kernel, "add_expert_outputs_and_norm",
        [((T, D), F32), ((T, D), BF), ((8, D), F32)], 4 * SLOTS * T * D,
        ins=[VM] * 4 + [ANY],
        scratch=[pltpu.VMEM((D, COLS - WR), BF), pltpu.SemaphoreType.DMA],
    )(middle, routed, spread, slot, mixers)


def back_through_norm(inputs, gain, grad_normed, grad_residual):
    unit, scale = unit_rows(inputs)
    grad_gain = jnp.sum(grad_normed * unit, axis=0, keepdims=True)
    grad_unit = grad_normed * gain
    back = grad_unit - unit * jnp.mean(grad_unit * unit, axis=-1, keepdims=True)
    return grad_residual + scale * back, grad_gain


def pre_back_kernel(
    dx, shares, middle, gains, grad, spread, gates, middle_out, out_out, routing_out, gain_out
):
    table = spread[...]
    if shares is None:
        share = dx[:, D : D + 1].astype(F32) + dx[:, D + 1 : D + 2].astype(F32)
    else:
        share = shares[...]
    high, low = split_two(jnp.where(slot_columns(), share, 0.0))
    dense = dot(table, high, ((0,), (0,))) + dot(table, low, ((0,), (0,)))
    routing = dense - gates[...] * jnp.sum(dense, axis=-1, keepdims=True)
    routing_out[...] = routing.astype(BF)
    grad_normed = dot(table, dx[:, :D], ((0,), (0,)))
    grad_middle, grad_gain = back_through_norm(
        middle[...], gains[1:2], grad_normed, grad[...].astype(F32)
    )
    middle_out[...] = grad_middle
    out_out[...] = grad_middle.astype(BF)
    gain_out[...] = grad_gain


def pre_back(dx, shares, *args):
    outs = [((T, D), F32), ((T, D), BF), ((T, 128), BF), ((1, D), F32)]
    if shares is None:
        return plain(
            lambda dx, *refs: pre_back_kernel(dx, None, *refs), "back_to_middle", outs,
            2 * SLOTS * T * D,
        )(dx, *args)
    return plain(pre_back_kernel, "back_to_middle", outs, 2 * SLOTS * T * D)(dx, shares, *args)


def post_back_kernel(own, other, hidden, gains, grad_middle, gain_two, *refs):
    grad_normed = own[...] + other[...].astype(F32)
    grad, gain_one = back_through_norm(
        hidden[...].astype(F32), gains[0:1], grad_normed, grad_middle[...]
    )
    if len(refs) == 2:
        grad_out, rows_out = refs
    else:
        spread, slot, routed, grad_out, rows_out, dy_out, share_out = refs
        high, low = split_two(grad)
        slots = dot(spread[...], high) + dot(spread[...], low)
        dy_out[...] = (slot[...] * slots).astype(BF)
        share = jnp.sum(routed[...].astype(F32) * slots, axis=-1, keepdims=True)
        share_out[...] = slot[...] * share
    grad_out[...] = grad
    rows_out[...] = jnp.zeros((16, D), BF)
    for n, gain in enumerate((gain_one, gain_two[...])):
        high, low = split_two(gain)
        rows_out[2 * n : 2 * n + 1] = high
        rows_out[2 * n + 1 : 2 * n + 2] = low


def post_back(*args):
    outs = [((T, D), F32), ((16, D), BF)]
    if len(args) > 6:
        outs += [((SLOTS, D), BF), ((SLOTS, 1), F32)]
    return plain(post_back_kernel, "back_to_hidden", outs, 4 * SLOTS * T * D)(*args)


def row_order(step, first):
    place = columns((1, D // 4))
    middle = sum((place >= 96 * n).astype(jnp.int32) for n in (1, 2, 3))
    place = place - 96 * middle
    dp = sum((place >= 24 * n).astype(jnp.int32) for n in (1, 2, 3))
    row = place - 24 * dp
    z, y = (step, middle) if first else (middle, step)
    source = ((dp * 4 + z) * 4 + y) * 24 + row
    return (rows_of((D, D // 4)) == source).astype(BF)


def products_kernel(
    normed, grads_own, grads_other, heads, att, routing, gains,
    first_out, second_out, third_out, grads,
):
    step = pl.program_id(0)

    @pl.when(step == 0)
    def _():
        grads[:T] = grads_own[...]
        grads[T:] = grads_other[...]

    def product(left, right):
        return dot(left, right, ((0,), (0,)))

    def pair(ref, start, stop):
        return jnp.concatenate([ref[0, :, start:stop], ref[1, :, start:stop]], axis=0)

    left = dot(normed[...], row_order(step, True)).astype(BF)
    first = product(left, pair(heads, 0, PART))
    first_out[0] = first.astype(BF).reshape(4, 96, PART)
    left = dot(grads[...], row_order(step, False)).astype(BF)
    second_out[0] = product(left, pair(att, 0, PART)).astype(BF).reshape(4, 96, PART)
    block = pl.ds(pl.multiple_of(step * (D // 4), 128), D // 4)
    left = normed[:, block]
    number, column = rows_of((16, 128)), columns((16, 128))
    gain_place = ((number < 2) & (column == E)) | (
        (number >= 2) & (number < 4) & (column == E + 1)
    )
    third = [
        product(left, pair(heads, PART, WO)),
        product(grads[:, block], pair(att, PART, WR - WO)),
        product(left[:T], routing[...]) + product(gains[:, block], gain_place.astype(BF)),
    ]
    third_out[0] = jnp.concatenate(third, axis=1).astype(BF).reshape(4, 96, PART)


def mixer_products(normed, grads_own, grads_other, heads, att, routing, gains):
    def whole(v):
        zeros = (0,) * len(v.shape)
        return pl.BlockSpec(v.shape, lambda i: zeros, pipeline_mode=pl.Buffered(1))

    args = [normed, grads_own, grads_other, heads, att, routing, gains]
    return pl.pallas_call(
        products_kernel,
        name="mixer_products",
        grid=(4,),
        out_shape=[jax.ShapeDtypeStruct((4, 4, 96, PART), BF)] * 3,
        in_specs=[whole(v) for v in args],
        out_specs=[pl.BlockSpec((1, 4, 96, PART), lambda i: (i, 0, 0, 0))] * 3,
        scratch_shapes=[pltpu.VMEM((2 * T, D), BF)],
        compiler_params=pltpu.CompilerParams(vmem_limit_bytes=VMEM),
        cost_estimate=pl.CostEstimate(
            flops=2 * 2 * T * D * COLS, bytes_accessed=11000000, transcendentals=0
        ),
    )(*args)


def turn(rows, cosine, sine):
    return rows * cosine + pltpu.roll(rows, HD // 2, 1) * sine


def head_rows(ref, sequence, heads):
    return jnp.concatenate([ref[sequence, :, h * HD : (h + 1) * HD] for h in heads], axis=0)


def weigh(queries, keys, mask):
    raw = dot(queries, keys, ((1,), (1,))).reshape(6, T, T)
    logits = jnp.where(mask[None] > 0, raw * SCALE, -1e30)
    terms = jnp.exp(logits - jnp.max(logits, axis=-1, keepdims=True))
    return (terms / jnp.sum(terms, axis=-1, keepdims=True)).reshape(6 * T, T)


PIECES = (pl.ds(WR, COLS - WR), pl.ds(0, WO), pl.ds(WO, WR - WO))


class Several:
    def __init__(self, copies):
        self.copies = copies
        for copy in copies:
            copy.start()

    def wait(self):
        for copy in self.copies:
            copy.wait()


def fetch_weights(mixers, weights, sem):
    groups = []
    for n, place in enumerate(PIECES):
        rows = [pl.ds(i * (D // 4), D // 4) for i in range(4)]
        groups.append(
            Several(
                [
                    pltpu.make_async_copy(
                        mixers.at[r, place], weights.at[r, place], sem.at[n * 4 + i]
                    )
                    for i, r in enumerate(rows)
                ]
            )
        )
    return groups


def attend_kernel(first, own, other, mixers, cosine, sine, mask, *refs):
    *refs, weights, sem = refs
    both, heads_out, att_out, own_out, other_out, routing_out = refs[:6]
    copies = fetch_weights(mixers, weights, sem)
    if first:
        units = [unit_rows(v[...].astype(F32))[0] for v in (own, other)]
        copies[0].wait()
        gains = gain_rows(weights[:, WR:])
        refs[6][...] = gains
        both[:T] = (units[0] * gains[0:1]).astype(BF)
        both[T:] = (units[1] * gains[0:1]).astype(BF)
    else:
        both[:T] = own[...]
        both[T:] = other[...]
        copies[0].wait()
    turns = [jnp.concatenate([t[...], t[...]], axis=0) for t in (cosine, sine)]
    copies[1].wait()
    for tile in range(4):
        wide = dot(both[...], weights[:, tile * 256 : (tile + 1) * 256])
        for part in range(2):
            head = tile * 2 + part
            rows = wide[:, part * HD : (part + 1) * HD]
            if head < 7:
                rows = turn(rows, *turns)
            rows = rows.astype(BF)
            for s in range(2):
                heads_out[s, :, head * HD : (head + 1) * HD] = rows[s * T : (s + 1) * T]
    for s in range(2):
        probs = weigh(head_rows(heads_out, s, range(6)), heads_out[s, :, 768:896], mask[s])
        mixed = dot(probs.astype(BF), heads_out[s, :, 896:]).astype(BF)
        for h in range(6):
            att_out[s, :, h * HD : (h + 1) * HD] = mixed[h * T : (h + 1) * T]
    copies[2].wait()
    att = att_out[...].reshape(2 * T, 768)
    for tile in range(6):
        place = slice(tile * 256, (tile + 1) * 256)
        rows = dot(att, weights[place, WO:WR], ((1,), (1,)))
        own_out[:, place] = rows[:T]
        other_out[:, place] = rows[T:].astype(BF)
    routing_out[...] = dot(both[:T], weights[:, WR:])


def attend(first, own, other, mixers, cosine, sine, mask):
    outs = [
        ((2 * T, D), BF), ((2, T, WO), BF), ((2, T, WR - WO), BF), ((T, D), F32), ((T, D), BF),
        ((T, 128), F32),
    ]
    return plain(
        lambda *refs: attend_kernel(first, *refs), "attention_forward",
        outs + [((8, D), F32)] * first, 1700000000, 9000000,
        ins=[VM, VM, ANY, VM, VM, VM],
        scratch=[pltpu.VMEM((D, COLS), BF), pltpu.SemaphoreType.DMA((12,))],
    )(own, other, mixers, cosine, sine, mask)


def attend_back_kernel(
    own, other, routing, mixers, heads, cosine, sine, mask,
    grad_heads, own_out, other_out, both, grad_att, weights, sem,
):
    copies = fetch_weights(mixers, weights, sem)
    both[:T] = own[...]
    both[T:] = other[...]
    copies[2].wait()
    for tile in range(3):
        place = slice(tile * 256, (tile + 1) * 256)
        wide = dot(both[...], weights[:, WO + tile * 256 : WO + (tile + 1) * 256]).astype(BF)
        for s in range(2):
            grad_att[s, :, place] = wide[s * T : (s + 1) * T]
    cos, sin = cosine[...], -sine[...]
    for s in range(2):
        queries, grads = head_rows(heads, s, range(6)), head_rows(grad_att, s, range(6))
        keys, values = heads[s, :, 768:896], heads[s, :, 896:]
        probs = weigh(queries, keys, mask[s])
        dp = dot(grads, values, ((1,), (1,)))
        draw = probs * (dp - jnp.sum(probs * dp, axis=-1, keepdims=True))
        draw = (draw * SCALE).astype(BF)
        dq = dot(draw, keys)
        for h in range(6):
            rows = turn(dq[h * T : (h + 1) * T], cos, sin)
            grad_heads[s, :, h * HD : (h + 1) * HD] = rows.astype(BF)
        dk = dot(draw, queries, ((0,), (0,)))
        grad_heads[s, :, 768:896] = turn(dk, cos, sin).astype(BF)
        grad_heads[s, :, 896:] = dot(probs.astype(BF), grads, ((0,), (0,))).astype(BF)
    copies[0].wait()
    copies[1].wait()
    wide = grad_heads[...].reshape(2 * T, 1024)
    for tile in range(6):
        place = slice(tile * 256, (tile + 1) * 256)
        rows = dot(wide, weights[place, :WO], ((1,), (1,)))
        own_out[:, place] = rows[:T] + dot(routing[...], weights[place, WR:], ((1,), (1,)))
        other_out[:, place] = rows[T:].astype(BF)


def attend_back(own, other, routing, mixers, heads, cosine, sine, mask):
    return pl.pallas_call(
        attend_back_kernel,
        name="attention_backward",
        out_shape=(
            jax.ShapeDtypeStruct((2, T, 1024), BF),
            jax.ShapeDtypeStruct((T, D), F32),
            jax.ShapeDtypeStruct((T, D), BF),
        ),
        in_specs=[VM, VM, VM, ANY, VM, VM, VM, VM],
        out_specs=[VM] * 3,
        scratch_shapes=[
            pltpu.VMEM((2 * T, D), BF),
            pltpu.VMEM((2, T, 768), BF),
            pltpu.VMEM((D, COLS), BF),
            pltpu.SemaphoreType.DMA((12,)),
        ],
        compiler_params=pltpu.CompilerParams(vmem_limit_bytes=VMEM),
        cost_estimate=pl.CostEstimate(flops=2200000000, bytes_accessed=9000000, transcendentals=200000),
    )(own, other, routing, mixers, heads, cosine, sine, mask)

ROWS = 256


def load_weights(pieces, weights, sem, order):
    step = pl.program_id(0)
    groups = {}
    matrix = 0
    for piece in pieces:
        count, several = piece.shape[:2]
        for m in range(several):
            rows = D // 4
            groups[matrix + m] = [
                pltpu.make_async_copy(
                    piece.at[0, m, pl.ds(n * rows, rows)] if count == 1 else piece.at[n, m],
                    weights.at[matrix + m, pl.ds(n * rows, rows)],
                    sem.at[(matrix + m) * 4 + n],
                )
                for n in range(4)
            ]
        matrix += several

    @pl.when(step == 0)
    def _():
        for m in order:
            for copy in groups[m]:
                copy.start()

    def ready(m):
        @pl.when(step == 0)
        def _():
            for copy in groups[m]:
                copy.wait()

    return ready


def expert_kernel(rows, *refs):
    *pieces, y_out, a_out, b_out, weights, sem = refs
    ready = load_weights(pieces, weights, sem, (0, 1, 2))
    ready(0)
    a = dot(rows[...], weights[0])
    ready(1)
    b = dot(rows[...], weights[1])
    a_out[...] = a
    b_out[...] = b
    inner = (a * jax.nn.sigmoid(a) * b).astype(BF)
    ready(2)
    y_out[...] = dot(inner, weights[2], ((1,), (1,))).astype(BF)


def expert_both_kernel(rows, target, *refs):
    *pieces, dx_out, da_out, db_out, inner_out, y_out, dy_out, weights, sem = refs
    ready = load_weights(pieces, weights, sem, (0, 1, 2))
    normed = rows[:, :D]
    gate = rows[:, D : D + 1].astype(F32) + rows[:, D + 1 : D + 2].astype(F32)
    dy = (gate * target[...].astype(F32)).astype(BF)
    dy_out[...] = dy
    ready(0)
    a = dot(normed, weights[0])
    ready(1)
    b = dot(normed, weights[1])
    ready(2)
    inner = expert_inner_gradients(a, b, dy, weights, dx_out, da_out, db_out, inner_out)
    y = dot(inner, weights[2], ((1,), (1,))).astype(BF)
    y_out[...] = y
    share = jnp.sum(y.astype(F32) * dy.astype(F32), axis=-1, keepdims=True)
    high = share.astype(BF).astype(F32)
    column = lax.broadcasted_iota(jnp.int32, (ROWS, WIDE - D), 1)
    parts = jnp.where(column == 0, high, jnp.where(column == 1, share - high, 0.0))
    dx_out[:, D:] = parts.astype(BF)


def expert_back_kernel(a_in, b_in, grads, *refs):
    *pieces, dx_out, da_out, db_out, inner_out, weights, sem = refs
    ready = load_weights(pieces, weights, sem, (2, 0, 1))
    ready(2)
    expert_inner_gradients(
        a_in[...], b_in[...], grads[...], weights, dx_out, da_out, db_out, inner_out, ready
    )


def expert_inner_gradients(
    a, b, dy, weights, dx_out, da_out, db_out, inner_out, ready=None
):
    du = dot(dy, weights[2])
    sig = jax.nn.sigmoid(a)
    act = a * sig
    inner = (act * b).astype(BF)
    da = (du * b * sig * (1.0 + a * (1.0 - sig))).astype(BF)
    db = (du * act).astype(BF)
    da_out[...], db_out[...], inner_out[...] = da, db, inner
    if ready:
        ready(0)
        ready(1)
    dx = dot(da, weights[0], ((1,), (1,))) + dot(db, weights[1], ((1,), (1,)))
    dx_out[:, :D] = dx.astype(BF)
    return inner


def expert_grad_kernel(rows, grads, da, db, inner, gate_out, up_out, down_out):
    gate_out[...] = dot(rows[...], da[...], ((0,), (0,))).astype(BF)
    up_out[...] = dot(rows[...], db[...], ((0,), (0,))).astype(BF)
    down_out[...] = dot(grads[...], inner[...], ((0,), (0,))).astype(BF)


def tiled(width):
    return pl.BlockSpec((ROWS, width), lambda i: (i, 0))


def expert_call(kernel, name, ins, pieces, out_widths, flops):
    outs = [jax.ShapeDtypeStruct((SLOTS, w), t) for w, t in out_widths]
    return pl.pallas_call(
        kernel,
        name=name,
        out_shape=outs,
        grid=(SLOTS // ROWS,),
        in_specs=[tiled(v.shape[1]) for v in ins] + [ANY] * len(pieces),
        out_specs=[tiled(w) for w, _ in out_widths],
        scratch_shapes=[pltpu.VMEM((3, D, FF), BF), pltpu.SemaphoreType.DMA((12,))],
        compiler_params=pltpu.CompilerParams(vmem_limit_bytes=VMEM),
        cost_estimate=pl.CostEstimate(
            flops=flops, bytes_accessed=18000000, transcendentals=SLOTS * FF
        ),
    )(*ins, *pieces)


UNIT = 2 * SLOTS * D * FF


def expert_forward(rows, pieces):
    return expert_call(
        expert_kernel, "expert_forward", [rows], pieces, [(D, BF), (FF, F32), (FF, F32)], 3 * UNIT
    )


def expert_both(rows, target, pieces):
    return expert_call(
        expert_both_kernel, "expert_forward_backward", [rows, target], pieces,
        [(WIDE, BF), (FF, BF), (FF, BF), (FF, BF), (D, BF), (D, BF)], 6 * UNIT,
    )


def expert_back(a, b, grads, pieces):
    return expert_call(
        expert_back_kernel, "expert_backward", [a, b, grads], pieces,
        [(D, BF), (FF, BF), (FF, BF), (FF, BF)], 3 * UNIT,
    )


def expert_grads(rows, grads, da, db, inner):
    columns = pl.BlockSpec((SLOTS, D // 4), lambda i: (0, i))
    whole = pl.BlockSpec((SLOTS, FF), lambda i: (0, 0), pipeline_mode=pl.Buffered(1))
    return pl.pallas_call(
        expert_grad_kernel,
        name="expert_weight_gradients",
        out_shape=[jax.ShapeDtypeStruct((D, FF), BF)] * 3,
        grid=(4,),
        in_specs=[columns, columns] + [whole] * 3,
        out_specs=[pl.BlockSpec((D // 4, FF), lambda i: (i, 0))] * 3,
        compiler_params=pltpu.CompilerParams(vmem_limit_bytes=VMEM),
        cost_estimate=pl.CostEstimate(
            flops=3 * UNIT, bytes_accessed=18000000, transcendentals=0
        ),
    )(rows, grads, da, db, inner)


def exchange(rows):
    width = rows.shape[1]
    rows = rows.reshape(E, C, width)
    rows = lax.all_to_all(rows, GROUP, split_axis=0, concat_axis=0, tiled=True)
    return rows.reshape(SLOTS, width)


def outputs_kernel(core, mine, theirs, *outs):
    for level in range(LAYERS):
        level_outputs(level, core[0] == 0, mine, theirs, *outs)


def level_outputs(level, first, mine, theirs, q_out, k_out, v_out, o_out, routing_out):

    def rows(ref, group):
        group = level * 3 + group
        return jnp.where(first, ref[group, :12], ref[group, 12:])

    halves = []
    for ref in (mine, theirs):
        a, b, c = (rows(ref, group) for group in range(3))
        halves.append(
            (
                jnp.concatenate([a, c[:, :HD]], axis=1),
                c[:, HD : 2 * HD],
                c[:, 2 * HD : 3 * HD],
                jnp.concatenate([b, c[:, 3 * HD : 4 * HD]], axis=1),
                c[:, 4 * HD :],
            )
        )
    for out, own, other in zip((q_out, k_out, v_out, o_out), *halves):
        width = own.shape[1]
        out[:, level, :width] = jnp.where(first, own, other)
        out[:, level, width:] = jnp.where(first, other, own)
    routing_out[:, level, :] = halves[0][4] + halves[1][4]


def mixer_outputs(sums, core):
    widths = (D, 2 * HD, 2 * HD, D, HD)
    *outs, routing = pl.pallas_call(
        outputs_kernel,
        name="mixer_outputs",
        out_shape=[jax.ShapeDtypeStruct((12, LAYERS, width), F32) for width in widths],
        grid=(1,),
        in_specs=[pl.BlockSpec(memory_space=pltpu.SMEM)]
        + [pl.BlockSpec((6, 24, PART), lambda i: (0, 0, 0))] * 2,
        out_specs=[pl.BlockSpec((12, LAYERS, width), lambda i: (0, 0, 0)) for width in widths],
    )(core.reshape(1), sums, swap(sums))
    *outs, routing = [v.transpose(1, 0, 2) for v in (*outs, routing)]
    return (*outs, routing[:, :, :E], routing[:, :, E], routing[:, :, E + 1])


def expert_outputs_kernel(*refs):
    for matrix in range(3):
        for level in range(LAYERS):
            refs[6 + matrix][level, 0] = refs[level * 3 + matrix][...].astype(F32)


def expert_outputs(sums):
    rows = 96
    return pl.pallas_call(
        expert_outputs_kernel,
        name="expert_outputs",
        grid=(D // 4 // rows,),
        out_shape=[jax.ShapeDtypeStruct((LAYERS, 1, D // 4, FF), F32)] * 3,
        in_specs=[pl.BlockSpec((rows, FF), lambda i: (i, 0))] * 6,
        out_specs=[pl.BlockSpec((LAYERS, 1, rows, FF), lambda i: (0, 0, i, 0))] * 3,
        compiler_params=pltpu.CompilerParams(vmem_limit_bytes=VMEM),
        cost_estimate=pl.CostEstimate(flops=0, bytes_accessed=11000000, transcendentals=0),
    )(*sums)


def reduce_expert(grads):
    return [
        lax.psum_scatter(g, "dp", scatter_dimension=0, tiled=True) for g in grads
    ]


def per_device(
    tokens, segments, route_ids, w_query, key_projection, value_projection, w_out, w_router,
    gain_attn, gain_moe, w_gate, w_up, w_down, cotangent,
):
    core = lax.axis_index("core")
    cosine, sine = rope_tables()
    position = jnp.arange(T)

    shared = jnp.concatenate(
        [
            w_router, gain_attn[:, :, None], gain_moe[:, :, None],
            jnp.zeros((LAYERS, 12, COLS - WR - E - 2), BF),
        ],
        axis=2,
    )

    def half(number):
        def cut(v):
            width = v.shape[2] // 2
            return v[:, :, number * width : (number + 1) * width]

        return jnp.concatenate(
            [cut(v) for v in (w_query, key_projection, value_projection, w_out)] + [shared], axis=2
        )

    halves = (half(0), half(1))
    mine = jnp.where(core == 0, halves[0], halves[1])
    theirs = swap(jnp.where(core == 0, halves[1], halves[0]))
    blocks = jnp.where(
        core == 0,
        jnp.concatenate([mine, theirs], axis=1),
        jnp.concatenate([theirs, mine], axis=1),
    )
    segment = segments.astype(F32)
    segment = jnp.concatenate([segment, swap(segment)])
    mask = (position[:, None] >= position[None, :])[None] & (
        segment[:, :, None] == segment[:, None, :]
    )
    mask = mask.astype(F32)

    *named, spread0, spread1 = route_tables(route_ids)
    spread = (spread0, spread1)
    target = dot(spread[1], cotangent).astype(BF)
    tokens_other = swap(tokens)
    first_mixer, first_experts = gather(blocks, w_gate, w_up)
    second = jnp.concatenate([w_gate[1, 0], w_up[1, 0]])
    second = lax.optimization_barrier((blocks[1], second, first_experts))
    second_mixer = lax.all_gather(second[0], AXES[:3], axis=0).reshape(D, COLS)
    second_experts = lax.all_gather(second[1], "dp", axis=0).reshape(4, 2, 384, FF)

    normed0, heads0, att0, own, other, routing, gains0 = attend(
        True, tokens, tokens_other, first_mixer, cosine, sine, mask
    )
    middle0, send, gates0, slot0 = post(
        D, tokens, own, swap(other), gains0, routing, named[0], spread[0]
    )
    rows0, last_expert = dispatch(send, w_down, 0)
    experts0 = (first_experts, last_expert)
    produced, a0, b0 = expert_forward(rows0, experts0)
    routed0, last_expert = dispatch(produced, w_down, 1)
    experts1 = (second_experts, last_expert)
    routed0, target = lax.optimization_barrier((routed0, target))
    target = exchange(target)
    hidden, normed, gains1 = combine_next(middle0, routed0, spread[0], slot0, second_mixer)

    normed1, heads1, att1, own, other, routing = attend(
        False, normed, swap(normed), second_mixer, cosine, sine, mask
    )
    middle1, send, gates1, slot1 = post(
        WIDE, hidden, own, swap(other), gains1, routing, named[1], spread[1]
    )
    rows1 = exchange(send)
    dx, da, db, inner, produced, dy = expert_both(rows1, target, experts1)
    dx = exchange(dx)
    parts1 = expert_grads(rows1, dy, da, db, inner)
    dx, parts1 = lax.optimization_barrier((dx, parts1))
    sums1 = reduce_expert(parts1)
    routed1 = exchange(produced)

    grad_middle, grad_out, grad_routing, gain_two = pre_back(
        dx, None, middle1, gains1, cotangent, spread[1], gates1
    )
    grad_out_other = swap(grad_out)
    grad_heads, own, other = attend_back(
        grad_out, grad_out_other, grad_routing, second_mixer, heads1, cosine, sine, mask
    )
    grad, gain_parts, dy, shares = post_back(
        own, swap(other), hidden, gains1, grad_middle, gain_two, spread[0], slot0, routed0
    )
    products1 = mixer_products(
        normed1, grad_out, grad_out_other, grad_heads, att1, grad_routing, gain_parts
    )
    dy = exchange(dy)
    dy, products1 = lax.optimization_barrier((dy, products1))
    dx, da, db, inner = expert_back(a0, b0, dy, experts0)
    dx = exchange(dx)
    parts0 = expert_grads(rows0, dy, da, db, inner)
    sums0 = reduce_expert(parts0)
    dx, sums1, parts0 = lax.optimization_barrier((dx, sums1, parts0))

    grad_middle, grad_out, grad_routing, gain_two = pre_back(
        dx, shares, middle0, gains0, grad, spread[0], gates0
    )
    grad_out_other = swap(grad_out)
    grad_heads, own, other = attend_back(
        grad_out, grad_out_other, grad_routing, first_mixer, heads0, cosine, sine, mask
    )
    routed1, grad_heads = lax.optimization_barrier((routed1, grad_heads))
    output = combine(middle1, routed1, spread[1], slot1)
    grad_tokens, gain_parts = post_back(
        own, swap(other), tokens, gains0, grad_middle, gain_two
    )
    products0 = mixer_products(
        normed0, grad_out, grad_out_other, grad_heads, att0, grad_routing, gain_parts
    )
    mixer_out = mixer_outputs(reduce_mixer(products0 + products1), core)
    expert_out = expert_outputs([*sums0, *sums1])
    return (output, grad_tokens, *mixer_out, *expert_out)


def solution(mesh):
    mesh = Mesh(mesh.devices.reshape(4, 4, 4, 2), AXES)
    rows = P(AXES, None)
    mixer = P(None, AXES, None)
    gain = P(None, AXES)
    expert = P(None, GROUP, "dp", None)
    return jax.shard_map(
        per_device,
        mesh=mesh,
        in_specs=(
            rows, rows, mixer, mixer, mixer, mixer, mixer, mixer, gain, gain, expert, expert,
            expert, rows,
        ),
        out_specs=(
            rows, rows, mixer, mixer, mixer, mixer, mixer, gain, gain, expert, expert, expert,
        ),
        check_vma=False,
    )
```

```python
import math

import jax
import jax.numpy as jnp
import numpy as np
from jax import lax
from jax.experimental import pallas as pl
from jax.experimental.pallas import tpu as pltpu
from jax.sharding import Mesh, PartitionSpec as P

MESH = pl.DeviceIdType.MESH
BF = jnp.bfloat16
F32 = jnp.float32
HEADS, KV, HD, TOP, LAYERS = 12, 2, 128, 4, 2
T, D, FF, E, C = 128, 1536, 768, 32, 24
SLOTS = E * C
THETA, EPS = 1000000.0, 1e-06
SCALE = 1.0 / math.sqrt(HD)
ANY = pl.BlockSpec(memory_space=pl.ANY)
VM = pl.BlockSpec(memory_space=pltpu.VMEM)
WO, WR, COLS = 1024, 1792, 1920
CUTS = (pl.ds(0, 1024), pl.ds(1024, COLS - 1024))
PART = 640
VMEM = 32 << 20
WIDE = D + 128
AXES = ("dp", "z", "y", "core")
GROUP = AXES[1:]


def dot(a, b, dims=((1,), (0,))):
    return lax.dot_general(a, b, (dims, ((), ())), preferred_element_type=F32)


def split_two(v):
    high = v.astype(BF)
    return high, (v - high.astype(F32)).astype(BF)


def rope_tables():
    frequency = np.exp(-(2.0 * np.arange(HD // 2) / HD) * math.log(THETA)).astype(np.float32)
    angles = np.arange(T, dtype=np.float32)[:, None] * frequency[None, :]
    cosine, sine = np.cos(angles), np.sin(angles)
    return (
        jnp.asarray(np.concatenate([cosine, cosine], 1), F32),
        jnp.asarray(np.concatenate([-sine, sine], 1), F32),
    )


def swap(v):
    return lax.ppermute(v, "core", [(0, 1), (1, 0)])


def neighbours():
    here = [lax.axis_index(axis) for axis in AXES]

    def along(axis, places):
        peer = list(here)
        peer[axis] = lax.rem(here[axis] + places, 4)
        return tuple(peer)

    return here, along


def greet(peers):
    barrier = pltpu.get_barrier_semaphore()
    for peer in peers:
        pl.semaphore_signal(barrier, inc=1, device_id=peer, device_id_type=MESH)
    pl.semaphore_wait(barrier, len(peers))


def sender(send_sem, recv_sem):
    def send(src, dst, number, peer):
        copy = pltpu.make_async_remote_copy(
            src, dst, send_sem.at[number], recv_sem.at[number], device_id=peer, device_id_type=MESH
        )
        copy.start()
        return copy

    return send


def ring_steps(own, view, me, right, left, send, number):
    first = [
        send(own(0), view(me, 0), number, right), send(own(1), view(me, 1), number + 1, left)
    ]
    second = [
        send(own(1), view(me, 1), number + 2, right), send(own(0), view(me, 0), number + 3, left)
    ]

    relays = []

    def relay():
        before, after = lax.rem(me + 3, 4), lax.rem(me + 1, 4)
        first[0].wait_recv()
        relays.append(send(view(before, 0), view(before, 0), number + 4, right))
        first[1].wait_recv()
        relays.append(send(view(after, 1), view(after, 1), number + 5, left))

    def finish():
        for copy in second:
            copy.wait_recv()
        for copy in first + second:
            copy.wait_send()
        for copy in relays:
            copy.wait()

    return relay, finish


def ring_of(shard, out, x, along, send, number):
    return ring_steps(
        lambda half: shard.at[pl.ds(half * 192, 192)],
        lambda place, half: out.at[place, pl.ds(half * 192, 192)],
        x, along(0, 1), along(0, 3), send, number,
    )


def gather_kernel(blocks, gate, up, out, experts, local_sem, send_sem, recv_sem):
    (x, z, y, _), along = neighbours()
    greet([along(axis, o) for o in (1, 2, 3) for axis in range(3)])
    send = sender(send_sem, recv_sem)
    block = blocks.at[0]
    copies = [send(block, out.at[x, z, y], o - 1, along(0, o)) for o in (1, 3, 2)]
    shards = [gate.at[0, 0], up.at[0, 0]]
    rings = [
        ring_of(shard, experts.at[n], x, along, send, 27 + 6 * n) for n, shard in enumerate(shards)
    ]
    own = pltpu.make_async_copy(block, out.at[x, z, y], local_sem.at[0])
    own.start()
    own_experts = [
        pltpu.make_async_copy(shard, experts.at[n, x], local_sem.at[1 + n])
        for n, shard in enumerate(shards)
    ]
    for copy in own_experts:
        copy.start()
    own.wait()
    for copy in copies:
        copy.wait()

    def ring(view, axis, me, number):
        return ring_steps(
            lambda half: view(me, half), view, me, along(axis, 1), along(axis, 3), send, number
        )

    def pair(half):
        return pl.ds(half * 2, 2)

    first = ring(lambda n, half: out.at[pair(half), n, y, :, CUTS[0]], 1, z, 3)
    second = ring(lambda n, half: out.at[pair(half), z, n, :, CUTS[1]], 2, y, 9)
    first[0]()
    second[0]()
    first[1]()
    first = ring(lambda n, half: out.at[pair(half), :, n, :, CUTS[0]], 2, y, 15)
    second[1]()
    second = ring(lambda n, half: out.at[pair(half), n, :, :, CUTS[1]], 1, z, 21)
    rings[0][0]()
    first[0]()
    second[0]()
    rings[1][0]()
    first[1]()
    second[1]()
    for ring in rings:
        ring[1]()
    for copy in own_experts:
        copy.wait()


def gather(blocks, gate, up):
    mixer, experts = pl.pallas_call(
        gather_kernel,
        name="gather_weights",
        out_shape=(
            jax.ShapeDtypeStruct((4, 4, 4, 24, COLS), BF),
            jax.ShapeDtypeStruct((2, 4, D // 4, FF), BF),
        ),
        in_specs=[ANY] * 3,
        out_specs=(ANY, ANY),
        scratch_shapes=[
            pltpu.SemaphoreType.DMA((3,)),
            pltpu.SemaphoreType.DMA((39,)),
            pltpu.SemaphoreType.DMA((39,)),
        ],
        compiler_params=pltpu.CompilerParams(
            collective_id=1, has_side_effects=True, vmem_limit_bytes=VMEM
        ),
    )(blocks, gate, up)
    return mixer.reshape(D, COLS), experts.reshape(1, 2, D, FF)


OFFSETS = sorted(
    ((a, b, c) for a in range(4) for b in range(4) for c in range(2) if a or b or c),
    key=lambda o: -min(o[0], 4 - o[0]) - min(o[1], 4 - o[1]),
)


def dispatch_kernel(level, rows, shards, out, experts, local_sem, send_sem, recv_sem):
    (x, z, y, core), along = neighbours()
    peers = [
        (x, lax.rem(z + a, 4), lax.rem(y + b, 4), lax.rem(core + c, 2)) for a, b, c in OFFSETS
    ]
    greet(peers + [along(0, 1), along(0, 3)])
    send = sender(send_sem, recv_sem)
    me = (z * 4 + y) * 2 + core
    shard = shards.at[level, 0]
    ring = ring_of(shard, experts.at[0], x, along, send, len(peers))
    copies = []
    for n, peer in enumerate(peers):
        index = (peer[1] * 4 + peer[2]) * 2 + peer[3]
        copies.append(send(rows.at[index], out.at[me], n, peer))
    local = [
        pltpu.make_async_copy(rows.at[me], out.at[me], local_sem.at[0]),
        pltpu.make_async_copy(shard, experts.at[0, x], local_sem.at[1]),
    ]
    for copy in local:
        copy.start()
    ring[0]()
    for copy in copies + local:
        copy.wait()
    ring[1]()


def dispatch(rows, shards, level):
    rows, experts = pl.pallas_call(
        lambda *refs: dispatch_kernel(level, *refs),
        name="dispatch_rows",
        out_shape=(
            jax.ShapeDtypeStruct((E, C, D), BF),
            jax.ShapeDtypeStruct((1, 4, D // 4, FF), BF),
        ),
        in_specs=[ANY, ANY],
        out_specs=(ANY, ANY),
        scratch_shapes=[
            pltpu.SemaphoreType.DMA((2,)),
            pltpu.SemaphoreType.DMA((len(OFFSETS) + 6,)),
            pltpu.SemaphoreType.DMA((len(OFFSETS) + 6,)),
        ],
        compiler_params=pltpu.CompilerParams(
            collective_id=3 + level, has_side_effects=True, vmem_limit_bytes=VMEM
        ),
    )(rows.reshape(E, C, D), shards)
    return rows.reshape(SLOTS, D), experts.reshape(1, 1, D, FF)


def reduce_mixer_kernel(*refs):
    sources, out, scratch = refs[:6], refs[6], refs[7:]
    (x, z, y, _), along = neighbours()
    local_sem, send_sem, recv_sem = scratch[-3:]
    greet([along(axis, o) for o in (1, 2, 3) for axis in range(3)])
    send = sender(send_sem, recv_sem)
    here = (x, z, y)
    ways = ((1, 0, 2), (2, 1, 0), (0, 2, 1))
    jobs = []
    for level in reversed(range(LAYERS)):
        for group, way in enumerate(ways):
            number = level * 3 + group
            held = scratch[number * 10 : number * 10 + 10]
            jobs.append((number, sources[number], out.at[number], way, held))

    def pick(ref, dim, index, half=None):
        place = [slice(None)] * 3
        place[dim] = index
        if half is not None:
            place[1 if dim == 0 else 0] = half
        return ref.at[tuple(place)]

    def start_first(job):
        number, source, _, (axis, *_), (got, passed, relay, mine, own, *_) = job
        me = here[axis]
        right, left = along(axis, 1), along(axis, 3)
        after, far, before = (lax.rem(me + o, 4) for o in (1, 2, 3))
        low, high = pl.ds(0, 2), pl.ds(2, 2)
        base = number * 12
        copies = [
            send(pick(source, axis, far, low), passed.at[0], base, right),
            send(pick(source, axis, far, high), passed.at[1], base + 1, left),
            send(pick(source, axis, after, high), got.at[0, high], base + 2, right),
            send(pick(source, axis, before, low), got.at[1, low], base + 3, left),
        ]
        local = []
        for n, (src, dst) in enumerate(
            (
                (pick(source, axis, after, low), mine.at[0]),
                (pick(source, axis, before, high), mine.at[1]),
                (pick(source, axis, me), own),
            )
        ):
            local.append(pltpu.make_async_copy(src, dst, local_sem.at[number * 3 + n]))
            local[n].start()

        def pass_on():
            for n, (part, peer) in enumerate(((low, right), (high, left))):
                copies[n].wait()
                local[n].wait()
                total = mine[n].astype(F32) + passed[n].astype(F32)
                relay[n] = total.astype(BF)
                copies.append(send(relay.at[n], got.at[n, part], base + 4 + n, peer))

        def finish():
            for copy in copies[2:]:
                copy.wait()
            local[2].wait()

        return pass_on, finish

    def start_second(job):
        number, _, _, (gone, axis, _), (got, _, _, _, own, total, ready, after, *_) = job
        total[...] = own[...].astype(F32) + got[0].astype(F32) + got[1].astype(F32)
        started = []
        for o in (2, 1, 3):
            ready[o - 1] = sub(total, gone, axis, lax.rem(here[axis] + o, 4)).astype(BF)
            started.append(
                send(ready.at[o - 1], after.at[o - 1], number * 12 + 5 + o, along(axis, o))
            )
        return started

    def sub(total, gone, axis, index):
        first = axis == min(a for a in range(3) if a != gone)
        return total[index] if first else total[:, index]

    def start_third(job, copies):
        number, _, _, (gone, middle, axis), (*_, total, _, after, small, last) = job
        for copy in copies:
            copy.wait()
        rows = sub(total, gone, middle, here[middle])
        for o in range(3):
            rows = rows + after[o].astype(F32)
        small[...] = rows.astype(BF)
        started = [
            send(
                small.at[lax.rem(here[axis] + o, 4)], last.at[o - 1], number * 12 + 8 + o,
                along(axis, o),
            )
            for o in (2, 1, 3)
        ]
        return started

    def end(job, copies):
        _, _, out, (_, _, axis), (*_, small, last) = job
        for copy in copies:
            copy.wait()
        rows = small[here[axis]].astype(F32)
        for o in range(3):
            rows = rows + last[o].astype(F32)
        out[...] = rows

    running = [start_first(job) for job in jobs]
    for pass_on, _ in running:
        pass_on()
    seconds = []
    for job, (_, finish) in zip(jobs, running):
        finish()
        seconds.append(start_second(job))
    running = seconds
    running = [start_third(job, copies) for job, copies in zip(jobs, running)]
    for job, copies in zip(jobs, running):
        end(job, copies)


def reduce_mixer(products):
    scratch = []
    for _ in products:
        scratch += [
            pltpu.VMEM((2, 4, 4, 24, PART), BF),
            pltpu.VMEM((2, 2, 4, 24, PART), BF),
            pltpu.VMEM((2, 2, 4, 24, PART), BF),
            pltpu.VMEM((2, 2, 4, 24, PART), BF),
            pltpu.VMEM((4, 4, 24, PART), BF),
            pltpu.VMEM((4, 4, 24, PART), F32),
            pltpu.VMEM((3, 4, 24, PART), BF),
            pltpu.VMEM((3, 4, 24, PART), BF),
            pltpu.VMEM((4, 24, PART), BF),
            pltpu.VMEM((3, 24, PART), BF),
        ]
    return pl.pallas_call(
        reduce_mixer_kernel,
        name="reduce_mixer_gradients",
        out_shape=jax.ShapeDtypeStruct((6, 24, PART), F32),
        in_specs=[ANY] * 6,
        out_specs=VM,
        scratch_shapes=scratch
        + [
            pltpu.SemaphoreType.DMA((18,)),
            pltpu.SemaphoreType.DMA((72,)),
            pltpu.SemaphoreType.DMA((72,)),
        ],
        compiler_params=pltpu.CompilerParams(
            collective_id=2, has_side_effects=True, vmem_limit_bytes=48 << 20
        ),
    )(*products)


def columns(shape):
    return lax.broadcasted_iota(jnp.int32, shape, 1)


def rows_of(shape):
    return lax.broadcasted_iota(jnp.int32, shape, 0)


def plain(kernel, name, outs, flops=0, bytes_accessed=4000000, ins=None, scratch=()):
    def call(*args):
        return pl.pallas_call(
            kernel,
            name=name,
            out_shape=[jax.ShapeDtypeStruct(shape, kind) for shape, kind in outs],
            in_specs=ins or [VM] * len(args),
            out_specs=[VM] * len(outs),
            scratch_shapes=list(scratch),
            compiler_params=pltpu.CompilerParams(vmem_limit_bytes=VMEM),
            cost_estimate=pl.CostEstimate(
                flops=flops, bytes_accessed=bytes_accessed, transcendentals=0
            ),
        )(*args)

    return call


def tables_kernel(routes, *outs):
    wide = (T, 128)
    earlier = (rows_of(wide) < columns(wide)).astype(BF)
    same = (rows_of(wide) == columns(wide)).astype(BF)
    for level in range(LAYERS):
        named = jnp.zeros(wide, F32)
        for k in range(TOP):
            named = named + (routes[level, :, k : k + 1] == columns(wide)).astype(F32)
        outs[level][...] = named
        turned = dot(named.astype(BF), same, ((0,), (0,)))[:E]
        rank = dot(named.astype(BF), earlier, ((0,), (0,)))[:E]
        place = lax.broadcasted_iota(jnp.int32, (E, C, T), 1).astype(F32)
        hit = jnp.where(rank[:, None, :] == place, turned[:, None, :], 0.0)
        outs[LAYERS + level][...] = hit.reshape(SLOTS, T).astype(BF)


def route_tables(routes):
    return plain(
        tables_kernel, "route_tables",
        [((T, 128), F32)] * LAYERS + [((SLOTS, T), BF)] * LAYERS,
    )(routes)


def unit_rows(rows):
    scale = lax.rsqrt(jnp.mean(rows * rows, axis=-1, keepdims=True) + EPS)
    return rows * scale, scale


def gain_rows(router):
    pick = (columns((8, 128)) == E + rows_of((8, 128))) & (rows_of((8, 128)) < 2)
    return dot(pick.astype(BF), router, ((1,), (1,)))


def slot_columns():
    shape = (SLOTS, 128)
    start = columns(shape) * C
    return (rows_of(shape) >= start) & (rows_of(shape) < start + C)


def post_kernel(
    hidden, own, other, gains, routing, named, spread, middle_out, send_out, gates_out, slot_out
):
    middle = hidden[...].astype(F32) + own[...] + other[...].astype(F32)
    middle_out[...] = middle
    normed = (unit_rows(middle)[0] * gains[1:2]).astype(BF)
    send_out[:, :D] = dot(spread[...], normed).astype(BF)
    masked = jnp.where(named[...] > 0, routing[...], -1e30)
    terms = jnp.exp(masked - jnp.max(masked, axis=-1, keepdims=True))
    terms = jnp.where(named[...] > 0, terms, 0.0)
    gates = terms / jnp.sum(terms, axis=-1, keepdims=True)
    gates_out[...] = gates
    high, low = split_two(gates)
    all_gates = dot(spread[...], high) + dot(spread[...], low)
    slot = jnp.sum(jnp.where(slot_columns(), all_gates, 0.0), axis=-1, keepdims=True)
    slot_out[...] = slot
    if send_out.shape[1] > D:
        send_out[:, D:] = two_columns(slot)


def two_columns(value):
    high = value.astype(BF).astype(F32)
    column = columns((value.shape[0], WIDE - D))
    return jnp.where(column == 0, high, jnp.where(column == 1, value - high, 0.0)).astype(BF)


def post(width, *args):
    return plain(
        post_kernel, "dispatch_rows_of_tokens",
        [((T, D), F32), ((SLOTS, width), BF), ((T, 128), F32), ((SLOTS, 1), F32)], 2 * SLOTS * T * D,
    )(*args)


def combine_kernel(middle, routed, spread, slot, *refs):
    mix = spread[...].astype(F32) * slot[...]
    high, low = split_two(mix)
    rows = routed[...]
    hidden = middle[...] + dot(high, rows, ((0,), (0,))) + dot(low, rows, ((0,), (0,)))
    if len(refs) == 1:
        refs[0][...] = hidden
        return
    mixers, hidden_out, normed_out, gains_out, router, sem = refs
    copy = pltpu.make_async_copy(mixers.at[:, pl.ds(WR, COLS - WR)], router, sem)
    copy.start()
    hidden_out[...] = hidden
    copy.wait()
    gains = gain_rows(router[...])
    gains_out[...] = gains
    normed_out[...] = (unit_rows(hidden)[0] * gains[0:1]).astype(BF)


def combine(middle, routed, spread, slot):
    return plain(combine_kernel, "add_expert_outputs", [((T, D), F32)], 4 * SLOTS * T * D)(
        middle, routed, spread, slot
    )[0]


def combine_next(middle, routed, spread, slot, mixers):
    return plain(
        combine_kernel, "add_expert_outputs_and_norm",
        [((T, D), F32), ((T, D), BF), ((8, D), F32)], 4 * SLOTS * T * D,
        ins=[VM] * 4 + [ANY],
        scratch=[pltpu.VMEM((D, COLS - WR), BF), pltpu.SemaphoreType.DMA],
    )(middle, routed, spread, slot, mixers)


def back_through_norm(inputs, gain, grad_normed, grad_residual):
    unit, scale = unit_rows(inputs)
    grad_gain = jnp.sum(grad_normed * unit, axis=0, keepdims=True)
    grad_unit = grad_normed * gain
    back = grad_unit - unit * jnp.mean(grad_unit * unit, axis=-1, keepdims=True)
    return grad_residual + scale * back, grad_gain


def pre_back_kernel(
    dx, shares, middle, gains, grad, spread, gates, middle_out, out_out, routing_out, gain_out
):
    table = spread[...]
    if shares is None:
        share = dx[:, D : D + 1].astype(F32) + dx[:, D + 1 : D + 2].astype(F32)
    else:
        share = shares[...]
    high, low = split_two(jnp.where(slot_columns(), share, 0.0))
    dense = dot(table, high, ((0,), (0,))) + dot(table, low, ((0,), (0,)))
    routing = dense - gates[...] * jnp.sum(dense, axis=-1, keepdims=True)
    routing_out[...] = routing.astype(BF)
    grad_normed = dot(table, dx[:, :D], ((0,), (0,)))
    grad_middle, grad_gain = back_through_norm(
        middle[...], gains[1:2], grad_normed, grad[...].astype(F32)
    )
    middle_out[...] = grad_middle
    out_out[...] = grad_middle.astype(BF)
    gain_out[...] = grad_gain


def pre_back(dx, shares, *args):
    outs = [((T, D), F32), ((T, D), BF), ((T, 128), BF), ((1, D), F32)]
    if shares is None:
        return plain(
            lambda dx, *refs: pre_back_kernel(dx, None, *refs), "back_to_middle", outs,
            2 * SLOTS * T * D,
        )(dx, *args)
    return plain(pre_back_kernel, "back_to_middle", outs, 2 * SLOTS * T * D)(dx, shares, *args)


def post_back_kernel(own, other, hidden, gains, grad_middle, gain_two, *refs):
    grad_normed = own[...] + other[...].astype(F32)
    grad, gain_one = back_through_norm(
        hidden[...].astype(F32), gains[0:1], grad_normed, grad_middle[...]
    )
    if len(refs) == 2:
        grad_out, rows_out = refs
    else:
        spread, slot, routed, grad_out, rows_out, dy_out, share_out = refs
        high, low = split_two(grad)
        slots = dot(spread[...], high) + dot(spread[...], low)
        dy_out[...] = (slot[...] * slots).astype(BF)
        share = jnp.sum(routed[...].astype(F32) * slots, axis=-1, keepdims=True)
        share_out[...] = slot[...] * share
    grad_out[...] = grad
    rows_out[...] = jnp.zeros((16, D), BF)
    for n, gain in enumerate((gain_one, gain_two[...])):
        high, low = split_two(gain)
        rows_out[2 * n : 2 * n + 1] = high
        rows_out[2 * n + 1 : 2 * n + 2] = low


def post_back(*args):
    outs = [((T, D), F32), ((16, D), BF)]
    if len(args) > 6:
        outs += [((SLOTS, D), BF), ((SLOTS, 1), F32)]
    return plain(post_back_kernel, "back_to_hidden", outs, 4 * SLOTS * T * D)(*args)


def products_kernel(
    normed, grads_own, grads_other, heads, att, routing, gains,
    first_out, second_out, third_out, grads,
):
    step = pl.program_id(0)

    @pl.when(step == 0)
    def _():
        grads[:T] = grads_own[...]
        grads[T:] = grads_other[...]

    def product(left, right):
        return dot(left, right, ((0,), (0,)))

    def pair(ref, start, stop):
        return jnp.concatenate([ref[0, :, start:stop], ref[1, :, start:stop]], axis=0)

    block = pl.ds(pl.multiple_of(step * (D // 4), 128), D // 4)
    def store(out, value):
        out[0] = value.reshape(4, 4, 24, PART).astype(BF)

    left, turned = normed[:, block], grads[:, block]
    number, column = rows_of((16, 128)), columns((16, 128))
    gain_place = ((number < 2) & (column == E)) | (
        (number >= 2) & (number < 4) & (column == E + 1)
    )
    store(first_out, product(left, pair(heads, 0, PART)))
    store(second_out, product(turned, pair(att, 0, PART)))
    third = [
        product(left, pair(heads, PART, WO)),
        product(turned, pair(att, PART, WR - WO)),
        product(left[:T], routing[...]) + product(gains[:, block], gain_place.astype(BF)),
    ]
    store(third_out, jnp.concatenate(third, axis=1))


def mixer_products(normed, grads_own, grads_other, heads, att, routing, gains):
    def whole(v):
        zeros = (0,) * len(v.shape)
        return pl.BlockSpec(v.shape, lambda i: zeros, pipeline_mode=pl.Buffered(1))

    args = [normed, grads_own, grads_other, heads, att, routing, gains]
    return pl.pallas_call(
        products_kernel,
        name="mixer_products",
        grid=(4,),
        out_shape=[jax.ShapeDtypeStruct((4, 4, 4, 24, PART), BF)] * 3,
        in_specs=[whole(v) for v in args],
        out_specs=[pl.BlockSpec((1, 4, 4, 24, PART), lambda i: (i, 0, 0, 0, 0))] * 3,
        scratch_shapes=[pltpu.VMEM((2 * T, D), BF)],
        compiler_params=pltpu.CompilerParams(vmem_limit_bytes=VMEM),
        cost_estimate=pl.CostEstimate(
            flops=2 * 2 * T * D * COLS, bytes_accessed=11000000, transcendentals=0
        ),
    )(*args)


def turn(rows, cosine, sine):
    return rows * cosine + pltpu.roll(rows, HD // 2, 1) * sine


def head_rows(ref, sequence, heads):
    return jnp.concatenate([ref[sequence, :, h * HD : (h + 1) * HD] for h in heads], axis=0)


def weigh(queries, keys, mask):
    raw = dot(queries, keys, ((1,), (1,))).reshape(6, T, T)
    logits = jnp.where(mask[None] > 0, raw * SCALE, -1e30)
    terms = jnp.exp(logits - jnp.max(logits, axis=-1, keepdims=True))
    return (terms / jnp.sum(terms, axis=-1, keepdims=True)).reshape(6 * T, T)


PIECES = (pl.ds(WR, COLS - WR), pl.ds(0, WO), pl.ds(WO, WR - WO))


class Several:
    def __init__(self, copies):
        self.copies = copies
        for copy in copies:
            copy.start()

    def wait(self):
        for copy in self.copies:
            copy.wait()


def fetch_weights(mixers, weights, sem):
    groups = []
    for n, place in enumerate(PIECES):
        rows = [pl.ds(i * (D // 4), D // 4) for i in range(4)]
        groups.append(
            Several(
                [
                    pltpu.make_async_copy(
                        mixers.at[r, place], weights.at[r, place], sem.at[n * 4 + i]
                    )
                    for i, r in enumerate(rows)
                ]
            )
        )
    return groups


def attend_kernel(first, own, other, mixers, cosine, sine, mask, *refs):
    *refs, weights, sem = refs
    both, heads_out, att_out, own_out, other_out, routing_out = refs[:6]
    copies = fetch_weights(mixers, weights, sem)
    if first:
        units = [unit_rows(v[...].astype(F32))[0] for v in (own, other)]
        copies[0].wait()
        gains = gain_rows(weights[:, WR:])
        refs[6][...] = gains
        both[:T] = (units[0] * gains[0:1]).astype(BF)
        both[T:] = (units[1] * gains[0:1]).astype(BF)
    else:
        both[:T] = own[...]
        both[T:] = other[...]
        copies[0].wait()
    turns = [jnp.concatenate([t[...], t[...]], axis=0) for t in (cosine, sine)]
    copies[1].wait()
    for tile in range(4):
        wide = dot(both[...], weights[:, tile * 256 : (tile + 1) * 256])
        for part in range(2):
            head = tile * 2 + part
            rows = wide[:, part * HD : (part + 1) * HD]
            if head < 7:
                rows = turn(rows, *turns)
            rows = rows.astype(BF)
            for s in range(2):
                heads_out[s, :, head * HD : (head + 1) * HD] = rows[s * T : (s + 1) * T]
    for s in range(2):
        probs = weigh(head_rows(heads_out, s, range(6)), heads_out[s, :, 768:896], mask[s])
        mixed = dot(probs.astype(BF), heads_out[s, :, 896:]).astype(BF)
        for h in range(6):
            att_out[s, :, h * HD : (h + 1) * HD] = mixed[h * T : (h + 1) * T]
    copies[2].wait()
    att = att_out[...].reshape(2 * T, 768)
    for tile in range(6):
        place = slice(tile * 256, (tile + 1) * 256)
        rows = dot(att, weights[place, WO:WR], ((1,), (1,)))
        own_out[:, place] = rows[:T]
        other_out[:, place] = rows[T:].astype(BF)
    routing_out[...] = dot(both[:T], weights[:, WR:])


def attend(first, own, other, mixers, cosine, sine, mask):
    outs = [
        ((2 * T, D), BF), ((2, T, WO), BF), ((2, T, WR - WO), BF), ((T, D), F32), ((T, D), BF),
        ((T, 128), F32),
    ]
    return plain(
        lambda *refs: attend_kernel(first, *refs), "attention_forward",
        outs + [((8, D), F32)] * first, 1700000000, 9000000,
        ins=[VM, VM, ANY, VM, VM, VM],
        scratch=[pltpu.VMEM((D, COLS), BF), pltpu.SemaphoreType.DMA((12,))],
    )(own, other, mixers, cosine, sine, mask)


def attend_back_kernel(
    own, other, routing, mixers, heads, cosine, sine, mask,
    grad_heads, own_out, other_out, both, grad_att, weights, sem,
):
    copies = fetch_weights(mixers, weights, sem)
    both[:T] = own[...]
    both[T:] = other[...]
    copies[2].wait()
    for tile in range(3):
        place = slice(tile * 256, (tile + 1) * 256)
        wide = dot(both[...], weights[:, WO + tile * 256 : WO + (tile + 1) * 256]).astype(BF)
        for s in range(2):
            grad_att[s, :, place] = wide[s * T : (s + 1) * T]
    cos, sin = cosine[...], -sine[...]
    for s in range(2):
        queries, grads = head_rows(heads, s, range(6)), head_rows(grad_att, s, range(6))
        keys, values = heads[s, :, 768:896], heads[s, :, 896:]
        probs = weigh(queries, keys, mask[s])
        dp = dot(grads, values, ((1,), (1,)))
        draw = probs * (dp - jnp.sum(probs * dp, axis=-1, keepdims=True))
        draw = (draw * SCALE).astype(BF)
        dq = dot(draw, keys)
        for h in range(6):
            rows = turn(dq[h * T : (h + 1) * T], cos, sin)
            grad_heads[s, :, h * HD : (h + 1) * HD] = rows.astype(BF)
        dk = dot(draw, queries, ((0,), (0,)))
        grad_heads[s, :, 768:896] = turn(dk, cos, sin).astype(BF)
        grad_heads[s, :, 896:] = dot(probs.astype(BF), grads, ((0,), (0,))).astype(BF)
    copies[0].wait()
    copies[1].wait()
    wide = grad_heads[...].reshape(2 * T, 1024)
    for tile in range(6):
        place = slice(tile * 256, (tile + 1) * 256)
        rows = dot(wide, weights[place, :WO], ((1,), (1,)))
        own_out[:, place] = rows[:T] + dot(routing[...], weights[place, WR:], ((1,), (1,)))
        other_out[:, place] = rows[T:].astype(BF)


def attend_back(own, other, routing, mixers, heads, cosine, sine, mask):
    return pl.pallas_call(
        attend_back_kernel,
        name="attention_backward",
        out_shape=(
            jax.ShapeDtypeStruct((2, T, 1024), BF),
            jax.ShapeDtypeStruct((T, D), F32),
            jax.ShapeDtypeStruct((T, D), BF),
        ),
        in_specs=[VM, VM, VM, ANY, VM, VM, VM, VM],
        out_specs=[VM] * 3,
        scratch_shapes=[
            pltpu.VMEM((2 * T, D), BF),
            pltpu.VMEM((2, T, 768), BF),
            pltpu.VMEM((D, COLS), BF),
            pltpu.SemaphoreType.DMA((12,)),
        ],
        compiler_params=pltpu.CompilerParams(vmem_limit_bytes=VMEM),
        cost_estimate=pl.CostEstimate(flops=2200000000, bytes_accessed=9000000, transcendentals=200000),
    )(own, other, routing, mixers, heads, cosine, sine, mask)

ROWS = 256


def load_weights(pieces, weights, sem, order):
    step = pl.program_id(0)
    groups = {}
    matrix = 0
    for piece in pieces:
        count, several = piece.shape[:2]
        for m in range(several):
            rows = D // 4
            groups[matrix + m] = [
                pltpu.make_async_copy(
                    piece.at[0, m, pl.ds(n * rows, rows)] if count == 1 else piece.at[n, m],
                    weights.at[matrix + m, pl.ds(n * rows, rows)],
                    sem.at[(matrix + m) * 4 + n],
                )
                for n in range(4)
            ]
        matrix += several

    @pl.when(step == 0)
    def _():
        for m in order:
            for copy in groups[m]:
                copy.start()

    def ready(m):
        @pl.when(step == 0)
        def _():
            for copy in groups[m]:
                copy.wait()

    return ready


def expert_kernel(rows, *refs):
    *pieces, y_out, a_out, b_out, weights, sem = refs
    ready = load_weights(pieces, weights, sem, (0, 1, 2))
    ready(0)
    a = dot(rows[...], weights[0])
    ready(1)
    b = dot(rows[...], weights[1])
    a_out[...] = a
    b_out[...] = b
    inner = (a * jax.nn.sigmoid(a) * b).astype(BF)
    ready(2)
    y_out[...] = dot(inner, weights[2], ((1,), (1,))).astype(BF)


def expert_both_kernel(rows, target, target_rest, *refs):
    *pieces, dx_out, da_out, db_out, inner_out, y_out, dy_out, weights, sem = refs
    ready = load_weights(pieces, weights, sem, (0, 1, 2))
    normed = rows[:, :D]
    gate = rows[:, D : D + 1].astype(F32) + rows[:, D + 1 : D + 2].astype(F32)
    target = jnp.concatenate([target[...], target_rest[...]], axis=1)
    dy = (gate * target.astype(F32)).astype(BF)
    dy_out[...] = dy
    ready(0)
    a = dot(normed, weights[0])
    ready(1)
    b = dot(normed, weights[1])
    ready(2)
    inner = expert_inner_gradients(a, b, dy, weights, dx_out, da_out, db_out, inner_out)
    y = dot(inner, weights[2], ((1,), (1,))).astype(BF)
    y_out[...] = y
    share = jnp.sum(y.astype(F32) * dy.astype(F32), axis=-1, keepdims=True)
    high = share.astype(BF).astype(F32)
    column = lax.broadcasted_iota(jnp.int32, (ROWS, WIDE - D), 1)
    parts = jnp.where(column == 0, high, jnp.where(column == 1, share - high, 0.0))
    dx_out[:, D:] = parts.astype(BF)


def expert_back_kernel(a_in, b_in, grads, *refs):
    *pieces, dx_out, da_out, db_out, inner_out, weights, sem = refs
    ready = load_weights(pieces, weights, sem, (2, 0, 1))
    ready(2)
    expert_inner_gradients(
        a_in[...], b_in[...], grads[...], weights, dx_out, da_out, db_out, inner_out, ready
    )


def expert_inner_gradients(
    a, b, dy, weights, dx_out, da_out, db_out, inner_out, ready=None
):
    du = dot(dy, weights[2])
    sig = jax.nn.sigmoid(a)
    act = a * sig
    inner = (act * b).astype(BF)
    da = (du * b * sig * (1.0 + a * (1.0 - sig))).astype(BF)
    db = (du * act).astype(BF)
    da_out[...], db_out[...], inner_out[...] = da, db, inner
    if ready:
        ready(0)
        ready(1)
    dx = dot(da, weights[0], ((1,), (1,))) + dot(db, weights[1], ((1,), (1,)))
    dx_out[:, :D] = dx.astype(BF)
    return inner


def expert_grad_kernel(rows, grads, da, db, inner, gate_out, up_out, down_out):
    gate_out[...] = dot(rows[...], da[...], ((0,), (0,))).astype(BF)
    up_out[...] = dot(rows[...], db[...], ((0,), (0,))).astype(BF)
    down_out[...] = dot(grads[...], inner[...], ((0,), (0,))).astype(BF)


def tiled(width):
    return pl.BlockSpec((ROWS, width), lambda i: (i, 0))


def expert_call(kernel, name, ins, pieces, out_widths, flops):
    outs = [jax.ShapeDtypeStruct((SLOTS, w), t) for w, t in out_widths]
    return pl.pallas_call(
        kernel,
        name=name,
        out_shape=outs,
        grid=(SLOTS // ROWS,),
        in_specs=[tiled(v.shape[1]) for v in ins] + [ANY] * len(pieces),
        out_specs=[tiled(w) for w, _ in out_widths],
        scratch_shapes=[pltpu.VMEM((3, D, FF), BF), pltpu.SemaphoreType.DMA((12,))],
        compiler_params=pltpu.CompilerParams(vmem_limit_bytes=VMEM),
        cost_estimate=pl.CostEstimate(
            flops=flops, bytes_accessed=18000000, transcendentals=SLOTS * FF
        ),
    )(*ins, *pieces)


UNIT = 2 * SLOTS * D * FF


def expert_forward(rows, pieces):
    return expert_call(
        expert_kernel, "expert_forward", [rows], pieces, [(D, BF), (FF, F32), (FF, F32)], 3 * UNIT
    )


def expert_both(rows, targets, pieces):
    return expert_call(
        expert_both_kernel, "expert_forward_backward", [rows, *targets], pieces,
        [(WIDE, BF), (FF, BF), (FF, BF), (FF, BF), (D, BF), (D, BF)], 6 * UNIT,
    )


def expert_back(a, b, grads, pieces):
    return expert_call(
        expert_back_kernel, "expert_backward", [a, b, grads], pieces,
        [(D, BF), (FF, BF), (FF, BF), (FF, BF)], 3 * UNIT,
    )


def expert_grads(rows, grads, da, db, inner):
    columns = pl.BlockSpec((SLOTS, D // 4), lambda i: (0, i))
    whole = pl.BlockSpec((SLOTS, FF), lambda i: (0, 0), pipeline_mode=pl.Buffered(1))
    return pl.pallas_call(
        expert_grad_kernel,
        name="expert_weight_gradients",
        out_shape=[jax.ShapeDtypeStruct((D, FF), BF)] * 3,
        grid=(4,),
        in_specs=[columns, columns] + [whole] * 3,
        out_specs=[pl.BlockSpec((D // 4, FF), lambda i: (i, 0))] * 3,
        compiler_params=pltpu.CompilerParams(vmem_limit_bytes=VMEM),
        cost_estimate=pl.CostEstimate(
            flops=3 * UNIT, bytes_accessed=18000000, transcendentals=0
        ),
    )(rows, grads, da, db, inner)


def exchange(rows):
    width = rows.shape[1]
    rows = rows.reshape(E, C, width)
    rows = lax.all_to_all(rows, GROUP, split_axis=0, concat_axis=0, tiled=True)
    return rows.reshape(SLOTS, width)


def outputs_kernel(core, mine, theirs, *outs):
    for level in range(LAYERS):
        level_outputs(level, core[0] == 0, mine, theirs, *outs)


def level_outputs(level, first, mine, theirs, q_out, k_out, v_out, o_out, routing_out):

    def rows(ref, group):
        group = level * 3 + group
        return jnp.where(first, ref[group, :12], ref[group, 12:])

    halves = []
    for ref in (mine, theirs):
        a, b, c = (rows(ref, group) for group in range(3))
        halves.append(
            (
                jnp.concatenate([a, c[:, :HD]], axis=1),
                c[:, HD : 2 * HD],
                c[:, 2 * HD : 3 * HD],
                jnp.concatenate([b, c[:, 3 * HD : 4 * HD]], axis=1),
                c[:, 4 * HD :],
            )
        )
    for out, own, other in zip((q_out, k_out, v_out, o_out), *halves):
        width = own.shape[1]
        out[:, level, :width] = jnp.where(first, own, other)
        out[:, level, width:] = jnp.where(first, other, own)
    routing_out[:, level, :] = halves[0][4] + halves[1][4]


def mixer_outputs(sums, core):
    widths = (D, 2 * HD, 2 * HD, D, HD)
    *outs, routing = pl.pallas_call(
        outputs_kernel,
        name="mixer_outputs",
        out_shape=[jax.ShapeDtypeStruct((12, LAYERS, width), F32) for width in widths],
        grid=(1,),
        in_specs=[pl.BlockSpec(memory_space=pltpu.SMEM)]
        + [pl.BlockSpec((6, 24, PART), lambda i: (0, 0, 0))] * 2,
        out_specs=[pl.BlockSpec((12, LAYERS, width), lambda i: (0, 0, 0)) for width in widths],
    )(core.reshape(1), sums, swap(sums))
    *outs, routing = [v.transpose(1, 0, 2) for v in (*outs, routing)]
    return (*outs, routing[:, :, :E], routing[:, :, E], routing[:, :, E + 1])


def expert_outputs_kernel(*refs):
    for matrix in range(3):
        for level in range(LAYERS):
            refs[6 + matrix][level, 0] = refs[level * 3 + matrix][...].astype(F32)


def expert_outputs(sums):
    rows = 96
    return pl.pallas_call(
        expert_outputs_kernel,
        name="expert_outputs",
        grid=(D // 4 // rows,),
        out_shape=[jax.ShapeDtypeStruct((LAYERS, 1, D // 4, FF), F32)] * 3,
        in_specs=[pl.BlockSpec((rows, FF), lambda i: (i, 0))] * 6,
        out_specs=[pl.BlockSpec((LAYERS, 1, rows, FF), lambda i: (0, 0, i, 0))] * 3,
        compiler_params=pltpu.CompilerParams(vmem_limit_bytes=VMEM),
        cost_estimate=pl.CostEstimate(flops=0, bytes_accessed=11000000, transcendentals=0),
    )(*sums)


def reduce_expert(grads):
    return [
        lax.psum_scatter(g, "dp", scatter_dimension=0, tiled=True) for g in grads
    ]


def per_device(
    tokens, segments, route_ids, w_query, key_projection, value_projection, w_out, w_router,
    gain_attn, gain_moe, w_gate, w_up, w_down, cotangent,
):
    core = lax.axis_index("core")
    cosine, sine = rope_tables()
    position = jnp.arange(T)

    shared = jnp.concatenate(
        [
            w_router, gain_attn[:, :, None], gain_moe[:, :, None],
            jnp.zeros((LAYERS, 12, COLS - WR - E - 2), BF),
        ],
        axis=2,
    )

    def half(number):
        def cut(v):
            width = v.shape[2] // 2
            return v[:, :, number * width : (number + 1) * width]

        return jnp.concatenate(
            [cut(v) for v in (w_query, key_projection, value_projection, w_out)] + [shared], axis=2
        )

    halves = (half(0), half(1))
    mine = jnp.where(core == 0, halves[0], halves[1])
    theirs = swap(jnp.where(core == 0, halves[1], halves[0]))
    blocks = jnp.where(
        core == 0,
        jnp.concatenate([mine, theirs], axis=1),
        jnp.concatenate([theirs, mine], axis=1),
    )
    segment = segments.astype(F32)
    segment = jnp.concatenate([segment, swap(segment)])
    mask = (position[:, None] >= position[None, :])[None] & (
        segment[:, :, None] == segment[:, None, :]
    )
    mask = mask.astype(F32)

    *named, spread0, spread1 = route_tables(route_ids)
    spread = (spread0, spread1)
    targets = [
        dot(spread[1], cotangent[:, half * 768 : (half + 1) * 768]).astype(BF) for half in range(2)
    ]
    tokens_other = swap(tokens)
    first_mixer, first_experts = gather(blocks, w_gate, w_up)
    second = jnp.concatenate([w_gate[1, 0], w_up[1, 0]])
    second = lax.optimization_barrier((blocks[1], second, first_experts))
    second_mixer = lax.all_gather(second[0], AXES[:3], axis=0).reshape(D, COLS)
    second_experts = lax.all_gather(second[1], "dp", axis=0).reshape(4, 2, 384, FF)

    targets[0], tokens_other, _ = lax.optimization_barrier((targets[0], tokens_other, first_mixer))
    targets[0] = exchange(targets[0])
    normed0, heads0, att0, own, other, routing, gains0 = attend(
        True, tokens, tokens_other, first_mixer, cosine, sine, mask
    )
    middle0, send, gates0, slot0 = post(
        D, tokens, own, swap(other), gains0, routing, named[0], spread[0]
    )
    send, targets[0] = lax.optimization_barrier((send, targets[0]))
    rows0, last_expert = dispatch(send, w_down, 0)
    experts0 = (first_experts, last_expert)
    produced, a0, b0 = expert_forward(rows0, experts0)
    routed0, last_expert = dispatch(produced, w_down, 1)
    experts1 = (second_experts, last_expert)
    routed0, targets[1] = lax.optimization_barrier((routed0, targets[1]))
    targets[1] = exchange(targets[1])
    hidden, normed, gains1 = combine_next(middle0, routed0, spread[0], slot0, second_mixer)

    normed1, heads1, att1, own, other, routing = attend(
        False, normed, swap(normed), second_mixer, cosine, sine, mask
    )
    middle1, send, gates1, slot1 = post(
        WIDE, hidden, own, swap(other), gains1, routing, named[1], spread[1]
    )
    rows1 = exchange(send)
    dx, da, db, inner, produced, dy = expert_both(rows1, targets, experts1)
    dx = exchange(dx)
    parts1 = expert_grads(rows1, dy, da, db, inner)
    dx, parts1 = lax.optimization_barrier((dx, parts1))
    sums1 = reduce_expert(parts1)
    routed1 = exchange(produced)

    grad_middle, grad_out, grad_routing, gain_two = pre_back(
        dx, None, middle1, gains1, cotangent, spread[1], gates1
    )
    grad_out_other = swap(grad_out)
    grad_heads, own, other = attend_back(
        grad_out, grad_out_other, grad_routing, second_mixer, heads1, cosine, sine, mask
    )
    grad, gain_parts, dy, shares = post_back(
        own, swap(other), hidden, gains1, grad_middle, gain_two, spread[0], slot0, routed0
    )
    products1 = mixer_products(
        normed1, grad_out, grad_out_other, grad_heads, att1, grad_routing, gain_parts
    )
    dy = exchange(dy)
    dy, products1 = lax.optimization_barrier((dy, products1))
    dx, da, db, inner = expert_back(a0, b0, dy, experts0)
    dx = exchange(dx)
    parts0 = expert_grads(rows0, dy, da, db, inner)
    sums0 = reduce_expert(parts0)
    dx, sums1, parts0 = lax.optimization_barrier((dx, sums1, parts0))

    grad_middle, grad_out, grad_routing, gain_two = pre_back(
        dx, shares, middle0, gains0, grad, spread[0], gates0
    )
    grad_out_other = swap(grad_out)
    grad_heads, own, other = attend_back(
        grad_out, grad_out_other, grad_routing, first_mixer, heads0, cosine, sine, mask
    )
    routed1 = lax.optimization_barrier((routed1, grad_heads))[0]
    output = combine(middle1, routed1, spread[1], slot1)
    grad_tokens, gain_parts = post_back(
        own, swap(other), tokens, gains0, grad_middle, gain_two
    )
    products0 = mixer_products(
        normed0, grad_out, grad_out_other, grad_heads, att0, grad_routing, gain_parts
    )
    mixer_out = mixer_outputs(reduce_mixer(products0 + products1), core)
    expert_out = expert_outputs([*sums0, *sums1])
    return (output, grad_tokens, *mixer_out, *expert_out)


def solution(mesh):
    mesh = Mesh(mesh.devices.reshape(4, 4, 4, 2), AXES)
    rows = P(AXES, None)
    mixer = P(None, AXES, None)
    gain = P(None, AXES)
    expert = P(None, GROUP, "dp", None)
    return jax.shard_map(
        per_device,
        mesh=mesh,
        in_specs=(
            rows, rows, mixer, mixer, mixer, mixer, mixer, mixer, gain, gain, expert, expert,
            expert, rows,
        ),
        out_specs=(
            rows, rows, mixer, mixer, mixer, mixer, mixer, gain, gain, expert, expert, expert,
        ),
        check_vma=False,
    )
```

```python
import math

import jax
import jax.numpy as jnp
import numpy as np
from jax import lax
from jax.experimental import pallas as pl
from jax.experimental.pallas import tpu as pltpu
from jax.sharding import Mesh, PartitionSpec as P

MESH = pl.DeviceIdType.MESH
BF = jnp.bfloat16
F32 = jnp.float32
HEADS, KV, HD, TOP, LAYERS = 12, 2, 128, 4, 2
T, D, FF, E, C = 128, 1536, 768, 32, 24
SLOTS = E * C
THETA, EPS = 1000000.0, 1e-06
SCALE = 1.0 / math.sqrt(HD)
ANY = pl.BlockSpec(memory_space=pl.ANY)
VM = pl.BlockSpec(memory_space=pltpu.VMEM)
WO, WR, COLS = 1024, 1792, 1920
CUTS = (pl.ds(0, 1024), pl.ds(1024, COLS - 1024))
PART = 640
VMEM = 32 << 20
WIDE = D + 128
AXES = ("dp", "z", "y", "core")
GROUP = AXES[1:]


def dot(a, b, dims=((1,), (0,))):
    return lax.dot_general(a, b, (dims, ((), ())), preferred_element_type=F32)


def split_two(v):
    high = v.astype(BF)
    return high, (v - high.astype(F32)).astype(BF)


def rope_tables():
    frequency = np.exp(-(2.0 * np.arange(HD // 2) / HD) * math.log(THETA)).astype(np.float32)
    angles = np.arange(T, dtype=np.float32)[:, None] * frequency[None, :]
    cosine, sine = np.cos(angles), np.sin(angles)
    return (
        jnp.asarray(np.concatenate([cosine, cosine], 1), F32),
        jnp.asarray(np.concatenate([-sine, sine], 1), F32),
    )


def swap(v):
    return lax.ppermute(v, "core", [(0, 1), (1, 0)])


def neighbours():
    here = [lax.axis_index(axis) for axis in AXES]

    def along(axis, places):
        peer = list(here)
        peer[axis] = lax.rem(here[axis] + places, 4)
        return tuple(peer)

    return here, along


def greet(peers):
    barrier = pltpu.get_barrier_semaphore()
    for peer in peers:
        pl.semaphore_signal(barrier, inc=1, device_id=peer, device_id_type=MESH)
    pl.semaphore_wait(barrier, len(peers))


def sender(send_sem, recv_sem):
    def send(src, dst, number, peer):
        copy = pltpu.make_async_remote_copy(
            src, dst, send_sem.at[number], recv_sem.at[number], device_id=peer, device_id_type=MESH
        )
        copy.start()
        return copy

    return send


def ring_steps(own, view, me, right, left, send, number):
    first = [
        send(own(0), view(me, 0), number, right), send(own(1), view(me, 1), number + 1, left)
    ]
    second = [
        send(own(1), view(me, 1), number + 2, right), send(own(0), view(me, 0), number + 3, left)
    ]

    relays = []

    def relay():
        before, after = lax.rem(me + 3, 4), lax.rem(me + 1, 4)
        first[0].wait_recv()
        relays.append(send(view(before, 0), view(before, 0), number + 4, right))
        first[1].wait_recv()
        relays.append(send(view(after, 1), view(after, 1), number + 5, left))

    def finish():
        for copy in second:
            copy.wait_recv()
        for copy in first + second:
            copy.wait_send()
        for copy in relays:
            copy.wait()

    return relay, finish


def ring_of(shard, out, x, along, send, number):
    return ring_steps(
        lambda half: shard.at[pl.ds(half * 192, 192)],
        lambda place, half: out.at[place, pl.ds(half * 192, 192)],
        x, along(0, 1), along(0, 3), send, number,
    )


def gather_kernel(blocks, gate, up, out, experts, local_sem, send_sem, recv_sem):
    (x, z, y, _), along = neighbours()
    greet([along(axis, o) for o in (1, 2, 3) for axis in range(3)])
    send = sender(send_sem, recv_sem)
    block = blocks.at[0]
    copies = [send(block, out.at[x, z, y], o - 1, along(0, o)) for o in (1, 3, 2)]
    shards = [gate.at[0, 0], up.at[0, 0]]
    rings = [
        ring_of(shard, experts.at[n], x, along, send, 27 + 6 * n) for n, shard in enumerate(shards)
    ]
    own = pltpu.make_async_copy(block, out.at[x, z, y], local_sem.at[0])
    own.start()
    own_experts = [
        pltpu.make_async_copy(shard, experts.at[n, x], local_sem.at[1 + n])
        for n, shard in enumerate(shards)
    ]
    for copy in own_experts:
        copy.start()
    own.wait()
    for copy in copies:
        copy.wait()

    def ring(view, axis, me, number):
        return ring_steps(
            lambda half: view(me, half), view, me, along(axis, 1), along(axis, 3), send, number
        )

    def pair(half):
        return pl.ds(half * 2, 2)

    first = ring(lambda n, half: out.at[pair(half), n, y, :, CUTS[0]], 1, z, 3)
    second = ring(lambda n, half: out.at[pair(half), z, n, :, CUTS[1]], 2, y, 9)
    first[0]()
    second[0]()
    first[1]()
    first = ring(lambda n, half: out.at[pair(half), :, n, :, CUTS[0]], 2, y, 15)
    second[1]()
    second = ring(lambda n, half: out.at[pair(half), n, :, :, CUTS[1]], 1, z, 21)
    rings[0][0]()
    first[0]()
    second[0]()
    rings[1][0]()
    first[1]()
    second[1]()
    for ring in rings:
        ring[1]()
    for copy in own_experts:
        copy.wait()


def gather(blocks, gate, up):
    mixer, experts = pl.pallas_call(
        gather_kernel,
        name="gather_weights",
        out_shape=(
            jax.ShapeDtypeStruct((4, 4, 4, 24, COLS), BF),
            jax.ShapeDtypeStruct((2, 4, D // 4, FF), BF),
        ),
        in_specs=[ANY] * 3,
        out_specs=(ANY, ANY),
        scratch_shapes=[
            pltpu.SemaphoreType.DMA((3,)),
            pltpu.SemaphoreType.DMA((39,)),
            pltpu.SemaphoreType.DMA((39,)),
        ],
        compiler_params=pltpu.CompilerParams(
            collective_id=1, has_side_effects=True, vmem_limit_bytes=VMEM
        ),
    )(blocks, gate, up)
    return mixer.reshape(D, COLS), experts.reshape(1, 2, D, FF)


def reduce_mixer_kernel(*refs):
    sources, out, scratch = refs[:6], refs[6], refs[7:]
    (x, z, y, _), along = neighbours()
    local_sem, send_sem, recv_sem = scratch[-3:]
    greet([along(axis, o) for o in (1, 2, 3) for axis in range(3)])
    send = sender(send_sem, recv_sem)
    here = (x, z, y)
    ways = ((1, 0, 2), (2, 1, 0), (0, 2, 1))
    jobs = []
    for level in reversed(range(LAYERS)):
        for group, way in enumerate(ways):
            number = level * 3 + group
            held = scratch[number * 10 : number * 10 + 10]
            jobs.append((number, sources[number], out.at[number], way, held))

    def pick(ref, dim, index, half=None):
        place = [slice(None)] * 3
        place[dim] = index
        if half is not None:
            place[1 if dim == 0 else 0] = half
        return ref.at[tuple(place)]

    def start_first(job):
        number, source, _, (axis, *_), (got, passed, relay, mine, own, *_) = job
        me = here[axis]
        right, left = along(axis, 1), along(axis, 3)
        after, far, before = (lax.rem(me + o, 4) for o in (1, 2, 3))
        low, high = pl.ds(0, 2), pl.ds(2, 2)
        base = number * 12
        copies = [
            send(pick(source, axis, far, low), passed.at[0], base, right),
            send(pick(source, axis, far, high), passed.at[1], base + 1, left),
            send(pick(source, axis, after, high), got.at[0, high], base + 2, right),
            send(pick(source, axis, before, low), got.at[1, low], base + 3, left),
        ]
        local = []
        for n, (src, dst) in enumerate(
            (
                (pick(source, axis, after, low), mine.at[0]),
                (pick(source, axis, before, high), mine.at[1]),
                (pick(source, axis, me), own),
            )
        ):
            local.append(pltpu.make_async_copy(src, dst, local_sem.at[number * 3 + n]))
            local[n].start()

        def pass_on():
            for n, (part, peer) in enumerate(((low, right), (high, left))):
                copies[n].wait()
                local[n].wait()
                total = mine[n].astype(F32) + passed[n].astype(F32)
                relay[n] = total.astype(BF)
                copies.append(send(relay.at[n], got.at[n, part], base + 4 + n, peer))

        def finish():
            for copy in copies[2:]:
                copy.wait()
            local[2].wait()

        return pass_on, finish

    def start_second(job):
        number, _, _, (gone, axis, _), (got, _, _, _, own, total, ready, after, *_) = job
        total[...] = own[...].astype(F32) + got[0].astype(F32) + got[1].astype(F32)
        started = []
        for o in (2, 1, 3):
            ready[o - 1] = sub(total, gone, axis, lax.rem(here[axis] + o, 4)).astype(BF)
            started.append(
                send(ready.at[o - 1], after.at[o - 1], number * 12 + 5 + o, along(axis, o))
            )
        return started

    def sub(total, gone, axis, index):
        first = axis == min(a for a in range(3) if a != gone)
        return total[index] if first else total[:, index]

    def start_third(job, copies):
        number, _, _, (gone, middle, axis), (*_, total, _, after, small, last) = job
        for copy in copies:
            copy.wait()
        rows = sub(total, gone, middle, here[middle])
        for o in range(3):
            rows = rows + after[o].astype(F32)
        small[...] = rows.astype(BF)
        started = [
            send(
                small.at[lax.rem(here[axis] + o, 4)], last.at[o - 1], number * 12 + 8 + o,
                along(axis, o),
            )
            for o in (2, 1, 3)
        ]
        return started

    def end(job, copies):
        _, _, out, (_, _, axis), (*_, small, last) = job
        for copy in copies:
            copy.wait()
        rows = small[here[axis]].astype(F32)
        for o in range(3):
            rows = rows + last[o].astype(F32)
        out[...] = rows

    running = [start_first(job) for job in jobs]
    for pass_on, _ in running:
        pass_on()
    seconds = []
    for job, (_, finish) in zip(jobs, running):
        finish()
        seconds.append(start_second(job))
    running = seconds
    running = [start_third(job, copies) for job, copies in zip(jobs, running)]
    for job, copies in zip(jobs, running):
        end(job, copies)


def reduce_mixer(products):
    scratch = []
    for _ in products:
        scratch += [
            pltpu.VMEM((2, 4, 4, 24, PART), BF),
            pltpu.VMEM((2, 2, 4, 24, PART), BF),
            pltpu.VMEM((2, 2, 4, 24, PART), BF),
            pltpu.VMEM((2, 2, 4, 24, PART), BF),
            pltpu.VMEM((4, 4, 24, PART), BF),
            pltpu.VMEM((4, 4, 24, PART), F32),
            pltpu.VMEM((3, 4, 24, PART), BF),
            pltpu.VMEM((3, 4, 24, PART), BF),
            pltpu.VMEM((4, 24, PART), BF),
            pltpu.VMEM((3, 24, PART), BF),
        ]
    return pl.pallas_call(
        reduce_mixer_kernel,
        name="reduce_mixer_gradients",
        out_shape=jax.ShapeDtypeStruct((6, 24, PART), F32),
        in_specs=[ANY] * 6,
        out_specs=VM,
        scratch_shapes=scratch
        + [
            pltpu.SemaphoreType.DMA((18,)),
            pltpu.SemaphoreType.DMA((72,)),
            pltpu.SemaphoreType.DMA((72,)),
        ],
        compiler_params=pltpu.CompilerParams(
            collective_id=2, has_side_effects=True, vmem_limit_bytes=48 << 20
        ),
    )(*products)


def columns(shape):
    return lax.broadcasted_iota(jnp.int32, shape, 1)


def rows_of(shape):
    return lax.broadcasted_iota(jnp.int32, shape, 0)


def plain(kernel, name, outs, flops=0, bytes_accessed=4000000, ins=None, scratch=()):
    def call(*args):
        return pl.pallas_call(
            kernel,
            name=name,
            out_shape=[jax.ShapeDtypeStruct(shape, kind) for shape, kind in outs],
            in_specs=ins or [VM] * len(args),
            out_specs=[VM] * len(outs),
            scratch_shapes=list(scratch),
            compiler_params=pltpu.CompilerParams(vmem_limit_bytes=VMEM),
            cost_estimate=pl.CostEstimate(
                flops=flops, bytes_accessed=bytes_accessed, transcendentals=0
            ),
        )(*args)

    return call


def tables_kernel(routes, *outs):
    wide = (T, 128)
    earlier = (rows_of(wide) < columns(wide)).astype(BF)
    same = (rows_of(wide) == columns(wide)).astype(BF)
    for level in range(LAYERS):
        named = jnp.zeros(wide, F32)
        for k in range(TOP):
            named = named + (routes[level, :, k : k + 1] == columns(wide)).astype(F32)
        outs[level][...] = named
        turned = dot(named.astype(BF), same, ((0,), (0,)))[:E]
        rank = dot(named.astype(BF), earlier, ((0,), (0,)))[:E]
        place = lax.broadcasted_iota(jnp.int32, (E, C, T), 1).astype(F32)
        hit = jnp.where(rank[:, None, :] == place, turned[:, None, :], 0.0)
        outs[LAYERS + level][...] = hit.reshape(SLOTS, T).astype(BF)


def route_tables(routes):
    return plain(
        tables_kernel, "route_tables",
        [((T, 128), F32)] * LAYERS + [((SLOTS, T), BF)] * LAYERS,
    )(routes)


def unit_rows(rows):
    scale = lax.rsqrt(jnp.mean(rows * rows, axis=-1, keepdims=True) + EPS)
    return rows * scale, scale


def gain_rows(router):
    pick = (columns((8, 128)) == E + rows_of((8, 128))) & (rows_of((8, 128)) < 2)
    return dot(pick.astype(BF), router, ((1,), (1,)))


def slot_columns():
    shape = (SLOTS, 128)
    start = columns(shape) * C
    return (rows_of(shape) >= start) & (rows_of(shape) < start + C)


def post_kernel(
    hidden, own, other, gains, routing, named, spread, middle_out, send_out, gates_out, slot_out
):
    middle = hidden[...].astype(F32) + own[...] + other[...].astype(F32)
    middle_out[...] = middle
    normed = (unit_rows(middle)[0] * gains[1:2]).astype(BF)
    send_out[:, :D] = dot(spread[...], normed).astype(BF)
    masked = jnp.where(named[...] > 0, routing[...], -1e30)
    terms = jnp.exp(masked - jnp.max(masked, axis=-1, keepdims=True))
    terms = jnp.where(named[...] > 0, terms, 0.0)
    gates = terms / jnp.sum(terms, axis=-1, keepdims=True)
    gates_out[...] = gates
    high, low = split_two(gates)
    all_gates = dot(spread[...], high) + dot(spread[...], low)
    slot = jnp.sum(jnp.where(slot_columns(), all_gates, 0.0), axis=-1, keepdims=True)
    slot_out[...] = slot
    if send_out.shape[1] > D:
        send_out[:, D:] = two_columns(slot)


def two_columns(value):
    high = value.astype(BF).astype(F32)
    column = columns((value.shape[0], WIDE - D))
    return jnp.where(column == 0, high, jnp.where(column == 1, value - high, 0.0)).astype(BF)


def post(width, *args):
    return plain(
        post_kernel, "dispatch_rows_of_tokens",
        [((T, D), F32), ((SLOTS, width), BF), ((T, 128), F32), ((SLOTS, 1), F32)], 2 * SLOTS * T * D,
    )(*args)


def combine_kernel(middle, routed, spread, slot, *refs):
    mix = spread[...].astype(F32) * slot[...]
    high, low = split_two(mix)
    rows = routed[...]
    hidden = middle[...] + dot(high, rows, ((0,), (0,))) + dot(low, rows, ((0,), (0,)))
    if len(refs) == 1:
        refs[0][...] = hidden
        return
    mixers, hidden_out, normed_out, gains_out, router, sem = refs
    copy = pltpu.make_async_copy(mixers.at[:, pl.ds(WR, COLS - WR)], router, sem)
    copy.start()
    hidden_out[...] = hidden
    copy.wait()
    gains = gain_rows(router[...])
    gains_out[...] = gains
    normed_out[...] = (unit_rows(hidden)[0] * gains[0:1]).astype(BF)


def combine(middle, routed, spread, slot):
    return plain(combine_kernel, "add_expert_outputs", [((T, D), F32)], 4 * SLOTS * T * D)(
        middle, routed, spread, slot
    )[0]


def combine_next(middle, routed, spread, slot, mixers):
    return plain(
        combine_kernel, "add_expert_outputs_and_norm",
        [((T, D), F32), ((T, D), BF), ((8, D), F32)], 4 * SLOTS * T * D,
        ins=[VM] * 4 + [ANY],
        scratch=[pltpu.VMEM((D, COLS - WR), BF), pltpu.SemaphoreType.DMA],
    )(middle, routed, spread, slot, mixers)


def back_through_norm(inputs, gain, grad_normed, grad_residual):
    unit, scale = unit_rows(inputs)
    grad_gain = jnp.sum(grad_normed * unit, axis=0, keepdims=True)
    grad_unit = grad_normed * gain
    back = grad_unit - unit * jnp.mean(grad_unit * unit, axis=-1, keepdims=True)
    return grad_residual + scale * back, grad_gain


def pre_back_kernel(
    dx, shares, middle, gains, grad, spread, gates, middle_out, out_out, routing_out, gain_out
):
    table = spread[...]
    if shares is None:
        share = dx[:, D : D + 1].astype(F32) + dx[:, D + 1 : D + 2].astype(F32)
    else:
        share = shares[...]
    high, low = split_two(jnp.where(slot_columns(), share, 0.0))
    dense = dot(table, high, ((0,), (0,))) + dot(table, low, ((0,), (0,)))
    routing = dense - gates[...] * jnp.sum(dense, axis=-1, keepdims=True)
    routing_out[...] = routing.astype(BF)
    grad_normed = dot(table, dx[:, :D], ((0,), (0,)))
    grad_middle, grad_gain = back_through_norm(
        middle[...], gains[1:2], grad_normed, grad[...].astype(F32)
    )
    middle_out[...] = grad_middle
    out_out[...] = grad_middle.astype(BF)
    gain_out[...] = grad_gain


def pre_back(dx, shares, *args):
    outs = [((T, D), F32), ((T, D), BF), ((T, 128), BF), ((1, D), F32)]
    if shares is None:
        return plain(
            lambda dx, *refs: pre_back_kernel(dx, None, *refs), "back_to_middle", outs,
            2 * SLOTS * T * D,
        )(dx, *args)
    return plain(pre_back_kernel, "back_to_middle", outs, 2 * SLOTS * T * D)(dx, shares, *args)


def post_back_kernel(own, other, hidden, gains, grad_middle, gain_two, *refs):
    grad_normed = own[...] + other[...].astype(F32)
    grad, gain_one = back_through_norm(
        hidden[...].astype(F32), gains[0:1], grad_normed, grad_middle[...]
    )
    if len(refs) == 2:
        grad_out, rows_out = refs
    else:
        spread, slot, routed, grad_out, rows_out, dy_out, share_out = refs
        high, low = split_two(grad)
        slots = dot(spread[...], high) + dot(spread[...], low)
        dy_out[...] = (slot[...] * slots).astype(BF)
        share = jnp.sum(routed[...].astype(F32) * slots, axis=-1, keepdims=True)
        share_out[...] = slot[...] * share
    grad_out[...] = grad
    rows_out[...] = jnp.zeros((16, D), BF)
    for n, gain in enumerate((gain_one, gain_two[...])):
        high, low = split_two(gain)
        rows_out[2 * n : 2 * n + 1] = high
        rows_out[2 * n + 1 : 2 * n + 2] = low


def post_back(*args):
    outs = [((T, D), F32), ((16, D), BF)]
    if len(args) > 6:
        outs += [((SLOTS, D), BF), ((SLOTS, 1), F32)]
    return plain(post_back_kernel, "back_to_hidden", outs, 4 * SLOTS * T * D)(*args)


def products_kernel(
    normed, grads_own, grads_other, heads, att, routing, gains,
    first_out, second_out, third_out, grads,
):
    step = pl.program_id(0)

    @pl.when(step == 0)
    def _():
        grads[:T] = grads_own[...]
        grads[T:] = grads_other[...]

    def product(left, right):
        return dot(left, right, ((0,), (0,)))

    def pair(ref, start, stop):
        return jnp.concatenate([ref[0, :, start:stop], ref[1, :, start:stop]], axis=0)

    block = pl.ds(pl.multiple_of(step * (D // 4), 128), D // 4)
    def store(out, value):
        out[0] = value.reshape(4, 4, 24, PART).astype(BF)

    left, turned = normed[:, block], grads[:, block]
    number, column = rows_of((16, 128)), columns((16, 128))
    gain_place = ((number < 2) & (column == E)) | (
        (number >= 2) & (number < 4) & (column == E + 1)
    )
    store(first_out, product(left, pair(heads, 0, PART)))
    store(second_out, product(turned, pair(att, 0, PART)))
    third = [
        product(left, pair(heads, PART, WO)),
        product(turned, pair(att, PART, WR - WO)),
        product(left[:T], routing[...]) + product(gains[:, block], gain_place.astype(BF)),
    ]
    store(third_out, jnp.concatenate(third, axis=1))


def mixer_products(normed, grads_own, grads_other, heads, att, routing, gains):
    def whole(v):
        zeros = (0,) * len(v.shape)
        return pl.BlockSpec(v.shape, lambda i: zeros, pipeline_mode=pl.Buffered(1))

    args = [normed, grads_own, grads_other, heads, att, routing, gains]
    return pl.pallas_call(
        products_kernel,
        name="mixer_products",
        grid=(4,),
        out_shape=[jax.ShapeDtypeStruct((4, 4, 4, 24, PART), BF)] * 3,
        in_specs=[whole(v) for v in args],
        out_specs=[pl.BlockSpec((1, 4, 4, 24, PART), lambda i: (i, 0, 0, 0, 0))] * 3,
        scratch_shapes=[pltpu.VMEM((2 * T, D), BF)],
        compiler_params=pltpu.CompilerParams(vmem_limit_bytes=VMEM),
        cost_estimate=pl.CostEstimate(
            flops=2 * 2 * T * D * COLS, bytes_accessed=11000000, transcendentals=0
        ),
    )(*args)


def turn(rows, cosine, sine):
    return rows * cosine + pltpu.roll(rows, HD // 2, 1) * sine


def head_rows(ref, sequence, heads):
    return jnp.concatenate([ref[sequence, :, h * HD : (h + 1) * HD] for h in heads], axis=0)


def weigh(queries, keys, mask):
    raw = dot(queries, keys, ((1,), (1,))).reshape(6, T, T)
    logits = jnp.where(mask[None] > 0, raw * SCALE, -1e30)
    terms = jnp.exp(logits - jnp.max(logits, axis=-1, keepdims=True))
    return (terms / jnp.sum(terms, axis=-1, keepdims=True)).reshape(6 * T, T)


PIECES = (pl.ds(WR, COLS - WR), pl.ds(0, WO), pl.ds(WO, WR - WO))


class Several:
    def __init__(self, copies):
        self.copies = copies
        for copy in copies:
            copy.start()

    def wait(self):
        for copy in self.copies:
            copy.wait()


def fetch_weights(mixers, weights, sem):
    groups = []
    for n, place in enumerate(PIECES):
        rows = [pl.ds(i * (D // 4), D // 4) for i in range(4)]
        groups.append(
            Several(
                [
                    pltpu.make_async_copy(
                        mixers.at[r, place], weights.at[r, place], sem.at[n * 4 + i]
                    )
                    for i, r in enumerate(rows)
                ]
            )
        )
    return groups


def attend_kernel(first, own, other, mixers, cosine, sine, mask, *refs):
    *refs, weights, sem = refs
    both, heads_out, att_out, own_out, other_out, routing_out = refs[:6]
    copies = fetch_weights(mixers, weights, sem)
    if first:
        units = [unit_rows(v[...].astype(F32))[0] for v in (own, other)]
        copies[0].wait()
        gains = gain_rows(weights[:, WR:])
        refs[6][...] = gains
        both[:T] = (units[0] * gains[0:1]).astype(BF)
        both[T:] = (units[1] * gains[0:1]).astype(BF)
    else:
        both[:T] = own[...]
        both[T:] = other[...]
        copies[0].wait()
    turns = [jnp.concatenate([t[...], t[...]], axis=0) for t in (cosine, sine)]
    copies[1].wait()
    for tile in range(4):
        wide = dot(both[...], weights[:, tile * 256 : (tile + 1) * 256])
        for part in range(2):
            head = tile * 2 + part
            rows = wide[:, part * HD : (part + 1) * HD]
            if head < 7:
                rows = turn(rows, *turns)
            rows = rows.astype(BF)
            for s in range(2):
                heads_out[s, :, head * HD : (head + 1) * HD] = rows[s * T : (s + 1) * T]
    for s in range(2):
        probs = weigh(head_rows(heads_out, s, range(6)), heads_out[s, :, 768:896], mask[s])
        mixed = dot(probs.astype(BF), heads_out[s, :, 896:]).astype(BF)
        for h in range(6):
            att_out[s, :, h * HD : (h + 1) * HD] = mixed[h * T : (h + 1) * T]
    copies[2].wait()
    att = att_out[...].reshape(2 * T, 768)
    for tile in range(6):
        place = slice(tile * 256, (tile + 1) * 256)
        rows = dot(att, weights[place, WO:WR], ((1,), (1,)))
        own_out[:, place] = rows[:T]
        other_out[:, place] = rows[T:].astype(BF)
    routing_out[...] = dot(both[:T], weights[:, WR:])


def attend(first, own, other, mixers, cosine, sine, mask):
    outs = [
        ((2 * T, D), BF), ((2, T, WO), BF), ((2, T, WR - WO), BF), ((T, D), F32), ((T, D), BF),
        ((T, 128), F32),
    ]
    return plain(
        lambda *refs: attend_kernel(first, *refs), "attention_forward",
        outs + [((8, D), F32)] * first, 1700000000, 9000000,
        ins=[VM, VM, ANY, VM, VM, VM],
        scratch=[pltpu.VMEM((D, COLS), BF), pltpu.SemaphoreType.DMA((12,))],
    )(own, other, mixers, cosine, sine, mask)


def attend_back_kernel(
    own, other, routing, mixers, heads, cosine, sine, mask,
    grad_heads, own_out, other_out, both, grad_att, weights, sem,
):
    copies = fetch_weights(mixers, weights, sem)
    both[:T] = own[...]
    both[T:] = other[...]
    copies[2].wait()
    for tile in range(3):
        place = slice(tile * 256, (tile + 1) * 256)
        wide = dot(both[...], weights[:, WO + tile * 256 : WO + (tile + 1) * 256]).astype(BF)
        for s in range(2):
            grad_att[s, :, place] = wide[s * T : (s + 1) * T]
    cos, sin = cosine[...], -sine[...]
    for s in range(2):
        queries, grads = head_rows(heads, s, range(6)), head_rows(grad_att, s, range(6))
        keys, values = heads[s, :, 768:896], heads[s, :, 896:]
        probs = weigh(queries, keys, mask[s])
        dp = dot(grads, values, ((1,), (1,)))
        draw = probs * (dp - jnp.sum(probs * dp, axis=-1, keepdims=True))
        draw = (draw * SCALE).astype(BF)
        dq = dot(draw, keys)
        for h in range(6):
            rows = turn(dq[h * T : (h + 1) * T], cos, sin)
            grad_heads[s, :, h * HD : (h + 1) * HD] = rows.astype(BF)
        dk = dot(draw, queries, ((0,), (0,)))
        grad_heads[s, :, 768:896] = turn(dk, cos, sin).astype(BF)
        grad_heads[s, :, 896:] = dot(probs.astype(BF), grads, ((0,), (0,))).astype(BF)
    copies[0].wait()
    copies[1].wait()
    wide = grad_heads[...].reshape(2 * T, 1024)
    for tile in range(6):
        place = slice(tile * 256, (tile + 1) * 256)
        rows = dot(wide, weights[place, :WO], ((1,), (1,)))
        own_out[:, place] = rows[:T] + dot(routing[...], weights[place, WR:], ((1,), (1,)))
        other_out[:, place] = rows[T:].astype(BF)


def attend_back(own, other, routing, mixers, heads, cosine, sine, mask):
    return pl.pallas_call(
        attend_back_kernel,
        name="attention_backward",
        out_shape=(
            jax.ShapeDtypeStruct((2, T, 1024), BF),
            jax.ShapeDtypeStruct((T, D), F32),
            jax.ShapeDtypeStruct((T, D), BF),
        ),
        in_specs=[VM, VM, VM, ANY, VM, VM, VM, VM],
        out_specs=[VM] * 3,
        scratch_shapes=[
            pltpu.VMEM((2 * T, D), BF),
            pltpu.VMEM((2, T, 768), BF),
            pltpu.VMEM((D, COLS), BF),
            pltpu.SemaphoreType.DMA((12,)),
        ],
        compiler_params=pltpu.CompilerParams(vmem_limit_bytes=VMEM),
        cost_estimate=pl.CostEstimate(flops=2200000000, bytes_accessed=9000000, transcendentals=200000),
    )(own, other, routing, mixers, heads, cosine, sine, mask)

class Exchange:
    def __init__(self, rows, held, result, back, sems, also=()):
        (self.x, self.z, self.y, self.core), self.along = neighbours()
        self.rows, self.held, self.result, self.back = rows, held, result, back
        self.sems, self.local = sems[:4], sems[4]
        self.me = self.index(self.z, self.y, self.core)
        greet([self.peer(k, 1) for k in range(1, E)] + [self.along(0, o) for o in also])

    def index(self, z, y, core):
        return (z * 4 + y) * 2 + core

    def peer(self, k, sign):
        a, b, c = k // 8, k // 2 % 4, k % 2
        return (
            self.x,
            lax.rem(self.z + (a * sign) % 4, 4),
            lax.rem(self.y + (b * sign) % 4, 4),
            lax.rem(self.core + c, 2),
        )

    def copy(self, k, returning):
        peer = self.peer(k, -1 if returning else 1)
        there = self.index(*peer[1:])
        source, target = (self.result, self.back) if returning else (self.rows, self.held)
        sems = self.sems[2:] if returning else self.sems[:2]
        return pltpu.make_async_remote_copy(
            source.at[there], target.at[self.me], sems[0].at[k], sems[1].at[k],
            device_id=peer, device_id_type=MESH,
        )

    def start(self):
        for a in (2, 1, 3, 0):
            for k in range(a * 8, a * 8 + 8):
                if k:
                    self.copy(k, False).start()
        self.own = pltpu.make_async_copy(
            self.rows.at[self.me], self.held.at[self.me], self.local.at[0]
        )
        self.own.start()

    def arrive(self, a):
        for k in range(a * 8, a * 8 + 8):
            if k:
                self.copy(k, False).wait_recv()
        if a == 0:
            self.own.wait()
        block = lax.rem(self.z + (-a) % 4, 4)
        rows = self.held[pl.ds(block * 8, 8)].astype(F32)
        return block, rows.reshape(8 * C, rows.shape[2]).astype(BF)

    def give(self, a, block, value):
        width = value.shape[1]
        self.result[pl.ds(block * 8, 8), :, :width] = value.reshape(8, C, width).astype(BF)

    def send_back(self, a):
        for k in range(a * 8, a * 8 + 8):
            if k:
                self.copy(k, True).start()
        if a == 0:
            self.last = pltpu.make_async_copy(
                self.result.at[self.me], self.back.at[self.me], self.local.at[1]
            )
            self.last.start()

    def finish(self):
        for k in range(1, E):
            self.copy(k, False).wait_send()
            self.copy(k, True).wait()
        self.last.wait()


GROUPS = (2, 0, 1, 3)


def start_weights(pieces, weights, sem):
    waits, matrix = [], 0
    for piece in pieces:
        count, several = piece.shape[:2]
        for m in range(several):
            copies = []
            for n in range(4):
                source = piece.at[n, m] if count == 4 else piece.at[0, m, pl.ds(n * 384, 384)]
                copies.append(
                    pltpu.make_async_copy(
                        source, weights.at[matrix, n], sem.at[matrix * 4 + n]
                    )
                )
                copies[n].start()
            waits.append(copies)
            matrix += 1

    def ready(m):
        for copy in waits[m]:
            copy.wait()

    return ready


def matrix_of(weights, m):
    return weights[m].reshape(D, FF)


def at_block(block):
    return pl.ds(pl.multiple_of(block * 8 * C, 8 * C), 8 * C)


def forward_phase_kernel(
    rows, gate_up, downs, back, flat_out, a_out, b_out, down_out, next_out,
    held, result, weights, weight_sem, ring_send, ring_recv, *sems,
):
    work = Exchange(rows, held, result, back, sems, (1, 3))
    work.start()
    send = sender(ring_send, ring_recv)
    x, local = work.x, work.local
    own = [
        pltpu.make_async_copy(downs.at[0, 0], weights.at[2, x], local.at[2]),
        pltpu.make_async_copy(downs.at[1, 0], next_out.at[0, x], local.at[3]),
    ]
    for copy in own:
        copy.start()
    ring = ring_of(downs.at[0, 0], weights.at[2], x, work.along, send, 0)
    other = ring_of(downs.at[1, 0], next_out.at[0], x, work.along, send, 6)
    ready = start_weights([gate_up], weights, weight_sem)
    ring[0]()
    for number, group in enumerate(GROUPS):
        block, got = work.arrive(group)
        place = at_block(block)
        flat_out[place] = got
        if number == 0:
            ready(0)
        a = dot(got, matrix_of(weights, 0))
        if number == 0:
            ready(1)
        b = dot(got, matrix_of(weights, 1))
        a_out[place] = a
        b_out[place] = b
        inner = (a * jax.nn.sigmoid(a) * b).astype(BF)
        if number == 0:
            ring[1]()
            own[0].wait()
        work.give(group, block, dot(inner, matrix_of(weights, 2), ((1,), (1,))))
        work.send_back(group)
        if number == 0:
            other[0]()
    kept = pltpu.make_async_copy(weights.at[2], down_out.at[0], local.at[2])
    kept.start()
    other[1]()
    own[1].wait()
    work.finish()
    kept.wait()


def inner_gradients(a, b, dy, weights, place, held):
    du = dot(dy, matrix_of(weights, 2))
    sig = jax.nn.sigmoid(a)
    act = a * sig
    inner = (act * b).astype(BF)
    da = (du * b * sig * (1.0 + a * (1.0 - sig))).astype(BF)
    db = (du * act).astype(BF)
    for ref, value in zip(held, (da, db, inner)):
        ref[place] = value
    dx = dot(da, matrix_of(weights, 0), ((1,), (1,)))
    return inner, dx + dot(db, matrix_of(weights, 1), ((1,), (1,)))


def weight_gradients(rows, dy, held, outs):
    @pl.loop(0, 4)
    def _(n):
        columns = pl.ds(pl.multiple_of(n * 384, 128), 384)
        place = pl.ds(pl.multiple_of(n * 384, 128), 384)
        for left, right, out in zip((rows, rows, dy), held, outs):
            out[place] = dot(left[:, columns], right[...], ((0,), (0,))).astype(BF)


def back_phase_kernel(
    rows, a_in, b_in, flat_in, gate_up, down, back, gate_out, up_out, down_out,
    held, result, weights, a, b, flat, dy, da, db, inner, weight_sem, load_sem, *sems,
):
    work = Exchange(rows, held, result, back, sems)
    work.start()
    ready = start_weights([gate_up, down], weights, weight_sem)
    loads = []
    for n, (src, dst) in enumerate(((a_in, a), (b_in, b), (flat_in, flat))):
        loads.append(pltpu.make_async_copy(src, dst, load_sem.at[n]))
        loads[n].start()
    for number, group in enumerate(GROUPS):
        block, got = work.arrive(group)
        place = at_block(block)
        dy[place] = got
        if number == 0:
            loads[0].wait()
            loads[1].wait()
            for m in range(3):
                ready(m)
        _, dx = inner_gradients(a[place], b[place], got, weights, place, (da, db, inner))
        work.give(group, block, dx)
        work.send_back(group)
    loads[2].wait()
    weight_gradients(flat, dy, (da, db, inner), (gate_out, up_out, down_out))
    work.finish()


def both_phase_kernel(
    rows, target_low, target_high, gate_up, down, back, y_out, gate_out, up_out, down_out,
    held, result, weights, low, high, flat, dy, da, db, inner, weight_sem, load_sem, *sems,
):
    work = Exchange(rows, held, result, back, sems)
    work.start()
    ready = start_weights([gate_up, down], weights, weight_sem)
    loads = []
    for n, (src, dst) in enumerate(((target_low, low), (target_high, high))):
        loads.append(pltpu.make_async_copy(src, dst, load_sem.at[n]))
        loads[n].start()
    for number, group in enumerate(GROUPS):
        block, got = work.arrive(group)
        place = at_block(block)
        normed = got[:, :D]
        flat[place] = normed
        gate = got[:, D : D + 1].astype(F32) + got[:, D + 1 : D + 2].astype(F32)
        if number == 0:
            loads[0].wait()
            loads[1].wait()
            for m in range(3):
                ready(m)
        target = jnp.concatenate([low[place], high[place]], axis=1)
        grads = (gate * target.astype(F32)).astype(BF)
        dy[place] = grads
        a = dot(normed, matrix_of(weights, 0))
        b = dot(normed, matrix_of(weights, 1))
        mixed, dx = inner_gradients(a, b, grads, weights, place, (da, db, inner))
        y = dot(mixed, matrix_of(weights, 2), ((1,), (1,))).astype(BF)
        y_out[place] = y
        share = jnp.sum(y.astype(F32) * grads.astype(F32), axis=-1, keepdims=True)
        parts = two_columns(share).astype(F32)
        work.give(group, block, jnp.concatenate([dx, parts], axis=1))
        work.send_back(group)
    weight_gradients(flat, dy, (da, db, inner), (gate_out, up_out, down_out))
    work.finish()


def phase_call(kernel, name, number, args, outs, scratch, width, flops):
    slots = (E, C, width)
    return pl.pallas_call(
        kernel,
        name=name,
        out_shape=[jax.ShapeDtypeStruct(slots, BF)]
        + [jax.ShapeDtypeStruct(shape, kind) for shape, kind, _ in outs],
        in_specs=[ANY] * len(args),
        out_specs=[ANY] + [spec for *_, spec in outs],
        scratch_shapes=[
            pltpu.VMEM(slots, BF), pltpu.VMEM(slots, BF), pltpu.VMEM((3, 4, D // 4, FF), BF)
        ]
        + scratch
        + [pltpu.SemaphoreType.DMA((E,))] * 4
        + [pltpu.SemaphoreType.DMA((4,))],
        compiler_params=pltpu.CompilerParams(
            collective_id=number, has_side_effects=True, vmem_limit_bytes=52 << 20
        ),
        cost_estimate=pl.CostEstimate(
            flops=flops, bytes_accessed=20000000, transcendentals=SLOTS * FF
        ),
    )(*args)


UNIT = 2 * SLOTS * D * FF
GRADS = [((D, FF), BF, VM)] * 3


def forward_phase(rows, gate_up, downs):
    shard = (1, 4, D // 4, FF)
    back, flat, a, b, down, after = phase_call(
        forward_phase_kernel, "expert_phase_forward", 3, (rows.reshape(E, C, D), gate_up, downs),
        [((SLOTS, D), BF, VM), ((SLOTS, FF), F32, VM), ((SLOTS, FF), F32, VM), (shard, BF, ANY),
         (shard, BF, ANY)],
        [pltpu.SemaphoreType.DMA((8,)), pltpu.SemaphoreType.DMA((12,)),
         pltpu.SemaphoreType.DMA((12,))],
        D, 3 * UNIT,
    )
    whole = (1, 1, D, FF)
    return back.reshape(SLOTS, D), flat, a, b, down.reshape(whole), after.reshape(whole)


def matrices(*widths):
    return [pltpu.VMEM((SLOTS, width), BF) for width in widths]


def back_phase(rows, a, b, flat, gate_up, down):
    back, *grads = phase_call(
        back_phase_kernel, "expert_phase_backward", 5,
        (rows.reshape(E, C, D), a, b, flat, gate_up, down), GRADS,
        [pltpu.VMEM((SLOTS, FF), F32)] * 2 + matrices(D, D, FF, FF, FF)
        + [pltpu.SemaphoreType.DMA((12,)), pltpu.SemaphoreType.DMA((3,))],
        D, 6 * UNIT,
    )
    return back.reshape(SLOTS, D), grads


def both_phase(rows, targets, gate_up, down):
    back, y, *grads = phase_call(
        both_phase_kernel, "expert_phase_both", 4,
        (rows.reshape(E, C, WIDE), *targets, gate_up, down), [((SLOTS, D), BF, VM)] + GRADS,
        matrices(FF, FF, D, D, FF, FF, FF)
        + [pltpu.SemaphoreType.DMA((12,)), pltpu.SemaphoreType.DMA((2,))],
        WIDE, 9 * UNIT,
    )
    return back.reshape(SLOTS, WIDE), y, grads


def exchange(rows):
    width = rows.shape[1]
    rows = rows.reshape(E, C, width)
    rows = lax.all_to_all(rows, GROUP, split_axis=0, concat_axis=0, tiled=True)
    return rows.reshape(SLOTS, width)


def outputs_kernel(core, mine, theirs, *outs):
    for level in range(LAYERS):
        level_outputs(level, core[0] == 0, mine, theirs, *outs)


def level_outputs(level, first, mine, theirs, q_out, k_out, v_out, o_out, routing_out):

    def rows(ref, group):
        group = level * 3 + group
        return jnp.where(first, ref[group, :12], ref[group, 12:])

    halves = []
    for ref in (mine, theirs):
        a, b, c = (rows(ref, group) for group in range(3))
        halves.append(
            (
                jnp.concatenate([a, c[:, :HD]], axis=1),
                c[:, HD : 2 * HD],
                c[:, 2 * HD : 3 * HD],
                jnp.concatenate([b, c[:, 3 * HD : 4 * HD]], axis=1),
                c[:, 4 * HD :],
            )
        )
    for out, own, other in zip((q_out, k_out, v_out, o_out), *halves):
        width = own.shape[1]
        out[:, level, :width] = jnp.where(first, own, other)
        out[:, level, width:] = jnp.where(first, other, own)
    routing_out[:, level, :] = halves[0][4] + halves[1][4]


def mixer_outputs(sums, core):
    widths = (D, 2 * HD, 2 * HD, D, HD)
    *outs, routing = pl.pallas_call(
        outputs_kernel,
        name="mixer_outputs",
        out_shape=[jax.ShapeDtypeStruct((12, LAYERS, width), F32) for width in widths],
        grid=(1,),
        in_specs=[pl.BlockSpec(memory_space=pltpu.SMEM)]
        + [pl.BlockSpec((6, 24, PART), lambda i: (0, 0, 0))] * 2,
        out_specs=[pl.BlockSpec((12, LAYERS, width), lambda i: (0, 0, 0)) for width in widths],
    )(core.reshape(1), sums, swap(sums))
    *outs, routing = [v.transpose(1, 0, 2) for v in (*outs, routing)]
    return (*outs, routing[:, :, :E], routing[:, :, E], routing[:, :, E + 1])


def expert_outputs_kernel(*refs):
    for matrix in range(3):
        for level in range(LAYERS):
            refs[6 + matrix][level, 0] = refs[level * 3 + matrix][...].astype(F32)


def expert_outputs(sums):
    rows = 96
    return pl.pallas_call(
        expert_outputs_kernel,
        name="expert_outputs",
        grid=(D // 4 // rows,),
        out_shape=[jax.ShapeDtypeStruct((LAYERS, 1, D // 4, FF), F32)] * 3,
        in_specs=[pl.BlockSpec((rows, FF), lambda i: (i, 0))] * 6,
        out_specs=[pl.BlockSpec((LAYERS, 1, rows, FF), lambda i: (0, 0, i, 0))] * 3,
        compiler_params=pltpu.CompilerParams(vmem_limit_bytes=VMEM),
        cost_estimate=pl.CostEstimate(flops=0, bytes_accessed=11000000, transcendentals=0),
    )(*sums)


def reduce_expert(grads):
    return [
        lax.psum_scatter(g, "dp", scatter_dimension=0, tiled=True) for g in grads
    ]


def per_device(
    tokens, segments, route_ids, w_query, key_projection, value_projection, w_out, w_router,
    gain_attn, gain_moe, w_gate, w_up, w_down, cotangent,
):
    core = lax.axis_index("core")
    cosine, sine = rope_tables()
    position = jnp.arange(T)

    shared = jnp.concatenate(
        [
            w_router, gain_attn[:, :, None], gain_moe[:, :, None],
            jnp.zeros((LAYERS, 12, COLS - WR - E - 2), BF),
        ],
        axis=2,
    )

    def half(number):
        def cut(v):
            width = v.shape[2] // 2
            return v[:, :, number * width : (number + 1) * width]

        return jnp.concatenate(
            [cut(v) for v in (w_query, key_projection, value_projection, w_out)] + [shared], axis=2
        )

    halves = (half(0), half(1))
    mine = jnp.where(core == 0, halves[0], halves[1])
    theirs = swap(jnp.where(core == 0, halves[1], halves[0]))
    blocks = jnp.where(
        core == 0,
        jnp.concatenate([mine, theirs], axis=1),
        jnp.concatenate([theirs, mine], axis=1),
    )
    segment = segments.astype(F32)
    segment = jnp.concatenate([segment, swap(segment)])
    mask = (position[:, None] >= position[None, :])[None] & (
        segment[:, :, None] == segment[:, None, :]
    )
    mask = mask.astype(F32)

    *named, spread0, spread1 = route_tables(route_ids)
    spread = (spread0, spread1)
    targets = [
        dot(spread[1], cotangent[:, half * 768 : (half + 1) * 768]).astype(BF) for half in range(2)
    ]
    tokens_other = swap(tokens)
    first_mixer, first_experts = gather(blocks, w_gate, w_up)
    second = jnp.concatenate([w_gate[1, 0], w_up[1, 0]])
    second = lax.optimization_barrier((blocks[1], second, first_experts))
    second_mixer = lax.all_gather(second[0], AXES[:3], axis=0).reshape(D, COLS)
    second_experts = lax.all_gather(second[1], "dp", axis=0).reshape(4, 2, 384, FF)

    targets[0], tokens_other, _ = lax.optimization_barrier((targets[0], tokens_other, first_mixer))
    targets[0] = exchange(targets[0])
    normed0, heads0, att0, own, other, routing, gains0 = attend(
        True, tokens, tokens_other, first_mixer, cosine, sine, mask
    )
    middle0, send, gates0, slot0 = post(
        D, tokens, own, swap(other), gains0, routing, named[0], spread[0]
    )
    send, targets[0] = lax.optimization_barrier((send, targets[0]))
    routed0, rows0, a0, b0, down0, down1 = forward_phase(send, first_experts, w_down)
    routed0, targets[1] = lax.optimization_barrier((routed0, targets[1]))
    targets[1] = exchange(targets[1])
    hidden, normed, gains1 = combine_next(middle0, routed0, spread[0], slot0, second_mixer)

    normed1, heads1, att1, own, other, routing = attend(
        False, normed, swap(normed), second_mixer, cosine, sine, mask
    )
    middle1, send, gates1, slot1 = post(
        WIDE, hidden, own, swap(other), gains1, routing, named[1], spread[1]
    )
    gate_up1 = second_experts.reshape(4, 2, D // 4, FF)
    dx, produced, parts1 = both_phase(send, targets, gate_up1, down1)
    sums1 = reduce_expert(parts1)
    routed1 = exchange(produced)

    grad_middle, grad_out, grad_routing, gain_two = pre_back(
        dx, None, middle1, gains1, cotangent, spread[1], gates1
    )
    grad_out_other = swap(grad_out)
    grad_heads, own, other = attend_back(
        grad_out, grad_out_other, grad_routing, second_mixer, heads1, cosine, sine, mask
    )
    grad, gain_parts, dy, shares = post_back(
        own, swap(other), hidden, gains1, grad_middle, gain_two, spread[0], slot0, routed0
    )
    products1 = mixer_products(
        normed1, grad_out, grad_out_other, grad_heads, att1, grad_routing, gain_parts
    )
    dx, parts0 = back_phase(dy, a0, b0, rows0, first_experts, down0)
    sums0 = reduce_expert(parts0)
    dx, sums1, products1 = lax.optimization_barrier((dx, sums1, products1))

    grad_middle, grad_out, grad_routing, gain_two = pre_back(
        dx, shares, middle0, gains0, grad, spread[0], gates0
    )
    grad_out_other = swap(grad_out)
    grad_heads, own, other = attend_back(
        grad_out, grad_out_other, grad_routing, first_mixer, heads0, cosine, sine, mask
    )
    routed1 = lax.optimization_barrier((routed1, grad_heads))[0]
    output = combine(middle1, routed1, spread[1], slot1)
    grad_tokens, gain_parts = post_back(
        own, swap(other), tokens, gains0, grad_middle, gain_two
    )
    products0 = mixer_products(
        normed0, grad_out, grad_out_other, grad_heads, att0, grad_routing, gain_parts
    )
    mixer_out = mixer_outputs(reduce_mixer(products0 + products1), core)
    expert_out = expert_outputs([*sums0, *sums1])
    return (output, grad_tokens, *mixer_out, *expert_out)


def solution(mesh):
    mesh = Mesh(mesh.devices.reshape(4, 4, 4, 2), AXES)
    rows = P(AXES, None)
    mixer = P(None, AXES, None)
    gain = P(None, AXES)
    expert = P(None, GROUP, "dp", None)
    return jax.shard_map(
        per_device,
        mesh=mesh,
        in_specs=(
            rows, rows, mixer, mixer, mixer, mixer, mixer, mixer, gain, gain, expert, expert,
            expert, rows,
        ),
        out_specs=(
            rows, rows, mixer, mixer, mixer, mixer, mixer, gain, gain, expert, expert, expert,
        ),
        check_vma=False,
    )
```

```python
import math

import jax
import jax.numpy as jnp
import numpy as np
from jax import lax
from jax.experimental import pallas as pl
from jax.experimental.pallas import tpu as pltpu
from jax.sharding import Mesh, PartitionSpec as P

MESH = pl.DeviceIdType.MESH
BF = jnp.bfloat16
F32 = jnp.float32
HEADS, KV, HD, TOP, LAYERS = 12, 2, 128, 4, 2
T, D, FF, E, C = 128, 1536, 768, 32, 24
SLOTS = E * C
THETA, EPS = 1000000.0, 1e-06
SCALE = 1.0 / math.sqrt(HD)
ANY = pl.BlockSpec(memory_space=pl.ANY)
VM = pl.BlockSpec(memory_space=pltpu.VMEM)
WO, WR, COLS = 1024, 1792, 1920
CUTS = (pl.ds(0, 1024), pl.ds(1024, COLS - 1024))
PARTS = (768, 768, 384)
VMEM = 32 << 20
WIDE = D + 128
AXES = ("dp", "z", "y", "core")
GROUP = AXES[1:]


def dot(a, b, dims=((1,), (0,))):
    return lax.dot_general(a, b, (dims, ((), ())), preferred_element_type=F32)


def split_two(v):
    high = v.astype(BF)
    return high, (v - high.astype(F32)).astype(BF)


def rope_tables():
    frequency = np.exp(-(2.0 * np.arange(HD // 2) / HD) * math.log(THETA)).astype(np.float32)
    angles = np.arange(T, dtype=np.float32)[:, None] * frequency[None, :]
    cosine, sine = np.cos(angles), np.sin(angles)
    return (
        jnp.asarray(np.concatenate([cosine, cosine], 1), F32),
        jnp.asarray(np.concatenate([-sine, sine], 1), F32),
    )


def swap(v):
    return lax.ppermute(v, "core", [(0, 1), (1, 0)])


def neighbours():
    here = [lax.axis_index(axis) for axis in AXES]

    def along(axis, places):
        peer = list(here)
        peer[axis] = lax.rem(here[axis] + places, 4)
        return tuple(peer)

    return here, along


def greet(peers):
    barrier = pltpu.get_barrier_semaphore()
    for peer in peers:
        pl.semaphore_signal(barrier, inc=1, device_id=peer, device_id_type=MESH)
    pl.semaphore_wait(barrier, len(peers))


def sender(send_sem, recv_sem):
    def send(src, dst, number, peer):
        copy = pltpu.make_async_remote_copy(
            src, dst, send_sem.at[number], recv_sem.at[number], device_id=peer, device_id_type=MESH
        )
        copy.start()
        return copy

    return send


def ring_steps(own, view, me, right, left, send, number):
    first = [
        send(own(0), view(me, 0), number, right), send(own(1), view(me, 1), number + 1, left)
    ]
    second = [
        send(own(1), view(me, 1), number + 2, right), send(own(0), view(me, 0), number + 3, left)
    ]

    relays = []

    def relay():
        before, after = lax.rem(me + 3, 4), lax.rem(me + 1, 4)
        first[0].wait_recv()
        relays.append(send(view(before, 0), view(before, 0), number + 4, right))
        first[1].wait_recv()
        relays.append(send(view(after, 1), view(after, 1), number + 5, left))

    def finish():
        for copy in second:
            copy.wait_recv()
        for copy in first + second:
            copy.wait_send()
        for copy in relays:
            copy.wait()

    return relay, finish


def ring_of(shard, out, x, along, send, number):
    return ring_steps(
        lambda half: shard.at[pl.ds(half * 192, 192)],
        lambda place, half: out.at[place, pl.ds(half * 192, 192)],
        x, along(0, 1), along(0, 3), send, number,
    )


def gather_kernel(blocks, gate, up, out, experts, local_sem, send_sem, recv_sem):
    (x, z, y, _), along = neighbours()
    greet([along(axis, o) for o in (1, 2, 3) for axis in range(3)])
    send = sender(send_sem, recv_sem)
    block = blocks.at[0]
    copies = [send(block, out.at[x, z, y], o - 1, along(0, o)) for o in (1, 3, 2)]
    shards = [gate.at[0, 0], up.at[0, 0]]
    rings = [
        ring_of(shard, experts.at[n], x, along, send, 27 + 6 * n) for n, shard in enumerate(shards)
    ]
    own = pltpu.make_async_copy(block, out.at[x, z, y], local_sem.at[0])
    own.start()
    own_experts = [
        pltpu.make_async_copy(shard, experts.at[n, x], local_sem.at[1 + n])
        for n, shard in enumerate(shards)
    ]
    for copy in own_experts:
        copy.start()
    own.wait()
    for copy in copies:
        copy.wait()

    def ring(view, axis, me, number):
        return ring_steps(
            lambda half: view(me, half), view, me, along(axis, 1), along(axis, 3), send, number
        )

    def pair(half):
        return pl.ds(half * 2, 2)

    first = ring(lambda n, half: out.at[pair(half), n, y, :, CUTS[0]], 1, z, 3)
    second = ring(lambda n, half: out.at[pair(half), z, n, :, CUTS[1]], 2, y, 9)
    first[0]()
    second[0]()
    first[1]()
    first = ring(lambda n, half: out.at[pair(half), :, n, :, CUTS[0]], 2, y, 15)
    second[1]()
    second = ring(lambda n, half: out.at[pair(half), n, :, :, CUTS[1]], 1, z, 21)
    rings[0][0]()
    first[0]()
    second[0]()
    rings[1][0]()
    first[1]()
    second[1]()
    for ring in rings:
        ring[1]()
    for copy in own_experts:
        copy.wait()


def gather(blocks, gate, up):
    mixer, experts = pl.pallas_call(
        gather_kernel,
        name="gather_weights",
        out_shape=(
            jax.ShapeDtypeStruct((4, 4, 4, 24, COLS), BF),
            jax.ShapeDtypeStruct((2, 4, D // 4, FF), BF),
        ),
        in_specs=[ANY] * 3,
        out_specs=(ANY, ANY),
        scratch_shapes=[
            pltpu.SemaphoreType.DMA((3,)),
            pltpu.SemaphoreType.DMA((39,)),
            pltpu.SemaphoreType.DMA((39,)),
        ],
        compiler_params=pltpu.CompilerParams(
            collective_id=1, has_side_effects=True, vmem_limit_bytes=VMEM
        ),
    )(blocks, gate, up)
    return mixer.reshape(D, COLS), experts.reshape(1, 2, D, FF)


def reduce_mixer_kernel(*refs):
    sources, out, scratch = refs[:6], refs[6], refs[7:]
    (x, z, y, _), along = neighbours()
    local_sem, send_sem, recv_sem = scratch[-3:]
    greet([along(axis, o) for o in (1, 2, 3) for axis in range(3)])
    send = sender(send_sem, recv_sem)
    here = (x, z, y)
    ways = ((1, 0, 2), (2, 1, 0), (0, 2, 1))
    jobs = []
    for level in reversed(range(LAYERS)):
        for group, way in enumerate(ways):
            number = level * 3 + group
            held = scratch[number * 10 : number * 10 + 10]
            jobs.append((number, sources[number], out.at[number], way, held))

    def pick(ref, dim, index, half=None):
        place = [slice(None)] * 3
        place[dim] = index
        if half is not None:
            place[1 if dim == 0 else 0] = half
        return ref.at[tuple(place)]

    def start_first(job):
        number, source, _, (axis, *_), (got, passed, relay, mine, own, *_) = job
        me = here[axis]
        right, left = along(axis, 1), along(axis, 3)
        after, far, before = (lax.rem(me + o, 4) for o in (1, 2, 3))
        low, high = pl.ds(0, 2), pl.ds(2, 2)
        base = number * 12
        copies = [
            send(pick(source, axis, far, low), passed.at[0], base, right),
            send(pick(source, axis, far, high), passed.at[1], base + 1, left),
            send(pick(source, axis, after, high), got.at[0, high], base + 2, right),
            send(pick(source, axis, before, low), got.at[1, low], base + 3, left),
        ]
        local = []
        for n, (src, dst) in enumerate(
            (
                (pick(source, axis, after, low), mine.at[0]),
                (pick(source, axis, before, high), mine.at[1]),
                (pick(source, axis, me), own),
            )
        ):
            local.append(pltpu.make_async_copy(src, dst, local_sem.at[number * 3 + n]))
            local[n].start()

        def pass_on():
            for n, (part, peer) in enumerate(((low, right), (high, left))):
                copies[n].wait()
                local[n].wait()
                total = mine[n].astype(F32) + passed[n].astype(F32)
                relay[n] = total.astype(BF)
                copies.append(send(relay.at[n], got.at[n, part], base + 4 + n, peer))

        def finish():
            for copy in copies[2:]:
                copy.wait()
            local[2].wait()

        return pass_on, finish

    def start_second(job):
        number, _, _, (gone, axis, _), (got, _, _, _, own, total, ready, after, *_) = job
        total[...] = own[...].astype(F32) + got[0].astype(F32) + got[1].astype(F32)
        started = []
        for o in (2, 1, 3):
            ready[o - 1] = sub(total, gone, axis, lax.rem(here[axis] + o, 4)).astype(BF)
            started.append(
                send(ready.at[o - 1], after.at[o - 1], number * 12 + 5 + o, along(axis, o))
            )
        return started

    def sub(total, gone, axis, index):
        first = axis == min(a for a in range(3) if a != gone)
        return total[index] if first else total[:, index]

    def start_third(job, copies):
        number, _, _, (gone, middle, axis), (*_, total, _, after, small, last) = job
        for copy in copies:
            copy.wait()
        rows = sub(total, gone, middle, here[middle])
        for o in range(3):
            rows = rows + after[o].astype(F32)
        small[...] = rows.astype(BF)
        started = [
            send(
                small.at[lax.rem(here[axis] + o, 4)], last.at[o - 1], number * 12 + 8 + o,
                along(axis, o),
            )
            for o in (2, 1, 3)
        ]
        return started

    def end(job, copies):
        _, _, out, (_, _, axis), (*_, small, last) = job
        for copy in copies:
            copy.wait()
        rows = small[here[axis]].astype(F32)
        for o in range(3):
            rows = rows + last[o].astype(F32)
        out[:, : rows.shape[1]] = rows

    running = [start_first(job) for job in jobs]
    for pass_on, _ in running:
        pass_on()
    seconds = []
    for job, (_, finish) in zip(jobs, running):
        finish()
        seconds.append(start_second(job))
    running = seconds
    running = [start_third(job, copies) for job, copies in zip(jobs, running)]
    for job, copies in zip(jobs, running):
        end(job, copies)


def reduce_mixer(products):
    scratch = []
    for n in range(len(products)):
        width = PARTS[n % 3]
        scratch += [
            pltpu.VMEM((2, 4, 4, 24, width), BF),
            pltpu.VMEM((2, 2, 4, 24, width), BF),
            pltpu.VMEM((2, 2, 4, 24, width), BF),
            pltpu.VMEM((2, 2, 4, 24, width), BF),
            pltpu.VMEM((4, 4, 24, width), BF),
            pltpu.VMEM((4, 4, 24, width), F32),
            pltpu.VMEM((3, 4, 24, width), BF),
            pltpu.VMEM((3, 4, 24, width), BF),
            pltpu.VMEM((4, 24, width), BF),
            pltpu.VMEM((3, 24, width), BF),
        ]
    return pl.pallas_call(
        reduce_mixer_kernel,
        name="reduce_mixer_gradients",
        out_shape=jax.ShapeDtypeStruct((6, 24, PARTS[0]), F32),
        in_specs=[ANY] * 6,
        out_specs=VM,
        scratch_shapes=scratch
        + [
            pltpu.SemaphoreType.DMA((18,)),
            pltpu.SemaphoreType.DMA((72,)),
            pltpu.SemaphoreType.DMA((72,)),
        ],
        compiler_params=pltpu.CompilerParams(
            collective_id=2, has_side_effects=True, vmem_limit_bytes=48 << 20
        ),
    )(*products)


def columns(shape):
    return lax.broadcasted_iota(jnp.int32, shape, 1)


def rows_of(shape):
    return lax.broadcasted_iota(jnp.int32, shape, 0)


def plain(kernel, name, outs, flops=0, bytes_accessed=4000000, ins=None, scratch=()):
    def call(*args):
        return pl.pallas_call(
            kernel,
            name=name,
            out_shape=[jax.ShapeDtypeStruct(shape, kind) for shape, kind in outs],
            in_specs=ins or [VM] * len(args),
            out_specs=[VM] * len(outs),
            scratch_shapes=list(scratch),
            compiler_params=pltpu.CompilerParams(vmem_limit_bytes=VMEM),
            cost_estimate=pl.CostEstimate(
                flops=flops, bytes_accessed=bytes_accessed, transcendentals=0
            ),
        )(*args)

    return call


def tables_kernel(routes, *outs):
    wide = (T, 128)
    earlier = (rows_of(wide) < columns(wide)).astype(BF)
    same = (rows_of(wide) == columns(wide)).astype(BF)
    for level in range(LAYERS):
        named = jnp.zeros(wide, F32)
        for k in range(TOP):
            named = named + (routes[level, :, k : k + 1] == columns(wide)).astype(F32)
        outs[level][...] = named
        turned = dot(named.astype(BF), same, ((0,), (0,)))[:E]
        rank = dot(named.astype(BF), earlier, ((0,), (0,)))[:E]
        place = lax.broadcasted_iota(jnp.int32, (E, C, T), 1).astype(F32)
        hit = jnp.where(rank[:, None, :] == place, turned[:, None, :], 0.0)
        outs[LAYERS + level][...] = hit.reshape(SLOTS, T).astype(BF)


def route_tables(routes):
    return plain(
        tables_kernel, "route_tables",
        [((T, 128), F32)] * LAYERS + [((SLOTS, T), BF)] * LAYERS,
    )(routes)


def unit_rows(rows):
    scale = lax.rsqrt(jnp.mean(rows * rows, axis=-1, keepdims=True) + EPS)
    return rows * scale, scale


def gain_rows(router):
    pick = (columns((8, 128)) == E + rows_of((8, 128))) & (rows_of((8, 128)) < 2)
    return dot(pick.astype(BF), router, ((1,), (1,)))


def slot_columns():
    shape = (SLOTS, 128)
    start = columns(shape) * C
    return (rows_of(shape) >= start) & (rows_of(shape) < start + C)


def post_kernel(
    hidden, own, other, gains, routing, named, spread, middle_out, send_out, gates_out, slot_out
):
    middle = hidden[...].astype(F32) + own[...] + other[...].astype(F32)
    middle_out[...] = middle
    normed = (unit_rows(middle)[0] * gains[1:2]).astype(BF)
    send_out[:, :D] = dot(spread[...], normed).astype(BF)
    masked = jnp.where(named[...] > 0, routing[...], -1e30)
    terms = jnp.exp(masked - jnp.max(masked, axis=-1, keepdims=True))
    terms = jnp.where(named[...] > 0, terms, 0.0)
    gates = terms / jnp.sum(terms, axis=-1, keepdims=True)
    gates_out[...] = gates
    high, low = split_two(gates)
    all_gates = dot(spread[...], high) + dot(spread[...], low)
    slot = jnp.sum(jnp.where(slot_columns(), all_gates, 0.0), axis=-1, keepdims=True)
    slot_out[...] = slot
    if send_out.shape[1] > D:
        send_out[:, D:] = two_columns(slot)


def two_columns(value):
    high = value.astype(BF).astype(F32)
    column = columns((value.shape[0], WIDE - D))
    return jnp.where(column == 0, high, jnp.where(column == 1, value - high, 0.0)).astype(BF)


def post(width, *args):
    return plain(
        post_kernel, "dispatch_rows_of_tokens",
        [((T, D), F32), ((SLOTS, width), BF), ((T, 128), F32), ((SLOTS, 1), F32)], 2 * SLOTS * T * D,
    )(*args)


def combine_kernel(middle, routed, spread, slot, *refs):
    mix = spread[...].astype(F32) * slot[...]
    high, low = split_two(mix)
    rows = routed[...]
    hidden = middle[...] + dot(high, rows, ((0,), (0,))) + dot(low, rows, ((0,), (0,)))
    if len(refs) == 1:
        refs[0][...] = hidden
        return
    mixers, hidden_out, normed_out, gains_out, router, sem = refs
    copy = pltpu.make_async_copy(mixers.at[:, pl.ds(WR, COLS - WR)], router, sem)
    copy.start()
    hidden_out[...] = hidden
    copy.wait()
    gains = gain_rows(router[...])
    gains_out[...] = gains
    normed_out[...] = (unit_rows(hidden)[0] * gains[0:1]).astype(BF)


def combine(middle, routed, spread, slot):
    return plain(combine_kernel, "add_expert_outputs", [((T, D), F32)], 4 * SLOTS * T * D)(
        middle, routed, spread, slot
    )[0]


def combine_next(middle, routed, spread, slot, mixers):
    return plain(
        combine_kernel, "add_expert_outputs_and_norm",
        [((T, D), F32), ((T, D), BF), ((8, D), F32)], 4 * SLOTS * T * D,
        ins=[VM] * 4 + [ANY],
        scratch=[pltpu.VMEM((D, COLS - WR), BF), pltpu.SemaphoreType.DMA],
    )(middle, routed, spread, slot, mixers)


def back_through_norm(inputs, gain, grad_normed, grad_residual):
    unit, scale = unit_rows(inputs)
    grad_gain = jnp.sum(grad_normed * unit, axis=0, keepdims=True)
    grad_unit = grad_normed * gain
    back = grad_unit - unit * jnp.mean(grad_unit * unit, axis=-1, keepdims=True)
    return grad_residual + scale * back, grad_gain


def pre_back_kernel(
    dx, shares, middle, gains, grad, spread, gates, middle_out, out_out, routing_out, gain_out
):
    table = spread[...]
    if shares is None:
        share = dx[:, D : D + 1].astype(F32) + dx[:, D + 1 : D + 2].astype(F32)
    else:
        share = shares[...]
    high, low = split_two(jnp.where(slot_columns(), share, 0.0))
    dense = dot(table, high, ((0,), (0,))) + dot(table, low, ((0,), (0,)))
    routing = dense - gates[...] * jnp.sum(dense, axis=-1, keepdims=True)
    routing_out[...] = routing.astype(BF)
    grad_normed = dot(table, dx[:, :D], ((0,), (0,)))
    grad_middle, grad_gain = back_through_norm(
        middle[...], gains[1:2], grad_normed, grad[...].astype(F32)
    )
    middle_out[...] = grad_middle
    out_out[...] = grad_middle.astype(BF)
    gain_out[...] = grad_gain


def pre_back(dx, shares, *args):
    outs = [((T, D), F32), ((T, D), BF), ((T, 128), BF), ((1, D), F32)]
    if shares is None:
        return plain(
            lambda dx, *refs: pre_back_kernel(dx, None, *refs), "back_to_middle", outs,
            2 * SLOTS * T * D,
        )(dx, *args)
    return plain(pre_back_kernel, "back_to_middle", outs, 2 * SLOTS * T * D)(dx, shares, *args)


def post_back_kernel(own, other, hidden, gains, grad_middle, gain_two, *refs):
    grad_normed = own[...] + other[...].astype(F32)
    grad, gain_one = back_through_norm(
        hidden[...].astype(F32), gains[0:1], grad_normed, grad_middle[...]
    )
    if len(refs) == 2:
        grad_out, rows_out = refs
    else:
        spread, slot, routed, grad_out, rows_out, dy_out, share_out = refs
        high, low = split_two(grad)
        slots = dot(spread[...], high) + dot(spread[...], low)
        dy_out[...] = (slot[...] * slots).astype(BF)
        share = jnp.sum(routed[...].astype(F32) * slots, axis=-1, keepdims=True)
        share_out[...] = slot[...] * share
    grad_out[...] = grad
    rows_out[...] = jnp.zeros((16, D), BF)
    for n, gain in enumerate((gain_one, gain_two[...])):
        high, low = split_two(gain)
        rows_out[2 * n : 2 * n + 1] = high
        rows_out[2 * n + 1 : 2 * n + 2] = low


def post_back(*args):
    outs = [((T, D), F32), ((16, D), BF)]
    if len(args) > 6:
        outs += [((SLOTS, D), BF), ((SLOTS, 1), F32)]
    return plain(post_back_kernel, "back_to_hidden", outs, 4 * SLOTS * T * D)(*args)


def products_kernel(
    normed, grads_own, grads_other, heads, att, routing, gains,
    first_out, second_out, third_out, grads,
):
    step = pl.program_id(0)

    @pl.when(step == 0)
    def _():
        grads[:T] = grads_own[...]
        grads[T:] = grads_other[...]

    def product(left, right):
        return dot(left, right, ((0,), (0,)))

    def pair(ref, start, stop):
        return jnp.concatenate([ref[0, :, start:stop], ref[1, :, start:stop]], axis=0)

    block = pl.ds(pl.multiple_of(step * (D // 4), 128), D // 4)
    def store(out, value):
        out[0] = value.reshape(4, 4, 24, value.shape[1]).astype(BF)

    left, turned = normed[:, block], grads[:, block]
    number, column = rows_of((16, 128)), columns((16, 128))
    gain_place = ((number < 2) & (column == E)) | (
        (number >= 2) & (number < 4) & (column == E + 1)
    )
    store(first_out, product(left, pair(heads, 0, 768)))
    store(second_out, product(turned, pair(att, 0, 768)))
    third = [
        product(left, pair(heads, 768, WO)),
        product(left[:T], routing[...]) + product(gains[:, block], gain_place.astype(BF)),
    ]
    store(third_out, jnp.concatenate(third, axis=1))


def mixer_products(normed, grads_own, grads_other, heads, att, routing, gains):
    def whole(v):
        zeros = (0,) * len(v.shape)
        return pl.BlockSpec(v.shape, lambda i: zeros, pipeline_mode=pl.Buffered(1))

    args = [normed, grads_own, grads_other, heads, att, routing, gains]
    return pl.pallas_call(
        products_kernel,
        name="mixer_products",
        grid=(4,),
        out_shape=[jax.ShapeDtypeStruct((4, 4, 4, 24, width), BF) for width in PARTS],
        in_specs=[whole(v) for v in args],
        out_specs=[
            pl.BlockSpec((1, 4, 4, 24, width), lambda i: (i, 0, 0, 0, 0)) for width in PARTS
        ],
        scratch_shapes=[pltpu.VMEM((2 * T, D), BF)],
        compiler_params=pltpu.CompilerParams(vmem_limit_bytes=VMEM),
        cost_estimate=pl.CostEstimate(
            flops=2 * 2 * T * D * COLS, bytes_accessed=11000000, transcendentals=0
        ),
    )(*args)


def turn(rows, cosine, sine):
    return rows * cosine + pltpu.roll(rows, HD // 2, 1) * sine


def head_rows(ref, sequence, heads):
    return jnp.concatenate([ref[sequence, :, h * HD : (h + 1) * HD] for h in heads], axis=0)


def weigh(queries, keys, mask):
    raw = dot(queries, keys, ((1,), (1,))).reshape(6, T, T)
    logits = jnp.where(mask[None] > 0, raw * SCALE, -1e30)
    terms = jnp.exp(logits - jnp.max(logits, axis=-1, keepdims=True))
    return (terms / jnp.sum(terms, axis=-1, keepdims=True)).reshape(6 * T, T)


PIECES = (pl.ds(WR, COLS - WR), pl.ds(0, WO), pl.ds(WO, WR - WO))


class Several:
    def __init__(self, copies):
        self.copies = copies
        for copy in copies:
            copy.start()

    def wait(self):
        for copy in self.copies:
            copy.wait()


def fetch_weights(mixers, weights, sem):
    groups = []
    for n, place in enumerate(PIECES):
        rows = [pl.ds(i * (D // 4), D // 4) for i in range(4)]
        groups.append(
            Several(
                [
                    pltpu.make_async_copy(
                        mixers.at[r, place], weights.at[r, place], sem.at[n * 4 + i]
                    )
                    for i, r in enumerate(rows)
                ]
            )
        )
    return groups


def attend_kernel(first, own, other, mixers, cosine, sine, mask, *refs):
    *refs, weights, sem = refs
    both, heads_out, att_out, own_out, other_out, routing_out = refs[:6]
    copies = fetch_weights(mixers, weights, sem)
    if first:
        units = [unit_rows(v[...].astype(F32))[0] for v in (own, other)]
        copies[0].wait()
        gains = gain_rows(weights[:, WR:])
        refs[6][...] = gains
        both[:T] = (units[0] * gains[0:1]).astype(BF)
        both[T:] = (units[1] * gains[0:1]).astype(BF)
    else:
        both[:T] = own[...]
        both[T:] = other[...]
        copies[0].wait()
    turns = [jnp.concatenate([t[...], t[...]], axis=0) for t in (cosine, sine)]
    copies[1].wait()
    for tile in range(4):
        wide = dot(both[...], weights[:, tile * 256 : (tile + 1) * 256])
        for part in range(2):
            head = tile * 2 + part
            rows = wide[:, part * HD : (part + 1) * HD]
            if head < 7:
                rows = turn(rows, *turns)
            rows = rows.astype(BF)
            for s in range(2):
                heads_out[s, :, head * HD : (head + 1) * HD] = rows[s * T : (s + 1) * T]
    for s in range(2):
        probs = weigh(head_rows(heads_out, s, range(6)), heads_out[s, :, 768:896], mask[s])
        mixed = dot(probs.astype(BF), heads_out[s, :, 896:]).astype(BF)
        for h in range(6):
            att_out[s, :, h * HD : (h + 1) * HD] = mixed[h * T : (h + 1) * T]
    copies[2].wait()
    att = att_out[...].reshape(2 * T, 768)
    for tile in range(6):
        place = slice(tile * 256, (tile + 1) * 256)
        rows = dot(att, weights[place, WO:WR], ((1,), (1,)))
        own_out[:, place] = rows[:T]
        other_out[:, place] = rows[T:].astype(BF)
    routing_out[...] = dot(both[:T], weights[:, WR:])


def attend(first, own, other, mixers, cosine, sine, mask):
    outs = [
        ((2 * T, D), BF), ((2, T, WO), BF), ((2, T, WR - WO), BF), ((T, D), F32), ((T, D), BF),
        ((T, 128), F32),
    ]
    return plain(
        lambda *refs: attend_kernel(first, *refs), "attention_forward",
        outs + [((8, D), F32)] * first, 1700000000, 9000000,
        ins=[VM, VM, ANY, VM, VM, VM],
        scratch=[pltpu.VMEM((D, COLS), BF), pltpu.SemaphoreType.DMA((12,))],
    )(own, other, mixers, cosine, sine, mask)


def attend_back_kernel(
    own, other, routing, mixers, heads, cosine, sine, mask,
    grad_heads, own_out, other_out, both, grad_att, weights, sem,
):
    copies = fetch_weights(mixers, weights, sem)
    both[:T] = own[...]
    both[T:] = other[...]
    copies[2].wait()
    for tile in range(3):
        place = slice(tile * 256, (tile + 1) * 256)
        wide = dot(both[...], weights[:, WO + tile * 256 : WO + (tile + 1) * 256]).astype(BF)
        for s in range(2):
            grad_att[s, :, place] = wide[s * T : (s + 1) * T]
    cos, sin = cosine[...], -sine[...]
    for s in range(2):
        queries, grads = head_rows(heads, s, range(6)), head_rows(grad_att, s, range(6))
        keys, values = heads[s, :, 768:896], heads[s, :, 896:]
        probs = weigh(queries, keys, mask[s])
        dp = dot(grads, values, ((1,), (1,)))
        draw = probs * (dp - jnp.sum(probs * dp, axis=-1, keepdims=True))
        draw = (draw * SCALE).astype(BF)
        dq = dot(draw, keys)
        for h in range(6):
            rows = turn(dq[h * T : (h + 1) * T], cos, sin)
            grad_heads[s, :, h * HD : (h + 1) * HD] = rows.astype(BF)
        dk = dot(draw, queries, ((0,), (0,)))
        grad_heads[s, :, 768:896] = turn(dk, cos, sin).astype(BF)
        grad_heads[s, :, 896:] = dot(probs.astype(BF), grads, ((0,), (0,))).astype(BF)
    copies[0].wait()
    copies[1].wait()
    wide = grad_heads[...].reshape(2 * T, 1024)
    for tile in range(6):
        place = slice(tile * 256, (tile + 1) * 256)
        rows = dot(wide, weights[place, :WO], ((1,), (1,)))
        own_out[:, place] = rows[:T] + dot(routing[...], weights[place, WR:], ((1,), (1,)))
        other_out[:, place] = rows[T:].astype(BF)


def attend_back(own, other, routing, mixers, heads, cosine, sine, mask):
    return pl.pallas_call(
        attend_back_kernel,
        name="attention_backward",
        out_shape=(
            jax.ShapeDtypeStruct((2, T, 1024), BF),
            jax.ShapeDtypeStruct((T, D), F32),
            jax.ShapeDtypeStruct((T, D), BF),
        ),
        in_specs=[VM, VM, VM, ANY, VM, VM, VM, VM],
        out_specs=[VM] * 3,
        scratch_shapes=[
            pltpu.VMEM((2 * T, D), BF),
            pltpu.VMEM((2, T, 768), BF),
            pltpu.VMEM((D, COLS), BF),
            pltpu.SemaphoreType.DMA((12,)),
        ],
        compiler_params=pltpu.CompilerParams(vmem_limit_bytes=VMEM),
        cost_estimate=pl.CostEstimate(flops=2200000000, bytes_accessed=9000000, transcendentals=200000),
    )(own, other, routing, mixers, heads, cosine, sine, mask)

class Exchange:
    def __init__(self, rows, held, result, back, sems, also=()):
        (self.x, self.z, self.y, self.core), self.along = neighbours()
        self.rows, self.held, self.result, self.back = rows, held, result, back
        self.sems, self.local = sems[:4], sems[4]
        self.me = self.index(self.z, self.y, self.core)
        greet([self.peer(k, 1) for k in range(1, E)] + [self.along(0, o) for o in also])

    def index(self, z, y, core):
        return (z * 4 + y) * 2 + core

    def peer(self, k, sign):
        a, b, c = k // 8, k // 2 % 4, k % 2
        return (
            self.x,
            lax.rem(self.z + (a * sign) % 4, 4),
            lax.rem(self.y + (b * sign) % 4, 4),
            lax.rem(self.core + c, 2),
        )

    def copy(self, k, returning):
        peer = self.peer(k, -1 if returning else 1)
        there = self.index(*peer[1:])
        source, target = (self.result, self.back) if returning else (self.rows, self.held)
        sems = self.sems[2:] if returning else self.sems[:2]
        return pltpu.make_async_remote_copy(
            source.at[there], target.at[self.me], sems[0].at[k], sems[1].at[k],
            device_id=peer, device_id_type=MESH,
        )

    def start(self):
        for pair in ((2, 0), (1, 3)):
            for n in range(8):
                for a in pair:
                    if a * 8 + n:
                        self.copy(a * 8 + n, False).start()
        self.own = pltpu.make_async_copy(
            self.rows.at[self.me], self.held.at[self.me], self.local.at[0]
        )
        self.own.start()

    def arrive(self, a):
        for k in range(a * 8, a * 8 + 8):
            if k:
                self.copy(k, False).wait_recv()
        if a == 0:
            self.own.wait()
        block = lax.rem(self.z + (-a) % 4, 4)
        rows = self.held[pl.ds(block * 8, 8)].astype(F32)
        return block, rows.reshape(8 * C, rows.shape[2]).astype(BF)

    def give(self, a, block, value):
        width = value.shape[1]
        self.result[pl.ds(block * 8, 8), :, :width] = value.reshape(8, C, width).astype(BF)

    def send_back(self, a):
        for k in range(a * 8, a * 8 + 8):
            if k:
                self.copy(k, True).start()
        if a == 0:
            self.last = pltpu.make_async_copy(
                self.result.at[self.me], self.back.at[self.me], self.local.at[1]
            )
            self.last.start()

    def finish(self):
        for k in range(1, E):
            self.copy(k, False).wait_send()
            self.copy(k, True).wait()
        self.last.wait()


GROUPS = (0, 2, 1, 3)


def start_weights(pieces, weights, sem):
    waits, matrix = [], 0
    for piece in pieces:
        count, several = piece.shape[:2]
        for m in range(several):
            copies = []
            for n in range(4):
                source = piece.at[n, m] if count == 4 else piece.at[0, m, pl.ds(n * 384, 384)]
                copies.append(
                    pltpu.make_async_copy(
                        source, weights.at[matrix, n], sem.at[matrix * 4 + n]
                    )
                )
                copies[n].start()
            waits.append(copies)
            matrix += 1

    def ready(m):
        for copy in waits[m]:
            copy.wait()

    return ready


def matrix_of(weights, m):
    return weights[m].reshape(D, FF)


def at_block(block):
    return pl.ds(pl.multiple_of(block * 8 * C, 8 * C), 8 * C)


def forward_phase_kernel(
    rows, gate_up, downs, ups, back, flat_out, a_out, b_out, down_out, next_out,
    held, result, weights, weight_sem, ring_send, ring_recv, *sems,
):
    work = Exchange(rows, held, result, back, sems, (1, 3))
    work.start()
    send = sender(ring_send, ring_recv)
    x, local = work.x, work.local
    own = [
        pltpu.make_async_copy(downs.at[0, 0], weights.at[2, x], local.at[2]),
        pltpu.make_async_copy(ups.at[1, 0], next_out.at[0, x], local.at[3]),
        pltpu.make_async_copy(downs.at[1, 0], next_out.at[1, x], local.at[4]),
    ]
    for copy in own:
        copy.start()
    ring = ring_of(downs.at[0, 0], weights.at[2], x, work.along, send, 0)
    others = [
        ring_of(ups.at[1, 0], next_out.at[0], x, work.along, send, 6),
        ring_of(downs.at[1, 0], next_out.at[1], x, work.along, send, 12),
    ]
    ready = start_weights([gate_up], weights, weight_sem)
    ring[0]()
    for number, group in enumerate(GROUPS):
        block, got = work.arrive(group)
        place = at_block(block)
        flat_out[place] = got
        if number == 0:
            ready(0)
        a = dot(got, matrix_of(weights, 0))
        if number == 0:
            ready(1)
        b = dot(got, matrix_of(weights, 1))
        a_out[place] = a
        b_out[place] = b
        inner = (a * jax.nn.sigmoid(a) * b).astype(BF)
        if number == 0:
            ring[1]()
            own[0].wait()
        work.give(group, block, dot(inner, matrix_of(weights, 2), ((1,), (1,))))
        work.send_back(group)
    kept = pltpu.make_async_copy(weights.at[2], down_out.at[0], local.at[2])
    kept.start()
    others[0][0]()
    others[1][0]()
    for other, copy in zip(others, own[1:]):
        other[1]()
        copy.wait()
    work.finish()
    kept.wait()


def inner_gradients(a, b, dy, weights, place, held):
    du = dot(dy, matrix_of(weights, 2))
    sig = jax.nn.sigmoid(a)
    act = a * sig
    inner = (act * b).astype(BF)
    da = (du * b * sig * (1.0 + a * (1.0 - sig))).astype(BF)
    db = (du * act).astype(BF)
    for ref, value in zip(held, (da, db, inner)):
        ref[place] = value
    dx = dot(da, matrix_of(weights, 0), ((1,), (1,)))
    return inner, dx + dot(db, matrix_of(weights, 1), ((1,), (1,)))


def weight_gradients(rows, dy, held, outs):
    @pl.loop(0, 4)
    def _(n):
        columns = pl.ds(pl.multiple_of(n * 384, 128), 384)
        place = pl.ds(pl.multiple_of(n * 384, 128), 384)
        for left, right, out in zip((rows, rows, dy), held, outs):
            out[place] = dot(left[:, columns], right[...], ((0,), (0,))).astype(BF)


def back_phase_kernel(
    rows, a_in, b_in, flat_in, gate_up, down, back, gate_out, up_out, down_out,
    held, result, weights, a, b, flat, dy, da, db, inner, weight_sem, load_sem, *sems,
):
    work = Exchange(rows, held, result, back, sems)
    work.start()
    ready = start_weights([gate_up, down], weights, weight_sem)
    loads = []
    for n, (src, dst) in enumerate(((a_in, a), (b_in, b), (flat_in, flat))):
        loads.append(pltpu.make_async_copy(src, dst, load_sem.at[n]))
        loads[n].start()
    for number, group in enumerate(GROUPS):
        block, got = work.arrive(group)
        place = at_block(block)
        dy[place] = got
        if number == 0:
            loads[0].wait()
            loads[1].wait()
            for m in range(3):
                ready(m)
        _, dx = inner_gradients(a[place], b[place], got, weights, place, (da, db, inner))
        work.give(group, block, dx)
        work.send_back(group)
    loads[2].wait()
    weight_gradients(flat, dy, (da, db, inner), (gate_out, up_out, down_out))
    work.finish()


def both_phase_kernel(
    rows, target_low, target_high, gate_up, down, back, y_out, gate_out, up_out, down_out,
    held, result, weights, low, high, flat, dy, da, db, inner, weight_sem, load_sem, *sems,
):
    work = Exchange(rows, held, result, back, sems)
    work.start()
    ready = start_weights([gate_up, down], weights, weight_sem)
    loads = []
    for n, (src, dst) in enumerate(((target_low, low), (target_high, high))):
        loads.append(pltpu.make_async_copy(src, dst, load_sem.at[n]))
        loads[n].start()
    for number, group in enumerate(GROUPS):
        block, got = work.arrive(group)
        place = at_block(block)
        normed = got[:, :D]
        flat[place] = normed
        gate = got[:, D : D + 1].astype(F32) + got[:, D + 1 : D + 2].astype(F32)
        if number == 0:
            loads[0].wait()
            loads[1].wait()
            for m in range(3):
                ready(m)
        target = jnp.concatenate([low[place], high[place]], axis=1)
        grads = (gate * target.astype(F32)).astype(BF)
        dy[place] = grads
        a = dot(normed, matrix_of(weights, 0))
        b = dot(normed, matrix_of(weights, 1))
        mixed, dx = inner_gradients(a, b, grads, weights, place, (da, db, inner))
        y = dot(mixed, matrix_of(weights, 2), ((1,), (1,))).astype(BF)
        y_out[place] = y
        share = jnp.sum(y.astype(F32) * grads.astype(F32), axis=-1, keepdims=True)
        parts = two_columns(share).astype(F32)
        work.give(group, block, jnp.concatenate([dx, parts], axis=1))
        work.send_back(group)
    weight_gradients(flat, dy, (da, db, inner), (gate_out, up_out, down_out))
    work.finish()


def phase_call(kernel, name, number, args, outs, scratch, width, flops):
    slots = (E, C, width)
    return pl.pallas_call(
        kernel,
        name=name,
        out_shape=[jax.ShapeDtypeStruct(slots, BF)]
        + [jax.ShapeDtypeStruct(shape, kind) for shape, kind, _ in outs],
        in_specs=[ANY] * len(args),
        out_specs=[ANY] + [spec for *_, spec in outs],
        scratch_shapes=[
            pltpu.VMEM(slots, BF), pltpu.VMEM(slots, BF), pltpu.VMEM((3, 4, D // 4, FF), BF)
        ]
        + scratch
        + [pltpu.SemaphoreType.DMA((E,))] * 4
        + [pltpu.SemaphoreType.DMA((5,))],
        compiler_params=pltpu.CompilerParams(
            collective_id=number, has_side_effects=True, vmem_limit_bytes=52 << 20
        ),
        cost_estimate=pl.CostEstimate(
            flops=flops, bytes_accessed=20000000, transcendentals=SLOTS * FF
        ),
    )(*args)


UNIT = 2 * SLOTS * D * FF
GRADS = [((D, FF), BF, VM)] * 3


def forward_phase(rows, gate_up, downs, ups):
    shard = (1, 4, D // 4, FF)
    back, flat, a, b, down, after = phase_call(
        forward_phase_kernel, "expert_phase_forward", 3, (rows.reshape(E, C, D), gate_up, downs, ups),
        [((SLOTS, D), BF, VM), ((SLOTS, FF), F32, VM), ((SLOTS, FF), F32, VM), (shard, BF, ANY),
         ((2, 4, D // 4, FF), BF, ANY)],
        [pltpu.SemaphoreType.DMA((8,)), pltpu.SemaphoreType.DMA((18,)),
         pltpu.SemaphoreType.DMA((18,))],
        D, 3 * UNIT,
    )
    down, after = down.reshape(1, 1, D, FF), after.reshape(1, 2, D, FF)
    return back.reshape(SLOTS, D), flat, a, b, down, after


def matrices(*widths):
    return [pltpu.VMEM((SLOTS, width), BF) for width in widths]


def back_phase(rows, a, b, flat, gate_up, down):
    back, *grads = phase_call(
        back_phase_kernel, "expert_phase_backward", 5,
        (rows.reshape(E, C, D), a, b, flat, gate_up, down), GRADS,
        [pltpu.VMEM((SLOTS, FF), F32)] * 2 + matrices(D, D, FF, FF, FF)
        + [pltpu.SemaphoreType.DMA((12,)), pltpu.SemaphoreType.DMA((3,))],
        D, 6 * UNIT,
    )
    return back.reshape(SLOTS, D), grads


def both_phase(rows, targets, gate_up, down):
    back, y, *grads = phase_call(
        both_phase_kernel, "expert_phase_both", 4,
        (rows.reshape(E, C, WIDE), *targets, gate_up, down), [((SLOTS, D), BF, VM)] + GRADS,
        matrices(FF, FF, D, D, FF, FF, FF)
        + [pltpu.SemaphoreType.DMA((12,)), pltpu.SemaphoreType.DMA((2,))],
        WIDE, 9 * UNIT,
    )
    return back.reshape(SLOTS, WIDE), y, grads


def exchange(rows):
    width = rows.shape[1]
    rows = rows.reshape(E, C, width)
    rows = lax.all_to_all(rows, GROUP, split_axis=0, concat_axis=0, tiled=True)
    return rows.reshape(SLOTS, width)


def outputs_kernel(core, mine, theirs, *outs):
    for level in range(LAYERS):
        level_outputs(level, core[0] == 0, mine, theirs, *outs)


def level_outputs(level, first, mine, theirs, q_out, k_out, v_out, o_out, routing_out):

    def rows(ref, group):
        group = level * 3 + group
        return jnp.where(first, ref[group, :12], ref[group, 12:])

    halves = []
    for ref in (mine, theirs):
        a, b, c = (rows(ref, group) for group in range(3))
        halves.append(
            (
                a, c[:, :HD], c[:, HD : 2 * HD], b, c[:, 2 * HD : 3 * HD],
            )
        )
    for out, own, other in zip((q_out, k_out, v_out, o_out), *halves):
        width = own.shape[1]
        out[:, level, :width] = jnp.where(first, own, other)
        out[:, level, width:] = jnp.where(first, other, own)
    routing_out[:, level, :] = halves[0][4] + halves[1][4]


def mixer_outputs(sums, core):
    widths = (D, 2 * HD, 2 * HD, D, HD)
    *outs, routing = pl.pallas_call(
        outputs_kernel,
        name="mixer_outputs",
        out_shape=[jax.ShapeDtypeStruct((12, LAYERS, width), F32) for width in widths],
        grid=(1,),
        in_specs=[pl.BlockSpec(memory_space=pltpu.SMEM)]
        + [pl.BlockSpec((6, 24, PARTS[0]), lambda i: (0, 0, 0))] * 2,
        out_specs=[pl.BlockSpec((12, LAYERS, width), lambda i: (0, 0, 0)) for width in widths],
    )(core.reshape(1), sums, swap(sums))
    *outs, routing = [v.transpose(1, 0, 2) for v in (*outs, routing)]
    return (*outs, routing[:, :, :E], routing[:, :, E], routing[:, :, E + 1])


def expert_outputs_kernel(*refs):
    for matrix in range(3):
        for level in range(LAYERS):
            refs[6 + matrix][level, 0] = refs[level * 3 + matrix][...].astype(F32)


def expert_outputs(sums):
    rows = 96
    return pl.pallas_call(
        expert_outputs_kernel,
        name="expert_outputs",
        grid=(D // 4 // rows,),
        out_shape=[jax.ShapeDtypeStruct((LAYERS, 1, D // 4, FF), F32)] * 3,
        in_specs=[pl.BlockSpec((rows, FF), lambda i: (i, 0))] * 6,
        out_specs=[pl.BlockSpec((LAYERS, 1, rows, FF), lambda i: (0, 0, i, 0))] * 3,
        compiler_params=pltpu.CompilerParams(vmem_limit_bytes=VMEM),
        cost_estimate=pl.CostEstimate(flops=0, bytes_accessed=11000000, transcendentals=0),
    )(*sums)


def reduce_expert(grads):
    return [
        lax.psum_scatter(g, "dp", scatter_dimension=0, tiled=True) for g in grads
    ]


def per_device(
    tokens, segments, route_ids, w_query, key_projection, value_projection, w_out, w_router,
    gain_attn, gain_moe, w_gate, w_up, w_down, cotangent,
):
    core = lax.axis_index("core")
    cosine, sine = rope_tables()
    position = jnp.arange(T)

    shared = jnp.concatenate(
        [
            w_router, gain_attn[:, :, None], gain_moe[:, :, None],
            jnp.zeros((LAYERS, 12, COLS - WR - E - 2), BF),
        ],
        axis=2,
    )

    def half(number):
        def cut(v):
            width = v.shape[2] // 2
            return v[:, :, number * width : (number + 1) * width]

        return jnp.concatenate(
            [cut(v) for v in (w_query, key_projection, value_projection, w_out)] + [shared], axis=2
        )

    halves = (half(0), half(1))
    mine = jnp.where(core == 0, halves[0], halves[1])
    theirs = swap(jnp.where(core == 0, halves[1], halves[0]))
    blocks = jnp.where(
        core == 0,
        jnp.concatenate([mine, theirs], axis=1),
        jnp.concatenate([theirs, mine], axis=1),
    )
    segment = segments.astype(F32)
    segment = jnp.concatenate([segment, swap(segment)])
    mask = (position[:, None] >= position[None, :])[None] & (
        segment[:, :, None] == segment[:, None, :]
    )
    mask = mask.astype(F32)

    *named, spread0, spread1 = route_tables(route_ids)
    spread = (spread0, spread1)
    targets = [
        dot(spread[1], cotangent[:, half * 768 : (half + 1) * 768]).astype(BF) for half in range(2)
    ]
    tokens_other = swap(tokens)
    first_mixer, first_experts = gather(blocks, w_gate, w_up)
    second = lax.optimization_barrier((blocks[1], w_gate[1, 0], first_experts))
    second_mixer = lax.all_gather(second[0], AXES[:3], axis=0).reshape(D, COLS)
    second_experts = lax.all_gather(second[1], "dp", axis=0)

    targets[0], tokens_other, _ = lax.optimization_barrier((targets[0], tokens_other, first_mixer))
    targets[0] = exchange(targets[0])
    normed0, heads0, att0, own, other, routing, gains0 = attend(
        True, tokens, tokens_other, first_mixer, cosine, sine, mask
    )
    middle0, send, gates0, slot0 = post(
        D, tokens, own, swap(other), gains0, routing, named[0], spread[0]
    )
    send, targets[0] = lax.optimization_barrier((send, targets[0]))
    routed0, rows0, a0, b0, down0, up_down1 = forward_phase(
        send, first_experts, w_down, w_up
    )
    routed0, targets[1] = lax.optimization_barrier((routed0, targets[1]))
    targets[1] = exchange(targets[1])
    hidden, normed, gains1 = combine_next(middle0, routed0, spread[0], slot0, second_mixer)

    normed1, heads1, att1, own, other, routing = attend(
        False, normed, swap(normed), second_mixer, cosine, sine, mask
    )
    middle1, send, gates1, slot1 = post(
        WIDE, hidden, own, swap(other), gains1, routing, named[1], spread[1]
    )
    gate1 = second_experts.reshape(4, 1, D // 4, FF)
    dx, produced, parts1 = both_phase(send, targets, gate1, up_down1)
    sums1 = reduce_expert(parts1)
    routed1 = exchange(produced)

    grad_middle, grad_out, grad_routing, gain_two = pre_back(
        dx, None, middle1, gains1, cotangent, spread[1], gates1
    )
    grad_out_other = swap(grad_out)
    grad_heads, own, other = attend_back(
        grad_out, grad_out_other, grad_routing, second_mixer, heads1, cosine, sine, mask
    )
    grad, gain_parts, dy, shares = post_back(
        own, swap(other), hidden, gains1, grad_middle, gain_two, spread[0], slot0, routed0
    )
    products1 = mixer_products(
        normed1, grad_out, grad_out_other, grad_heads, att1, grad_routing, gain_parts
    )
    dx, parts0 = back_phase(dy, a0, b0, rows0, first_experts, down0)
    sums0 = reduce_expert(parts0)
    dx, sums1, products1 = lax.optimization_barrier((dx, sums1, products1))

    grad_middle, grad_out, grad_routing, gain_two = pre_back(
        dx, shares, middle0, gains0, grad, spread[0], gates0
    )
    grad_out_other = swap(grad_out)
    grad_heads, own, other = attend_back(
        grad_out, grad_out_other, grad_routing, first_mixer, heads0, cosine, sine, mask
    )
    routed1 = lax.optimization_barrier((routed1, grad_heads))[0]
    output = combine(middle1, routed1, spread[1], slot1)
    grad_tokens, gain_parts = post_back(
        own, swap(other), tokens, gains0, grad_middle, gain_two
    )
    products0 = mixer_products(
        normed0, grad_out, grad_out_other, grad_heads, att0, grad_routing, gain_parts
    )
    mixer_out = mixer_outputs(reduce_mixer(products0 + products1), core)
    expert_out = expert_outputs([*sums0, *sums1])
    return (output, grad_tokens, *mixer_out, *expert_out)


def solution(mesh):
    mesh = Mesh(mesh.devices.reshape(4, 4, 4, 2), AXES)
    rows = P(AXES, None)
    mixer = P(None, AXES, None)
    gain = P(None, AXES)
    expert = P(None, GROUP, "dp", None)
    return jax.shard_map(
        per_device,
        mesh=mesh,
        in_specs=(
            rows, rows, mixer, mixer, mixer, mixer, mixer, mixer, gain, gain, expert, expert,
            expert, rows,
        ),
        out_specs=(
            rows, rows, mixer, mixer, mixer, mixer, mixer, gain, gain, expert, expert, expert,
        ),
        check_vma=False,
    )
```

```python
import math

import jax
import jax.numpy as jnp
import numpy as np
from jax import lax
from jax.experimental import pallas as pl
from jax.experimental.pallas import tpu as pltpu
from jax.sharding import Mesh, PartitionSpec as P

MESH = pl.DeviceIdType.MESH
BF = jnp.bfloat16
F32 = jnp.float32
HEADS, KV, HD, TOP, LAYERS = 12, 2, 128, 4, 2
T, D, FF, E, C = 128, 1536, 768, 32, 24
SLOTS = E * C
THETA, EPS = 1000000.0, 1e-06
SCALE = 1.0 / math.sqrt(HD)
ANY = pl.BlockSpec(memory_space=pl.ANY)
VM = pl.BlockSpec(memory_space=pltpu.VMEM)
WO, WR, COLS = 1024, 1792, 1920
CUTS = (pl.ds(0, 1024), pl.ds(1024, COLS - 1024))
PARTS = (768, 768, 384)
VMEM = 32 << 20
WIDE = D + 128
AXES = ("dp", "z", "y", "core")
GROUP = AXES[1:]


def dot(a, b, dims=((1,), (0,))):
    return lax.dot_general(a, b, (dims, ((), ())), preferred_element_type=F32)


def split_two(v):
    high = v.astype(BF)
    return high, (v - high.astype(F32)).astype(BF)


def rope_tables():
    frequency = np.exp(-(2.0 * np.arange(HD // 2) / HD) * math.log(THETA)).astype(np.float32)
    angles = np.arange(T, dtype=np.float32)[:, None] * frequency[None, :]
    cosine, sine = np.cos(angles), np.sin(angles)
    return (
        jnp.asarray(np.concatenate([cosine, cosine], 1), F32),
        jnp.asarray(np.concatenate([-sine, sine], 1), F32),
    )


def swap(v):
    return lax.ppermute(v, "core", [(0, 1), (1, 0)])


def neighbours():
    here = [lax.axis_index(axis) for axis in AXES]

    def along(axis, places):
        peer = list(here)
        peer[axis] = lax.rem(here[axis] + places, 4)
        return tuple(peer)

    return here, along


def greet(peers):
    barrier = pltpu.get_barrier_semaphore()
    for peer in peers:
        pl.semaphore_signal(barrier, inc=1, device_id=peer, device_id_type=MESH)
    pl.semaphore_wait(barrier, len(peers))


def sender(send_sem, recv_sem):
    def send(src, dst, number, peer):
        copy = pltpu.make_async_remote_copy(
            src, dst, send_sem.at[number], recv_sem.at[number], device_id=peer, device_id_type=MESH
        )
        copy.start()
        return copy

    return send


def ring_steps(own, view, me, right, left, send, number):
    first = [
        send(own(0), view(me, 0), number, right), send(own(1), view(me, 1), number + 1, left)
    ]
    second = [
        send(own(1), view(me, 1), number + 2, right), send(own(0), view(me, 0), number + 3, left)
    ]

    relays = []

    def relay():
        before, after = lax.rem(me + 3, 4), lax.rem(me + 1, 4)
        first[0].wait_recv()
        relays.append(send(view(before, 0), view(before, 0), number + 4, right))
        first[1].wait_recv()
        relays.append(send(view(after, 1), view(after, 1), number + 5, left))

    def finish():
        for copy in second:
            copy.wait_recv()
        for copy in first + second:
            copy.wait_send()
        for copy in relays:
            copy.wait()

    return relay, finish


def ring_of(shard, out, x, along, send, number):
    return ring_steps(
        lambda half: shard.at[pl.ds(half * 192, 192)],
        lambda place, half: out.at[place, pl.ds(half * 192, 192)],
        x, along(0, 1), along(0, 3), send, number,
    )


def gather_kernel(blocks, gate, up, out, experts, local_sem, send_sem, recv_sem):
    (x, z, y, _), along = neighbours()
    greet([along(axis, o) for o in (1, 2, 3) for axis in range(3)])
    send = sender(send_sem, recv_sem)
    block = blocks.at[0]
    copies = [send(block, out.at[x, z, y], o - 1, along(0, o)) for o in (1, 3, 2)]
    shards = [gate.at[0, 0], up.at[0, 0]]
    rings = [
        ring_of(shard, experts.at[n], x, along, send, 27 + 6 * n) for n, shard in enumerate(shards)
    ]
    own = pltpu.make_async_copy(block, out.at[x, z, y], local_sem.at[0])
    own.start()
    own_experts = [
        pltpu.make_async_copy(shard, experts.at[n, x], local_sem.at[1 + n])
        for n, shard in enumerate(shards)
    ]
    for copy in own_experts:
        copy.start()
    own.wait()
    for copy in copies:
        copy.wait()

    def ring(view, axis, me, number):
        return ring_steps(
            lambda half: view(me, half), view, me, along(axis, 1), along(axis, 3), send, number
        )

    def pair(half):
        return pl.ds(half * 2, 2)

    first = ring(lambda n, half: out.at[pair(half), n, y, :, CUTS[0]], 1, z, 3)
    second = ring(lambda n, half: out.at[pair(half), z, n, :, CUTS[1]], 2, y, 9)
    first[0]()
    second[0]()
    first[1]()
    first = ring(lambda n, half: out.at[pair(half), :, n, :, CUTS[0]], 2, y, 15)
    second[1]()
    second = ring(lambda n, half: out.at[pair(half), n, :, :, CUTS[1]], 1, z, 21)
    rings[0][0]()
    first[0]()
    second[0]()
    rings[1][0]()
    first[1]()
    second[1]()
    for ring in rings:
        ring[1]()
    for copy in own_experts:
        copy.wait()


def gather(blocks, gate, up):
    mixer, experts = pl.pallas_call(
        gather_kernel,
        name="gather_weights",
        out_shape=(
            jax.ShapeDtypeStruct((4, 4, 4, 24, COLS), BF),
            jax.ShapeDtypeStruct((2, 4, D // 4, FF), BF),
        ),
        in_specs=[ANY] * 3,
        out_specs=(ANY, ANY),
        scratch_shapes=[
            pltpu.SemaphoreType.DMA((3,)),
            pltpu.SemaphoreType.DMA((39,)),
            pltpu.SemaphoreType.DMA((39,)),
        ],
        compiler_params=pltpu.CompilerParams(
            collective_id=1, has_side_effects=True, vmem_limit_bytes=VMEM
        ),
    )(blocks, gate, up)
    return mixer.reshape(D, COLS), experts.reshape(1, 2, D, FF)


def reduce_mixer_kernel(*refs):
    sources, out, scratch = refs[:6], refs[6], refs[7:]
    (x, z, y, _), along = neighbours()
    local_sem, send_sem, recv_sem = scratch[-3:]
    greet([along(axis, o) for o in (1, 2, 3) for axis in range(3)])
    send = sender(send_sem, recv_sem)
    here = (x, z, y)
    ways = ((1, 0, 2), (2, 1, 0), (0, 2, 1))
    jobs = []
    for level in reversed(range(LAYERS)):
        for group, way in enumerate(ways):
            number = level * 3 + group
            held = scratch[number * 10 : number * 10 + 10]
            jobs.append((number, sources[number], out.at[number], way, held))

    def pick(ref, dim, index, half=None):
        place = [slice(None)] * 3
        place[dim] = index
        if half is not None:
            place[1 if dim == 0 else 0] = half
        return ref.at[tuple(place)]

    def start_first(job):
        number, source, _, (axis, *_), (got, passed, relay, mine, own, *_) = job
        me = here[axis]
        right, left = along(axis, 1), along(axis, 3)
        after, far, before = (lax.rem(me + o, 4) for o in (1, 2, 3))
        low, high = pl.ds(0, 2), pl.ds(2, 2)
        base = number * 12
        copies = [
            send(pick(source, axis, far, low), passed.at[0], base, right),
            send(pick(source, axis, far, high), passed.at[1], base + 1, left),
            send(pick(source, axis, after, high), got.at[0, high], base + 2, right),
            send(pick(source, axis, before, low), got.at[1, low], base + 3, left),
        ]
        local = []
        for n, (src, dst) in enumerate(
            (
                (pick(source, axis, after, low), mine.at[0]),
                (pick(source, axis, before, high), mine.at[1]),
                (pick(source, axis, me), own),
            )
        ):
            local.append(pltpu.make_async_copy(src, dst, local_sem.at[number * 3 + n]))
            local[n].start()

        def pass_on():
            for n, (part, peer) in enumerate(((low, right), (high, left))):
                copies[n].wait()
                local[n].wait()
                total = mine[n].astype(F32) + passed[n].astype(F32)
                relay[n] = total.astype(BF)
                copies.append(send(relay.at[n], got.at[n, part], base + 4 + n, peer))

        def finish():
            for copy in copies[2:]:
                copy.wait()
            local[2].wait()

        return pass_on, finish

    def start_second(job):
        number, _, _, (gone, axis, _), (got, _, _, _, own, total, ready, after, *_) = job
        total[...] = own[...].astype(F32) + got[0].astype(F32) + got[1].astype(F32)
        started = []
        for o in (2, 1, 3):
            ready[o - 1] = sub(total, gone, axis, lax.rem(here[axis] + o, 4)).astype(BF)
            started.append(
                send(ready.at[o - 1], after.at[o - 1], number * 12 + 5 + o, along(axis, o))
            )
        return started

    def sub(total, gone, axis, index):
        first = axis == min(a for a in range(3) if a != gone)
        return total[index] if first else total[:, index]

    def start_third(job, copies):
        number, _, _, (gone, middle, axis), (*_, total, _, after, small, last) = job
        for copy in copies:
            copy.wait()
        rows = sub(total, gone, middle, here[middle])
        for o in range(3):
            rows = rows + after[o].astype(F32)
        small[...] = rows.astype(BF)
        started = [
            send(
                small.at[lax.rem(here[axis] + o, 4)], last.at[o - 1], number * 12 + 8 + o,
                along(axis, o),
            )
            for o in (2, 1, 3)
        ]
        return started

    def end(job, copies):
        _, _, out, (_, _, axis), (*_, small, last) = job
        for copy in copies:
            copy.wait()
        rows = small[here[axis]].astype(F32)
        for o in range(3):
            rows = rows + last[o].astype(F32)
        out[:, : rows.shape[1]] = rows

    running = [start_first(job) for job in jobs]
    for pass_on, _ in running:
        pass_on()
    seconds = []
    for job, (_, finish) in zip(jobs, running):
        finish()
        seconds.append(start_second(job))
    running = seconds
    running = [start_third(job, copies) for job, copies in zip(jobs, running)]
    for job, copies in zip(jobs, running):
        end(job, copies)


def reduce_mixer(products):
    scratch = []
    for n in range(len(products)):
        width = PARTS[n % 3]
        scratch += [
            pltpu.VMEM((2, 4, 4, 24, width), BF),
            pltpu.VMEM((2, 2, 4, 24, width), BF),
            pltpu.VMEM((2, 2, 4, 24, width), BF),
            pltpu.VMEM((2, 2, 4, 24, width), BF),
            pltpu.VMEM((4, 4, 24, width), BF),
            pltpu.VMEM((4, 4, 24, width), F32),
            pltpu.VMEM((3, 4, 24, width), BF),
            pltpu.VMEM((3, 4, 24, width), BF),
            pltpu.VMEM((4, 24, width), BF),
            pltpu.VMEM((3, 24, width), BF),
        ]
    return pl.pallas_call(
        reduce_mixer_kernel,
        name="reduce_mixer_gradients",
        out_shape=jax.ShapeDtypeStruct((6, 24, PARTS[0]), F32),
        in_specs=[ANY] * 6,
        out_specs=VM,
        scratch_shapes=scratch
        + [
            pltpu.SemaphoreType.DMA((18,)),
            pltpu.SemaphoreType.DMA((72,)),
            pltpu.SemaphoreType.DMA((72,)),
        ],
        compiler_params=pltpu.CompilerParams(
            collective_id=2, has_side_effects=True, vmem_limit_bytes=48 << 20
        ),
    )(*products)


def columns(shape):
    return lax.broadcasted_iota(jnp.int32, shape, 1)


def rows_of(shape):
    return lax.broadcasted_iota(jnp.int32, shape, 0)


def plain(kernel, name, outs, flops=0, bytes_accessed=4000000, ins=None, scratch=()):
    def call(*args):
        return pl.pallas_call(
            kernel,
            name=name,
            out_shape=[jax.ShapeDtypeStruct(shape, kind) for shape, kind in outs],
            in_specs=ins or [VM] * len(args),
            out_specs=[VM] * len(outs),
            scratch_shapes=list(scratch),
            compiler_params=pltpu.CompilerParams(vmem_limit_bytes=VMEM),
            cost_estimate=pl.CostEstimate(
                flops=flops, bytes_accessed=bytes_accessed, transcendentals=0
            ),
        )(*args)

    return call


def tables_kernel(routes, *outs):
    wide = (T, 128)
    earlier = (rows_of(wide) < columns(wide)).astype(BF)
    same = (rows_of(wide) == columns(wide)).astype(BF)
    for level in range(LAYERS):
        named = jnp.zeros(wide, F32)
        for k in range(TOP):
            named = named + (routes[level, :, k : k + 1] == columns(wide)).astype(F32)
        outs[level][...] = named
        turned = dot(named.astype(BF), same, ((0,), (0,)))[:E]
        rank = dot(named.astype(BF), earlier, ((0,), (0,)))[:E]
        place = lax.broadcasted_iota(jnp.int32, (E, C, T), 1).astype(F32)
        hit = jnp.where(rank[:, None, :] == place, turned[:, None, :], 0.0)
        outs[LAYERS + level][...] = hit.reshape(SLOTS, T).astype(BF)


def route_tables(routes):
    return plain(
        tables_kernel, "route_tables",
        [((T, 128), F32)] * LAYERS + [((SLOTS, T), BF)] * LAYERS,
    )(routes)


def unit_rows(rows):
    scale = lax.rsqrt(jnp.mean(rows * rows, axis=-1, keepdims=True) + EPS)
    return rows * scale, scale


def gain_rows(router):
    pick = (columns((8, 128)) == E + rows_of((8, 128))) & (rows_of((8, 128)) < 2)
    return dot(pick.astype(BF), router, ((1,), (1,)))


def slot_columns():
    shape = (SLOTS, 128)
    start = columns(shape) * C
    return (rows_of(shape) >= start) & (rows_of(shape) < start + C)


def post_kernel(
    hidden, own, other, gains, routing, named, spread, middle_out, send_out, gates_out, slot_out
):
    middle = hidden[...].astype(F32) + own[...] + other[...].astype(F32)
    middle_out[...] = middle
    normed = (unit_rows(middle)[0] * gains[1:2]).astype(BF)
    send_out[:, :D] = dot(spread[...], normed).astype(BF)
    masked = jnp.where(named[...] > 0, routing[...], -1e30)
    terms = jnp.exp(masked - jnp.max(masked, axis=-1, keepdims=True))
    terms = jnp.where(named[...] > 0, terms, 0.0)
    gates = terms / jnp.sum(terms, axis=-1, keepdims=True)
    gates_out[...] = gates
    high, low = split_two(gates)
    all_gates = dot(spread[...], high) + dot(spread[...], low)
    slot = jnp.sum(jnp.where(slot_columns(), all_gates, 0.0), axis=-1, keepdims=True)
    slot_out[...] = slot
    if send_out.shape[1] > D:
        send_out[:, D:] = two_columns(slot)


def two_columns(value):
    high = value.astype(BF).astype(F32)
    column = columns((value.shape[0], WIDE - D))
    return jnp.where(column == 0, high, jnp.where(column == 1, value - high, 0.0)).astype(BF)


def post(width, *args):
    return plain(
        post_kernel, "dispatch_rows_of_tokens",
        [((T, D), F32), ((SLOTS, width), BF), ((T, 128), F32), ((SLOTS, 1), F32)], 2 * SLOTS * T * D,
    )(*args)


def combine_kernel(middle, routed, spread, slot, *refs):
    mix = spread[...].astype(F32) * slot[...]
    high, low = split_two(mix)
    rows = routed[...]
    hidden = middle[...] + dot(high, rows, ((0,), (0,))) + dot(low, rows, ((0,), (0,)))
    if len(refs) == 1:
        refs[0][...] = hidden
        return
    mixers, hidden_out, normed_out, gains_out, router, sem = refs
    copy = pltpu.make_async_copy(mixers.at[:, pl.ds(WR, COLS - WR)], router, sem)
    copy.start()
    hidden_out[...] = hidden
    copy.wait()
    gains = gain_rows(router[...])
    gains_out[...] = gains
    normed_out[...] = (unit_rows(hidden)[0] * gains[0:1]).astype(BF)


def combine(middle, routed, spread, slot):
    return plain(combine_kernel, "add_expert_outputs", [((T, D), F32)], 4 * SLOTS * T * D)(
        middle, routed, spread, slot
    )[0]


def combine_next(middle, routed, spread, slot, mixers):
    return plain(
        combine_kernel, "add_expert_outputs_and_norm",
        [((T, D), F32), ((T, D), BF), ((8, D), F32)], 4 * SLOTS * T * D,
        ins=[VM] * 4 + [ANY],
        scratch=[pltpu.VMEM((D, COLS - WR), BF), pltpu.SemaphoreType.DMA],
    )(middle, routed, spread, slot, mixers)


def back_through_norm(inputs, gain, grad_normed, grad_residual):
    unit, scale = unit_rows(inputs)
    grad_gain = jnp.sum(grad_normed * unit, axis=0, keepdims=True)
    grad_unit = grad_normed * gain
    back = grad_unit - unit * jnp.mean(grad_unit * unit, axis=-1, keepdims=True)
    return grad_residual + scale * back, grad_gain


def pre_back_kernel(
    dx, shares, middle, gains, grad, spread, gates, middle_out, out_out, routing_out, gain_out
):
    table = spread[...]
    if shares is None:
        share = dx[:, D : D + 1].astype(F32) + dx[:, D + 1 : D + 2].astype(F32)
    else:
        share = shares[...]
    high, low = split_two(jnp.where(slot_columns(), share, 0.0))
    dense = dot(table, high, ((0,), (0,))) + dot(table, low, ((0,), (0,)))
    routing = dense - gates[...] * jnp.sum(dense, axis=-1, keepdims=True)
    routing_out[...] = routing.astype(BF)
    grad_normed = dot(table, dx[:, :D], ((0,), (0,)))
    grad_middle, grad_gain = back_through_norm(
        middle[...], gains[1:2], grad_normed, grad[...].astype(F32)
    )
    middle_out[...] = grad_middle
    out_out[...] = grad_middle.astype(BF)
    gain_out[...] = grad_gain


def pre_back(dx, shares, *args):
    outs = [((T, D), F32), ((T, D), BF), ((T, 128), BF), ((1, D), F32)]
    if shares is None:
        return plain(
            lambda dx, *refs: pre_back_kernel(dx, None, *refs), "back_to_middle", outs,
            2 * SLOTS * T * D,
        )(dx, *args)
    return plain(pre_back_kernel, "back_to_middle", outs, 2 * SLOTS * T * D)(dx, shares, *args)


def post_back_kernel(own, other, hidden, gains, grad_middle, gain_two, *refs):
    grad_normed = own[...] + other[...].astype(F32)
    grad, gain_one = back_through_norm(
        hidden[...].astype(F32), gains[0:1], grad_normed, grad_middle[...]
    )
    if len(refs) == 2:
        grad_out, rows_out = refs
    else:
        spread, slot, routed, grad_out, rows_out, dy_out, share_out = refs
        high, low = split_two(grad)
        slots = dot(spread[...], high) + dot(spread[...], low)
        dy_out[...] = (slot[...] * slots).astype(BF)
        share = jnp.sum(routed[...].astype(F32) * slots, axis=-1, keepdims=True)
        share_out[...] = slot[...] * share
    grad_out[...] = grad
    rows_out[...] = jnp.zeros((16, D), BF)
    for n, gain in enumerate((gain_one, gain_two[...])):
        high, low = split_two(gain)
        rows_out[2 * n : 2 * n + 1] = high
        rows_out[2 * n + 1 : 2 * n + 2] = low


def post_back(*args):
    outs = [((T, D), F32), ((16, D), BF)]
    if len(args) > 6:
        outs += [((SLOTS, D), BF), ((SLOTS, 1), F32)]
    return plain(post_back_kernel, "back_to_hidden", outs, 4 * SLOTS * T * D)(*args)


def products_kernel(
    normed, grads_own, grads_other, heads, att, routing, gains,
    first_out, second_out, third_out, grads,
):
    step = pl.program_id(0)

    @pl.when(step == 0)
    def _():
        grads[:T] = grads_own[...]
        grads[T:] = grads_other[...]

    def product(left, right):
        return dot(left, right, ((0,), (0,)))

    def pair(ref, start, stop):
        return jnp.concatenate([ref[0, :, start:stop], ref[1, :, start:stop]], axis=0)

    block = pl.ds(pl.multiple_of(step * (D // 4), 128), D // 4)
    def store(out, value):
        out[0] = value.reshape(4, 4, 24, value.shape[1]).astype(BF)

    left, turned = normed[:, block], grads[:, block]
    number, column = rows_of((16, 128)), columns((16, 128))
    gain_place = ((number < 2) & (column == E)) | (
        (number >= 2) & (number < 4) & (column == E + 1)
    )
    store(first_out, product(left, pair(heads, 0, 768)))
    store(second_out, product(turned, pair(att, 0, 768)))
    third = [
        product(left, pair(heads, 768, WO)),
        product(left[:T], routing[...]) + product(gains[:, block], gain_place.astype(BF)),
    ]
    store(third_out, jnp.concatenate(third, axis=1))


def mixer_products(normed, grads_own, grads_other, heads, att, routing, gains):
    def whole(v):
        zeros = (0,) * len(v.shape)
        return pl.BlockSpec(v.shape, lambda i: zeros, pipeline_mode=pl.Buffered(1))

    args = [normed, grads_own, grads_other, heads, att, routing, gains]
    return pl.pallas_call(
        products_kernel,
        name="mixer_products",
        grid=(4,),
        out_shape=[jax.ShapeDtypeStruct((4, 4, 4, 24, width), BF) for width in PARTS],
        in_specs=[whole(v) for v in args],
        out_specs=[
            pl.BlockSpec((1, 4, 4, 24, width), lambda i: (i, 0, 0, 0, 0)) for width in PARTS
        ],
        scratch_shapes=[pltpu.VMEM((2 * T, D), BF)],
        compiler_params=pltpu.CompilerParams(vmem_limit_bytes=58 << 20),
        cost_estimate=pl.CostEstimate(
            flops=2 * 2 * T * D * COLS, bytes_accessed=11000000, transcendentals=0
        ),
    )(*args)


def turn(rows, cosine, sine):
    return rows * cosine + pltpu.roll(rows, HD // 2, 1) * sine


def head_rows(ref, sequence, heads):
    return jnp.concatenate([ref[sequence, :, h * HD : (h + 1) * HD] for h in heads], axis=0)


def weigh(queries, keys, mask):
    raw = dot(queries, keys, ((1,), (1,))).reshape(6, T, T)
    logits = jnp.where(mask[None] > 0, raw * SCALE, -1e30)
    terms = jnp.exp(logits - jnp.max(logits, axis=-1, keepdims=True))
    return (terms / jnp.sum(terms, axis=-1, keepdims=True)).reshape(6 * T, T)


PIECES = (pl.ds(WR, COLS - WR), pl.ds(0, WO), pl.ds(WO, WR - WO))


class Several:
    def __init__(self, copies):
        self.copies = copies
        for copy in copies:
            copy.start()

    def wait(self):
        for copy in self.copies:
            copy.wait()


def fetch_weights(mixers, weights, sem):
    groups = []
    for n, place in enumerate(PIECES):
        rows = [pl.ds(i * (D // 4), D // 4) for i in range(4)]
        groups.append(
            Several(
                [
                    pltpu.make_async_copy(
                        mixers.at[r, place], weights.at[r, place], sem.at[n * 4 + i]
                    )
                    for i, r in enumerate(rows)
                ]
            )
        )
    return groups


def attend_kernel(first, own, other, mixers, cosine, sine, mask, *refs):
    *refs, weights, sem = refs
    both, heads_out, att_out, own_out, other_out, routing_out = refs[:6]
    copies = fetch_weights(mixers, weights, sem)
    if first:
        units = [unit_rows(v[...].astype(F32))[0] for v in (own, other)]
        copies[0].wait()
        gains = gain_rows(weights[:, WR:])
        refs[6][...] = gains
        both[:T] = (units[0] * gains[0:1]).astype(BF)
        both[T:] = (units[1] * gains[0:1]).astype(BF)
    else:
        both[:T] = own[...]
        both[T:] = other[...]
        copies[0].wait()
    turns = [jnp.concatenate([t[...], t[...]], axis=0) for t in (cosine, sine)]
    copies[1].wait()
    for tile in range(4):
        wide = dot(both[...], weights[:, tile * 256 : (tile + 1) * 256])
        for part in range(2):
            head = tile * 2 + part
            rows = wide[:, part * HD : (part + 1) * HD]
            if head < 7:
                rows = turn(rows, *turns)
            rows = rows.astype(BF)
            for s in range(2):
                heads_out[s, :, head * HD : (head + 1) * HD] = rows[s * T : (s + 1) * T]
    for s in range(2):
        probs = weigh(head_rows(heads_out, s, range(6)), heads_out[s, :, 768:896], mask[s])
        mixed = dot(probs.astype(BF), heads_out[s, :, 896:]).astype(BF)
        for h in range(6):
            att_out[s, :, h * HD : (h + 1) * HD] = mixed[h * T : (h + 1) * T]
    copies[2].wait()
    att = att_out[...].reshape(2 * T, 768)
    for tile in range(6):
        place = slice(tile * 256, (tile + 1) * 256)
        rows = dot(att, weights[place, WO:WR], ((1,), (1,)))
        own_out[:, place] = rows[:T]
        other_out[:, place] = rows[T:].astype(BF)
    routing_out[...] = dot(both[:T], weights[:, WR:])


def attend(first, own, other, mixers, cosine, sine, mask):
    outs = [
        ((2 * T, D), BF), ((2, T, WO), BF), ((2, T, WR - WO), BF), ((T, D), F32), ((T, D), BF),
        ((T, 128), F32),
    ]
    return plain(
        lambda *refs: attend_kernel(first, *refs), "attention_forward",
        outs + [((8, D), F32)] * first, 1700000000, 9000000,
        ins=[VM, VM, ANY, VM, VM, VM],
        scratch=[pltpu.VMEM((D, COLS), BF), pltpu.SemaphoreType.DMA((12,))],
    )(own, other, mixers, cosine, sine, mask)


def attend_back_kernel(
    own, other, routing, mixers, heads, cosine, sine, mask,
    grad_heads, own_out, other_out, both, grad_att, weights, sem,
):
    copies = fetch_weights(mixers, weights, sem)
    both[:T] = own[...]
    both[T:] = other[...]
    copies[2].wait()
    for tile in range(3):
        place = slice(tile * 256, (tile + 1) * 256)
        wide = dot(both[...], weights[:, WO + tile * 256 : WO + (tile + 1) * 256]).astype(BF)
        for s in range(2):
            grad_att[s, :, place] = wide[s * T : (s + 1) * T]
    cos, sin = cosine[...], -sine[...]
    for s in range(2):
        queries, grads = head_rows(heads, s, range(6)), head_rows(grad_att, s, range(6))
        keys, values = heads[s, :, 768:896], heads[s, :, 896:]
        probs = weigh(queries, keys, mask[s])
        dp = dot(grads, values, ((1,), (1,)))
        draw = probs * (dp - jnp.sum(probs * dp, axis=-1, keepdims=True))
        draw = (draw * SCALE).astype(BF)
        dq = dot(draw, keys)
        for h in range(6):
            rows = turn(dq[h * T : (h + 1) * T], cos, sin)
            grad_heads[s, :, h * HD : (h + 1) * HD] = rows.astype(BF)
        dk = dot(draw, queries, ((0,), (0,)))
        grad_heads[s, :, 768:896] = turn(dk, cos, sin).astype(BF)
        grad_heads[s, :, 896:] = dot(probs.astype(BF), grads, ((0,), (0,))).astype(BF)
    copies[0].wait()
    copies[1].wait()
    wide = grad_heads[...].reshape(2 * T, 1024)
    for tile in range(6):
        place = slice(tile * 256, (tile + 1) * 256)
        rows = dot(wide, weights[place, :WO], ((1,), (1,)))
        own_out[:, place] = rows[:T] + dot(routing[...], weights[place, WR:], ((1,), (1,)))
        other_out[:, place] = rows[T:].astype(BF)


def attend_back(own, other, routing, mixers, heads, cosine, sine, mask):
    return pl.pallas_call(
        attend_back_kernel,
        name="attention_backward",
        out_shape=(
            jax.ShapeDtypeStruct((2, T, 1024), BF),
            jax.ShapeDtypeStruct((T, D), F32),
            jax.ShapeDtypeStruct((T, D), BF),
        ),
        in_specs=[VM, VM, VM, ANY, VM, VM, VM, VM],
        out_specs=[VM] * 3,
        scratch_shapes=[
            pltpu.VMEM((2 * T, D), BF),
            pltpu.VMEM((2, T, 768), BF),
            pltpu.VMEM((D, COLS), BF),
            pltpu.SemaphoreType.DMA((12,)),
        ],
        compiler_params=pltpu.CompilerParams(vmem_limit_bytes=VMEM),
        cost_estimate=pl.CostEstimate(flops=2200000000, bytes_accessed=9000000, transcendentals=200000),
    )(own, other, routing, mixers, heads, cosine, sine, mask)

class Exchange:
    def __init__(self, rows, held, result, back, sems, also=()):
        (self.x, self.z, self.y, self.core), self.along = neighbours()
        self.rows, self.held, self.result, self.back = rows, held, result, back
        self.sems, self.local = sems[:4], sems[4]
        self.me = self.index(self.z, self.y, self.core)
        greet([self.peer(k, 1) for k in range(1, E)] + [self.along(0, o) for o in also])

    def index(self, z, y, core):
        return (z * 4 + y) * 2 + core

    def peer(self, k, sign):
        a, b, c = k // 8, k // 2 % 4, k % 2
        return (
            self.x,
            lax.rem(self.z + (a * sign) % 4, 4),
            lax.rem(self.y + (b * sign) % 4, 4),
            lax.rem(self.core + c, 2),
        )

    def copy(self, k, returning):
        peer = self.peer(k, -1 if returning else 1)
        there = self.index(*peer[1:])
        source, target = (self.result, self.back) if returning else (self.rows, self.held)
        sems = self.sems[2:] if returning else self.sems[:2]
        return pltpu.make_async_remote_copy(
            source.at[there], target.at[self.me], sems[0].at[k], sems[1].at[k],
            device_id=peer, device_id_type=MESH,
        )

    def start(self):
        for pair in ((2, 0), (1, 3)):
            for n in range(8):
                for a in pair:
                    if a * 8 + n:
                        self.copy(a * 8 + n, False).start()
        self.own = pltpu.make_async_copy(
            self.rows.at[self.me], self.held.at[self.me], self.local.at[0]
        )
        self.own.start()

    def arrive(self, a):
        for k in range(a * 8, a * 8 + 8):
            if k:
                self.copy(k, False).wait_recv()
        if a == 0:
            self.own.wait()
        block = lax.rem(self.z + (-a) % 4, 4)
        rows = self.held[pl.ds(block * 8, 8)].astype(F32)
        return block, rows.reshape(8 * C, rows.shape[2]).astype(BF)

    def give(self, a, block, value):
        width = value.shape[1]
        self.result[pl.ds(block * 8, 8), :, :width] = value.reshape(8, C, width).astype(BF)

    def send_back(self, a):
        for k in range(a * 8, a * 8 + 8):
            if k:
                self.copy(k, True).start()
        if a == 0:
            self.last = pltpu.make_async_copy(
                self.result.at[self.me], self.back.at[self.me], self.local.at[1]
            )
            self.last.start()

    def finish(self):
        for k in range(1, E):
            self.copy(k, False).wait_send()
            self.copy(k, True).wait()
        self.last.wait()


GROUPS = (0, 2, 1, 3)


def start_weights(pieces, weights, sem):
    waits, matrix = [], 0
    for piece in pieces:
        count, several = piece.shape[:2]
        for m in range(several):
            copies = []
            for n in range(4):
                source = piece.at[n, m] if count == 4 else piece.at[0, m, pl.ds(n * 384, 384)]
                copies.append(
                    pltpu.make_async_copy(
                        source, weights.at[matrix, n], sem.at[matrix * 4 + n]
                    )
                )
                copies[n].start()
            waits.append(copies)
            matrix += 1

    def ready(m):
        for copy in waits[m]:
            copy.wait()

    return ready


def matrix_of(weights, m):
    return weights[m].reshape(D, FF)


def at_block(block):
    return pl.ds(pl.multiple_of(block * 8 * C, 8 * C), 8 * C)


def forward_phase_kernel(
    rows, gate_up, downs, ups, back, flat_out, a_out, b_out, down_out, next_out,
    held, result, weights, weight_sem, ring_send, ring_recv, *sems,
):
    work = Exchange(rows, held, result, back, sems, (1, 3))
    work.start()
    send = sender(ring_send, ring_recv)
    x, local = work.x, work.local
    own = [
        pltpu.make_async_copy(downs.at[0, 0], weights.at[2, x], local.at[2]),
        pltpu.make_async_copy(ups.at[1, 0], next_out.at[0, x], local.at[3]),
        pltpu.make_async_copy(downs.at[1, 0], next_out.at[1, x], local.at[4]),
    ]
    for copy in own:
        copy.start()
    ring = ring_of(downs.at[0, 0], weights.at[2], x, work.along, send, 0)
    others = [
        ring_of(ups.at[1, 0], next_out.at[0], x, work.along, send, 6),
        ring_of(downs.at[1, 0], next_out.at[1], x, work.along, send, 12),
    ]
    ready = start_weights([gate_up], weights, weight_sem)
    ring[0]()
    for number, group in enumerate(GROUPS):
        block, got = work.arrive(group)
        place = at_block(block)
        flat_out[place] = got
        if number == 0:
            ready(0)
        a = dot(got, matrix_of(weights, 0))
        if number == 0:
            ready(1)
        b = dot(got, matrix_of(weights, 1))
        a_out[place] = a
        b_out[place] = b
        inner = (a * jax.nn.sigmoid(a) * b).astype(BF)
        if number == 0:
            ring[1]()
            own[0].wait()
        work.give(group, block, dot(inner, matrix_of(weights, 2), ((1,), (1,))))
        work.send_back(group)
    kept = pltpu.make_async_copy(weights.at[2], down_out.at[0], local.at[2])
    kept.start()
    others[0][0]()
    others[1][0]()
    for other, copy in zip(others, own[1:]):
        other[1]()
        copy.wait()
    work.finish()
    kept.wait()


def inner_gradients(a, b, dy, weights, place, held):
    du = dot(dy, matrix_of(weights, 2))
    sig = jax.nn.sigmoid(a)
    act = a * sig
    inner = (act * b).astype(BF)
    da = (du * b * sig * (1.0 + a * (1.0 - sig))).astype(BF)
    db = (du * act).astype(BF)
    for ref, value in zip(held, (da, db, inner)):
        ref[place] = value
    dx = dot(da, matrix_of(weights, 0), ((1,), (1,)))
    return inner, dx + dot(db, matrix_of(weights, 1), ((1,), (1,)))


def weight_gradients(rows, dy, held, outs):
    @pl.loop(0, 4)
    def _(n):
        columns = pl.ds(pl.multiple_of(n * 384, 128), 384)
        place = pl.ds(pl.multiple_of(n * 384, 128), 384)
        for left, right, out in zip((rows, rows, dy), held, outs):
            out[place] = dot(left[:, columns], right[...], ((0,), (0,))).astype(BF)


def back_phase_kernel(
    rows, a_in, b_in, flat_in, gate_up, down, parts, back, gate_out, up_out, down_out, sum_out,
    held, result, weights, a, b, flat, dy, da, db, inner, got_parts, weight_sem, load_sem,
    part_send, part_recv, *sems,
):
    work = Exchange(rows, held, result, back, sems, (1, 2, 3))
    work.start()
    send = sender(part_send, part_recv)
    others = [
        send(parts.at[lax.rem(work.x + o, 4)], got_parts.at[o], o - 1, work.along(0, o))
        for o in (1, 3, 2)
    ]
    mine = pltpu.make_async_copy(parts.at[work.x], got_parts.at[0], work.local.at[2])
    mine.start()
    ready = start_weights([gate_up, down], weights, weight_sem)
    loads = []
    for n, (src, dst) in enumerate(((a_in, a), (b_in, b), (flat_in, flat))):
        loads.append(pltpu.make_async_copy(src, dst, load_sem.at[n]))
        loads[n].start()
    for number, group in enumerate(GROUPS):
        block, got = work.arrive(group)
        place = at_block(block)
        dy[place] = got
        if number == 0:
            loads[0].wait()
            loads[1].wait()
            for m in range(3):
                ready(m)
        _, dx = inner_gradients(a[place], b[place], got, weights, place, (da, db, inner))
        work.give(group, block, dx)
        work.send_back(group)
    loads[2].wait()
    weight_gradients(flat, dy, (da, db, inner), (gate_out, up_out, down_out))
    for copy in others + [mine]:
        copy.wait()
    total = got_parts[0].astype(F32) + got_parts[1].astype(F32)
    total = total + got_parts[2].astype(F32) + got_parts[3].astype(F32)
    sum_out[...] = total.astype(BF)
    work.finish()


def both_phase_kernel(
    rows, target_low, target_high, gate_up, down, back, y_out, gate_out, up_out, down_out,
    held, result, weights, low, high, flat, dy, da, db, inner, weight_sem, load_sem, *sems,
):
    work = Exchange(rows, held, result, back, sems)
    work.start()
    ready = start_weights([gate_up, down], weights, weight_sem)
    loads = []
    for n, (src, dst) in enumerate(((target_low, low), (target_high, high))):
        loads.append(pltpu.make_async_copy(src, dst, load_sem.at[n]))
        loads[n].start()
    for number, group in enumerate(GROUPS):
        block, got = work.arrive(group)
        place = at_block(block)
        normed = got[:, :D]
        flat[place] = normed
        gate = got[:, D : D + 1].astype(F32) + got[:, D + 1 : D + 2].astype(F32)
        if number == 0:
            loads[0].wait()
            loads[1].wait()
            for m in range(3):
                ready(m)
        target = jnp.concatenate([low[place], high[place]], axis=1)
        grads = (gate * target.astype(F32)).astype(BF)
        dy[place] = grads
        a = dot(normed, matrix_of(weights, 0))
        b = dot(normed, matrix_of(weights, 1))
        mixed, dx = inner_gradients(a, b, grads, weights, place, (da, db, inner))
        y = dot(mixed, matrix_of(weights, 2), ((1,), (1,))).astype(BF)
        y_out[place] = y
        share = jnp.sum(y.astype(F32) * grads.astype(F32), axis=-1, keepdims=True)
        parts = two_columns(share).astype(F32)
        work.give(group, block, jnp.concatenate([dx, parts], axis=1))
        work.send_back(group)
    weight_gradients(flat, dy, (da, db, inner), (gate_out, up_out, down_out))
    work.finish()


def phase_call(kernel, name, number, args, outs, scratch, width, flops):
    slots = (E, C, width)
    return pl.pallas_call(
        kernel,
        name=name,
        out_shape=[jax.ShapeDtypeStruct(slots, BF)]
        + [jax.ShapeDtypeStruct(shape, kind) for shape, kind, _ in outs],
        in_specs=[ANY] * len(args),
        out_specs=[ANY] + [spec for *_, spec in outs],
        scratch_shapes=[
            pltpu.VMEM(slots, BF), pltpu.VMEM(slots, BF), pltpu.VMEM((3, 4, D // 4, FF), BF)
        ]
        + scratch
        + [pltpu.SemaphoreType.DMA((E,))] * 4
        + [pltpu.SemaphoreType.DMA((5,))],
        compiler_params=pltpu.CompilerParams(
            collective_id=number, has_side_effects=True, vmem_limit_bytes=52 << 20
        ),
        cost_estimate=pl.CostEstimate(
            flops=flops, bytes_accessed=20000000, transcendentals=SLOTS * FF
        ),
    )(*args)


UNIT = 2 * SLOTS * D * FF
GRADS = [((D, FF), BF, VM)] * 3


def forward_phase(rows, gate_up, downs, ups):
    shard = (1, 4, D // 4, FF)
    back, flat, a, b, down, after = phase_call(
        forward_phase_kernel, "expert_phase_forward", 3, (rows.reshape(E, C, D), gate_up, downs, ups),
        [((SLOTS, D), BF, VM), ((SLOTS, FF), F32, VM), ((SLOTS, FF), F32, VM), (shard, BF, ANY),
         ((2, 4, D // 4, FF), BF, ANY)],
        [pltpu.SemaphoreType.DMA((8,)), pltpu.SemaphoreType.DMA((18,)),
         pltpu.SemaphoreType.DMA((18,))],
        D, 3 * UNIT,
    )
    down, after = down.reshape(1, 1, D, FF), after.reshape(1, 2, D, FF)
    return back.reshape(SLOTS, D), flat, a, b, down, after


def matrices(*widths):
    return [pltpu.VMEM((SLOTS, width), BF) for width in widths]


def back_phase(rows, a, b, flat, gate_up, down, parts):
    back, *grads, total = phase_call(
        back_phase_kernel, "expert_phase_backward", 5,
        (rows.reshape(E, C, D), a, b, flat, gate_up, down, parts.reshape(4, D // 4, FF)),
        GRADS + [((D // 4, FF), BF, VM)],
        [pltpu.VMEM((SLOTS, FF), F32)] * 2 + matrices(D, D, FF, FF, FF)
        + [pltpu.VMEM((4, D // 4, FF), BF)]
        + [pltpu.SemaphoreType.DMA((count,)) for count in (12, 3, 3, 3)],
        D, 6 * UNIT,
    )
    return back.reshape(SLOTS, D), grads, total


def both_phase(rows, targets, gate_up, down):
    back, y, *grads = phase_call(
        both_phase_kernel, "expert_phase_both", 4,
        (rows.reshape(E, C, WIDE), *targets, gate_up, down), [((SLOTS, D), BF, VM)] + GRADS,
        matrices(FF, FF, D, D, FF, FF, FF)
        + [pltpu.SemaphoreType.DMA((12,)), pltpu.SemaphoreType.DMA((2,))],
        WIDE, 9 * UNIT,
    )
    return back.reshape(SLOTS, WIDE), y, grads


def exchange(rows):
    width = rows.shape[1]
    rows = rows.reshape(E, C, width)
    rows = lax.all_to_all(rows, GROUP, split_axis=0, concat_axis=0, tiled=True)
    return rows.reshape(SLOTS, width)


def outputs_kernel(core, mine, theirs, *outs):
    for level in range(LAYERS):
        level_outputs(level, core[0] == 0, mine, theirs, *outs)


def level_outputs(level, first, mine, theirs, q_out, k_out, v_out, o_out, routing_out):

    def rows(ref, group):
        group = level * 3 + group
        return jnp.where(first, ref[group, :12], ref[group, 12:])

    halves = []
    for ref in (mine, theirs):
        a, b, c = (rows(ref, group) for group in range(3))
        halves.append(
            (
                a, c[:, :HD], c[:, HD : 2 * HD], b, c[:, 2 * HD : 3 * HD],
            )
        )
    for out, own, other in zip((q_out, k_out, v_out, o_out), *halves):
        width = own.shape[1]
        out[:, level, :width] = jnp.where(first, own, other)
        out[:, level, width:] = jnp.where(first, other, own)
    routing_out[:, level, :] = halves[0][4] + halves[1][4]


def mixer_outputs(sums, core):
    widths = (D, 2 * HD, 2 * HD, D, HD)
    *outs, routing = pl.pallas_call(
        outputs_kernel,
        name="mixer_outputs",
        out_shape=[jax.ShapeDtypeStruct((12, LAYERS, width), F32) for width in widths],
        grid=(1,),
        in_specs=[pl.BlockSpec(memory_space=pltpu.SMEM)]
        + [pl.BlockSpec((6, 24, PARTS[0]), lambda i: (0, 0, 0))] * 2,
        out_specs=[pl.BlockSpec((12, LAYERS, width), lambda i: (0, 0, 0)) for width in widths],
    )(core.reshape(1), sums, swap(sums))
    *outs, routing = [v.transpose(1, 0, 2) for v in (*outs, routing)]
    return (*outs, routing[:, :, :E], routing[:, :, E], routing[:, :, E + 1])


def expert_outputs_kernel(*refs):
    for matrix in range(3):
        for level in range(LAYERS):
            refs[6 + matrix][level, 0] = refs[level * 3 + matrix][...].astype(F32)


def expert_outputs(sums):
    rows = 96
    return pl.pallas_call(
        expert_outputs_kernel,
        name="expert_outputs",
        grid=(D // 4 // rows,),
        out_shape=[jax.ShapeDtypeStruct((LAYERS, 1, D // 4, FF), F32)] * 3,
        in_specs=[pl.BlockSpec((rows, FF), lambda i: (i, 0))] * 6,
        out_specs=[pl.BlockSpec((LAYERS, 1, rows, FF), lambda i: (0, 0, i, 0))] * 3,
        compiler_params=pltpu.CompilerParams(vmem_limit_bytes=58 << 20),
        cost_estimate=pl.CostEstimate(flops=0, bytes_accessed=11000000, transcendentals=0),
    )(*sums)


def reduce_expert(grads):
    return [
        lax.psum_scatter(g, "dp", scatter_dimension=0, tiled=True) for g in grads
    ]


def per_device(
    tokens, segments, route_ids, w_query, key_projection, value_projection, w_out, w_router,
    gain_attn, gain_moe, w_gate, w_up, w_down, cotangent,
):
    core = lax.axis_index("core")
    cosine, sine = rope_tables()
    position = jnp.arange(T)

    shared = jnp.concatenate(
        [
            w_router, gain_attn[:, :, None], gain_moe[:, :, None],
            jnp.zeros((LAYERS, 12, COLS - WR - E - 2), BF),
        ],
        axis=2,
    )

    def half(number):
        def cut(v):
            width = v.shape[2] // 2
            return v[:, :, number * width : (number + 1) * width]

        return jnp.concatenate(
            [cut(v) for v in (w_query, key_projection, value_projection, w_out)] + [shared], axis=2
        )

    halves = (half(0), half(1))
    mine = jnp.where(core == 0, halves[0], halves[1])
    theirs = swap(jnp.where(core == 0, halves[1], halves[0]))
    blocks = jnp.where(
        core == 0,
        jnp.concatenate([mine, theirs], axis=1),
        jnp.concatenate([theirs, mine], axis=1),
    )
    segment = segments.astype(F32)
    segment = jnp.concatenate([segment, swap(segment)])
    mask = (position[:, None] >= position[None, :])[None] & (
        segment[:, :, None] == segment[:, None, :]
    )
    mask = mask.astype(F32)

    *named, spread0, spread1 = route_tables(route_ids)
    spread = (spread0, spread1)
    targets = [
        dot(spread[1], cotangent[:, half * 768 : (half + 1) * 768]).astype(BF) for half in range(2)
    ]
    tokens_other = swap(tokens)
    first_mixer, first_experts = gather(blocks, w_gate, w_up)
    second = lax.optimization_barrier((blocks[1], w_gate[1, 0], first_experts))
    second_mixer = lax.all_gather(second[0], AXES[:3], axis=0).reshape(D, COLS)
    second_experts = lax.all_gather(second[1], "dp", axis=0)

    targets[0], tokens_other, _ = lax.optimization_barrier((targets[0], tokens_other, first_mixer))
    targets[0] = exchange(targets[0])
    normed0, heads0, att0, own, other, routing, gains0 = attend(
        True, tokens, tokens_other, first_mixer, cosine, sine, mask
    )
    middle0, send, gates0, slot0 = post(
        D, tokens, own, swap(other), gains0, routing, named[0], spread[0]
    )
    send, targets[0] = lax.optimization_barrier((send, targets[0]))
    routed0, rows0, a0, b0, down0, up_down1 = forward_phase(
        send, first_experts, w_down, w_up
    )
    routed0, targets[1] = lax.optimization_barrier((routed0, targets[1]))
    targets[1] = exchange(targets[1])
    hidden, normed, gains1 = combine_next(middle0, routed0, spread[0], slot0, second_mixer)

    normed1, heads1, att1, own, other, routing = attend(
        False, normed, swap(normed), second_mixer, cosine, sine, mask
    )
    middle1, send, gates1, slot1 = post(
        WIDE, hidden, own, swap(other), gains1, routing, named[1], spread[1]
    )
    gate1 = second_experts.reshape(4, 1, D // 4, FF)
    dx, produced, parts1 = both_phase(send, targets, gate1, up_down1)
    sums1 = reduce_expert(parts1[:2])
    routed1 = exchange(produced)

    grad_middle, grad_out, grad_routing, gain_two = pre_back(
        dx, None, middle1, gains1, cotangent, spread[1], gates1
    )
    grad_out_other = swap(grad_out)
    grad_heads, own, other = attend_back(
        grad_out, grad_out_other, grad_routing, second_mixer, heads1, cosine, sine, mask
    )
    grad, gain_parts, dy, shares = post_back(
        own, swap(other), hidden, gains1, grad_middle, gain_two, spread[0], slot0, routed0
    )
    products1 = mixer_products(
        normed1, grad_out, grad_out_other, grad_heads, att1, grad_routing, gain_parts
    )
    dx, parts0, last_sum = back_phase(
        dy, a0, b0, rows0, first_experts, down0, parts1[2]
    )
    sums0 = reduce_expert(parts0)
    dx, sums1, products1 = lax.optimization_barrier((dx, sums1, products1))

    grad_middle, grad_out, grad_routing, gain_two = pre_back(
        dx, shares, middle0, gains0, grad, spread[0], gates0
    )
    grad_out_other = swap(grad_out)
    grad_heads, own, other = attend_back(
        grad_out, grad_out_other, grad_routing, first_mixer, heads0, cosine, sine, mask
    )
    routed1 = lax.optimization_barrier((routed1, grad_heads))[0]
    output = combine(middle1, routed1, spread[1], slot1)
    grad_tokens, gain_parts = post_back(
        own, swap(other), tokens, gains0, grad_middle, gain_two
    )
    products0 = mixer_products(
        normed0, grad_out, grad_out_other, grad_heads, att0, grad_routing, gain_parts
    )
    mixer_out = mixer_outputs(reduce_mixer(products0 + products1), core)
    expert_out = expert_outputs([*sums0, *sums1, last_sum])
    return (output, grad_tokens, *mixer_out, *expert_out)


def solution(mesh):
    mesh = Mesh(mesh.devices.reshape(4, 4, 4, 2), AXES)
    rows = P(AXES, None)
    mixer = P(None, AXES, None)
    gain = P(None, AXES)
    expert = P(None, GROUP, "dp", None)
    return jax.shard_map(
        per_device,
        mesh=mesh,
        in_specs=(
            rows, rows, mixer, mixer, mixer, mixer, mixer, mixer, gain, gain, expert, expert,
            expert, rows,
        ),
        out_specs=(
            rows, rows, mixer, mixer, mixer, mixer, mixer, gain, gain, expert, expert, expert,
        ),
        check_vma=False,
    )
```

```python
import math

import jax
import jax.numpy as jnp
import numpy as np
from jax import lax
from jax.experimental import pallas as pl
from jax.experimental.pallas import tpu as pltpu
from jax.sharding import Mesh, PartitionSpec as P

MESH = pl.DeviceIdType.MESH
BF = jnp.bfloat16
F32 = jnp.float32
HEADS, KV, HD, TOP, LAYERS = 12, 2, 128, 4, 2
T, D, FF, E, C = 128, 1536, 768, 32, 24
SLOTS = E * C
THETA, EPS = 1000000.0, 1e-06
SCALE = 1.0 / math.sqrt(HD)
ANY = pl.BlockSpec(memory_space=pl.ANY)
VM = pl.BlockSpec(memory_space=pltpu.VMEM)
WO, WR, COLS = 1024, 1792, 1920
CUTS = (pl.ds(0, 1024), pl.ds(1024, COLS - 1024))
PARTS = (768, 768, 384)
VMEM = 32 << 20
WIDE = D + 128
AXES = ("dp", "z", "y", "core")
GROUP = AXES[1:]


def dot(a, b, dims=((1,), (0,))):
    return lax.dot_general(a, b, (dims, ((), ())), preferred_element_type=F32)


def split_two(v):
    high = v.astype(BF)
    return high, (v - high.astype(F32)).astype(BF)


def rope_tables():
    frequency = np.exp(-(2.0 * np.arange(HD // 2) / HD) * math.log(THETA)).astype(np.float32)
    angles = np.arange(T, dtype=np.float32)[:, None] * frequency[None, :]
    cosine, sine = np.cos(angles), np.sin(angles)
    return (
        jnp.asarray(np.concatenate([cosine, cosine], 1), F32),
        jnp.asarray(np.concatenate([-sine, sine], 1), F32),
    )


def swap(v):
    return lax.ppermute(v, "core", [(0, 1), (1, 0)])


def neighbours():
    here = [lax.axis_index(axis) for axis in AXES]

    def along(axis, places):
        peer = list(here)
        peer[axis] = lax.rem(here[axis] + places, 4)
        return tuple(peer)

    return here, along


def greet(peers):
    barrier = pltpu.get_barrier_semaphore()
    for peer in peers:
        pl.semaphore_signal(barrier, inc=1, device_id=peer, device_id_type=MESH)
    pl.semaphore_wait(barrier, len(peers))


def sender(send_sem, recv_sem):
    def send(src, dst, number, peer):
        copy = pltpu.make_async_remote_copy(
            src, dst, send_sem.at[number], recv_sem.at[number], device_id=peer, device_id_type=MESH
        )
        copy.start()
        return copy

    return send


def ring_steps(own, view, me, right, left, send, number):
    first = [
        send(own(0), view(me, 0), number, right), send(own(1), view(me, 1), number + 1, left)
    ]
    second = [
        send(own(1), view(me, 1), number + 2, right), send(own(0), view(me, 0), number + 3, left)
    ]

    relays = []

    def relay():
        before, after = lax.rem(me + 3, 4), lax.rem(me + 1, 4)
        first[0].wait_recv()
        relays.append(send(view(before, 0), view(before, 0), number + 4, right))
        first[1].wait_recv()
        relays.append(send(view(after, 1), view(after, 1), number + 5, left))

    def finish():
        for copy in second:
            copy.wait_recv()
        for copy in first + second:
            copy.wait_send()
        for copy in relays:
            copy.wait()

    return relay, finish


def ring_of(shard, out, x, along, send, number):
    return ring_steps(
        lambda half: shard.at[pl.ds(half * 192, 192)],
        lambda place, half: out.at[place, pl.ds(half * 192, 192)],
        x, along(0, 1), along(0, 3), send, number,
    )


def gather_kernel(blocks, gate, up, out, experts, local_sem, send_sem, recv_sem):
    (x, z, y, _), along = neighbours()
    greet([along(axis, o) for o in (1, 2, 3) for axis in range(3)])
    send = sender(send_sem, recv_sem)
    block = blocks.at[0]
    copies = [send(block, out.at[x, z, y], o - 1, along(0, o)) for o in (1, 3, 2)]
    shards = [gate.at[0, 0], up.at[0, 0]]
    rings = [
        ring_of(shard, experts.at[n], x, along, send, 27 + 6 * n) for n, shard in enumerate(shards)
    ]
    own = pltpu.make_async_copy(block, out.at[x, z, y], local_sem.at[0])
    own.start()
    own_experts = [
        pltpu.make_async_copy(shard, experts.at[n, x], local_sem.at[1 + n])
        for n, shard in enumerate(shards)
    ]
    for copy in own_experts:
        copy.start()
    own.wait()
    for copy in copies:
        copy.wait()

    def ring(view, axis, me, number):
        return ring_steps(
            lambda half: view(me, half), view, me, along(axis, 1), along(axis, 3), send, number
        )

    def pair(half):
        return pl.ds(half * 2, 2)

    first = ring(lambda n, half: out.at[pair(half), n, y, :, CUTS[0]], 1, z, 3)
    second = ring(lambda n, half: out.at[pair(half), z, n, :, CUTS[1]], 2, y, 9)
    first[0]()
    second[0]()
    first[1]()
    first = ring(lambda n, half: out.at[pair(half), :, n, :, CUTS[0]], 2, y, 15)
    second[1]()
    second = ring(lambda n, half: out.at[pair(half), n, :, :, CUTS[1]], 1, z, 21)
    rings[0][0]()
    first[0]()
    second[0]()
    rings[1][0]()
    first[1]()
    second[1]()
    for ring in rings:
        ring[1]()
    for copy in own_experts:
        copy.wait()


def gather(blocks, gate, up):
    mixer, experts = pl.pallas_call(
        gather_kernel,
        name="gather_weights",
        out_shape=(
            jax.ShapeDtypeStruct((4, 4, 4, 24, COLS), BF),
            jax.ShapeDtypeStruct((2, 4, D // 4, FF), BF),
        ),
        in_specs=[ANY] * 3,
        out_specs=(ANY, ANY),
        scratch_shapes=[
            pltpu.SemaphoreType.DMA((3,)),
            pltpu.SemaphoreType.DMA((39,)),
            pltpu.SemaphoreType.DMA((39,)),
        ],
        compiler_params=pltpu.CompilerParams(
            collective_id=1, has_side_effects=True, vmem_limit_bytes=VMEM
        ),
    )(blocks, gate, up)
    return mixer.reshape(D, COLS), experts.reshape(1, 2, D, FF)


def reduce_mixer_kernel(*refs):
    sources, out, scratch = refs[:6], refs[6], refs[7:]
    (x, z, y, _), along = neighbours()
    local_sem, send_sem, recv_sem = scratch[-3:]
    greet([along(axis, o) for o in (1, 2, 3) for axis in range(3)])
    send = sender(send_sem, recv_sem)
    here = (x, z, y)
    ways = ((1, 0, 2), (2, 1, 0), (0, 2, 1))
    jobs = []
    for level in reversed(range(LAYERS)):
        for group, way in enumerate(ways):
            number = level * 3 + group
            held = scratch[number * 10 : number * 10 + 10]
            jobs.append((number, sources[number], out.at[number], way, held))

    def pick(ref, dim, index, half=None):
        place = [slice(None)] * 3
        place[dim] = index
        if half is not None:
            place[1 if dim == 0 else 0] = half
        return ref.at[tuple(place)]

    def start_first(job):
        number, source, _, (axis, *_), (got, passed, relay, mine, own, *_) = job
        me = here[axis]
        right, left = along(axis, 1), along(axis, 3)
        after, far, before = (lax.rem(me + o, 4) for o in (1, 2, 3))
        low, high = pl.ds(0, 2), pl.ds(2, 2)
        base = number * 12
        copies = [
            send(pick(source, axis, far, low), passed.at[0], base, right),
            send(pick(source, axis, far, high), passed.at[1], base + 1, left),
            send(pick(source, axis, after, high), got.at[0, high], base + 2, right),
            send(pick(source, axis, before, low), got.at[1, low], base + 3, left),
        ]
        local = []
        for n, (src, dst) in enumerate(
            (
                (pick(source, axis, after, low), mine.at[0]),
                (pick(source, axis, before, high), mine.at[1]),
                (pick(source, axis, me), own),
            )
        ):
            local.append(pltpu.make_async_copy(src, dst, local_sem.at[number * 3 + n]))
            local[n].start()

        def pass_on():
            for n, (part, peer) in enumerate(((low, right), (high, left))):
                copies[n].wait()
                local[n].wait()
                total = mine[n].astype(F32) + passed[n].astype(F32)
                relay[n] = total.astype(BF)
                copies.append(send(relay.at[n], got.at[n, part], base + 4 + n, peer))

        def finish():
            for copy in copies[2:]:
                copy.wait()
            local[2].wait()

        return pass_on, finish

    def start_second(job):
        number, _, _, (gone, axis, _), (got, _, _, _, own, total, ready, after, *_) = job
        total[...] = own[...].astype(F32) + got[0].astype(F32) + got[1].astype(F32)
        started = []
        for o in (2, 1, 3):
            ready[o - 1] = sub(total, gone, axis, lax.rem(here[axis] + o, 4)).astype(BF)
            started.append(
                send(ready.at[o - 1], after.at[o - 1], number * 12 + 5 + o, along(axis, o))
            )
        return started

    def sub(total, gone, axis, index):
        first = axis == min(a for a in range(3) if a != gone)
        return total[index] if first else total[:, index]

    def start_third(job, copies):
        number, _, _, (gone, middle, axis), (*_, total, _, after, small, last) = job
        for copy in copies:
            copy.wait()
        rows = sub(total, gone, middle, here[middle])
        for o in range(3):
            rows = rows + after[o].astype(F32)
        small[...] = rows.astype(BF)
        started = [
            send(
                small.at[lax.rem(here[axis] + o, 4)], last.at[o - 1], number * 12 + 8 + o,
                along(axis, o),
            )
            for o in (2, 1, 3)
        ]
        return started

    def end(job, copies):
        _, _, out, (_, _, axis), (*_, small, last) = job
        for copy in copies:
            copy.wait()
        rows = small[here[axis]].astype(F32)
        for o in range(3):
            rows = rows + last[o].astype(F32)
        out[:, : rows.shape[1]] = rows

    running = [start_first(job) for job in jobs]
    for pass_on, _ in running:
        pass_on()
    seconds = []
    for job, (_, finish) in zip(jobs, running):
        finish()
        seconds.append(start_second(job))
    running = seconds
    running = [start_third(job, copies) for job, copies in zip(jobs, running)]
    for job, copies in zip(jobs, running):
        end(job, copies)


def reduce_mixer(products):
    scratch = []
    for n in range(len(products)):
        width = PARTS[n % 3]
        scratch += [
            pltpu.VMEM((2, 4, 4, 24, width), BF),
            pltpu.VMEM((2, 2, 4, 24, width), BF),
            pltpu.VMEM((2, 2, 4, 24, width), BF),
            pltpu.VMEM((2, 2, 4, 24, width), BF),
            pltpu.VMEM((4, 4, 24, width), BF),
            pltpu.VMEM((4, 4, 24, width), F32),
            pltpu.VMEM((3, 4, 24, width), BF),
            pltpu.VMEM((3, 4, 24, width), BF),
            pltpu.VMEM((4, 24, width), BF),
            pltpu.VMEM((3, 24, width), BF),
        ]
    return pl.pallas_call(
        reduce_mixer_kernel,
        name="reduce_mixer_gradients",
        out_shape=jax.ShapeDtypeStruct((6, 24, PARTS[0]), F32),
        in_specs=[ANY] * 6,
        out_specs=VM,
        scratch_shapes=scratch
        + [
            pltpu.SemaphoreType.DMA((18,)),
            pltpu.SemaphoreType.DMA((72,)),
            pltpu.SemaphoreType.DMA((72,)),
        ],
        compiler_params=pltpu.CompilerParams(
            collective_id=2, has_side_effects=True, vmem_limit_bytes=48 << 20
        ),
    )(*products)


def columns(shape):
    return lax.broadcasted_iota(jnp.int32, shape, 1)


def rows_of(shape):
    return lax.broadcasted_iota(jnp.int32, shape, 0)


def plain(kernel, name, outs, flops=0, bytes_accessed=4000000, ins=None, scratch=()):
    def call(*args):
        return pl.pallas_call(
            kernel,
            name=name,
            out_shape=[jax.ShapeDtypeStruct(shape, kind) for shape, kind in outs],
            in_specs=ins or [VM] * len(args),
            out_specs=[VM] * len(outs),
            scratch_shapes=list(scratch),
            compiler_params=pltpu.CompilerParams(vmem_limit_bytes=VMEM),
            cost_estimate=pl.CostEstimate(
                flops=flops, bytes_accessed=bytes_accessed, transcendentals=0
            ),
        )(*args)

    return call


def tables_kernel(routes, *outs):
    wide = (T, 128)
    earlier = (rows_of(wide) < columns(wide)).astype(BF)
    same = (rows_of(wide) == columns(wide)).astype(BF)
    for level in range(LAYERS):
        named = jnp.zeros(wide, F32)
        for k in range(TOP):
            named = named + (routes[level, :, k : k + 1] == columns(wide)).astype(F32)
        outs[level][...] = named
        turned = dot(named.astype(BF), same, ((0,), (0,)))[:E]
        rank = dot(named.astype(BF), earlier, ((0,), (0,)))[:E]
        place = lax.broadcasted_iota(jnp.int32, (E, C, T), 1).astype(F32)
        hit = jnp.where(rank[:, None, :] == place, turned[:, None, :], 0.0)
        outs[LAYERS + level][...] = hit.reshape(SLOTS, T).astype(BF)


def route_tables(routes):
    return plain(
        tables_kernel, "route_tables",
        [((T, 128), F32)] * LAYERS + [((SLOTS, T), BF)] * LAYERS,
    )(routes)


def unit_rows(rows):
    scale = lax.rsqrt(jnp.mean(rows * rows, axis=-1, keepdims=True) + EPS)
    return rows * scale, scale


def gain_rows(router):
    pick = (columns((8, 128)) == E + rows_of((8, 128))) & (rows_of((8, 128)) < 2)
    return dot(pick.astype(BF), router, ((1,), (1,)))


def slot_columns():
    shape = (SLOTS, 128)
    start = columns(shape) * C
    return (rows_of(shape) >= start) & (rows_of(shape) < start + C)


def post_kernel(
    hidden, own, other, gains, routing, named, spread, middle_out, send_out, gates_out, slot_out
):
    middle = hidden[...].astype(F32) + own[...] + other[...].astype(F32)
    middle_out[...] = middle
    normed = (unit_rows(middle)[0] * gains[1:2]).astype(BF)
    send_out[:, :D] = dot(spread[...], normed).astype(BF)
    masked = jnp.where(named[...] > 0, routing[...], -1e30)
    terms = jnp.exp(masked - jnp.max(masked, axis=-1, keepdims=True))
    terms = jnp.where(named[...] > 0, terms, 0.0)
    gates = terms / jnp.sum(terms, axis=-1, keepdims=True)
    gates_out[...] = gates
    high, low = split_two(gates)
    all_gates = dot(spread[...], high) + dot(spread[...], low)
    slot = jnp.sum(jnp.where(slot_columns(), all_gates, 0.0), axis=-1, keepdims=True)
    slot_out[...] = slot
    if send_out.shape[1] > D:
        send_out[:, D:] = two_columns(slot)


def two_columns(value):
    high = value.astype(BF).astype(F32)
    column = columns((value.shape[0], WIDE - D))
    return jnp.where(column == 0, high, jnp.where(column == 1, value - high, 0.0)).astype(BF)


def post(width, *args):
    return plain(
        post_kernel, "dispatch_rows_of_tokens",
        [((T, D), F32), ((SLOTS, width), BF), ((T, 128), F32), ((SLOTS, 1), F32)], 2 * SLOTS * T * D,
    )(*args)


def combine_kernel(middle, routed, spread, slot, *refs):
    mix = spread[...].astype(F32) * slot[...]
    high, low = split_two(mix)
    rows = routed[...]
    hidden = middle[...] + dot(high, rows, ((0,), (0,))) + dot(low, rows, ((0,), (0,)))
    if len(refs) == 1:
        refs[0][...] = hidden
        return
    mixers, hidden_out, normed_out, gains_out, router, sem = refs
    copy = pltpu.make_async_copy(mixers.at[:, pl.ds(WR, COLS - WR)], router, sem)
    copy.start()
    hidden_out[...] = hidden
    copy.wait()
    gains = gain_rows(router[...])
    gains_out[...] = gains
    normed_out[...] = (unit_rows(hidden)[0] * gains[0:1]).astype(BF)


def combine(middle, routed, spread, slot):
    return plain(combine_kernel, "add_expert_outputs", [((T, D), F32)], 4 * SLOTS * T * D)(
        middle, routed, spread, slot
    )[0]


def combine_next(middle, routed, spread, slot, mixers):
    return plain(
        combine_kernel, "add_expert_outputs_and_norm",
        [((T, D), F32), ((T, D), BF), ((8, D), F32)], 4 * SLOTS * T * D,
        ins=[VM] * 4 + [ANY],
        scratch=[pltpu.VMEM((D, COLS - WR), BF), pltpu.SemaphoreType.DMA],
    )(middle, routed, spread, slot, mixers)


def back_through_norm(inputs, gain, grad_normed, grad_residual):
    unit, scale = unit_rows(inputs)
    grad_gain = jnp.sum(grad_normed * unit, axis=0, keepdims=True)
    grad_unit = grad_normed * gain
    back = grad_unit - unit * jnp.mean(grad_unit * unit, axis=-1, keepdims=True)
    return grad_residual + scale * back, grad_gain


def pre_back_kernel(
    dx, shares, middle, gains, grad, spread, gates, middle_out, out_out, routing_out, gain_out
):
    table = spread[...]
    if shares is None:
        share = dx[:, D : D + 1].astype(F32) + dx[:, D + 1 : D + 2].astype(F32)
    else:
        share = shares[...]
    high, low = split_two(jnp.where(slot_columns(), share, 0.0))
    dense = dot(table, high, ((0,), (0,))) + dot(table, low, ((0,), (0,)))
    routing = dense - gates[...] * jnp.sum(dense, axis=-1, keepdims=True)
    routing_out[...] = routing.astype(BF)
    grad_normed = dot(table, dx[:, :D], ((0,), (0,)))
    grad_middle, grad_gain = back_through_norm(
        middle[...], gains[1:2], grad_normed, grad[...].astype(F32)
    )
    middle_out[...] = grad_middle
    out_out[...] = grad_middle.astype(BF)
    gain_out[...] = grad_gain


def pre_back(dx, shares, *args):
    outs = [((T, D), F32), ((T, D), BF), ((T, 128), BF), ((1, D), F32)]
    if shares is None:
        return plain(
            lambda dx, *refs: pre_back_kernel(dx, None, *refs), "back_to_middle", outs,
            2 * SLOTS * T * D,
        )(dx, *args)
    return plain(pre_back_kernel, "back_to_middle", outs, 2 * SLOTS * T * D)(dx, shares, *args)


def post_back_kernel(own, other, hidden, gains, grad_middle, gain_two, *refs):
    grad_normed = own[...] + other[...].astype(F32)
    grad, gain_one = back_through_norm(
        hidden[...].astype(F32), gains[0:1], grad_normed, grad_middle[...]
    )
    if len(refs) == 2:
        grad_out, rows_out = refs
    else:
        spread, slot, routed, grad_out, rows_out, dy_out, share_out = refs
        high, low = split_two(grad)
        slots = dot(spread[...], high) + dot(spread[...], low)
        dy_out[...] = (slot[...] * slots).astype(BF)
        share = jnp.sum(routed[...].astype(F32) * slots, axis=-1, keepdims=True)
        share_out[...] = slot[...] * share
    grad_out[...] = grad
    rows_out[...] = jnp.zeros((16, D), BF)
    for n, gain in enumerate((gain_one, gain_two[...])):
        high, low = split_two(gain)
        rows_out[2 * n : 2 * n + 1] = high
        rows_out[2 * n + 1 : 2 * n + 2] = low


def post_back(*args):
    outs = [((T, D), F32), ((16, D), BF)]
    if len(args) > 6:
        outs += [((SLOTS, D), BF), ((SLOTS, 1), F32)]
    return plain(post_back_kernel, "back_to_hidden", outs, 4 * SLOTS * T * D)(*args)


def products_kernel(
    normed, grads_own, grads_other, heads, att, routing, gains,
    first_out, second_out, third_out, grads,
):
    step = pl.program_id(0)

    @pl.when(step == 0)
    def _():
        grads[:T] = grads_own[...]
        grads[T:] = grads_other[...]

    def product(left, right):
        return dot(left, right, ((0,), (0,)))

    def pair(ref, start, stop):
        return jnp.concatenate([ref[0, :, start:stop], ref[1, :, start:stop]], axis=0)

    block = pl.ds(pl.multiple_of(step * (D // 4), 128), D // 4)
    def store(out, value):
        out[0] = value.reshape(4, 4, 24, value.shape[1]).astype(BF)

    left, turned = normed[:, block], grads[:, block]
    number, column = rows_of((16, 128)), columns((16, 128))
    gain_place = ((number < 2) & (column == E)) | (
        (number >= 2) & (number < 4) & (column == E + 1)
    )
    store(first_out, product(left, pair(heads, 0, 768)))
    store(second_out, product(turned, pair(att, 0, 768)))
    third = [
        product(left, pair(heads, 768, WO)),
        product(left[:T], routing[...]) + product(gains[:, block], gain_place.astype(BF)),
    ]
    store(third_out, jnp.concatenate(third, axis=1))


def mixer_products(normed, grads_own, grads_other, heads, att, routing, gains):
    def whole(v):
        zeros = (0,) * len(v.shape)
        return pl.BlockSpec(v.shape, lambda i: zeros, pipeline_mode=pl.Buffered(1))

    args = [normed, grads_own, grads_other, heads, att, routing, gains]
    return pl.pallas_call(
        products_kernel,
        name="mixer_products",
        grid=(4,),
        out_shape=[jax.ShapeDtypeStruct((4, 4, 4, 24, width), BF) for width in PARTS],
        in_specs=[whole(v) for v in args],
        out_specs=[
            pl.BlockSpec((1, 4, 4, 24, width), lambda i: (i, 0, 0, 0, 0)) for width in PARTS
        ],
        scratch_shapes=[pltpu.VMEM((2 * T, D), BF)],
        compiler_params=pltpu.CompilerParams(vmem_limit_bytes=58 << 20),
        cost_estimate=pl.CostEstimate(
            flops=2 * 2 * T * D * COLS, bytes_accessed=11000000, transcendentals=0
        ),
    )(*args)


def turn(rows, cosine, sine):
    return rows * cosine + pltpu.roll(rows, HD // 2, 1) * sine


def head_rows(ref, sequence, heads):
    return jnp.concatenate([ref[sequence, :, h * HD : (h + 1) * HD] for h in heads], axis=0)


def weigh(queries, keys, mask):
    raw = dot(queries, keys, ((1,), (1,))).reshape(6, T, T)
    logits = jnp.where(mask[None] > 0, raw * SCALE, -1e30)
    terms = jnp.exp(logits - jnp.max(logits, axis=-1, keepdims=True))
    return (terms / jnp.sum(terms, axis=-1, keepdims=True)).reshape(6 * T, T)


PIECES = (pl.ds(WR, COLS - WR), pl.ds(0, WO), pl.ds(WO, WR - WO))


class Several:
    def __init__(self, copies):
        self.copies = copies
        for copy in copies:
            copy.start()

    def wait(self):
        for copy in self.copies:
            copy.wait()


def fetch_weights(mixers, weights, sem):
    groups = []
    for n, place in enumerate(PIECES):
        rows = [pl.ds(i * (D // 4), D // 4) for i in range(4)]
        groups.append(
            Several(
                [
                    pltpu.make_async_copy(
                        mixers.at[r, place], weights.at[r, place], sem.at[n * 4 + i]
                    )
                    for i, r in enumerate(rows)
                ]
            )
        )
    return groups


def attend_kernel(first, own, other, mixers, cosine, sine, mask, *refs):
    *refs, weights, sem = refs
    both, heads_out, att_out, own_out, other_out, routing_out = refs[:6]
    copies = fetch_weights(mixers, weights, sem)
    if first:
        units = [unit_rows(v[...].astype(F32))[0] for v in (own, other)]
        copies[0].wait()
        gains = gain_rows(weights[:, WR:])
        refs[6][...] = gains
        both[:T] = (units[0] * gains[0:1]).astype(BF)
        both[T:] = (units[1] * gains[0:1]).astype(BF)
    else:
        both[:T] = own[...]
        both[T:] = other[...]
        copies[0].wait()
    turns = [jnp.concatenate([t[...], t[...]], axis=0) for t in (cosine, sine)]
    copies[1].wait()
    for tile in range(4):
        wide = dot(both[...], weights[:, tile * 256 : (tile + 1) * 256])
        for part in range(2):
            head = tile * 2 + part
            rows = wide[:, part * HD : (part + 1) * HD]
            if head < 7:
                rows = turn(rows, *turns)
            rows = rows.astype(BF)
            for s in range(2):
                heads_out[s, :, head * HD : (head + 1) * HD] = rows[s * T : (s + 1) * T]
    for s in range(2):
        probs = weigh(head_rows(heads_out, s, range(6)), heads_out[s, :, 768:896], mask[s])
        mixed = dot(probs.astype(BF), heads_out[s, :, 896:]).astype(BF)
        for h in range(6):
            att_out[s, :, h * HD : (h + 1) * HD] = mixed[h * T : (h + 1) * T]
    copies[2].wait()
    att = att_out[...].reshape(2 * T, 768)
    for tile in range(6):
        place = slice(tile * 256, (tile + 1) * 256)
        rows = dot(att, weights[place, WO:WR], ((1,), (1,)))
        own_out[:, place] = rows[:T]
        other_out[:, place] = rows[T:].astype(BF)
    routing_out[...] = dot(both[:T], weights[:, WR:])


def attend(first, own, other, mixers, cosine, sine, mask):
    outs = [
        ((2 * T, D), BF), ((2, T, WO), BF), ((2, T, WR - WO), BF), ((T, D), F32), ((T, D), BF),
        ((T, 128), F32),
    ]
    return plain(
        lambda *refs: attend_kernel(first, *refs), "attention_forward",
        outs + [((8, D), F32)] * first, 1700000000, 9000000,
        ins=[VM, VM, ANY, VM, VM, VM],
        scratch=[pltpu.VMEM((D, COLS), BF), pltpu.SemaphoreType.DMA((12,))],
    )(own, other, mixers, cosine, sine, mask)


def attend_back_kernel(
    own, other, routing, mixers, heads, cosine, sine, mask,
    grad_heads, own_out, other_out, both, grad_att, weights, sem,
):
    copies = fetch_weights(mixers, weights, sem)
    both[:T] = own[...]
    both[T:] = other[...]
    copies[2].wait()
    for tile in range(3):
        place = slice(tile * 256, (tile + 1) * 256)
        wide = dot(both[...], weights[:, WO + tile * 256 : WO + (tile + 1) * 256]).astype(BF)
        for s in range(2):
            grad_att[s, :, place] = wide[s * T : (s + 1) * T]
    cos, sin = cosine[...], -sine[...]
    for s in range(2):
        queries, grads = head_rows(heads, s, range(6)), head_rows(grad_att, s, range(6))
        keys, values = heads[s, :, 768:896], heads[s, :, 896:]
        probs = weigh(queries, keys, mask[s])
        dp = dot(grads, values, ((1,), (1,)))
        draw = probs * (dp - jnp.sum(probs * dp, axis=-1, keepdims=True))
        draw = (draw * SCALE).astype(BF)
        dq = dot(draw, keys)
        for h in range(6):
            rows = turn(dq[h * T : (h + 1) * T], cos, sin)
            grad_heads[s, :, h * HD : (h + 1) * HD] = rows.astype(BF)
        dk = dot(draw, queries, ((0,), (0,)))
        grad_heads[s, :, 768:896] = turn(dk, cos, sin).astype(BF)
        grad_heads[s, :, 896:] = dot(probs.astype(BF), grads, ((0,), (0,))).astype(BF)
    copies[0].wait()
    copies[1].wait()
    wide = grad_heads[...].reshape(2 * T, 1024)
    for tile in range(6):
        place = slice(tile * 256, (tile + 1) * 256)
        rows = dot(wide, weights[place, :WO], ((1,), (1,)))
        own_out[:, place] = rows[:T] + dot(routing[...], weights[place, WR:], ((1,), (1,)))
        other_out[:, place] = rows[T:].astype(BF)


def attend_back(own, other, routing, mixers, heads, cosine, sine, mask):
    return pl.pallas_call(
        attend_back_kernel,
        name="attention_backward",
        out_shape=(
            jax.ShapeDtypeStruct((2, T, 1024), BF),
            jax.ShapeDtypeStruct((T, D), F32),
            jax.ShapeDtypeStruct((T, D), BF),
        ),
        in_specs=[VM, VM, VM, ANY, VM, VM, VM, VM],
        out_specs=[VM] * 3,
        scratch_shapes=[
            pltpu.VMEM((2 * T, D), BF),
            pltpu.VMEM((2, T, 768), BF),
            pltpu.VMEM((D, COLS), BF),
            pltpu.SemaphoreType.DMA((12,)),
        ],
        compiler_params=pltpu.CompilerParams(vmem_limit_bytes=VMEM),
        cost_estimate=pl.CostEstimate(flops=2200000000, bytes_accessed=9000000, transcendentals=200000),
    )(own, other, routing, mixers, heads, cosine, sine, mask)

class Exchange:
    def __init__(self, rows, held, result, back, sems, also=()):
        (self.x, self.z, self.y, self.core), self.along = neighbours()
        self.rows, self.held, self.result, self.back = rows, held, result, back
        self.sems, self.local = sems[:4], sems[4]
        self.me = self.index(self.z, self.y, self.core)
        greet([self.peer(k, 1) for k in range(1, E)] + [self.along(0, o) for o in also])

    def index(self, z, y, core):
        return (z * 4 + y) * 2 + core

    def peer(self, k, sign):
        a, b, c = k // 8, k // 2 % 4, k % 2
        return (
            self.x,
            lax.rem(self.z + (a * sign) % 4, 4),
            lax.rem(self.y + (b * sign) % 4, 4),
            lax.rem(self.core + c, 2),
        )

    def copy(self, k, returning):
        peer = self.peer(k, -1 if returning else 1)
        there = self.index(*peer[1:])
        source, target = (self.result, self.back) if returning else (self.rows, self.held)
        sems = self.sems[2:] if returning else self.sems[:2]
        return pltpu.make_async_remote_copy(
            source.at[there], target.at[self.me], sems[0].at[k], sems[1].at[k],
            device_id=peer, device_id_type=MESH,
        )

    def start(self):
        for pair in ((2, 0), (1, 3)):
            for n in range(8):
                for a in pair:
                    if a * 8 + n:
                        self.copy(a * 8 + n, False).start()
        self.own = pltpu.make_async_copy(
            self.rows.at[self.me], self.held.at[self.me], self.local.at[0]
        )
        self.own.start()

    def arrive(self, a):
        for k in range(a * 8, a * 8 + 8):
            if k:
                self.copy(k, False).wait_recv()
        if a == 0:
            self.own.wait()
        block = lax.rem(self.z + (-a) % 4, 4)
        rows = self.held[pl.ds(block * 8, 8)].astype(F32)
        return block, rows.reshape(8 * C, rows.shape[2]).astype(BF)

    def give(self, a, block, value):
        width = value.shape[1]
        self.result[pl.ds(block * 8, 8), :, :width] = value.reshape(8, C, width).astype(BF)

    def send_back(self, a):
        for k in range(a * 8, a * 8 + 8):
            if k:
                self.copy(k, True).start()
        if a == 0:
            self.last = pltpu.make_async_copy(
                self.result.at[self.me], self.back.at[self.me], self.local.at[1]
            )
            self.last.start()

    def finish(self):
        for k in range(1, E):
            self.copy(k, False).wait_send()
            self.copy(k, True).wait()
        self.last.wait()


GROUPS = (0, 2, 1, 3)


def start_weights(pieces, weights, sem):
    waits, matrix = [], 0
    for piece in pieces:
        count, several = piece.shape[:2]
        for m in range(several):
            copies = []
            for n in range(4):
                source = piece.at[n, m] if count == 4 else piece.at[0, m, pl.ds(n * 384, 384)]
                copies.append(
                    pltpu.make_async_copy(
                        source, weights.at[matrix, n], sem.at[matrix * 4 + n]
                    )
                )
                copies[n].start()
            waits.append(copies)
            matrix += 1

    def ready(m):
        for copy in waits[m]:
            copy.wait()

    return ready


def matrix_of(weights, m):
    return weights[m].reshape(D, FF)


def at_block(block):
    return pl.ds(pl.multiple_of(block * 8 * C, 8 * C), 8 * C)


def forward_phase_kernel(
    rows, gate_up, downs, ups, targets, back, flat_out, a_out, b_out, down_out, next_out, targets_out,
    held, result, weights, weight_sem, ring_send, ring_recv, target_send, target_recv, *sems,
):
    work = Exchange(rows, held, result, back, sems, (1, 3))
    work.start()
    send = sender(ring_send, ring_recv)
    x, local = work.x, work.local
    own = [
        pltpu.make_async_copy(downs.at[0, 0], weights.at[2, x], local.at[2]),
        pltpu.make_async_copy(ups.at[1, 0], next_out.at[0, x], local.at[3]),
        pltpu.make_async_copy(downs.at[1, 0], next_out.at[1, x], local.at[4]),
    ]
    for copy in own:
        copy.start()
    ring = ring_of(downs.at[0, 0], weights.at[2], x, work.along, send, 0)
    others = [
        ring_of(ups.at[1, 0], next_out.at[0], x, work.along, send, 6),
        ring_of(downs.at[1, 0], next_out.at[1], x, work.along, send, 12),
    ]
    ready = start_weights([gate_up], weights, weight_sem)
    ring[0]()
    for number, group in enumerate(GROUPS):
        block, got = work.arrive(group)
        place = at_block(block)
        flat_out[place] = got
        if number == 0:
            ready(0)
        a = dot(got, matrix_of(weights, 0))
        if number == 0:
            ready(1)
        b = dot(got, matrix_of(weights, 1))
        a_out[place] = a
        b_out[place] = b
        inner = (a * jax.nn.sigmoid(a) * b).astype(BF)
        if number == 0:
            ring[1]()
            own[0].wait()
        work.give(group, block, dot(inner, matrix_of(weights, 2), ((1,), (1,))))
        work.send_back(group)
    send = sender(target_send, target_recv)
    more = [
        send(targets.at[work.index(*peer[1:])], targets_out.at[work.me], k, peer)
        for k, peer in ((k, work.peer(k, 1)) for k in range(1, E))
    ]
    kept = [
        pltpu.make_async_copy(weights.at[2], down_out.at[0], local.at[2]),
        pltpu.make_async_copy(targets.at[work.me], targets_out.at[work.me], local.at[5]),
    ]
    for copy in kept:
        copy.start()
    others[0][0]()
    others[1][0]()
    for other, copy in zip(others, own[1:]):
        other[1]()
        copy.wait()
    work.finish()
    for copy in more + kept:
        copy.wait()


def inner_gradients(a, b, dy, weights, place, held):
    du = dot(dy, matrix_of(weights, 2))
    sig = jax.nn.sigmoid(a)
    act = a * sig
    inner = (act * b).astype(BF)
    da = (du * b * sig * (1.0 + a * (1.0 - sig))).astype(BF)
    db = (du * act).astype(BF)
    for ref, value in zip(held, (da, db, inner)):
        ref[place] = value
    dx = dot(da, matrix_of(weights, 0), ((1,), (1,)))
    return inner, dx + dot(db, matrix_of(weights, 1), ((1,), (1,)))


def weight_gradients(rows, dy, held, outs):
    @pl.loop(0, 4)
    def _(n):
        columns = pl.ds(pl.multiple_of(n * 384, 128), 384)
        place = pl.ds(pl.multiple_of(n * 384, 128), 384)
        for left, right, out in zip((rows, rows, dy), held, outs):
            out[place] = dot(left[:, columns], right[...], ((0,), (0,))).astype(BF)


def back_phase_kernel(
    rows, a_in, b_in, flat_in, gate_up, down, parts, back, gate_out, up_out, down_out, sum_out,
    held, result, weights, a, b, flat, dy, da, db, inner, got_parts, weight_sem, load_sem,
    part_send, part_recv, *sems,
):
    work = Exchange(rows, held, result, back, sems, (1, 2, 3))
    work.start()
    send = sender(part_send, part_recv)
    others = [
        send(parts.at[lax.rem(work.x + o, 4)], got_parts.at[o], o - 1, work.along(0, o))
        for o in (1, 3, 2)
    ]
    mine = pltpu.make_async_copy(parts.at[work.x], got_parts.at[0], work.local.at[2])
    mine.start()
    ready = start_weights([gate_up, down], weights, weight_sem)
    loads = []
    for n, (src, dst) in enumerate(((a_in, a), (b_in, b), (flat_in, flat))):
        loads.append(pltpu.make_async_copy(src, dst, load_sem.at[n]))
        loads[n].start()
    for number, group in enumerate(GROUPS):
        block, got = work.arrive(group)
        place = at_block(block)
        dy[place] = got
        if number == 0:
            loads[0].wait()
            loads[1].wait()
            for m in range(3):
                ready(m)
        _, dx = inner_gradients(a[place], b[place], got, weights, place, (da, db, inner))
        work.give(group, block, dx)
        work.send_back(group)
    loads[2].wait()
    weight_gradients(flat, dy, (da, db, inner), (gate_out, up_out, down_out))
    for copy in others + [mine]:
        copy.wait()
    total = got_parts[0].astype(F32) + got_parts[1].astype(F32)
    total = total + got_parts[2].astype(F32) + got_parts[3].astype(F32)
    sum_out[...] = total.astype(BF)
    work.finish()


def both_phase_kernel(
    rows, target_in, gate_up, down, back, y_out, gate_out, up_out, down_out,
    held, result, weights, target, flat, dy, da, db, inner, weight_sem, load_sem, *sems,
):
    work = Exchange(rows, held, result, back, sems)
    work.start()
    ready = start_weights([gate_up, down], weights, weight_sem)
    load = pltpu.make_async_copy(target_in, target, load_sem)
    load.start()
    for number, group in enumerate(GROUPS):
        block, got = work.arrive(group)
        place = at_block(block)
        normed = got[:, :D]
        flat[place] = normed
        gate = got[:, D : D + 1].astype(F32) + got[:, D + 1 : D + 2].astype(F32)
        if number == 0:
            load.wait()
            for m in range(3):
                ready(m)
        grads = (gate * target[place].astype(F32)).astype(BF)
        dy[place] = grads
        a = dot(normed, matrix_of(weights, 0))
        b = dot(normed, matrix_of(weights, 1))
        mixed, dx = inner_gradients(a, b, grads, weights, place, (da, db, inner))
        y = dot(mixed, matrix_of(weights, 2), ((1,), (1,))).astype(BF)
        y_out[place] = y
        share = jnp.sum(y.astype(F32) * grads.astype(F32), axis=-1, keepdims=True)
        parts = two_columns(share).astype(F32)
        work.give(group, block, jnp.concatenate([dx, parts], axis=1))
        work.send_back(group)
    weight_gradients(flat, dy, (da, db, inner), (gate_out, up_out, down_out))
    work.finish()


def phase_call(kernel, name, number, args, outs, scratch, width, flops):
    slots = (E, C, width)
    return pl.pallas_call(
        kernel,
        name=name,
        out_shape=[jax.ShapeDtypeStruct(slots, BF)]
        + [jax.ShapeDtypeStruct(shape, kind) for shape, kind, _ in outs],
        in_specs=[ANY] * len(args),
        out_specs=[ANY] + [spec for *_, spec in outs],
        scratch_shapes=[
            pltpu.VMEM(slots, BF), pltpu.VMEM(slots, BF), pltpu.VMEM((3, 4, D // 4, FF), BF)
        ]
        + scratch
        + [pltpu.SemaphoreType.DMA((E,))] * 4
        + [pltpu.SemaphoreType.DMA((6,))],
        compiler_params=pltpu.CompilerParams(
            collective_id=number, has_side_effects=True, vmem_limit_bytes=52 << 20
        ),
        cost_estimate=pl.CostEstimate(
            flops=flops, bytes_accessed=20000000, transcendentals=SLOTS * FF
        ),
    )(*args)


UNIT = 2 * SLOTS * D * FF
GRADS = [((D, FF), BF, VM)] * 3


def forward_phase(rows, gate_up, downs, ups, targets):
    shard = (1, 4, D // 4, FF)
    back, flat, a, b, down, after, targets = phase_call(
        forward_phase_kernel, "expert_phase_forward", 3, (rows.reshape(E, C, D), gate_up, downs, ups, targets.reshape(E, C, D)),
        [((SLOTS, D), BF, VM), ((SLOTS, FF), F32, VM), ((SLOTS, FF), F32, VM), (shard, BF, ANY),
         ((2, 4, D // 4, FF), BF, ANY), ((E, C, D), BF, ANY)],
        [pltpu.SemaphoreType.DMA((count,)) for count in (8, 18, 18, E, E)],
        D, 3 * UNIT,
    )
    down, after = down.reshape(1, 1, D, FF), after.reshape(1, 2, D, FF)
    return back.reshape(SLOTS, D), flat, a, b, down, after, targets.reshape(SLOTS, D)


def matrices(*widths):
    return [pltpu.VMEM((SLOTS, width), BF) for width in widths]


def back_phase(rows, a, b, flat, gate_up, down, parts):
    back, *grads, total = phase_call(
        back_phase_kernel, "expert_phase_backward", 5,
        (rows.reshape(E, C, D), a, b, flat, gate_up, down, parts.reshape(4, D // 4, FF)),
        GRADS + [((D // 4, FF), BF, VM)],
        [pltpu.VMEM((SLOTS, FF), F32)] * 2 + matrices(D, D, FF, FF, FF)
        + [pltpu.VMEM((4, D // 4, FF), BF)]
        + [pltpu.SemaphoreType.DMA((count,)) for count in (12, 3, 3, 3)],
        D, 6 * UNIT,
    )
    return back.reshape(SLOTS, D), grads, total


def both_phase(rows, target, gate_up, down):
    back, y, *grads = phase_call(
        both_phase_kernel, "expert_phase_both", 4,
        (rows.reshape(E, C, WIDE), target, gate_up, down), [((SLOTS, D), BF, VM)] + GRADS,
        matrices(D, D, D, FF, FF, FF)
        + [pltpu.SemaphoreType.DMA((12,)), pltpu.SemaphoreType.DMA],
        WIDE, 9 * UNIT,
    )
    return back.reshape(SLOTS, WIDE), y, grads


def exchange(rows):
    width = rows.shape[1]
    rows = rows.reshape(E, C, width)
    rows = lax.all_to_all(rows, GROUP, split_axis=0, concat_axis=0, tiled=True)
    return rows.reshape(SLOTS, width)


def outputs_kernel(core, mine, theirs, *outs):
    for level in range(LAYERS):
        level_outputs(level, core[0] == 0, mine, theirs, *outs)


def level_outputs(level, first, mine, theirs, q_out, k_out, v_out, o_out, routing_out):

    def rows(ref, group):
        group = level * 3 + group
        return jnp.where(first, ref[group, :12], ref[group, 12:])

    halves = []
    for ref in (mine, theirs):
        a, b, c = (rows(ref, group) for group in range(3))
        halves.append(
            (
                a, c[:, :HD], c[:, HD : 2 * HD], b, c[:, 2 * HD : 3 * HD],
            )
        )
    for out, own, other in zip((q_out, k_out, v_out, o_out), *halves):
        width = own.shape[1]
        out[:, level, :width] = jnp.where(first, own, other)
        out[:, level, width:] = jnp.where(first, other, own)
    routing_out[:, level, :] = halves[0][4] + halves[1][4]


def mixer_outputs(sums, core):
    widths = (D, 2 * HD, 2 * HD, D, HD)
    *outs, routing = pl.pallas_call(
        outputs_kernel,
        name="mixer_outputs",
        out_shape=[jax.ShapeDtypeStruct((12, LAYERS, width), F32) for width in widths],
        grid=(1,),
        in_specs=[pl.BlockSpec(memory_space=pltpu.SMEM)]
        + [pl.BlockSpec((6, 24, PARTS[0]), lambda i: (0, 0, 0))] * 2,
        out_specs=[pl.BlockSpec((12, LAYERS, width), lambda i: (0, 0, 0)) for width in widths],
    )(core.reshape(1), sums, swap(sums))
    *outs, routing = [v.transpose(1, 0, 2) for v in (*outs, routing)]
    return (*outs, routing[:, :, :E], routing[:, :, E], routing[:, :, E + 1])


def expert_outputs_kernel(*refs):
    for matrix in range(3):
        for level in range(LAYERS):
            refs[6 + matrix][level, 0] = refs[level * 3 + matrix][...].astype(F32)


def expert_outputs(sums):
    rows = 96
    return pl.pallas_call(
        expert_outputs_kernel,
        name="expert_outputs",
        grid=(D // 4 // rows,),
        out_shape=[jax.ShapeDtypeStruct((LAYERS, 1, D // 4, FF), F32)] * 3,
        in_specs=[pl.BlockSpec((rows, FF), lambda i: (i, 0))] * 6,
        out_specs=[pl.BlockSpec((LAYERS, 1, rows, FF), lambda i: (0, 0, i, 0))] * 3,
        compiler_params=pltpu.CompilerParams(vmem_limit_bytes=58 << 20),
        cost_estimate=pl.CostEstimate(flops=0, bytes_accessed=11000000, transcendentals=0),
    )(*sums)


def reduce_expert(grads):
    return [
        lax.psum_scatter(g, "dp", scatter_dimension=0, tiled=True) for g in grads
    ]


def per_device(
    tokens, segments, route_ids, w_query, key_projection, value_projection, w_out, w_router,
    gain_attn, gain_moe, w_gate, w_up, w_down, cotangent,
):
    core = lax.axis_index("core")
    cosine, sine = rope_tables()
    position = jnp.arange(T)

    shared = jnp.concatenate(
        [
            w_router, gain_attn[:, :, None], gain_moe[:, :, None],
            jnp.zeros((LAYERS, 12, COLS - WR - E - 2), BF),
        ],
        axis=2,
    )

    def half(number):
        def cut(v):
            width = v.shape[2] // 2
            return v[:, :, number * width : (number + 1) * width]

        return jnp.concatenate(
            [cut(v) for v in (w_query, key_projection, value_projection, w_out)] + [shared], axis=2
        )

    halves = (half(0), half(1))
    mine = jnp.where(core == 0, halves[0], halves[1])
    theirs = swap(jnp.where(core == 0, halves[1], halves[0]))
    blocks = jnp.where(
        core == 0,
        jnp.concatenate([mine, theirs], axis=1),
        jnp.concatenate([theirs, mine], axis=1),
    )
    segment = segments.astype(F32)
    segment = jnp.concatenate([segment, swap(segment)])
    mask = (position[:, None] >= position[None, :])[None] & (
        segment[:, :, None] == segment[:, None, :]
    )
    mask = mask.astype(F32)

    *named, spread0, spread1 = route_tables(route_ids)
    spread = (spread0, spread1)
    targets = dot(spread[1], cotangent).astype(BF)
    tokens_other = swap(tokens)
    first_mixer, first_experts = gather(blocks, w_gate, w_up)
    second = lax.optimization_barrier((blocks[1], w_gate[1, 0], first_experts))
    second_mixer = lax.all_gather(second[0], AXES[:3], axis=0).reshape(D, COLS)
    second_experts = lax.all_gather(second[1], "dp", axis=0)

    normed0, heads0, att0, own, other, routing, gains0 = attend(
        True, tokens, tokens_other, first_mixer, cosine, sine, mask
    )
    middle0, send, gates0, slot0 = post(
        D, tokens, own, swap(other), gains0, routing, named[0], spread[0]
    )
    routed0, rows0, a0, b0, down0, up_down1, targets = forward_phase(
        send, first_experts, w_down, w_up, targets
    )
    hidden, normed, gains1 = combine_next(middle0, routed0, spread[0], slot0, second_mixer)

    normed1, heads1, att1, own, other, routing = attend(
        False, normed, swap(normed), second_mixer, cosine, sine, mask
    )
    middle1, send, gates1, slot1 = post(
        WIDE, hidden, own, swap(other), gains1, routing, named[1], spread[1]
    )
    gate1 = second_experts.reshape(4, 1, D // 4, FF)
    dx, produced, parts1 = both_phase(send, targets, gate1, up_down1)
    sums1 = reduce_expert(parts1[:2])
    routed1 = exchange(produced)

    grad_middle, grad_out, grad_routing, gain_two = pre_back(
        dx, None, middle1, gains1, cotangent, spread[1], gates1
    )
    grad_out_other = swap(grad_out)
    grad_heads, own, other = attend_back(
        grad_out, grad_out_other, grad_routing, second_mixer, heads1, cosine, sine, mask
    )
    grad, gain_parts, dy, shares = post_back(
        own, swap(other), hidden, gains1, grad_middle, gain_two, spread[0], slot0, routed0
    )
    products1 = mixer_products(
        normed1, grad_out, grad_out_other, grad_heads, att1, grad_routing, gain_parts
    )
    dx, parts0, last_sum = back_phase(
        dy, a0, b0, rows0, first_experts, down0, parts1[2]
    )
    sums0 = reduce_expert(parts0)
    dx, sums1, products1 = lax.optimization_barrier((dx, sums1, products1))

    grad_middle, grad_out, grad_routing, gain_two = pre_back(
        dx, shares, middle0, gains0, grad, spread[0], gates0
    )
    grad_out_other = swap(grad_out)
    grad_heads, own, other = attend_back(
        grad_out, grad_out_other, grad_routing, first_mixer, heads0, cosine, sine, mask
    )
    routed1 = lax.optimization_barrier((routed1, grad_heads))[0]
    output = combine(middle1, routed1, spread[1], slot1)
    grad_tokens, gain_parts = post_back(
        own, swap(other), tokens, gains0, grad_middle, gain_two
    )
    products0 = mixer_products(
        normed0, grad_out, grad_out_other, grad_heads, att0, grad_routing, gain_parts
    )
    mixer_out = mixer_outputs(reduce_mixer(products0 + products1), core)
    expert_out = expert_outputs([*sums0, *sums1, last_sum])
    return (output, grad_tokens, *mixer_out, *expert_out)


def solution(mesh):
    mesh = Mesh(mesh.devices.reshape(4, 4, 4, 2), AXES)
    rows = P(AXES, None)
    mixer = P(None, AXES, None)
    gain = P(None, AXES)
    expert = P(None, GROUP, "dp", None)
    return jax.shard_map(
        per_device,
        mesh=mesh,
        in_specs=(
            rows, rows, mixer, mixer, mixer, mixer, mixer, mixer, gain, gain, expert, expert,
            expert, rows,
        ),
        out_specs=(
            rows, rows, mixer, mixer, mixer, mixer, mixer, gain, gain, expert, expert, expert,
        ),
        check_vma=False,
    )
```

```python
import math

import jax
import jax.numpy as jnp
import numpy as np
from jax import lax
from jax.experimental import pallas as pl
from jax.experimental.pallas import tpu as pltpu
from jax.sharding import Mesh, PartitionSpec as P

MESH = pl.DeviceIdType.MESH
BF = jnp.bfloat16
F32 = jnp.float32
HEADS, KV, HD, TOP, LAYERS = 12, 2, 128, 4, 2
T, D, FF, E, C = 128, 1536, 768, 32, 24
SLOTS = E * C
THETA, EPS = 1000000.0, 1e-06
SCALE = 1.0 / math.sqrt(HD)
ANY = pl.BlockSpec(memory_space=pl.ANY)
VM = pl.BlockSpec(memory_space=pltpu.VMEM)
WO, WR, COLS = 1024, 1792, 1920
CUTS = (pl.ds(0, 1024), pl.ds(1024, COLS - 1024))
PARTS = (768, 768, 384)
VMEM = 32 << 20
WIDE = D + 128
AXES = ("dp", "z", "y", "core")
GROUP = AXES[1:]


def dot(a, b, dims=((1,), (0,))):
    return lax.dot_general(a, b, (dims, ((), ())), preferred_element_type=F32)


def split_two(v):
    high = v.astype(BF)
    return high, (v - high.astype(F32)).astype(BF)


def rope_tables():
    frequency = np.exp(-(2.0 * np.arange(HD // 2) / HD) * math.log(THETA)).astype(np.float32)
    angles = np.arange(T, dtype=np.float32)[:, None] * frequency[None, :]
    cosine, sine = np.cos(angles), np.sin(angles)
    return (
        jnp.asarray(np.concatenate([cosine, cosine], 1), F32),
        jnp.asarray(np.concatenate([-sine, sine], 1), F32),
    )


def swap(v):
    return lax.ppermute(v, "core", [(0, 1), (1, 0)])


def neighbours():
    here = [lax.axis_index(axis) for axis in AXES]

    def along(axis, places):
        peer = list(here)
        peer[axis] = lax.rem(here[axis] + places, 4)
        return tuple(peer)

    return here, along


def greet(peers):
    barrier = pltpu.get_barrier_semaphore()
    for peer in peers:
        pl.semaphore_signal(barrier, inc=1, device_id=peer, device_id_type=MESH)
    pl.semaphore_wait(barrier, len(peers))


def sender(send_sem, recv_sem):
    def send(src, dst, number, peer):
        copy = pltpu.make_async_remote_copy(
            src, dst, send_sem.at[number], recv_sem.at[number], device_id=peer, device_id_type=MESH
        )
        copy.start()
        return copy

    return send


def ring_steps(own, view, me, right, left, send, number):
    first = [
        send(own(0), view(me, 0), number, right), send(own(1), view(me, 1), number + 1, left)
    ]
    second = [
        send(own(1), view(me, 1), number + 2, right), send(own(0), view(me, 0), number + 3, left)
    ]

    relays = []

    def relay():
        before, after = lax.rem(me + 3, 4), lax.rem(me + 1, 4)
        first[0].wait_recv()
        relays.append(send(view(before, 0), view(before, 0), number + 4, right))
        first[1].wait_recv()
        relays.append(send(view(after, 1), view(after, 1), number + 5, left))

    def finish():
        for copy in second:
            copy.wait_recv()
        for copy in first + second:
            copy.wait_send()
        for copy in relays:
            copy.wait()

    return relay, finish


def ring_of(shard, out, x, along, send, number):
    return ring_steps(
        lambda half: shard.at[pl.ds(half * 192, 192)],
        lambda place, half: out.at[place, pl.ds(half * 192, 192)],
        x, along(0, 1), along(0, 3), send, number,
    )


def gather_kernel(blocks, gate, up, out, experts, local_sem, send_sem, recv_sem):
    (x, z, y, _), along = neighbours()
    greet([along(axis, o) for o in (1, 2, 3) for axis in range(3)])
    send = sender(send_sem, recv_sem)
    block = blocks.at[0]
    copies = [send(block, out.at[x, z, y], o - 1, along(0, o)) for o in (1, 3, 2)]
    shards = [gate.at[0, 0], up.at[0, 0]]
    rings = [
        ring_of(shard, experts.at[n], x, along, send, 27 + 6 * n) for n, shard in enumerate(shards)
    ]
    own = pltpu.make_async_copy(block, out.at[x, z, y], local_sem.at[0])
    own.start()
    own_experts = [
        pltpu.make_async_copy(shard, experts.at[n, x], local_sem.at[1 + n])
        for n, shard in enumerate(shards)
    ]
    for copy in own_experts:
        copy.start()
    own.wait()
    for copy in copies:
        copy.wait()

    def ring(view, axis, me, number):
        return ring_steps(
            lambda half: view(me, half), view, me, along(axis, 1), along(axis, 3), send, number
        )

    def pair(half):
        return pl.ds(half * 2, 2)

    first = ring(lambda n, half: out.at[pair(half), n, y, :, CUTS[0]], 1, z, 3)
    second = ring(lambda n, half: out.at[pair(half), z, n, :, CUTS[1]], 2, y, 9)
    first[0]()
    second[0]()
    first[1]()
    first = ring(lambda n, half: out.at[pair(half), :, n, :, CUTS[0]], 2, y, 15)
    second[1]()
    second = ring(lambda n, half: out.at[pair(half), n, :, :, CUTS[1]], 1, z, 21)
    rings[0][0]()
    first[0]()
    second[0]()
    rings[1][0]()
    first[1]()
    second[1]()
    for ring in rings:
        ring[1]()
    for copy in own_experts:
        copy.wait()


def gather(blocks, gate, up):
    mixer, experts = pl.pallas_call(
        gather_kernel,
        name="gather_weights",
        out_shape=(
            jax.ShapeDtypeStruct((4, 4, 4, 24, COLS), BF),
            jax.ShapeDtypeStruct((2, 4, D // 4, FF), BF),
        ),
        in_specs=[ANY] * 3,
        out_specs=(ANY, ANY),
        scratch_shapes=[
            pltpu.SemaphoreType.DMA((3,)),
            pltpu.SemaphoreType.DMA((39,)),
            pltpu.SemaphoreType.DMA((39,)),
        ],
        compiler_params=pltpu.CompilerParams(
            collective_id=1, has_side_effects=True, vmem_limit_bytes=VMEM
        ),
    )(blocks, gate, up)
    return mixer.reshape(D, COLS), experts.reshape(1, 2, D, FF)


def reduce_mixer_kernel(*refs):
    sources, out, scratch = refs[:6], refs[6], refs[7:]
    (x, z, y, _), along = neighbours()
    local_sem, send_sem, recv_sem = scratch[-3:]
    greet([along(axis, o) for o in (1, 2, 3) for axis in range(3)])
    send = sender(send_sem, recv_sem)
    here = (x, z, y)
    ways = ((1, 0, 2), (2, 1, 0), (0, 2, 1))
    jobs = []
    for level in reversed(range(LAYERS)):
        for group, way in enumerate(ways):
            number = level * 3 + group
            held = scratch[number * 10 : number * 10 + 10]
            jobs.append((number, sources[number], out.at[number], way, held))

    def pick(ref, dim, index, half=None):
        place = [slice(None)] * 3
        place[dim] = index
        if half is not None:
            place[1 if dim == 0 else 0] = half
        return ref.at[tuple(place)]

    def start_first(job):
        number, source, _, (axis, *_), (got, passed, relay, mine, own, *_) = job
        me = here[axis]
        right, left = along(axis, 1), along(axis, 3)
        after, far, before = (lax.rem(me + o, 4) for o in (1, 2, 3))
        low, high = pl.ds(0, 2), pl.ds(2, 2)
        base = number * 12
        copies = [
            send(pick(source, axis, far, low), passed.at[0], base, right),
            send(pick(source, axis, far, high), passed.at[1], base + 1, left),
            send(pick(source, axis, after, high), got.at[0, high], base + 2, right),
            send(pick(source, axis, before, low), got.at[1, low], base + 3, left),
        ]
        local = []
        for n, (src, dst) in enumerate(
            (
                (pick(source, axis, after, low), mine.at[0]),
                (pick(source, axis, before, high), mine.at[1]),
                (pick(source, axis, me), own),
            )
        ):
            local.append(pltpu.make_async_copy(src, dst, local_sem.at[number * 3 + n]))
            local[n].start()

        def pass_on():
            for n, (part, peer) in enumerate(((low, right), (high, left))):
                copies[n].wait()
                local[n].wait()
                total = mine[n].astype(F32) + passed[n].astype(F32)
                relay[n] = total.astype(BF)
                copies.append(send(relay.at[n], got.at[n, part], base + 4 + n, peer))

        def finish():
            for copy in copies[2:]:
                copy.wait()
            local[2].wait()

        return pass_on, finish

    def start_second(job):
        number, _, _, (gone, axis, _), (got, _, _, _, own, total, ready, after, *_) = job
        total[...] = own[...].astype(F32) + got[0].astype(F32) + got[1].astype(F32)
        started = []
        for o in (2, 1, 3):
            ready[o - 1] = sub(total, gone, axis, lax.rem(here[axis] + o, 4)).astype(BF)
            started.append(
                send(ready.at[o - 1], after.at[o - 1], number * 12 + 5 + o, along(axis, o))
            )
        return started

    def sub(total, gone, axis, index):
        first = axis == min(a for a in range(3) if a != gone)
        return total[index] if first else total[:, index]

    def start_third(job, copies):
        number, _, _, (gone, middle, axis), (*_, total, _, after, small, last) = job
        for copy in copies:
            copy.wait()
        rows = sub(total, gone, middle, here[middle])
        for o in range(3):
            rows = rows + after[o].astype(F32)
        small[...] = rows.astype(BF)
        started = [
            send(
                small.at[lax.rem(here[axis] + o, 4)], last.at[o - 1], number * 12 + 8 + o,
                along(axis, o),
            )
            for o in (2, 1, 3)
        ]
        return started

    def end(job, copies):
        _, _, out, (_, _, axis), (*_, small, last) = job
        for copy in copies:
            copy.wait()
        rows = small[here[axis]].astype(F32)
        for o in range(3):
            rows = rows + last[o].astype(F32)
        out[:, : rows.shape[1]] = rows

    running = [start_first(job) for job in jobs]
    for pass_on, _ in running:
        pass_on()
    seconds = []
    for job, (_, finish) in zip(jobs, running):
        finish()
        seconds.append(start_second(job))
    running = seconds
    running = [start_third(job, copies) for job, copies in zip(jobs, running)]
    for job, copies in zip(jobs, running):
        end(job, copies)


def reduce_mixer(products):
    scratch = []
    for n in range(len(products)):
        width = PARTS[n % 3]
        scratch += [
            pltpu.VMEM((2, 4, 4, 24, width), BF),
            pltpu.VMEM((2, 2, 4, 24, width), BF),
            pltpu.VMEM((2, 2, 4, 24, width), BF),
            pltpu.VMEM((2, 2, 4, 24, width), BF),
            pltpu.VMEM((4, 4, 24, width), BF),
            pltpu.VMEM((4, 4, 24, width), F32),
            pltpu.VMEM((3, 4, 24, width), BF),
            pltpu.VMEM((3, 4, 24, width), BF),
            pltpu.VMEM((4, 24, width), BF),
            pltpu.VMEM((3, 24, width), BF),
        ]
    return pl.pallas_call(
        reduce_mixer_kernel,
        name="reduce_mixer_gradients",
        out_shape=jax.ShapeDtypeStruct((6, 24, PARTS[0]), F32),
        in_specs=[ANY] * 6,
        out_specs=VM,
        scratch_shapes=scratch
        + [
            pltpu.SemaphoreType.DMA((18,)),
            pltpu.SemaphoreType.DMA((72,)),
            pltpu.SemaphoreType.DMA((72,)),
        ],
        compiler_params=pltpu.CompilerParams(
            collective_id=2, has_side_effects=True, vmem_limit_bytes=48 << 20
        ),
    )(*products)


def columns(shape):
    return lax.broadcasted_iota(jnp.int32, shape, 1)


def rows_of(shape):
    return lax.broadcasted_iota(jnp.int32, shape, 0)


def plain(kernel, name, outs, flops=0, bytes_accessed=4000000, ins=None, scratch=()):
    def call(*args):
        return pl.pallas_call(
            kernel,
            name=name,
            out_shape=[jax.ShapeDtypeStruct(shape, kind) for shape, kind in outs],
            in_specs=ins or [VM] * len(args),
            out_specs=[VM] * len(outs),
            scratch_shapes=list(scratch),
            compiler_params=pltpu.CompilerParams(vmem_limit_bytes=VMEM),
            cost_estimate=pl.CostEstimate(
                flops=flops, bytes_accessed=bytes_accessed, transcendentals=0
            ),
        )(*args)

    return call


def tables_kernel(routes, *outs):
    wide = (T, 128)
    earlier = (rows_of(wide) < columns(wide)).astype(BF)
    same = (rows_of(wide) == columns(wide)).astype(BF)
    for level in range(LAYERS):
        named = jnp.zeros(wide, F32)
        for k in range(TOP):
            named = named + (routes[level, :, k : k + 1] == columns(wide)).astype(F32)
        outs[level][...] = named
        turned = dot(named.astype(BF), same, ((0,), (0,)))[:E]
        rank = dot(named.astype(BF), earlier, ((0,), (0,)))[:E]
        place = lax.broadcasted_iota(jnp.int32, (E, C, T), 1).astype(F32)
        hit = jnp.where(rank[:, None, :] == place, turned[:, None, :], 0.0)
        outs[LAYERS + level][...] = hit.reshape(SLOTS, T).astype(BF)


def route_tables(routes):
    return plain(
        tables_kernel, "route_tables",
        [((T, 128), F32)] * LAYERS + [((SLOTS, T), BF)] * LAYERS,
    )(routes)


def unit_rows(rows):
    scale = lax.rsqrt(jnp.mean(rows * rows, axis=-1, keepdims=True) + EPS)
    return rows * scale, scale


def gain_rows(router):
    pick = (columns((8, 128)) == E + rows_of((8, 128))) & (rows_of((8, 128)) < 2)
    return dot(pick.astype(BF), router, ((1,), (1,)))


def slot_columns():
    shape = (SLOTS, 128)
    start = columns(shape) * C
    return (rows_of(shape) >= start) & (rows_of(shape) < start + C)


def post_kernel(
    hidden, own, other, gains, routing, named, spread, middle_out, send_out, gates_out, slot_out
):
    middle = hidden[...].astype(F32) + own[...] + other[...].astype(F32)
    middle_out[...] = middle
    normed = (unit_rows(middle)[0] * gains[1:2]).astype(BF)
    send_out[:, :D] = dot(spread[...], normed).astype(BF)
    masked = jnp.where(named[...] > 0, routing[...], -1e30)
    terms = jnp.exp(masked - jnp.max(masked, axis=-1, keepdims=True))
    terms = jnp.where(named[...] > 0, terms, 0.0)
    gates = terms / jnp.sum(terms, axis=-1, keepdims=True)
    gates_out[...] = gates
    high, low = split_two(gates)
    all_gates = dot(spread[...], high) + dot(spread[...], low)
    slot = jnp.sum(jnp.where(slot_columns(), all_gates, 0.0), axis=-1, keepdims=True)
    slot_out[...] = slot
    if send_out.shape[1] > D:
        send_out[:, D:] = two_columns(slot)


def two_columns(value):
    high = value.astype(BF).astype(F32)
    column = columns((value.shape[0], WIDE - D))
    return jnp.where(column == 0, high, jnp.where(column == 1, value - high, 0.0)).astype(BF)


def post(width, *args):
    return plain(
        post_kernel, "dispatch_rows_of_tokens",
        [((T, D), F32), ((SLOTS, width), BF), ((T, 128), F32), ((SLOTS, 1), F32)], 2 * SLOTS * T * D,
    )(*args)


def combine_kernel(middle, routed, spread, slot, *refs):
    mix = spread[...].astype(F32) * slot[...]
    high, low = split_two(mix)
    rows = routed[...]
    hidden = middle[...] + dot(high, rows, ((0,), (0,))) + dot(low, rows, ((0,), (0,)))
    if len(refs) == 1:
        refs[0][...] = hidden
        return
    mixers, hidden_out, normed_out, gains_out, router, sem = refs
    copy = pltpu.make_async_copy(mixers.at[:, pl.ds(WR, COLS - WR)], router, sem)
    copy.start()
    hidden_out[...] = hidden
    copy.wait()
    gains = gain_rows(router[...])
    gains_out[...] = gains
    normed_out[...] = (unit_rows(hidden)[0] * gains[0:1]).astype(BF)


def combine(middle, routed, spread, slot):
    return plain(combine_kernel, "add_expert_outputs", [((T, D), F32)], 4 * SLOTS * T * D)(
        middle, routed, spread, slot
    )[0]


def combine_next(middle, routed, spread, slot, mixers):
    return plain(
        combine_kernel, "add_expert_outputs_and_norm",
        [((T, D), F32), ((T, D), BF), ((8, D), F32)], 4 * SLOTS * T * D,
        ins=[VM] * 4 + [ANY],
        scratch=[pltpu.VMEM((D, COLS - WR), BF), pltpu.SemaphoreType.DMA],
    )(middle, routed, spread, slot, mixers)


def back_through_norm(inputs, gain, grad_normed, grad_residual):
    unit, scale = unit_rows(inputs)
    grad_gain = jnp.sum(grad_normed * unit, axis=0, keepdims=True)
    grad_unit = grad_normed * gain
    back = grad_unit - unit * jnp.mean(grad_unit * unit, axis=-1, keepdims=True)
    return grad_residual + scale * back, grad_gain


def pre_back_kernel(
    dx, shares, middle, gains, grad, spread, gates, middle_out, out_out, routing_out, gain_out
):
    table = spread[...]
    if shares is None:
        share = dx[:, D : D + 1].astype(F32) + dx[:, D + 1 : D + 2].astype(F32)
    else:
        share = shares[...]
    high, low = split_two(jnp.where(slot_columns(), share, 0.0))
    dense = dot(table, high, ((0,), (0,))) + dot(table, low, ((0,), (0,)))
    routing = dense - gates[...] * jnp.sum(dense, axis=-1, keepdims=True)
    routing_out[...] = routing.astype(BF)
    grad_normed = dot(table, dx[:, :D], ((0,), (0,)))
    grad_middle, grad_gain = back_through_norm(
        middle[...], gains[1:2], grad_normed, grad[...].astype(F32)
    )
    middle_out[...] = grad_middle
    out_out[...] = grad_middle.astype(BF)
    gain_out[...] = grad_gain


def pre_back(dx, shares, *args):
    outs = [((T, D), F32), ((T, D), BF), ((T, 128), BF), ((1, D), F32)]
    if shares is None:
        return plain(
            lambda dx, *refs: pre_back_kernel(dx, None, *refs), "back_to_middle", outs,
            2 * SLOTS * T * D,
        )(dx, *args)
    return plain(pre_back_kernel, "back_to_middle", outs, 2 * SLOTS * T * D)(dx, shares, *args)


def post_back_kernel(own, other, hidden, gains, grad_middle, gain_two, *refs):
    grad_normed = own[...] + other[...].astype(F32)
    grad, gain_one = back_through_norm(
        hidden[...].astype(F32), gains[0:1], grad_normed, grad_middle[...]
    )
    if len(refs) == 2:
        grad_out, rows_out = refs
    else:
        spread, slot, routed, grad_out, rows_out, dy_out, share_out = refs
        high, low = split_two(grad)
        slots = dot(spread[...], high) + dot(spread[...], low)
        dy_out[...] = (slot[...] * slots).astype(BF)
        share = jnp.sum(routed[...].astype(F32) * slots, axis=-1, keepdims=True)
        share_out[...] = slot[...] * share
    grad_out[...] = grad
    rows_out[...] = jnp.zeros((16, D), BF)
    for n, gain in enumerate((gain_one, gain_two[...])):
        high, low = split_two(gain)
        rows_out[2 * n : 2 * n + 1] = high
        rows_out[2 * n + 1 : 2 * n + 2] = low


def post_back(*args):
    outs = [((T, D), F32), ((16, D), BF)]
    if len(args) > 6:
        outs += [((SLOTS, D), BF), ((SLOTS, 1), F32)]
    return plain(post_back_kernel, "back_to_hidden", outs, 4 * SLOTS * T * D)(*args)


def products_kernel(
    normed, grads_own, grads_other, heads, att, routing, gains,
    first_out, second_out, third_out, grads,
):
    step = pl.program_id(0)

    @pl.when(step == 0)
    def _():
        grads[:T] = grads_own[...]
        grads[T:] = grads_other[...]

    def product(left, right):
        return dot(left, right, ((0,), (0,)))

    def pair(ref, start, stop):
        return jnp.concatenate([ref[0, :, start:stop], ref[1, :, start:stop]], axis=0)

    block = pl.ds(pl.multiple_of(step * (D // 4), 128), D // 4)
    def store(out, value):
        out[0] = value.reshape(4, 4, 24, value.shape[1]).astype(BF)

    left, turned = normed[:, block], grads[:, block]
    number, column = rows_of((16, 128)), columns((16, 128))
    gain_place = ((number < 2) & (column == E)) | (
        (number >= 2) & (number < 4) & (column == E + 1)
    )
    store(first_out, product(left, pair(heads, 0, 768)))
    store(second_out, product(turned, pair(att, 0, 768)))
    third = [
        product(left, pair(heads, 768, WO)),
        product(left[:T], routing[...]) + product(gains[:, block], gain_place.astype(BF)),
    ]
    store(third_out, jnp.concatenate(third, axis=1))


def mixer_products(normed, grads_own, grads_other, heads, att, routing, gains):
    def whole(v):
        zeros = (0,) * len(v.shape)
        return pl.BlockSpec(v.shape, lambda i: zeros, pipeline_mode=pl.Buffered(1))

    args = [normed, grads_own, grads_other, heads, att, routing, gains]
    return pl.pallas_call(
        products_kernel,
        name="mixer_products",
        grid=(4,),
        out_shape=[jax.ShapeDtypeStruct((4, 4, 4, 24, width), BF) for width in PARTS],
        in_specs=[whole(v) for v in args],
        out_specs=[
            pl.BlockSpec((1, 4, 4, 24, width), lambda i: (i, 0, 0, 0, 0)) for width in PARTS
        ],
        scratch_shapes=[pltpu.VMEM((2 * T, D), BF)],
        compiler_params=pltpu.CompilerParams(vmem_limit_bytes=58 << 20),
        cost_estimate=pl.CostEstimate(
            flops=2 * 2 * T * D * COLS, bytes_accessed=11000000, transcendentals=0
        ),
    )(*args)


def turn(rows, cosine, sine):
    return rows * cosine + pltpu.roll(rows, HD // 2, 1) * sine


def head_rows(ref, sequence, heads):
    return jnp.concatenate([ref[sequence, :, h * HD : (h + 1) * HD] for h in heads], axis=0)


def weigh(queries, keys, mask):
    raw = dot(queries, keys, ((1,), (1,))).reshape(6, T, T)
    logits = jnp.where(mask[None] > 0, raw * SCALE, -1e30)
    terms = jnp.exp(logits - jnp.max(logits, axis=-1, keepdims=True))
    return (terms / jnp.sum(terms, axis=-1, keepdims=True)).reshape(6 * T, T)


PIECES = (pl.ds(WR, COLS - WR), pl.ds(0, WO), pl.ds(WO, WR - WO))


class Several:
    def __init__(self, copies):
        self.copies = copies
        for copy in copies:
            copy.start()

    def wait(self):
        for copy in self.copies:
            copy.wait()


def fetch_weights(mixers, weights, sem):
    groups = []
    for n, place in enumerate(PIECES):
        rows = [pl.ds(i * (D // 4), D // 4) for i in range(4)]
        groups.append(
            Several(
                [
                    pltpu.make_async_copy(
                        mixers.at[r, place], weights.at[r, place], sem.at[n * 4 + i]
                    )
                    for i, r in enumerate(rows)
                ]
            )
        )
    return groups


def attend_kernel(first, own, other, mixers, cosine, sine, mask, *refs):
    *refs, weights, sem = refs
    both, heads_out, att_out, own_out, other_out, routing_out = refs[:6]
    copies = fetch_weights(mixers, weights, sem)
    if first:
        units = [unit_rows(v[...].astype(F32))[0] for v in (own, other)]
        copies[0].wait()
        gains = gain_rows(weights[:, WR:])
        refs[6][...] = gains
        both[:T] = (units[0] * gains[0:1]).astype(BF)
        both[T:] = (units[1] * gains[0:1]).astype(BF)
    else:
        both[:T] = own[...]
        both[T:] = other[...]
        copies[0].wait()
    turns = [jnp.concatenate([t[...], t[...]], axis=0) for t in (cosine, sine)]
    copies[1].wait()
    for tile in range(4):
        wide = dot(both[...], weights[:, tile * 256 : (tile + 1) * 256])
        for part in range(2):
            head = tile * 2 + part
            rows = wide[:, part * HD : (part + 1) * HD]
            if head < 7:
                rows = turn(rows, *turns)
            rows = rows.astype(BF)
            for s in range(2):
                heads_out[s, :, head * HD : (head + 1) * HD] = rows[s * T : (s + 1) * T]
    for s in range(2):
        probs = weigh(head_rows(heads_out, s, range(6)), heads_out[s, :, 768:896], mask[s])
        mixed = dot(probs.astype(BF), heads_out[s, :, 896:]).astype(BF)
        for h in range(6):
            att_out[s, :, h * HD : (h + 1) * HD] = mixed[h * T : (h + 1) * T]
    copies[2].wait()
    att = att_out[...].reshape(2 * T, 768)
    for tile in range(6):
        place = slice(tile * 256, (tile + 1) * 256)
        rows = dot(att, weights[place, WO:WR], ((1,), (1,)))
        own_out[:, place] = rows[:T]
        other_out[:, place] = rows[T:].astype(BF)
    routing_out[...] = dot(both[:T], weights[:, WR:])


def attend(first, own, other, mixers, cosine, sine, mask):
    outs = [
        ((2 * T, D), BF), ((2, T, WO), BF), ((2, T, WR - WO), BF), ((T, D), F32), ((T, D), BF),
        ((T, 128), F32),
    ]
    return plain(
        lambda *refs: attend_kernel(first, *refs), "attention_forward",
        outs + [((8, D), F32)] * first, 1700000000, 9000000,
        ins=[VM, VM, ANY, VM, VM, VM],
        scratch=[pltpu.VMEM((D, COLS), BF), pltpu.SemaphoreType.DMA((12,))],
    )(own, other, mixers, cosine, sine, mask)


def attend_back_kernel(
    own, other, routing, mixers, heads, cosine, sine, mask,
    grad_heads, own_out, other_out, both, grad_att, weights, sem,
):
    copies = fetch_weights(mixers, weights, sem)
    both[:T] = own[...]
    both[T:] = other[...]
    copies[2].wait()
    for tile in range(3):
        place = slice(tile * 256, (tile + 1) * 256)
        wide = dot(both[...], weights[:, WO + tile * 256 : WO + (tile + 1) * 256]).astype(BF)
        for s in range(2):
            grad_att[s, :, place] = wide[s * T : (s + 1) * T]
    cos, sin = cosine[...], -sine[...]
    for s in range(2):
        queries, grads = head_rows(heads, s, range(6)), head_rows(grad_att, s, range(6))
        keys, values = heads[s, :, 768:896], heads[s, :, 896:]
        probs = weigh(queries, keys, mask[s])
        dp = dot(grads, values, ((1,), (1,)))
        draw = probs * (dp - jnp.sum(probs * dp, axis=-1, keepdims=True))
        draw = (draw * SCALE).astype(BF)
        dq = dot(draw, keys)
        for h in range(6):
            rows = turn(dq[h * T : (h + 1) * T], cos, sin)
            grad_heads[s, :, h * HD : (h + 1) * HD] = rows.astype(BF)
        dk = dot(draw, queries, ((0,), (0,)))
        grad_heads[s, :, 768:896] = turn(dk, cos, sin).astype(BF)
        grad_heads[s, :, 896:] = dot(probs.astype(BF), grads, ((0,), (0,))).astype(BF)
    copies[0].wait()
    copies[1].wait()
    wide = grad_heads[...].reshape(2 * T, 1024)
    for tile in range(6):
        place = slice(tile * 256, (tile + 1) * 256)
        rows = dot(wide, weights[place, :WO], ((1,), (1,)))
        own_out[:, place] = rows[:T] + dot(routing[...], weights[place, WR:], ((1,), (1,)))
        other_out[:, place] = rows[T:].astype(BF)


def attend_back(own, other, routing, mixers, heads, cosine, sine, mask):
    return pl.pallas_call(
        attend_back_kernel,
        name="attention_backward",
        out_shape=(
            jax.ShapeDtypeStruct((2, T, 1024), BF),
            jax.ShapeDtypeStruct((T, D), F32),
            jax.ShapeDtypeStruct((T, D), BF),
        ),
        in_specs=[VM, VM, VM, ANY, VM, VM, VM, VM],
        out_specs=[VM] * 3,
        scratch_shapes=[
            pltpu.VMEM((2 * T, D), BF),
            pltpu.VMEM((2, T, 768), BF),
            pltpu.VMEM((D, COLS), BF),
            pltpu.SemaphoreType.DMA((12,)),
        ],
        compiler_params=pltpu.CompilerParams(vmem_limit_bytes=VMEM),
        cost_estimate=pl.CostEstimate(flops=2200000000, bytes_accessed=9000000, transcendentals=200000),
    )(own, other, routing, mixers, heads, cosine, sine, mask)

class Exchange:
    def __init__(self, rows, held, result, back, sems, also=()):
        (self.x, self.z, self.y, self.core), self.along = neighbours()
        self.rows, self.held, self.result, self.back = rows, held, result, back
        self.sems, self.local = sems[:4], sems[4]
        self.me = self.index(self.z, self.y, self.core)
        greet([self.peer(k, 1) for k in range(1, E)] + [self.along(0, o) for o in also])

    def index(self, z, y, core):
        return (z * 4 + y) * 2 + core

    def peer(self, k, sign):
        a, b, c = k // 8, k // 2 % 4, k % 2
        return (
            self.x,
            lax.rem(self.z + (a * sign) % 4, 4),
            lax.rem(self.y + (b * sign) % 4, 4),
            lax.rem(self.core + c, 2),
        )

    def copy(self, k, returning):
        peer = self.peer(k, -1 if returning else 1)
        there = self.index(*peer[1:])
        source, target = (self.result, self.back) if returning else (self.rows, self.held)
        sems = self.sems[2:] if returning else self.sems[:2]
        return pltpu.make_async_remote_copy(
            source.at[there], target.at[self.me], sems[0].at[k], sems[1].at[k],
            device_id=peer, device_id_type=MESH,
        )

    def start(self):
        for pair in ((2, 0), (1, 3)):
            for n in range(8):
                for a in pair:
                    if a * 8 + n:
                        self.copy(a * 8 + n, False).start()
        self.own = pltpu.make_async_copy(
            self.rows.at[self.me], self.held.at[self.me], self.local.at[0]
        )
        self.own.start()

    def arrive(self, a):
        for k in range(a * 8, a * 8 + 8):
            if k:
                self.copy(k, False).wait_recv()
        if a == 0:
            self.own.wait()
        block = lax.rem(self.z + (-a) % 4, 4)
        rows = self.held[pl.ds(block * 8, 8)].astype(F32)
        return block, rows.reshape(8 * C, rows.shape[2]).astype(BF)

    def give(self, a, block, value):
        width = value.shape[1]
        self.result[pl.ds(block * 8, 8), :, :width] = value.reshape(8, C, width).astype(BF)

    def send_back(self, a):
        for k in range(a * 8, a * 8 + 8):
            if k:
                self.copy(k, True).start()
        if a == 0:
            self.last = pltpu.make_async_copy(
                self.result.at[self.me], self.back.at[self.me], self.local.at[1]
            )
            self.last.start()

    def finish(self):
        for k in range(1, E):
            self.copy(k, False).wait_send()
            self.copy(k, True).wait()
        self.last.wait()


GROUPS = (0, 2, 1, 3)


def start_weights(pieces, weights, sem):
    waits, matrix = [], 0
    for piece in pieces:
        count, several = piece.shape[:2]
        for m in range(several):
            copies = []
            for n in range(4):
                source = piece.at[n, m] if count == 4 else piece.at[0, m, pl.ds(n * 384, 384)]
                copies.append(
                    pltpu.make_async_copy(
                        source, weights.at[matrix, n], sem.at[matrix * 4 + n]
                    )
                )
                copies[n].start()
            waits.append(copies)
            matrix += 1

    def ready(m):
        for copy in waits[m]:
            copy.wait()

    return ready


def matrix_of(weights, m):
    return weights[m].reshape(D, FF)


def at_block(block):
    return pl.ds(pl.multiple_of(block * 8 * C, 8 * C), 8 * C)


def forward_phase_kernel(
    rows, gate_up, downs, ups, back, flat_out, a_out, b_out, down_out, next_out,
    held, result, weights, weight_sem, ring_send, ring_recv, *sems,
):
    work = Exchange(rows, held, result, back, sems, (1, 3))
    work.start()
    send = sender(ring_send, ring_recv)
    x, local = work.x, work.local
    own = [
        pltpu.make_async_copy(downs.at[0, 0], weights.at[2, x], local.at[2]),
        pltpu.make_async_copy(ups.at[1, 0], next_out.at[0, x], local.at[3]),
        pltpu.make_async_copy(downs.at[1, 0], next_out.at[1, x], local.at[4]),
    ]
    for copy in own:
        copy.start()
    ring = ring_of(downs.at[0, 0], weights.at[2], x, work.along, send, 0)
    others = [
        ring_of(ups.at[1, 0], next_out.at[0], x, work.along, send, 6),
        ring_of(downs.at[1, 0], next_out.at[1], x, work.along, send, 12),
    ]
    ready = start_weights([gate_up], weights, weight_sem)
    ring[0]()
    for number, group in enumerate(GROUPS):
        block, got = work.arrive(group)
        place = at_block(block)
        flat_out[place] = got
        if number == 0:
            ready(0)
        a = dot(got, matrix_of(weights, 0))
        if number == 0:
            ready(1)
        b = dot(got, matrix_of(weights, 1))
        a_out[place] = a
        b_out[place] = b
        inner = (a * jax.nn.sigmoid(a) * b).astype(BF)
        if number == 0:
            ring[1]()
            own[0].wait()
        work.give(group, block, dot(inner, matrix_of(weights, 2), ((1,), (1,))))
        work.send_back(group)
    kept = pltpu.make_async_copy(weights.at[2], down_out.at[0], local.at[2])
    kept.start()
    others[0][0]()
    others[1][0]()
    for other, copy in zip(others, own[1:]):
        other[1]()
        copy.wait()
    work.finish()
    kept.wait()


def inner_gradients(a, b, dy, weights, place, held):
    du = dot(dy, matrix_of(weights, 2))
    sig = jax.nn.sigmoid(a)
    act = a * sig
    inner = (act * b).astype(BF)
    da = (du * b * sig * (1.0 + a * (1.0 - sig))).astype(BF)
    db = (du * act).astype(BF)
    for ref, value in zip(held, (da, db, inner)):
        ref[place] = value
    dx = dot(da, matrix_of(weights, 0), ((1,), (1,)))
    return inner, dx + dot(db, matrix_of(weights, 1), ((1,), (1,)))


def weight_gradients(rows, dy, held, outs):
    @pl.loop(0, 4)
    def _(n):
        columns = pl.ds(pl.multiple_of(n * 384, 128), 384)
        place = pl.ds(pl.multiple_of(n * 384, 128), 384)
        for left, right, out in zip((rows, rows, dy), held, outs):
            out[place] = dot(left[:, columns], right[...], ((0,), (0,))).astype(BF)


def back_phase_kernel(
    rows, a_in, b_in, flat_in, gate_up, down, parts, back, gate_out, up_out, down_out, sum_out,
    held, result, weights, a, b, flat, dy, da, db, inner, got_parts, weight_sem, load_sem,
    part_send, part_recv, *sems,
):
    work = Exchange(rows, held, result, back, sems, (1, 2, 3))
    work.start()
    send = sender(part_send, part_recv)
    others = [
        send(parts.at[lax.rem(work.x + o, 4)], got_parts.at[o], o - 1, work.along(0, o))
        for o in (1, 3, 2)
    ]
    mine = pltpu.make_async_copy(parts.at[work.x], got_parts.at[0], work.local.at[2])
    mine.start()
    ready = start_weights([gate_up, down], weights, weight_sem)
    loads = []
    for n, (src, dst) in enumerate(((a_in, a), (b_in, b), (flat_in, flat))):
        loads.append(pltpu.make_async_copy(src, dst, load_sem.at[n]))
        loads[n].start()
    for number, group in enumerate(GROUPS):
        block, got = work.arrive(group)
        place = at_block(block)
        dy[place] = got
        if number == 0:
            loads[0].wait()
            loads[1].wait()
            for m in range(3):
                ready(m)
        _, dx = inner_gradients(a[place], b[place], got, weights, place, (da, db, inner))
        work.give(group, block, dx)
        work.send_back(group)
    loads[2].wait()
    weight_gradients(flat, dy, (da, db, inner), (gate_out, up_out, down_out))
    for copy in others + [mine]:
        copy.wait()
    total = got_parts[0].astype(F32) + got_parts[1].astype(F32)
    total = total + got_parts[2].astype(F32) + got_parts[3].astype(F32)
    sum_out[...] = total.astype(BF)
    work.finish()


def both_phase_kernel(
    rows, target_low, target_high, gate_up, down, back, y_out, gate_out, up_out, down_out,
    held, result, weights, low, high, flat, dy, da, db, inner, weight_sem, load_sem, *sems,
):
    work = Exchange(rows, held, result, back, sems)
    work.start()
    ready = start_weights([gate_up, down], weights, weight_sem)
    loads = []
    for n, (src, dst) in enumerate(((target_low, low), (target_high, high))):
        loads.append(pltpu.make_async_copy(src, dst, load_sem.at[n]))
        loads[n].start()
    for number, group in enumerate(GROUPS):
        block, got = work.arrive(group)
        place = at_block(block)
        normed = got[:, :D]
        flat[place] = normed
        gate = got[:, D : D + 1].astype(F32) + got[:, D + 1 : D + 2].astype(F32)
        if number == 0:
            loads[0].wait()
            loads[1].wait()
            for m in range(3):
                ready(m)
        target = jnp.concatenate([low[place], high[place]], axis=1)
        grads = (gate * target.astype(F32)).astype(BF)
        dy[place] = grads
        a = dot(normed, matrix_of(weights, 0))
        b = dot(normed, matrix_of(weights, 1))
        mixed, dx = inner_gradients(a, b, grads, weights, place, (da, db, inner))
        y = dot(mixed, matrix_of(weights, 2), ((1,), (1,))).astype(BF)
        y_out[place] = y
        share = jnp.sum(y.astype(F32) * grads.astype(F32), axis=-1, keepdims=True)
        parts = two_columns(share).astype(F32)
        work.give(group, block, jnp.concatenate([dx, parts], axis=1))
        work.send_back(group)
    weight_gradients(flat, dy, (da, db, inner), (gate_out, up_out, down_out))
    work.finish()


def phase_call(kernel, name, number, args, outs, scratch, width, flops):
    slots = (E, C, width)
    return pl.pallas_call(
        kernel,
        name=name,
        out_shape=[jax.ShapeDtypeStruct(slots, BF)]
        + [jax.ShapeDtypeStruct(shape, kind) for shape, kind, _ in outs],
        in_specs=[ANY] * len(args),
        out_specs=[ANY] + [spec for *_, spec in outs],
        scratch_shapes=[
            pltpu.VMEM(slots, BF), pltpu.VMEM(slots, BF), pltpu.VMEM((3, 4, D // 4, FF), BF)
        ]
        + scratch
        + [pltpu.SemaphoreType.DMA((E,))] * 4
        + [pltpu.SemaphoreType.DMA((5,))],
        compiler_params=pltpu.CompilerParams(
            collective_id=number, has_side_effects=True, vmem_limit_bytes=52 << 20
        ),
        cost_estimate=pl.CostEstimate(
            flops=flops, bytes_accessed=20000000, transcendentals=SLOTS * FF
        ),
    )(*args)


UNIT = 2 * SLOTS * D * FF
GRADS = [((D, FF), BF, VM)] * 3


def forward_phase(rows, gate_up, downs, ups):
    shard = (1, 4, D // 4, FF)
    back, flat, a, b, down, after = phase_call(
        forward_phase_kernel, "expert_phase_forward", 3, (rows.reshape(E, C, D), gate_up, downs, ups),
        [((SLOTS, D), BF, VM), ((SLOTS, FF), F32, VM), ((SLOTS, FF), F32, VM), (shard, BF, ANY),
         ((2, 4, D // 4, FF), BF, ANY)],
        [pltpu.SemaphoreType.DMA((8,)), pltpu.SemaphoreType.DMA((18,)),
         pltpu.SemaphoreType.DMA((18,))],
        D, 3 * UNIT,
    )
    down, after = down.reshape(1, 1, D, FF), after.reshape(1, 2, D, FF)
    return back.reshape(SLOTS, D), flat, a, b, down, after


def matrices(*widths):
    return [pltpu.VMEM((SLOTS, width), BF) for width in widths]


def back_phase(rows, a, b, flat, gate_up, down, parts):
    back, *grads, total = phase_call(
        back_phase_kernel, "expert_phase_backward", 5,
        (rows.reshape(E, C, D), a, b, flat, gate_up, down, parts.reshape(4, D // 4, FF)),
        GRADS + [((D // 4, FF), BF, VM)],
        [pltpu.VMEM((SLOTS, FF), F32)] * 2 + matrices(D, D, FF, FF, FF)
        + [pltpu.VMEM((4, D // 4, FF), BF)]
        + [pltpu.SemaphoreType.DMA((count,)) for count in (12, 3, 3, 3)],
        D, 6 * UNIT,
    )
    return back.reshape(SLOTS, D), grads, total


def both_phase(rows, targets, gate_up, down):
    back, y, *grads = phase_call(
        both_phase_kernel, "expert_phase_both", 4,
        (rows.reshape(E, C, WIDE), *targets, gate_up, down), [((SLOTS, D), BF, VM)] + GRADS,
        matrices(FF, FF, D, D, FF, FF, FF)
        + [pltpu.SemaphoreType.DMA((12,)), pltpu.SemaphoreType.DMA((2,))],
        WIDE, 9 * UNIT,
    )
    return back.reshape(SLOTS, WIDE), y, grads


def exchange(rows):
    width = rows.shape[1]
    rows = rows.reshape(E, C, width)
    rows = lax.all_to_all(rows, GROUP, split_axis=0, concat_axis=0, tiled=True)
    return rows.reshape(SLOTS, width)


def outputs_kernel(core, mine, theirs, *outs):
    for level in range(LAYERS):
        level_outputs(level, core[0] == 0, mine, theirs, *outs)


def level_outputs(level, first, mine, theirs, q_out, k_out, v_out, o_out, routing_out):

    def rows(ref, group):
        group = level * 3 + group
        return jnp.where(first, ref[group, :12], ref[group, 12:])

    halves = []
    for ref in (mine, theirs):
        a, b, c = (rows(ref, group) for group in range(3))
        halves.append(
            (
                a, c[:, :HD], c[:, HD : 2 * HD], b, c[:, 2 * HD : 3 * HD],
            )
        )
    for out, own, other in zip((q_out, k_out, v_out, o_out), *halves):
        width = own.shape[1]
        out[:, level, :width] = jnp.where(first, own, other)
        out[:, level, width:] = jnp.where(first, other, own)
    routing_out[:, level, :] = halves[0][4] + halves[1][4]


def mixer_outputs(sums, core):
    widths = (D, 2 * HD, 2 * HD, D, HD)
    *outs, routing = pl.pallas_call(
        outputs_kernel,
        name="mixer_outputs",
        out_shape=[jax.ShapeDtypeStruct((12, LAYERS, width), F32) for width in widths],
        grid=(1,),
        in_specs=[pl.BlockSpec(memory_space=pltpu.SMEM)]
        + [pl.BlockSpec((6, 24, PARTS[0]), lambda i: (0, 0, 0))] * 2,
        out_specs=[pl.BlockSpec((12, LAYERS, width), lambda i: (0, 0, 0)) for width in widths],
    )(core.reshape(1), sums, swap(sums))
    *outs, routing = [v.transpose(1, 0, 2) for v in (*outs, routing)]
    return (*outs, routing[:, :, :E], routing[:, :, E], routing[:, :, E + 1])


def expert_outputs_kernel(*refs):
    for matrix in range(3):
        for level in range(LAYERS):
            refs[6 + matrix][level, 0] = refs[level * 3 + matrix][...].astype(F32)


def expert_outputs(sums):
    rows = 96
    return pl.pallas_call(
        expert_outputs_kernel,
        name="expert_outputs",
        grid=(D // 4 // rows,),
        out_shape=[jax.ShapeDtypeStruct((LAYERS, 1, D // 4, FF), F32)] * 3,
        in_specs=[pl.BlockSpec((rows, FF), lambda i: (i, 0))] * 6,
        out_specs=[pl.BlockSpec((LAYERS, 1, rows, FF), lambda i: (0, 0, i, 0))] * 3,
        compiler_params=pltpu.CompilerParams(vmem_limit_bytes=58 << 20),
        cost_estimate=pl.CostEstimate(flops=0, bytes_accessed=11000000, transcendentals=0),
    )(*sums)


def reduce_expert(grads):
    return [
        lax.psum_scatter(g, "dp", scatter_dimension=0, tiled=True) for g in grads
    ]


def per_device(
    tokens, segments, route_ids, w_query, key_projection, value_projection, w_out, w_router,
    gain_attn, gain_moe, w_gate, w_up, w_down, cotangent,
):
    core = lax.axis_index("core")
    cosine, sine = rope_tables()
    position = jnp.arange(T)

    shared = jnp.concatenate(
        [
            w_router, gain_attn[:, :, None], gain_moe[:, :, None],
            jnp.zeros((LAYERS, 12, COLS - WR - E - 2), BF),
        ],
        axis=2,
    )

    def half(number):
        def cut(v):
            width = v.shape[2] // 2
            return v[:, :, number * width : (number + 1) * width]

        return jnp.concatenate(
            [cut(v) for v in (w_query, key_projection, value_projection, w_out)] + [shared], axis=2
        )

    halves = (half(0), half(1))
    mine = jnp.where(core == 0, halves[0], halves[1])
    theirs = swap(jnp.where(core == 0, halves[1], halves[0]))
    blocks = jnp.where(
        core == 0,
        jnp.concatenate([mine, theirs], axis=1),
        jnp.concatenate([theirs, mine], axis=1),
    )
    segment = segments.astype(F32)
    segment = jnp.concatenate([segment, swap(segment)])
    mask = (position[:, None] >= position[None, :])[None] & (
        segment[:, :, None] == segment[:, None, :]
    )
    mask = mask.astype(F32)

    *named, spread0, spread1 = route_tables(route_ids)
    spread = (spread0, spread1)
    targets = [
        dot(spread[1], cotangent[:, half * 768 : (half + 1) * 768]).astype(BF) for half in range(2)
    ]
    tokens_other = swap(tokens)
    first_mixer, first_experts = gather(blocks, w_gate, w_up)
    second = lax.optimization_barrier((w_gate[1, 0], first_experts))
    second_mixer = lax.all_gather(blocks[1], AXES[:3], axis=0).reshape(D, COLS)
    second_experts = lax.all_gather(second[0], "dp", axis=0)

    targets[0], tokens_other, _ = lax.optimization_barrier((targets[0], tokens_other, first_mixer))
    targets[0] = exchange(targets[0])
    normed0, heads0, att0, own, other, routing, gains0 = attend(
        True, tokens, tokens_other, first_mixer, cosine, sine, mask
    )
    middle0, send, gates0, slot0 = post(
        D, tokens, own, swap(other), gains0, routing, named[0], spread[0]
    )
    send, targets[0] = lax.optimization_barrier((send, targets[0]))
    routed0, rows0, a0, b0, down0, up_down1 = forward_phase(
        send, first_experts, w_down, w_up
    )
    routed0, targets[1] = lax.optimization_barrier((routed0, targets[1]))
    targets[1] = exchange(targets[1])
    hidden, normed, gains1 = combine_next(middle0, routed0, spread[0], slot0, second_mixer)

    normed1, heads1, att1, own, other, routing = attend(
        False, normed, swap(normed), second_mixer, cosine, sine, mask
    )
    middle1, send, gates1, slot1 = post(
        WIDE, hidden, own, swap(other), gains1, routing, named[1], spread[1]
    )
    gate1 = second_experts.reshape(4, 1, D // 4, FF)
    dx, produced, parts1 = both_phase(send, targets, gate1, up_down1)
    sums1 = reduce_expert(parts1[:2])
    routed1 = exchange(produced)

    grad_middle, grad_out, grad_routing, gain_two = pre_back(
        dx, None, middle1, gains1, cotangent, spread[1], gates1
    )
    grad_out_other = swap(grad_out)
    grad_heads, own, other = attend_back(
        grad_out, grad_out_other, grad_routing, second_mixer, heads1, cosine, sine, mask
    )
    grad, gain_parts, dy, shares = post_back(
        own, swap(other), hidden, gains1, grad_middle, gain_two, spread[0], slot0, routed0
    )
    products1 = mixer_products(
        normed1, grad_out, grad_out_other, grad_heads, att1, grad_routing, gain_parts
    )
    dx, parts0, last_sum = back_phase(
        dy, a0, b0, rows0, first_experts, down0, parts1[2]
    )
    sums0 = reduce_expert(parts0)
    dx, sums1, products1 = lax.optimization_barrier((dx, sums1, products1))

    grad_middle, grad_out, grad_routing, gain_two = pre_back(
        dx, shares, middle0, gains0, grad, spread[0], gates0
    )
    grad_out_other = swap(grad_out)
    grad_heads, own, other = attend_back(
        grad_out, grad_out_other, grad_routing, first_mixer, heads0, cosine, sine, mask
    )
    routed1 = lax.optimization_barrier((routed1, grad_heads))[0]
    output = combine(middle1, routed1, spread[1], slot1)
    grad_tokens, gain_parts = post_back(
        own, swap(other), tokens, gains0, grad_middle, gain_two
    )
    products0 = mixer_products(
        normed0, grad_out, grad_out_other, grad_heads, att0, grad_routing, gain_parts
    )
    mixer_out = mixer_outputs(reduce_mixer(products0 + products1), core)
    expert_out = expert_outputs([*sums0, *sums1, last_sum])
    return (output, grad_tokens, *mixer_out, *expert_out)


def solution(mesh):
    mesh = Mesh(mesh.devices.reshape(4, 4, 4, 2), AXES)
    rows = P(AXES, None)
    mixer = P(None, AXES, None)
    gain = P(None, AXES)
    expert = P(None, GROUP, "dp", None)
    return jax.shard_map(
        per_device,
        mesh=mesh,
        in_specs=(
            rows, rows, mixer, mixer, mixer, mixer, mixer, mixer, gain, gain, expert, expert,
            expert, rows,
        ),
        out_specs=(
            rows, rows, mixer, mixer, mixer, mixer, mixer, gain, gain, expert, expert, expert,
        ),
        check_vma=False,
    )
```
